32 devices in a mesh: dp: 16 (over z, y, core), mp: 2 (over x).
Axes of the slice: x: 2, y: 2, z: 4, core: 2. Of those that a mesh axis runs over, the one named last changes fastest.
Arguments:
- tokens: bfloat16 [20480, 640], P('dp'), may hold values from -6 to 6
- cotangent: bfloat16 [20480, 640], P('dp'), may hold values from -6 to 6
- lengths: int32 [16, 5], P('dp'), may hold values from 1 to 1024, 1280 in all within a row
- owners: int32 [120], replicated, may hold values from 0 to 15, as said below
- weight_table: float32 [2, 240, 32, 640], P('mp', 'dp')
- moment_table: float32 [2, 240, 32, 640], P('mp', 'dp')
- square_table: float32 [2, 240, 32, 640], P('mp', 'dp')
- norm_params: float32 [6, 640], replicated
- norm_moment: float32 [6, 640], replicated
- norm_square: float32 [6, 640], replicated
- bias_params: float32 [2, 2240], P('mp'), may hold values from -1.2 to 1.2
- bias_moment: float32 [2, 2240], P('mp')
- bias_square: float32 [2, 2240], P('mp')
Outputs:
- block_out: float32 [20480, 640], P('dp')
- grad_tokens: float32 [20480, 640], P('dp')
- weights_next: float32 [2, 240, 32, 640], P('mp', 'dp')
- moments_next: float32 [2, 240, 32, 640], P('mp', 'dp')
- squares_next: float32 [2, 240, 32, 640], P('mp', 'dp')
- norms_next: float32 [6, 640], replicated
- norm_moments: float32 [6, 640], replicated
- norm_squares: float32 [6, 640], replicated
- biases_next: float32 [2, 2240], P('mp')
- bias_moments: float32 [2, 2240], P('mp')
- bias_squares: float32 [2, 2240], P('mp')
The draws below stay inside these ranges and needn't reach their ends.
Inputs may be any that keep to these rules, and one draw needn't show every extreme that they name: `owners`: no dp index owns more than 15 pieces, and one owns exactly 15. `lengths`: each row sums to 1280, and its longest sequence has exactly 1024 tokens.
All inputs are finite; a program needn't handle non-finite values.
Results may differ from the reference program's by a relative error of at most 0.012.
The reference program's roundings to bfloat16 on the way count: a program that leaves them out, or rounds other values in their place, can miss the bound.
Values may be sent and summed in bfloat16 or wider, within the bound.
No kernel may reach another device: no remote copies, remote signals or barrier semaphores. Data moves between devices by JAX's collectives and lax.ppermute only.
A program may use at most 320 MiB of HBM per device.

```python
import math
import jax
import jax.numpy as jnp
import numpy as np
from jax import lax

D = 640
HEADS = 20
HEAD_DIM = 32
FF = 2560
TOK_DEV = 1280
LONGEST = 1024
PR = 32
STEP = 10
DOCS = 5
TOKENS = 20480
HD_MP = 320
FF_MP = 1280
ROWS_MP = 3840
NPIECE = 120
CAP = 15
BIAS_MP = 2240
N_DP = 16
N_MP = 2


def owner_list(key):
    key = jax.random.fold_in(key, 101)
    first_key, second_key, third_key = jax.random.split(key, 3)
    slot_total = N_DP * CAP
    ranking = jax.random.permutation(first_key, slot_total).astype(jnp.int32)
    chosen = jax.random.randint(second_key, (), 0, N_DP)
    holders = jnp.arange(slot_total, dtype=jnp.int32) // CAP
    ranking = jnp.where(holders == chosen, ranking + slot_total, ranking)
    picked = lax.top_k(ranking, NPIECE)[1]
    shuffle = jax.random.permutation(third_key, NPIECE)
    return (picked[shuffle] // CAP).astype(jnp.int32)


def slot_kinds(key):
    owners = owner_list(key)
    piece_ids = jnp.arange(NPIECE, dtype=jnp.int32)
    earlier = (owners[None, :] == owners[:, None]) & (piece_ids[None, :] < piece_ids[:, None])
    placed = owners * CAP + jnp.sum(earlier.astype(jnp.int32), axis=1)
    landing = placed[None, :] == jnp.arange(N_DP * CAP, dtype=jnp.int32)[:, None]
    starts = piece_ids * PR
    piece_kind = (starts >= HD_MP).astype(jnp.int32) + (starts >= 2 * HD_MP).astype(jnp.int32) + (starts >= 3 * HD_MP).astype(jnp.int32) + (starts >= 4 * HD_MP).astype(jnp.int32) + (starts >= 4 * HD_MP + FF_MP).astype(jnp.int32)
    slot_kind = jnp.sum(jnp.where(landing, piece_kind[None, :], 0), axis=1)
    return jnp.where(jnp.any(landing, axis=1), slot_kind, 6)


def grad_scales():
    return jnp.array([1.0, 1.0, 1.0, 0.12, 0.3, 0.65, 1.0], jnp.float32) * math.sqrt(TOKENS)


def draw_owners(key, part):
    return owner_list(key)


def draw_weight_table(key, part):
    slot_kind = slot_kinds(key)
    key = jax.random.fold_in(key, 1)
    scales = jnp.array([1.22 / math.sqrt(D), 1.22 / math.sqrt(D), 1.0 / math.sqrt(D), math.sqrt(LONGEST / (16.0 * D)), 1.0 / math.sqrt(D), 1.0 / math.sqrt(FF), 1.0 / math.sqrt(D)], jnp.float32)[slot_kind]
    noise_vals = jax.random.normal(key, (N_MP, N_DP * CAP, PR, D), jnp.float32)
    return noise_vals * scales[None, :, None, None]


def draw_moment_table(key, part):
    slot_kind = slot_kinds(key)
    key = jax.random.fold_in(key, 2)
    scales = grad_scales()[slot_kind]
    noise_vals = jax.random.normal(key, (N_MP, N_DP * CAP, PR, D), jnp.float32)
    return noise_vals * scales[None, :, None, None]


def draw_square_table(key, part):
    slot_kind = slot_kinds(key)
    key = jax.random.fold_in(key, 3)
    scales = grad_scales()[slot_kind]
    factor = jnp.exp(jax.random.uniform(key, (N_MP, N_DP * CAP, PR, D), jnp.float32, 0.0, math.log(4.0)))
    return factor * (scales * scales)[None, :, None, None]


def draw_norm_params(key, part):
    key = jax.random.fold_in(key, 4)
    gain_key, shift_key = jax.random.split(key)
    gains = jax.random.uniform(gain_key, (6, D), jnp.float32, 0.6, 1.4)
    shifts = 0.2 * jax.random.normal(shift_key, (6, D), jnp.float32)
    is_gain = (jnp.arange(6) % 2 == 0) & (jnp.arange(6) < 4)
    return jnp.where(is_gain[:, None], gains, shifts)


def norm_scales():
    return jnp.array([1.5, 1.5, 0.6, 0.6, 1.2, 1.0], jnp.float32) * math.sqrt(TOKENS)


def norm_square_scales():
    return jnp.array([1.5, 1.5, 0.6, 1.2, 1.2, 1.0], jnp.float32) * math.sqrt(TOKENS)


def draw_norm_moment(key, part):
    key = jax.random.fold_in(key, 5)
    return jax.random.normal(key, (6, D), jnp.float32) * norm_scales()[:, None]


def draw_norm_square(key, part):
    key = jax.random.fold_in(key, 6)
    factor = jnp.exp(jax.random.uniform(key, (6, D), jnp.float32, 0.0, math.log(4.0)))
    scales = norm_square_scales()
    return factor * (scales * scales)[:, None]


def bias_scales():
    columns = jnp.arange(BIAS_MP)
    return jnp.where(columns < 3 * HD_MP, 1.0, 0.3).astype(jnp.float32) * math.sqrt(TOKENS)


def draw_bias_moment(key, part):
    key = jax.random.fold_in(key, 7)
    return jax.random.normal(key, (N_MP, BIAS_MP), jnp.float32) * bias_scales()[None, :]


def draw_bias_square(key, part):
    key = jax.random.fold_in(key, 8)
    factor = jnp.exp(jax.random.uniform(key, (N_MP, BIAS_MP), jnp.float32, 0.0, math.log(4.0)))
    scales = bias_scales()
    return factor * (scales * scales)[None, :]


def block_levels(rng, dims, cuts, least, high):
    loudness, own = 1.0, jax.random.fold_in(rng, 6)
    for axis_at, blocks in cuts:
        heights = jnp.exp(jax.random.uniform(jax.random.fold_in(own, axis_at), (blocks,), jnp.float32, least / len(cuts), high / len(cuts)))
        loudness = loudness * jnp.repeat(heights, dims[axis_at] // blocks).reshape([-1 if axis == axis_at else 1 for axis in range(len(dims))])
    return loudness


def split_up(count, total, limit, lean):
    loads = [(1 << 20) // math.isqrt(standing ** lean) + 1 for standing in range(2, count + 1)]
    spare, counts = total - limit - (count - 1), [1] * (count - 1)
    while spare > 0:
        candidates = [i for i in range(count - 1) if counts[i] < limit]
        whole, left = sum([loads[i] for i in candidates]), spare
        for i in candidates:
            extra = min(limit - counts[i], max(1, left * loads[i] // whole), spare)
            counts[i] = counts[i] + extra
            spare = spare - extra
    return np.array([limit] + counts)


def ragged(rng, count, total, bound, lean):
    if count == 2:
        one = jax.random.randint(rng, (), max(1, total - bound), min(bound, total - 1) + 1)
        return jnp.stack([one, total - one])
    sizes = jnp.asarray(split_up(count, total, bound, lean), jnp.int32)
    pairs = (count - 1) // 2
    giver, receiver = sizes[1:1 + 2 * pairs:2], sizes[2:2 + 2 * pairs:2]
    margin = jnp.minimum(giver - 1, bound - receiver)
    moved = jax.random.randint(jax.random.fold_in(rng, 1), (pairs,), 0, 1 << 20) % (margin + 1)
    sizes = sizes.at[1:1 + 2 * pairs:2].set(giver - moved).at[2:2 + 2 * pairs:2].set(receiver + moved)
    return sizes[jax.random.permutation(jax.random.fold_in(rng, 2), count)]


def bell_draw(stream_key, shape, spread, limit, cuts=(), kind=jnp.bfloat16):
    values = jax.random.normal(stream_key, shape, jnp.float32) * spread
    if len(cuts) > 0:
        values = block_levels(stream_key, shape, cuts, -0.22, 0.18) * values
    return jnp.clip(values, min=-limit, max=limit).astype(kind)


def setup_inputs(seed: int = 0) -> dict:
    keys = jax.random.split(jax.random.key(seed), 14)
    tokens = bell_draw(keys[0], (TOKENS, D), 1.0, 6.0, ((0, 16),))
    cotangent = bell_draw(keys[1], (TOKENS, D), 1.0, 6.0, ((0, 16),))
    lengths = jax.vmap(lambda own: ragged(own, DOCS, TOK_DEV, LONGEST, 1))(jax.random.split(keys[2], N_DP)).reshape((N_DP, DOCS)).astype(jnp.int32)
    owners = draw_owners(jax.random.fold_in(keys[13], 71), 0)
    weight_table = draw_weight_table(jax.random.fold_in(keys[13], 71), 0)
    moment_table = draw_moment_table(jax.random.fold_in(keys[13], 71), 0)
    square_table = draw_square_table(jax.random.fold_in(keys[13], 71), 0)
    norm_params = draw_norm_params(jax.random.fold_in(keys[13], 71), 0)
    norm_moment = draw_norm_moment(jax.random.fold_in(keys[13], 71), 0)
    norm_square = draw_norm_square(jax.random.fold_in(keys[13], 71), 0)
    bias_params = bell_draw(keys[10], (N_MP, BIAS_MP), 0.2, 1.2, ((0, 2),), jnp.float32)
    bias_moment = draw_bias_moment(jax.random.fold_in(keys[13], 71), 0)
    bias_square = draw_bias_square(jax.random.fold_in(keys[13], 71), 0)
    return dict(tokens=tokens, cotangent=cotangent, lengths=lengths, owners=owners, weight_table=weight_table, moment_table=moment_table, square_table=square_table, norm_params=norm_params, norm_moment=norm_moment, norm_square=norm_square, bias_params=bias_params, bias_moment=bias_moment, bias_square=bias_square)


HIGHEST_PREC = lax.Precision.HIGHEST
EPS_NORM = 1e-05
BETA_ONE = 0.5
BETA_TWO = 0.5
ADAM_EPS = 1e-08
DECAY_RATE = 0.01
NEG_FILL = -1e+30
NORM_RATES = (0.5, 0.1, 0.5, 0.1, 0.1, 0.1)
BIAS_RATE = 0.1

@jax.custom_vjp
def low(v):
    return lax.optimization_barrier(v.astype(jnp.bfloat16)).astype(jnp.float32)

@jax.custom_vjp
def low_back(v):
    return v

def low_keep(v):
    return (low(v), None)

def low_pass(kept, grad):
    return (grad,)

def back_keep(v):
    return (v, None)

def back_low(kept, grad):
    return (low(grad),)
low.defvjp(low_keep, low_pass)
low_back.defvjp(back_keep, back_low)

def layer_norm(values, gain_vec, shift_vec):
    centred = values - lax.optimization_barrier(jnp.mean(values, axis=-1, keepdims=True))
    spread_sq = lax.optimization_barrier(jnp.mean(centred * centred, axis=-1, keepdims=True))
    return centred * lax.rsqrt(spread_sq + EPS_NORM) * gain_vec + shift_vec

def rotate_half(values):
    half_dim = values.shape[-1] // 2
    return jnp.concatenate([-values[..., half_dim:], values[..., :half_dim]], axis=-1)

def rotary_tables(position, head_dim):
    frequency = 10000.0 ** (-(jnp.arange(0, head_dim, 2).astype(jnp.float32) / head_dim))
    angles = position.astype(jnp.float32)[:, None] * frequency[None, :]
    angles = jnp.concatenate([angles, angles], axis=-1)
    return (jnp.cos(angles), jnp.sin(angles))

def rotate(values, cos_tab, sin_tab):
    return values * cos_tab[:, None, :] + rotate_half(values) * sin_tab[:, None, :]

def document_layout(lengths, tok_count):
    doc_ends = jnp.cumsum(lengths).astype(jnp.int32)
    doc_starts = doc_ends - lengths
    places = jnp.arange(tok_count, dtype=jnp.int32)
    doc_index = lax.optimization_barrier(jnp.sum((places[:, None] >= doc_ends[None, :]).astype(jnp.int32), axis=1))
    numbers = jnp.arange(lengths.shape[0], dtype=jnp.int32)
    doc_begin = lax.optimization_barrier(jnp.sum(jnp.where(doc_index[:, None] == numbers[None, :], doc_starts[None, :], 0), axis=1))
    return (doc_index, places - doc_begin)

def slot_rows(owners, slot_cap):
    piece_ids = jnp.arange(owners.shape[0], dtype=jnp.int32)
    earlier = (owners[None, :] == owners[:, None]) & (piece_ids[None, :] < piece_ids[:, None])
    return (owners * slot_cap + lax.optimization_barrier(jnp.sum(earlier.astype(jnp.int32), axis=1))).astype(jnp.int32)

def piece_rates(piece_total, piece_rows, head_width, ffn_here):
    starts = jnp.arange(piece_total, dtype=jnp.int32) * piece_rows
    inner_rate = jnp.where(starts < 4 * head_width + ffn_here, 0.03, 0.015)
    return jnp.where(starts < 3 * head_width, 0.03, jnp.where(starts < 4 * head_width, 0.2, inner_rate)).astype(jnp.float32)

def adam_step(weights, first_mom, second_mom, gradient, rate_arr, decay_rate):
    first_new = BETA_ONE * first_mom + (1.0 - BETA_ONE) * gradient
    second_new = BETA_TWO * second_mom + (1.0 - BETA_TWO) * gradient * gradient
    first_fix = first_new / (1.0 - BETA_ONE ** STEP)
    second_fix = second_new / (1.0 - BETA_TWO ** STEP)
    weights_new = weights * (1.0 - rate_arr * decay_rate) - rate_arr * first_fix / (jnp.sqrt(second_fix) + ADAM_EPS)
    return (weights_new, first_new, second_new)

def split_weights(stacked):

    def columns(block_rows):
        return jnp.transpose(block_rows, (2, 0, 1)).reshape(D, -1)
    w_query = columns(stacked[:, 0:HD_MP])
    w_keys = columns(stacked[:, HD_MP:2 * HD_MP])
    w_values = columns(stacked[:, 2 * HD_MP:3 * HD_MP])
    w_out = stacked[:, 3 * HD_MP:4 * HD_MP].reshape(-1, D)
    w_up = columns(stacked[:, 4 * HD_MP:4 * HD_MP + FF_MP])
    w_down = stacked[:, 4 * HD_MP + FF_MP:].reshape(-1, D)
    return (w_query, w_keys, w_values, w_out, w_up, w_down)

def join_grads(grad_query, grad_keys, grad_values, grad_out, grad_up, grad_down):

    def rows_back(block_rows, col_count):
        return jnp.transpose(block_rows.reshape(D, N_MP, col_count), (1, 2, 0))
    return jnp.concatenate([rows_back(grad_query, HD_MP), rows_back(grad_keys, HD_MP), rows_back(grad_values, HD_MP), grad_out.reshape(N_MP, HD_MP, D), rows_back(grad_up, FF_MP), grad_down.reshape(N_MP, FF_MP, D)], axis=1)

def forward(tok_float, params, doc_sizes):
    w_query, w_keys, w_values, w_out, w_up, w_down, b_query, b_keys, b_values, b_up, norm_vals = params
    tok_count = tok_float.shape[0]
    head_width = HEADS * HEAD_DIM
    doc_index, position = document_layout(doc_sizes, tok_count)
    cos_tab, sin_tab = rotary_tables(position, HEAD_DIM)
    low_one = low(layer_norm(tok_float, norm_vals[0], norm_vals[1]))
    w_all = jnp.concatenate([w_query, w_keys, w_values], axis=1)
    b_all = jnp.concatenate([b_query, b_keys, b_values])
    qkv_full = low_back(jnp.dot(low_one, w_all, precision=HIGHEST_PREC) + b_all)
    queries = rotate(qkv_full[:, 0:head_width].reshape(tok_count, HEADS, HEAD_DIM), cos_tab, sin_tab)
    keys_rot = rotate(qkv_full[:, head_width:2 * head_width].reshape(tok_count, HEADS, HEAD_DIM), cos_tab, sin_tab)
    values_all = qkv_full[:, 2 * head_width:].reshape(tok_count, HEADS, HEAD_DIM)
    queries = low(queries)
    keys_rot = low(keys_rot)
    values_all = low(values_all)
    scores = low_back(jnp.einsum('qhd,khd->hqk', queries, keys_rot, precision=HIGHEST_PREC) * HEAD_DIM ** (-0.5))
    same_doc = doc_index[:, None] == doc_index[None, :]
    scores = jnp.where(same_doc[None], scores, NEG_FILL)
    prob_low = low(jax.nn.softmax(scores, axis=-1))
    context = jnp.einsum('hqk,khd->qhd', prob_low, values_all, precision=HIGHEST_PREC).reshape(tok_count, head_width)
    context = low(low_back(context))
    x_mid = tok_float + low_back(jnp.dot(context, w_out, precision=HIGHEST_PREC)) + norm_vals[4]
    low_two = low(layer_norm(x_mid, norm_vals[2], norm_vals[3]))
    pre_act = low_back(jnp.dot(low_two, w_up, precision=HIGHEST_PREC) + b_up)
    act_low = low(jax.nn.gelu(pre_act, approximate=False))
    return x_mid + low_back(jnp.dot(act_low, w_down, precision=HIGHEST_PREC)) + norm_vals[5]

def reference(tokens, cotangent, lengths, owners, weight_table, moment_table, square_table, norm_params, norm_moment, norm_square, bias_params, bias_moment, bias_square):
    piece_rows = slot_rows(owners, CAP)
    stacked = low(weight_table[:, piece_rows].reshape(N_MP, ROWS_MP, D))
    weights = split_weights(stacked)
    biases = (bias_params[:, 0:HD_MP].reshape(-1), bias_params[:, HD_MP:2 * HD_MP].reshape(-1), bias_params[:, 2 * HD_MP:3 * HD_MP].reshape(-1), bias_params[:, 3 * HD_MP:].reshape(-1))
    params = weights + biases + (norm_params,)
    zero_sums = jax.tree.map(jnp.zeros_like, params)
    inputs = (tokens.astype(jnp.float32).reshape(N_DP, TOK_DEV, D), cotangent.astype(jnp.float32).reshape(N_DP, TOK_DEV, D), lengths)

    def one_group(grad_sums, group_item):
        tok_float, grad_float, doc_sizes = group_item

        def run(tok_arg, param_arg):
            return forward(tok_arg, param_arg, doc_sizes)
        output, pullback = jax.vjp(run, tok_float, params)
        grad_in, grad_params = pullback(grad_float)
        return (jax.tree.map(jnp.add, grad_sums, grad_params), (output, grad_in))
    grad_sums, (outputs, grad_inputs) = lax.scan(one_group, zero_sums, inputs)
    pieces = join_grads(*grad_sums[0:6]).reshape(N_MP, NPIECE, PR, D)
    rate_grid = piece_rates(NPIECE, PR, HD_MP, FF_MP)[None, :, None, None]
    new_w, new_m, new_v = adam_step(weight_table[:, piece_rows], moment_table[:, piece_rows], square_table[:, piece_rows], pieces, rate_grid, DECAY_RATE)
    zero_table = jnp.zeros_like(weight_table)
    weights_next = zero_table.at[:, piece_rows].set(new_w)
    moments_next = zero_table.at[:, piece_rows].set(new_m)
    squares_next = zero_table.at[:, piece_rows].set(new_v)
    norm_rate = jnp.array(NORM_RATES, jnp.float32)[:, None]
    norms_next, norm_moments, norm_squares = adam_step(norm_params, norm_moment, norm_square, grad_sums[10], norm_rate, 0.0)
    bias_grad = jnp.concatenate([grad_sums[6].reshape(N_MP, HD_MP), grad_sums[7].reshape(N_MP, HD_MP), grad_sums[8].reshape(N_MP, HD_MP), grad_sums[9].reshape(N_MP, FF_MP)], axis=1)
    biases_next, bias_moments, bias_squares = adam_step(bias_params, bias_moment, bias_square, bias_grad, BIAS_RATE, 0.0)
    return (outputs.reshape(TOKENS, D), grad_inputs.reshape(TOKENS, D), weights_next, moments_next, squares_next, norms_next, norm_moments, norm_squares, biases_next, bias_moments, bias_squares)
```

```python
import functools

import jax
import jax.numpy as jnp
from jax import lax
from jax.experimental import pallas as pl
from jax.experimental.pallas import tpu as pltpu
from jax.sharding import PartitionSpec as P

HEADS = 20
HEAD_DIM = 32
HALF = HEAD_DIM // 2
FF = 2560
LONGEST = 1024
STEP = 10

EPS_NORM = 1e-05
BETA_ONE = 0.5
BETA_TWO = 0.5
ADAM_EPS = 1e-08
DECAY_RATE = 0.01
NEG_FILL = -1e30
NORM_RATES = (0.5, 0.1, 0.5, 0.1, 0.1, 0.1)
BIAS_RATE = 0.1
SCALE = HEAD_DIM**-0.5
SCALE_LOG2 = SCALE * 1.4426950408889634
SAFE_EXP = 100.0

BF = jnp.bfloat16
F32 = jnp.float32
I32 = jnp.int32
TILE = 256
LANES = 128
VMEM_LIMIT = 56 << 20


def params(*kinds):
    return pltpu.CompilerParams(dimension_semantics=kinds or None, vmem_limit_bytes=VMEM_LIMIT)


def cost(flops, moved):
    return pl.CostEstimate(flops=int(flops), bytes_accessed=int(moved), transcendentals=0)


def dot_nn(a, b):
    return lax.dot_general(a, b, (((1,), (0,)), ((), ())), preferred_element_type=F32)


def dot_nt(a, b):
    return lax.dot_general(a, b, (((1,), (1,)), ((), ())), preferred_element_type=F32)


def dot_tn(a, b):
    return lax.dot_general(a, b, (((0,), (0,)), ((), ())), preferred_element_type=F32)


def split_two(v):
    hi = v.astype(BF).astype(F32)
    return hi, v - hi


def split_three(v):
    hi = v.astype(BF).astype(F32)
    mid = (v - hi).astype(BF).astype(F32)
    return hi, mid, v - hi - mid


def normalized(v):
    centred = v - jnp.mean(v, axis=-1, keepdims=True)
    inv = lax.rsqrt(jnp.mean(centred * centred, axis=-1, keepdims=True) + EPS_NORM)
    return centred * inv, inv


def whole(shape):
    return pl.BlockSpec(shape, lambda *_: (0,) * len(shape))


def rows(width, tile=TILE):
    return pl.BlockSpec((tile, width), lambda t: (t, 0))


def cols(height, tile=TILE):
    return pl.BlockSpec((height, tile), lambda t: (0, t))


def shaped(shape, dtype):
    return jax.ShapeDtypeStruct(shape, dtype)


def qkv_kernel(x_ref, norm_ref, w_ref, b_ref, cos_ref, sin_ref, qkv_ref, a_ref):
    n1, _ = normalized(x_ref[...].astype(F32))
    a1 = (n1 * norm_ref[0:1] + norm_ref[1:2]).astype(BF)
    a_ref[...] = a1
    full = dot_nt(w_ref[...], a1) + b_ref[...]
    width = w_ref.shape[0] // 3
    cos, sin = cos_ref[...], sin_ref[...]
    for at in range(0, 2 * width, HEAD_DIM):
        lower, upper = full[at : at + HALF], full[at + HALF : at + HEAD_DIM]
        qkv_ref[at : at + HALF, :] = (lower * cos - upper * sin).astype(BF)
        qkv_ref[at + HALF : at + HEAD_DIM, :] = (upper * cos + lower * sin).astype(BF)
    qkv_ref[2 * width :, :] = full[2 * width :].astype(BF)


def qkv_call(x, norms, w_qkv, b_qkv, cos, sin):
    tok, width = x.shape
    out = w_qkv.shape[0]
    return pl.pallas_call(
        qkv_kernel,
        grid=(tok // TILE,),
        in_specs=[
            rows(width), whole(norms.shape), whole(w_qkv.shape), whole(b_qkv.shape),
            cols(HALF), cols(HALF),
        ],
        out_specs=[cols(out), rows(width)],
        out_shape=[shaped((out, tok), BF), shaped((tok, width), BF)],
        compiler_params=params("arbitrary"),
        cost_estimate=cost(2 * tok * width * out, 8e6),
        name="ln_qkv",
    )(x, norms, w_qkv, b_qkv, cos, sin)


def mlp_kernel(
    x_ref, gy_ref, ctx_a, ctx_b, wo_a, wo_b, up_ref, down_ref, bup_ref, norm_ref,
    x1_ref, a2_ref, act_ref, gpre_ref, ffn_ref, gh_ref, gbup_ref,
):
    gy = gy_ref[...]
    attn = dot_tn(ctx_a[...], wo_a[...]) + dot_tn(ctx_b[...], wo_b[...])
    x1 = x_ref[...].astype(F32) + attn + norm_ref[4:5]
    x1_ref[...] = x1
    n2, _ = normalized(x1)
    a2 = (n2 * norm_ref[2:3] + norm_ref[3:4]).astype(BF)
    a2_ref[...] = a2
    pre = dot_nt(a2, up_ref[...]) + bup_ref[...]
    cdf = 0.5 * (1.0 + lax.erf(pre * 0.7071067811865476))
    act = (pre * cdf).astype(BF)
    act_ref[...] = act
    slope = cdf + pre * (jnp.exp(-0.5 * pre * pre) * 0.3989422804014327)
    gpre = (slope * dot_nt(gy, down_ref[...])).astype(BF)
    gpre_ref[...] = gpre
    ffn_ref[...] = dot_nn(act, down_ref[...]).astype(BF)
    gh_ref[...] = dot_nn(gpre, up_ref[...]).astype(BF)
    part = jnp.sum(gpre.astype(F32), axis=0, keepdims=True)

    @pl.when(pl.program_id(0) == 0)
    def _():
        gbup_ref[...] = part

    @pl.when(pl.program_id(0) > 0)
    def _():
        gbup_ref[...] += part


def mlp_call(x, gy, ctx_a, ctx_b, wo_a, wo_b, w_up, w_down, b_up, norms):
    tok, width = x.shape
    hidden = w_up.shape[0]
    head = ctx_a.shape[0]
    return pl.pallas_call(
        mlp_kernel,
        grid=(tok // TILE,),
        in_specs=[
            rows(width), rows(width), cols(head), cols(head),
            whole(wo_a.shape), whole(wo_b.shape), whole(w_up.shape), whole(w_down.shape),
            whole(b_up.shape), whole(norms.shape),
        ],
        out_specs=[
            rows(width), rows(width), rows(hidden), rows(hidden), rows(width), rows(width),
            whole((1, hidden)),
        ],
        out_shape=[
            shaped((tok, width), F32), shaped((tok, width), BF), shaped((tok, hidden), BF),
            shaped((tok, hidden), BF), shaped((tok, width), BF), shaped((tok, width), BF),
            shaped((1, hidden), F32),
        ],
        compiler_params=params("arbitrary"),
        cost_estimate=cost(2 * tok * width * (hidden * 4 + 2 * head) * 1.6, 3e7),
        name="mlp",
    )(x, gy, ctx_a, ctx_b, wo_a, wo_b, w_up, w_down, b_up, norms)


def mlp_grads_kernel(act_ref, gpre_ref, a2_ref, gy_ref, down_ref, up_ref, down_sum, up_sum):
    step = pl.program_id(0)

    @pl.when(step == 0)
    def _():
        down_sum[...] = jnp.zeros_like(down_sum)
        up_sum[...] = jnp.zeros_like(up_sum)

    down_sum[...] += dot_tn(act_ref[...], gy_ref[...])
    up_sum[...] += dot_tn(gpre_ref[...], a2_ref[...])

    @pl.when(step == pl.num_programs(0) - 1)
    def _():
        down_ref[...] = down_sum[...].astype(BF)
        up_ref[...] = up_sum[...].astype(BF)


def mlp_grads_call(act, gpre, a2, gy):
    tok, hidden = act.shape
    width = a2.shape[1]
    return pl.pallas_call(
        mlp_grads_kernel,
        grid=(tok // TILE,),
        in_specs=[rows(hidden), rows(hidden), rows(width), rows(width)],
        out_specs=[whole((hidden, width))] * 2,
        out_shape=[shaped((hidden, width), BF)] * 2,
        scratch_shapes=[pltpu.VMEM((hidden, width), F32)] * 2,
        compiler_params=params("arbitrary"),
        cost_estimate=cost(4 * tok * width * hidden * 1.3, 1.4e7),
        name="mlp_grads",
    )(act, gpre, a2, gy)


def mid_kernel(
    x1_ref, gy_ref, gh_a, gh_b, ctx_ref, wo_ref, norm_ref,
    gx_ref, gctx_ref, go_ref, sum_ref, go_sum,
):
    step = pl.program_id(0)
    gy = gy_ref[...].astype(F32)
    gh = gh_a[...].astype(F32) + gh_b[...].astype(F32)
    n2, inv = normalized(x1_ref[...])
    e = gh * norm_ref[2:3]
    gx = gy + inv * (
        e - jnp.mean(e, axis=-1, keepdims=True) - n2 * jnp.mean(e * n2, axis=-1, keepdims=True)
    )
    gx_ref[...] = gx
    gm = gx.astype(BF)
    gctx_ref[...] = dot_nt(wo_ref[...], gm).astype(BF)
    sums = jnp.concatenate(
        [jnp.sum(v, axis=0, keepdims=True) for v in (gh * n2, gh, gx, gy)]
        + [jnp.zeros((4, gy.shape[1]), F32)],
        axis=0,
    )

    @pl.when(step == 0)
    def _():
        go_sum[...] = jnp.zeros_like(go_sum)
        sum_ref[...] = jnp.zeros_like(sum_ref)

    go_sum[...] += dot_nn(ctx_ref[...], gm)
    sum_ref[...] += sums

    @pl.when(step == pl.num_programs(0) - 1)
    def _():
        go_ref[...] = go_sum[...].astype(BF)


def mid_call(x1, gy, gh_a, gh_b, ctx, w_out, norms):
    tok, width = x1.shape
    head = ctx.shape[0]
    return pl.pallas_call(
        mid_kernel,
        grid=(tok // TILE,),
        in_specs=[
            rows(width), rows(width), rows(width), rows(width), cols(head),
            whole(w_out.shape), whole(norms.shape),
        ],
        out_specs=[rows(width), cols(head), whole((head, width)), whole((8, width))],
        out_shape=[
            shaped((tok, width), F32), shaped((head, tok), BF), shaped((head, width), BF),
            shaped((8, width), F32),
        ],
        scratch_shapes=[pltpu.VMEM((head, width), F32)],
        compiler_params=params("arbitrary"),
        cost_estimate=cost(4 * tok * width * head * 2, 1.5e7),
        name="mid_back",
    )(x1, gy, gh_a, gh_b, ctx, w_out, norms)


def in_grads_kernel(
    gq_ref, gk_ref, gv_ref, a1_ref, x_ref, w_ref, g_ref, gh_ref, gb_ref, sum_ref, g_sum,
):
    step = pl.program_id(0)
    parts = (gq_ref[...], gk_ref[...], gv_ref[...])
    head = parts[0].shape[0]

    @pl.when(step == 0)
    def _():
        g_sum[...] = jnp.zeros_like(g_sum)
        gb_ref[...] = jnp.zeros_like(gb_ref)
        sum_ref[...] = jnp.zeros_like(sum_ref)

    a1 = a1_ref[...]
    gh = None
    for at, part in enumerate(parts):
        here = pl.ds(at * head, head)
        g_sum[here, :] += dot_nn(part, a1)
        gb_ref[here, :] += jnp.sum(part.astype(F32), axis=1, keepdims=True)
        piece = dot_tn(part, w_ref[here, :])
        gh = piece if gh is None else gh + piece
    gh_ref[...] = gh.astype(BF)
    n1, _ = normalized(x_ref[...].astype(F32))
    sum_ref[...] += jnp.concatenate(
        [jnp.sum(gh * n1, axis=0, keepdims=True), jnp.sum(gh, axis=0, keepdims=True)]
        + [jnp.zeros((6, gh.shape[1]), F32)],
        axis=0,
    )

    @pl.when(step == pl.num_programs(0) - 1)
    def _():
        g_ref[...] = g_sum[...].astype(BF)


def in_grads_call(gq, gk, gv, a1, x, w_qkv):
    tok, width = a1.shape
    head = gq.shape[0]
    return pl.pallas_call(
        in_grads_kernel,
        grid=(tok // TILE,),
        in_specs=[cols(head)] * 3 + [rows(width), rows(width), whole(w_qkv.shape)],
        out_specs=[
            whole((3 * head, width)), rows(width), whole((3 * head, 1)), whole((8, width)),
        ],
        out_shape=[
            shaped((3 * head, width), BF), shaped((tok, width), BF), shaped((3 * head, 1), F32),
            shaped((8, width), F32),
        ],
        scratch_shapes=[pltpu.VMEM((3 * head, width), F32)],
        compiler_params=params("arbitrary"),
        cost_estimate=cost(12 * tok * width * head * 1.3, 1e7),
        name="in_grads",
    )(gq, gk, gv, a1, x, w_qkv)


def last_kernel(x_ref, gx_ref, gh_a, gh_b, norm_ref, out_ref):
    n1, inv = normalized(x_ref[...].astype(F32))
    e = (gh_a[...].astype(F32) + gh_b[...].astype(F32)) * norm_ref[0:1]
    out_ref[...] = gx_ref[...] + inv * (
        e - jnp.mean(e, axis=-1, keepdims=True) - n1 * jnp.mean(e * n1, axis=-1, keepdims=True)
    )


def last_call(x, gx, gh_a, gh_b, norms):
    tok, width = x.shape
    return pl.pallas_call(
        last_kernel,
        grid=(tok // TILE,),
        in_specs=[rows(width)] * 4 + [whole(norms.shape)],
        out_specs=rows(width),
        out_shape=shaped((tok, width), F32),
        compiler_params=params("arbitrary"),
        cost_estimate=cost(1e6, 1.2e7),
        name="last_back",
    )(x, gx, gh_a, gh_b, norms)


def attend_kernel(seg_row, seg_col, q_ref, k_ref, v_ref, ctx_ref, log_ref):
    tok = q_ref.shape[1]
    rest = tok - LONGEST
    qs = q_ref[...].astype(F32) * SCALE_LOG2
    hi, lo = split_two(qs)
    qx = jnp.transpose(jnp.concatenate([hi, lo], axis=0)).astype(BF)
    k_t = k_ref[...]
    kx = jnp.concatenate([k_t, k_t], axis=0)
    v_f = v_ref[...].astype(F32)
    vx = jnp.transpose(jnp.concatenate([v_f, jnp.ones((8, tok), F32)], axis=0)).astype(BF)
    k_f = k_t.astype(F32)
    q_top = jnp.max(jnp.sum(qs * qs, axis=0, keepdims=True))
    k_top = jnp.max(jnp.sum(k_f * k_f, axis=0, keepdims=True))
    safe = q_top * k_top < SAFE_EXP * SAFE_EXP
    same = seg_col[...] == seg_row[...]

    def finish(sums, shift, at, count):
        turned = jnp.transpose(sums)
        total = turned[HEAD_DIM : HEAD_DIM + 1]
        ctx_ref[:, at : at + count] = (turned[0:HEAD_DIM] / total).astype(BF)
        log_total = jnp.log2(total)
        if shift is not None:
            log_total = log_total + jnp.transpose(jnp.broadcast_to(shift, (count, LANES)))[0:1]
        log_ref[0, :, at : at + count] = log_total

    def run(exact):
        for at in range(0, LONGEST, TILE):
            scores = dot_nn(qx[at : at + TILE], kx[:, :LONGEST])
            shift = None
            if exact:
                shift = jnp.max(scores, axis=1, keepdims=True)
                scores = scores - shift
            finish(dot_nn(jnp.exp2(scores).astype(BF), vx[:LONGEST]), shift, at, TILE)
        if rest:
            scores = jnp.where(same, dot_nn(qx[LONGEST:], kx[:, LONGEST:]), NEG_FILL)
            shift = None
            if exact:
                shift = jnp.max(scores, axis=1, keepdims=True)
                scores = scores - shift
            finish(dot_nn(jnp.exp2(scores).astype(BF), vx[LONGEST:]), shift, LONGEST, rest)

    @pl.when(safe)
    def _():
        run(False)

    @pl.when(jnp.logical_not(safe))
    def _():
        run(True)


def attend_call(seg, qkv, first, count, heads):
    tok = qkv.shape[1]
    rest = seg.shape[0]

    def part(which):
        return pl.BlockSpec((HEAD_DIM, tok), lambda h: (which * heads + first + h, 0))

    return pl.pallas_call(
        attend_kernel,
        grid=(count,),
        in_specs=[whole((1, rest)), whole((rest, 1)), part(0), part(1), part(2)],
        out_specs=[
            pl.BlockSpec((HEAD_DIM, tok), lambda h: (h, 0)),
            pl.BlockSpec((1, 1, tok), lambda h: (h, 0, 0)),
        ],
        out_shape=[shaped((count * HEAD_DIM, tok), BF), shaped((count, 1, tok), F32)],
        compiler_params=params("arbitrary"),
        cost_estimate=cost(count * 2.5e9, 3e6),
        name="attend",
    )(seg[None, :], seg[:, None], qkv, qkv, qkv)


def attend_back_kernel(
    seg_row, seg_col, cos_ref, sin_ref, q_ref, k_ref, v_ref, g_ref, ctx_ref, log_ref,
    gq_ref, gk_ref, gv_ref,
):
    tok = q_ref.shape[1]
    rest = tok - LONGEST
    k_t = k_ref[...]
    q_f = q_ref[...].astype(F32)
    g_f = g_ref[...].astype(F32)
    hi, lo = split_two(q_f * SCALE_LOG2)
    weighted = jnp.sum(g_f * ctx_ref[...].astype(F32), axis=0, keepdims=True)
    pad = jnp.zeros((13, tok), F32)
    qx = jnp.concatenate([hi, lo, *split_three(log_ref[0]), pad], axis=0).astype(BF)
    minus = jnp.concatenate([jnp.full((3, tok), -1.0, F32), pad], axis=0)
    k_f = k_t.astype(F32)
    kx = jnp.transpose(jnp.concatenate([k_f, k_f, minus], axis=0)).astype(BF)
    gx = jnp.concatenate([g_f, *split_three(weighted), pad], axis=0).astype(BF)
    vx = jnp.transpose(jnp.concatenate([v_ref[...].astype(F32), minus], axis=0)).astype(BF)
    qn = jnp.transpose(q_f).astype(BF)
    gn = jnp.transpose(g_f).astype(BF)
    same = seg_col[...] == seg_row[...]

    def turn_back(ref, grad, at, count):
        cos, sin = cos_ref[:, at : at + count], sin_ref[:, at : at + count]
        lower, upper = grad[0:HALF] * SCALE, grad[HALF:] * SCALE
        ref[0:HALF, at : at + count] = (lower * cos + upper * sin).astype(BF)
        ref[HALF:, at : at + count] = (upper * cos - lower * sin).astype(BF)

    def block(k_at, k_count, q_at, q_count, mask):
        scores = dot_nn(kx[k_at : k_at + k_count], qx[:, q_at : q_at + q_count])
        if mask is not None:
            scores = jnp.where(mask, scores, NEG_FILL)
        prob = jnp.exp2(scores)
        grad_prob = dot_nn(vx[k_at : k_at + k_count], gx[:, q_at : q_at + q_count])
        grad_score = (prob * grad_prob).astype(BF)
        grad_v = dot_nn(prob.astype(BF), gn[q_at : q_at + q_count])
        grad_k = dot_nn(grad_score, qn[q_at : q_at + q_count])
        gv_ref[:, k_at : k_at + k_count] = jnp.transpose(grad_v).astype(BF)
        turn_back(gk_ref, jnp.transpose(grad_k), k_at, k_count)
        return dot_nn(k_t[:, k_at : k_at + k_count], grad_score)

    grad_q = None
    for at in range(0, LONGEST, TILE):
        piece = block(at, TILE, 0, LONGEST, None)
        grad_q = piece if grad_q is None else grad_q + piece
    turn_back(gq_ref, grad_q, 0, LONGEST)
    if rest:
        turn_back(gq_ref, block(LONGEST, rest, LONGEST, rest, same), LONGEST, rest)


def attend_back_call(seg, cos, sin, qkv, g_ctx, ctx, logs, heads):
    tok = qkv.shape[1]
    rest = seg.shape[0]

    def part(which):
        return pl.BlockSpec((HEAD_DIM, tok), lambda h: (which * heads + h, 0))

    table = whole((HALF, tok))
    return pl.pallas_call(
        attend_back_kernel,
        grid=(heads,),
        in_specs=[
            whole((1, rest)), whole((rest, 1)), table, table, part(0), part(1), part(2),
            part(0), part(0), pl.BlockSpec((1, 1, tok), lambda h: (h, 0, 0)),
        ],
        out_specs=[part(0)] * 3,
        out_shape=[shaped((heads * HEAD_DIM, tok), BF)] * 3,
        compiler_params=params("arbitrary"),
        cost_estimate=cost(heads * 4.2e9, 6e6),
        name="attend_back",
    )(seg[None, :], seg[:, None], cos, sin, qkv, qkv, qkv, g_ctx, ctx, logs)


class Routes:
    def __init__(self, dp_size, slot_cap, pieces, phases):
        self.dp = dp_size
        self.cap = slot_cap
        self.chips = dp_size // 2
        self.pieces = pieces
        self.phases = phases
        if self.chips == 8:
            self.stages = ((2, 4), (1, 2))
        elif self.chips == 64:
            self.stages = ((1, 8), (8, 2), (16, 4))
        else:
            self.stages = ((1, self.chips),)
        self.names = []

    def chip_cap(self, phase):
        count = phase[1] - phase[0]
        worst = min(count, 2 * self.cap)
        return min(worst, count // 5 + 5) if self.chips == 8 else worst

    def side_cap(self, phase, level):
        if level == len(self.stages):
            return self.chip_cap(phase)
        count = phase[1] - phase[0]
        group = self.dp
        for _, size in self.stages[len(self.stages) - level :]:
            group //= size
        worst = min(count, group * self.cap)
        return min(worst, (count * 11) // 20 + 7) if self.chips == 8 else worst

    def move(self, array, stage, shift):
        stride, size = self.stages[stage]
        pairs = []
        for device in range(self.dp):
            chip, core = device // 2, device % 2
            at = (chip // stride) % size
            pairs.append((device, 2 * (chip + ((at + shift) % size - at) * stride) + core))
        return lax.ppermute(array, "dp", pairs)

    def swap_cores(self, array):
        return lax.ppermute(array, "dp", [(d, d ^ 1) for d in range(self.dp)])

    def tables(self, owners, me):
        own_row = jnp.pad(owners, (0, LANES - self.pieces), constant_values=-2)[None, :]
        made = {}
        place = {}

        def kernel(me_ref, row_ref, col_ref, out_ref):
            here = me_ref[0]
            my_chip, my_core = here // 2, here % 2
            row, col = row_ref[...], col_ref[...]
            id_row = lax.broadcasted_iota(I32, (1, LANES), 1)
            id_col = lax.broadcasted_iota(I32, (LANES, 1), 0)
            lane = lax.broadcasted_iota(I32, (LANES, LANES), 1)
            sub = lax.broadcasted_iota(I32, (LANES, LANES), 0)

            def rank_col(key_row, key_col):
                hit = (key_row == key_col) & (lane < sub)
                return jnp.sum(hit.astype(F32), axis=1, keepdims=True).astype(I32)

            def rank_row(key_row, key_col):
                hit = (key_row == key_col) & (sub < lane)
                return jnp.sum(hit.astype(F32), axis=0, keepdims=True).astype(I32)

            def gather(valid_col, entry_col, value_col):
                hit = valid_col & (entry_col == lane)
                return jnp.sum(
                    jnp.where(hit, value_col.astype(F32), 0.0), axis=0, keepdims=True
                ).astype(I32)

            def put(name, value):
                at = place.setdefault(name, len(place))
                out_ref[at : at + 1, :] = value

            def coord(chip, stage):
                stride, size = self.stages[stage]
                return (chip // stride) % size

            def group(chip, level):
                key = 0
                for stage in range(len(self.stages) - level, len(self.stages)):
                    key = key * self.stages[stage][1] + coord(chip, stage)
                return key

            slot_col = rank_col(row, col)
            filled = gather(col == here, slot_col, id_col + 1)
            put("piece", filled - 1)
            over = jnp.zeros((1, 1), I32)
            depth = len(self.stages)
            for number, (low, high) in enumerate(self.phases):
                phase = (low, high)
                in_col = (id_col >= low) & (id_col < high)
                in_row = (id_row >= low) & (id_row < high)
                base_col = jnp.where(in_col, col, -2)
                base_row = jnp.where(in_row, row, -2)
                chip_col, chip_row = base_col // 2, base_row // 2
                cap = self.chip_cap(phase)
                ranks = {depth: rank_col(chip_row, chip_col)}
                rank_in_row = rank_row(chip_row, chip_col)
                fullest = jnp.max(jnp.where(in_col, ranks[depth], 0), axis=0, keepdims=True)
                over = jnp.maximum(over, fullest - cap + 1)
                put(
                    ("send", number),
                    gather(
                        in_col & (chip_col == my_chip),
                        ranks[depth],
                        jnp.where(col % 2 == my_core, 0, self.cap) + slot_col,
                    ),
                )
                spot, scale = rank_in_row, cap
                for stage, (_, size) in enumerate(self.stages):
                    away = (coord(my_chip, stage) - coord(chip_row, stage) + size) % size
                    spot = spot + away * scale
                    scale = scale * size
                put(("take", number), spot)
                for level in range(1, depth):
                    key_col = jnp.where(in_col, group(chip_col, level), -1)
                    key_row = jnp.where(in_row, group(chip_row, level), -1)
                    ranks[level] = rank_col(key_row, key_col)
                    fullest = jnp.max(jnp.where(in_col, ranks[level], 0), axis=0, keepdims=True)
                    over = jnp.maximum(over, fullest - self.side_cap(phase, level) + 1)
                value = id_col - low
                for level in range(1, depth + 1):
                    stage = depth - level
                    size = self.stages[stage][1]
                    mine = in_col
                    if level > 1:
                        mine = mine & (group(chip_col, level - 1) == group(my_chip, level - 1))
                    for shift in range(size):
                        goal = (coord(my_chip, stage) + shift) % size
                        put(
                            ("back", number, level, shift),
                            gather(mine & (coord(chip_col, stage) == goal), ranks[level], value),
                        )
                    value = ranks[level]
                for which in range(2):
                    goal = my_chip * 2 + (my_core + which) % 2
                    put(
                        ("slot", number, which),
                        gather(in_col & (col == goal), slot_col, ranks[depth]),
                    )
            put("over", jnp.broadcast_to(over, (1, LANES)))

        count = 2 + len(self.phases) * (4 + sum(size for _, size in self.stages))
        height = -(-count // 8) * 8
        table = pl.pallas_call(
            kernel,
            in_specs=[pl.BlockSpec(memory_space=pltpu.SMEM), whole((1, LANES)), whole((LANES, 1))],
            out_specs=whole((height, LANES)),
            out_shape=shaped((height, LANES), I32),
            compiler_params=params(),
            name="routes",
        )(me[None], own_row, own_row.reshape(LANES, 1))
        return table, place


def pick_call(table, picks, parts, sizes, dtype=BF, name="pick"):
    rows_each = [part.shape[0] for part in parts]
    shape = parts[0].shape[1:]
    joined = len(parts) > 1

    def kernel(table_ref, *refs):
        ins, outs = refs[: len(parts)], refs[len(parts) : len(parts) + len(sizes)]
        if joined:
            source = refs[-1]
            at = 0
            for ref, count in zip(ins, rows_each):
                source[at : at + count] = ref[...]
                at += count
        else:
            source = ins[0]
        for (row, start), size, out in zip(picks, sizes, outs):
            for j in range(size):
                out[j] = source[table_ref[row, start + j]].astype(dtype)

    return pl.pallas_call(
        kernel,
        in_specs=[pl.BlockSpec(memory_space=pltpu.SMEM)] + [whole(p.shape) for p in parts],
        out_specs=[whole((size,) + shape) for size in sizes],
        out_shape=[shaped((size,) + shape, dtype) for size in sizes],
        scratch_shapes=[pltpu.VMEM((sum(rows_each),) + shape, parts[0].dtype)] if joined else [],
        compiler_params=params(),
        name=name,
    )(table, *parts)


def add_pick_call(table, picks, parts, sizes, dtype=BF, name="add_pick"):
    shape = parts[0].shape[1:]

    def kernel(table_ref, *refs):
        ins, outs = refs[: len(parts)], refs[len(parts) :]
        for (row, start), size, out in zip(picks, sizes, outs):
            for j in range(size):
                at = table_ref[row, start + j]
                total = ins[0][at].astype(F32)
                for ref in ins[1:]:
                    total = total + ref[at].astype(F32)
                out[j] = total.astype(dtype)

    return pl.pallas_call(
        kernel,
        in_specs=[pl.BlockSpec(memory_space=pltpu.SMEM)] + [whole(p.shape) for p in parts],
        out_specs=[whole((size,) + shape) for size in sizes],
        out_shape=[shaped((size,) + shape, dtype) for size in sizes],
        compiler_params=params(),
        name=name,
    )(table, *parts)


def adam_step(weights, first_mom, second_mom, gradient, rate_arr, decay_rate):
    first_new = BETA_ONE * first_mom + (1.0 - BETA_ONE) * gradient
    second_new = BETA_TWO * second_mom + (1.0 - BETA_TWO) * gradient * gradient
    first_fix = first_new / (1.0 - BETA_ONE**STEP)
    second_fix = second_new / (1.0 - BETA_TWO**STEP)
    weights_new = weights * (1.0 - rate_arr * decay_rate) - rate_arr * first_fix / (
        jnp.sqrt(second_fix) + ADAM_EPS
    )
    return (weights_new, first_new, second_new)


def swap_mp(array):
    return lax.ppermute(array, "mp", [(0, 1), (1, 0)])


def roll_rows(array, start):
    return lax.dynamic_slice_in_dim(
        jnp.concatenate([array, array], axis=0), start, array.shape[0], axis=0
    )


def body(
    tokens, cotangent, lengths, owners, weight_table, moment_table, square_table,
    norm_params, norm_moment, norm_square, bias_params, bias_moment, bias_square,
):
    dp_size = lax.axis_size("dp")
    mp_size = lax.axis_size("mp")
    heads = HEADS // mp_size
    head_width = heads * HEAD_DIM
    hidden = FF // mp_size
    tok, width = tokens.shape
    slot_cap, piece_len = weight_table.shape[1:3]
    half_len = piece_len // 2
    piece_total = owners.shape[0]
    me = lax.axis_index("dp").astype(I32)
    core = me % 2
    first_core = core == 0

    cuts = (
        0, 3 * head_width // piece_len, (4 * head_width + hidden) // piece_len, piece_total,
    )
    phases = tuple(zip(cuts[:-1], cuts[1:]))
    routes = Routes(dp_size, slot_cap, piece_total, phases)
    table, place = routes.tables(owners, me)
    fits = table[place["over"], 0] <= 0

    low_table = weight_table[0].astype(BF).reshape(slot_cap, 2, half_len, width)

    def half(array, which):
        return lax.dynamic_index_in_dim(array, which, axis=1, keepdims=False)

    own_half = half(low_table, core)
    chip_slots = [own_half, routes.swap_cores(half(low_table, 1 - core))]

    def slow_gather(low, high):
        everyone = lax.all_gather(weight_table[0].astype(BF), "dp", axis=0, tiled=True)
        earlier = (owners[None, :] == owners[:, None]) & (
            jnp.arange(piece_total)[None, :] < jnp.arange(piece_total)[:, None]
        )
        at = owners * slot_cap + jnp.sum(earlier.astype(I32), axis=1)
        return everyone[at[low:high]].reshape(-1, width)

    sends = pick_call(
        table,
        [(place[("send", number)], 0) for number in range(len(phases))],
        chip_slots,
        [routes.chip_cap(phase) for phase in phases],
        name="pick_owned",
    )

    def gather_phase(number):
        low, high = phases[number]
        buffers = [sends[number]]
        for stage, (_, size) in enumerate(routes.stages):
            buffers = buffers + [
                routes.move(buffer, stage, shift)
                for shift in range(1, size)
                for buffer in buffers
            ]
        (mine,) = pick_call(
            table, [(place[("take", number)], low)], buffers, [high - low], name="pick_all"
        )
        other = routes.swap_cores(mine)
        pair = jnp.where(first_core, jnp.stack([mine, other], 1), jnp.stack([other, mine], 1))
        fast = pair.reshape(-1, width)
        return lax.cond(fits, lambda: fast, lambda: slow_gather(low, high))

    w_qkv = gather_phase(0)
    w_second = gather_phase(1)
    w_out, w_up = w_second[:head_width], w_second[head_width:]
    w_down = gather_phase(2)
    w_out_other = swap_mp(w_out)

    sizes = lengths[0]
    ends = jnp.cumsum(sizes)
    starts = ends - sizes
    start = jnp.sum(jnp.where(jnp.arange(sizes.shape[0]) == jnp.argmax(sizes), starts, 0))
    origin = lax.rem(jnp.arange(tok, dtype=I32) + start, tok)
    document = jnp.sum((origin[:, None] >= ends[None, :]).astype(I32), axis=1)
    first = jnp.sum(
        jnp.where(document[:, None] == jnp.arange(sizes.shape[0])[None, :], starts[None, :], 0), axis=1
    )
    seg = document[LONGEST:]
    frequency = 10000.0 ** (-(jnp.arange(0, HEAD_DIM, 2).astype(F32) / HEAD_DIM))
    angles = frequency[:, None] * (origin - first).astype(F32)[None, :]
    cos, sin = jnp.cos(angles), jnp.sin(angles)
    x = roll_rows(tokens, start)
    gy = roll_rows(cotangent, start)
    bias_row = bias_params[0]
    b_qkv = bias_row[: 3 * head_width, None]
    b_up = bias_params[:, 3 * head_width :]

    qkv, a1 = qkv_call(x, norm_params, w_qkv, b_qkv, cos, sin)
    ctx, logs = attend_call(seg, qkv, 0, heads, heads)
    ctx_other = swap_mp(ctx)
    x1, a2, act, g_pre, ffn, g_h2, gb_up = mlp_call(
        x, gy, ctx, ctx_other, w_out, w_out_other, w_up, w_down, b_up, norm_params
    )
    g_h2_other = swap_mp(g_h2)
    ffn_other = swap_mp(ffn)
    g_down, g_up = mlp_grads_call(act, g_pre, a2, gy)
    gx1, g_ctx, g_out, mid_sums = mid_call(x1, gy, g_h2, g_h2_other, ctx, w_out, norm_params)

    out_roll = x1 + (ffn.astype(F32) + ffn_other.astype(F32)) + norm_params[5]
    block_out = roll_rows(out_roll, tok - start)

    gq, gk, gv = attend_back_call(seg, cos, sin, qkv, g_ctx, ctx, logs, heads)
    g_qkv, g_h1, gb_qkv, in_sums = in_grads_call(gq, gk, gv, a1, x, w_qkv)
    g_h1_other = swap_mp(g_h1)
    grad_roll = last_call(x, gx1, g_h1, g_h1_other, norm_params)
    grad_tokens = roll_rows(grad_roll, tok - start)

    def owner_lists(number, grad):
        low, high = phases[number]
        phase = phases[number]
        grad = grad.reshape(high - low, 2, half_len, width)
        parts = [half(grad, core), routes.swap_cores(half(grad, 1 - core))]
        for level in range(1, len(routes.stages) + 1):
            stage = len(routes.stages) - level
            size = routes.stages[stage][1]
            lists = add_pick_call(
                table,
                [(place[("back", number, level, shift)], 0) for shift in range(size)],
                parts,
                [routes.side_cap(phase, level)] * size,
            )
            parts = [lists[0]] + [
                routes.move(lists[shift], stage, shift) for shift in range(1, size)
            ]
        return parts

    dense = (g_qkv, jnp.concatenate([g_out, g_up], axis=0), g_down)
    pieces_in = {}
    for number in (2, 1, 0):
        parts = owner_lists(number, dense[number])
        pieces_in[number] = add_pick_call(
            table,
            [(place[("slot", number, which)], 0) for which in range(2)],
            parts,
            [slot_cap] * 2,
            dtype=F32,
            name="owned",
        )
    piece_ids = table[place["piece"], :slot_cap]

    def choose(which):
        ids = piece_ids
        if which:
            ids = lax.ppermute(piece_ids, "dp", [(d, d ^ 1) for d in range(dp_size)])
        ids = ids[:, None, None]
        value = pieces_in[0][which]
        for number in (1, 2):
            value = jnp.where(ids >= phases[number][0], pieces_in[number][which], value)
        return value

    kept = choose(0)
    arrived = routes.swap_cores(choose(1))
    fast_grad = jnp.where(
        first_core, jnp.concatenate([kept, arrived], 1), jnp.concatenate([arrived, kept], 1)
    )
    ids = piece_ids[:, None, None]
    occupied = ids >= 0

    def slow_grad():
        stack = jnp.concatenate(dense, axis=0).reshape(-1, piece_len, width).astype(F32)
        total = lax.psum(stack, "dp")
        return total[jnp.maximum(piece_ids, 0)]

    owned_grad = lax.cond(fits, lambda: fast_grad, slow_grad)
    begins = ids * piece_len
    rate = jnp.where(begins < 4 * head_width + hidden, 0.03, 0.015)
    rate = jnp.where(
        begins < 3 * head_width, 0.03, jnp.where(begins < 4 * head_width, 0.2, rate)
    ).astype(F32)
    new_w, new_m, new_v = adam_step(
        weight_table[0], moment_table[0], square_table[0], owned_grad, rate, DECAY_RATE
    )
    weights_next = jnp.where(occupied, new_w, 0.0)[None]
    moments_next = jnp.where(occupied, new_m, 0.0)[None]
    squares_next = jnp.where(occupied, new_v, 0.0)[None]

    in_total = in_sums[0:2] + swap_mp(in_sums[0:2])
    norm_total = jnp.concatenate([in_total, mid_sums[0:4]], axis=0)
    bias_total = jnp.concatenate([gb_qkv.reshape(1, -1), gb_up], axis=1)
    bit = 1
    while bit < dp_size:
        pairs = [(d, d ^ bit) for d in range(dp_size)]
        norm_total = norm_total + lax.ppermute(norm_total, "dp", pairs)
        bias_total = bias_total + lax.ppermute(bias_total, "dp", pairs)
        bit *= 2
    norm_rate = jnp.array(NORM_RATES, F32)[:, None]
    norms_next, norm_moments, norm_squares = adam_step(
        norm_params, norm_moment, norm_square, norm_total, norm_rate, 0.0
    )
    biases_next, bias_moments, bias_squares = adam_step(
        bias_params, bias_moment, bias_square, bias_total, BIAS_RATE, 0.0
    )
    return (
        block_out, grad_tokens, weights_next, moments_next, squares_next,
        norms_next, norm_moments, norm_squares, biases_next, bias_moments, bias_squares,
    )


def solution(mesh):
    flat = P("dp", None)
    pieces = P("mp", "dp", None, None)
    bias = P("mp", None)
    return jax.shard_map(
        body,
        mesh=mesh,
        in_specs=(flat, flat, flat, P(), pieces, pieces, pieces, P(), P(), P(), bias, bias, bias),
        out_specs=(flat, flat, pieces, pieces, pieces, P(), P(), P(), bias, bias, bias),
        check_vma=False,
    )
```

```python
import functools

import jax
import jax.numpy as jnp
from jax import lax
from jax.experimental import pallas as pl
from jax.experimental.pallas import tpu as pltpu
from jax.sharding import PartitionSpec as P

HEADS = 20
HEAD_DIM = 32
HALF = HEAD_DIM // 2
FF = 2560
LONGEST = 1024
STEP = 10

EPS_NORM = 1e-05
BETA_ONE = 0.5
BETA_TWO = 0.5
ADAM_EPS = 1e-08
DECAY_RATE = 0.01
NEG_FILL = -1e30
NORM_RATES = (0.5, 0.1, 0.5, 0.1, 0.1, 0.1)
BIAS_RATE = 0.1
SCALE = HEAD_DIM**-0.5
SCALE_LOG2 = SCALE * 1.4426950408889634
SAFE_EXP = 100.0

BF = jnp.bfloat16
F32 = jnp.float32
I32 = jnp.int32
TILE = 256
LANES = 128
VMEM_LIMIT = 56 << 20


def params(*kinds):
    return pltpu.CompilerParams(dimension_semantics=kinds or None, vmem_limit_bytes=VMEM_LIMIT)


def cost(flops, moved):
    return pl.CostEstimate(flops=int(flops), bytes_accessed=int(moved), transcendentals=0)


def dot_nn(a, b):
    return lax.dot_general(a, b, (((1,), (0,)), ((), ())), preferred_element_type=F32)


def dot_nt(a, b):
    return lax.dot_general(a, b, (((1,), (1,)), ((), ())), preferred_element_type=F32)


def dot_tn(a, b):
    return lax.dot_general(a, b, (((0,), (0,)), ((), ())), preferred_element_type=F32)


def split_two(v):
    hi = v.astype(BF).astype(F32)
    return hi, v - hi


def split_three(v):
    hi = v.astype(BF).astype(F32)
    mid = (v - hi).astype(BF).astype(F32)
    return hi, mid, v - hi - mid


def normalized(v):
    centred = v - jnp.mean(v, axis=-1, keepdims=True)
    inv = lax.rsqrt(jnp.mean(centred * centred, axis=-1, keepdims=True) + EPS_NORM)
    return centred * inv, inv


def whole(shape):
    return pl.BlockSpec(shape, lambda *_: (0,) * len(shape))


def rows(width, tile=TILE):
    return pl.BlockSpec((tile, width), lambda t: (t, 0))


def cols(height, tile=TILE):
    return pl.BlockSpec((height, tile), lambda t: (0, t))


def shaped(shape, dtype):
    return jax.ShapeDtypeStruct(shape, dtype)


def call(kernel, args, in_specs, out_specs, out_shape, name, deps=(), scratch=(), **more):
    count = len(args)

    def wrapped(*refs):
        kernel(*refs[:count], *refs[count + len(deps) :])

    return pl.pallas_call(
        wrapped,
        in_specs=list(in_specs) + [pl.BlockSpec(memory_space=pl.ANY)] * len(deps),
        out_specs=out_specs,
        out_shape=out_shape,
        scratch_shapes=list(scratch),
        compiler_params=params(*(("arbitrary",) if "grid" in more else ())),
        name=name,
        **more,
    )(*args, *deps)


def qkv_kernel(x_ref, norm_ref, wm_ref, wo_ref, bm_ref, bo_ref, cos_ref, sin_ref, m_ref, o_ref, a_ref):
    n1, _ = normalized(x_ref[...].astype(F32))
    a1 = (n1 * norm_ref[0:1] + norm_ref[1:2]).astype(BF)
    a_ref[...] = a1
    mine = dot_nt(wm_ref[...], a1) + bm_ref[...]
    other = dot_nt(wo_ref[...], a1) + bo_ref[...]
    width = m_ref.shape[1]
    cos, sin = cos_ref[...], sin_ref[...]
    for which in range(2):
        for at in range(0, width, HALF):
            here = which * width + at
            p, r = mine[here : here + HALF], other[here : here + HALF]
            m_ref[which, at : at + HALF, :] = (p * cos - r * sin).astype(BF)
            o_ref[which, at : at + HALF, :] = (r * cos + p * sin).astype(BF)
    m_ref[2] = mine[2 * width :].astype(BF)
    o_ref[2] = other[2 * width :].astype(BF)


def qkv_call(x, norms, w_mine, w_other, b_mine, b_other, cos, sin, deps=()):
    tok, width = x.shape
    out = w_mine.shape[0]
    third = pl.BlockSpec((3, out // 3, TILE), lambda t: (0, 0, t))
    return call(
        qkv_kernel,
        (x, norms, w_mine, w_other, b_mine, b_other, cos, sin),
        [
            rows(width), whole(norms.shape), whole(w_mine.shape), whole(w_mine.shape),
            whole(b_mine.shape), whole(b_mine.shape), cols(HALF), cols(HALF),
        ],
        [third, third, rows(width)],
        [shaped((3, out // 3, tok), BF)] * 2 + [shaped((tok, width), BF)],
        "ln_qkv",
        deps,
        grid=(tok // TILE,),
        cost_estimate=cost(4 * tok * width * out, 8e6),
    )


def mlp_kernel(
    groups, x_ref, gy_ref, *refs,
):
    ctx_refs, refs = refs[: 4 * groups], refs[4 * groups :]
    (
        w0, w1, w2, w3, um_ref, uo_ref, dm_ref, do_ref, bup_ref, norm_ref, x1_ref, a2_ref, act_ref, gpre_ref, ffn_ref, gh_ref, gbup_ref,
        out_w, up_w, down_w,
    ) = refs

    @pl.when(pl.program_id(0) == 0)
    def _():
        quarter, half = w0.shape[0], um_ref.shape[0]
        for at, ref in enumerate((w0, w1, w2, w3)):
            out_w[at * quarter : (at + 1) * quarter, :] = ref[...]
        up_w[:half, :] = um_ref[...]
        up_w[half:, :] = uo_ref[...]
        down_w[:half, :] = dm_ref[...]
        down_w[half:, :] = do_ref[...]

    gy = gy_ref[...]
    ctx = jnp.concatenate([ref[...] for ref in ctx_refs], axis=0)
    x1 = x_ref[...].astype(F32) + dot_tn(ctx, out_w[...]) + norm_ref[4:5]
    x1_ref[...] = x1
    n2, _ = normalized(x1)
    a2 = (n2 * norm_ref[2:3] + norm_ref[3:4]).astype(BF)
    a2_ref[...] = a2
    pre = dot_nt(a2, up_w[...]) + bup_ref[...]
    cdf = 0.5 * (1.0 + lax.erf(pre * 0.7071067811865476))
    act = (pre * cdf).astype(BF)
    act_ref[...] = act
    slope = cdf + pre * (jnp.exp(-0.5 * pre * pre) * 0.3989422804014327)
    gpre = (slope * dot_nt(gy, down_w[...])).astype(BF)
    gpre_ref[...] = gpre
    ffn_ref[...] = dot_nn(act, down_w[...]).astype(BF)
    gh_ref[...] = dot_nn(gpre, up_w[...]).astype(BF)
    part = jnp.sum(gpre.astype(F32), axis=0, keepdims=True)

    @pl.when(pl.program_id(0) == 0)
    def _():
        gbup_ref[...] = part

    @pl.when(pl.program_id(0) > 0)
    def _():
        gbup_ref[...] += part


def mlp_call(x, gy, ctx, w_out, w_up, w_down, b_up, norms, deps=()):
    tok, width = x.shape
    hidden = 2 * w_up[0].shape[0]
    quarter = w_out[0].shape[0]
    return call(
        functools.partial(mlp_kernel, len(ctx) // 4),
        (x, gy, *ctx, *w_out, *w_up, *w_down, b_up, norms),
        [rows(width), rows(width)]
        + [cols(part.shape[0]) for part in ctx]
        + [whole((quarter, width))] * 4
        + [whole((hidden // 2, width))] * 4
        + [whole(b_up.shape), whole(norms.shape)],
        [
            rows(width), rows(width), rows(hidden), rows(hidden), rows(width), rows(width),
            whole((1, hidden)),
        ],
        [
            shaped((tok, width), F32), shaped((tok, width), BF), shaped((tok, hidden), BF),
            shaped((tok, hidden), BF), shaped((tok, width), BF), shaped((tok, width), BF),
            shaped((1, hidden), F32),
        ],
        "mlp",
        deps,
        scratch=[
            pltpu.VMEM((4 * quarter, width), BF), pltpu.VMEM((hidden, width), BF),
            pltpu.VMEM((hidden, width), BF),
        ],
        grid=(tok // TILE,),
        cost_estimate=cost(2 * tok * width * (hidden * 4 + 4 * quarter) * 1.6, 3e7),
    )


def mlp_grads_kernel(act_ref, gpre_ref, a2_ref, gy_ref, mine_ref, other_ref, down_sum, up_sum):
    step = pl.program_id(0)
    down = dot_tn(act_ref[...], gy_ref[...])
    up = dot_tn(gpre_ref[...], a2_ref[...])

    @pl.when(step == 0)
    def _():
        down_sum[...] = down
        up_sum[...] = up

    @pl.when(step > 0)
    def _():
        down_sum[...] += down
        up_sum[...] += up

    @pl.when(step == pl.num_programs(0) - 1)
    def _():
        half = down_sum.shape[0] // 2
        mine_ref[:half, :] = up_sum[:half, :].astype(BF)
        mine_ref[half:, :] = down_sum[:half, :].astype(BF)
        other_ref[:half, :] = up_sum[half:, :].astype(BF)
        other_ref[half:, :] = down_sum[half:, :].astype(BF)


def mlp_grads_call(act, gpre, a2, gy, deps=()):
    tok, hidden = act.shape
    width = a2.shape[1]
    tile = tok // 2
    return call(
        mlp_grads_kernel,
        (act, gpre, a2, gy),
        [rows(hidden, tile), rows(hidden, tile), rows(width, tile), rows(width, tile)],
        [whole((hidden, width))] * 2,
        [shaped((hidden, width), BF)] * 2,
        "mlp_grads",
        deps,
        scratch=[pltpu.VMEM((hidden, width), F32)] * 2,
        grid=(tok // tile,),
        cost_estimate=cost(4 * tok * width * hidden * 1.3, 1.4e7),
    )


def mid_kernel(
    groups, x1_ref, gy_ref, gh_a, gh_b, *refs,
):
    ctx_refs, refs = refs[: 2 * groups], refs[2 * groups :]
    (
        wm_ref, wo_ref, norm_ref, _,
        gx_ref, gm_out, go_out, goutm_ref, gouto_ref, sum_ref, _, m_sum, o_sum,
    ) = refs
    cm, co = (
        jnp.concatenate([ref[...] for ref in ctx_refs[at : at + groups]], axis=0)
        for at in (0, groups)
    )
    step = pl.program_id(0)
    gy = gy_ref[...].astype(F32)
    gh = gh_a[...].astype(F32) + gh_b[...].astype(F32)
    n2, inv = normalized(x1_ref[...])
    e = gh * norm_ref[2:3]
    gx = gy + inv * (
        e - jnp.mean(e, axis=-1, keepdims=True) - n2 * jnp.mean(e * n2, axis=-1, keepdims=True)
    )
    gx_ref[...] = gx
    gm = gx.astype(BF)
    gm_out[...] = dot_nt(wm_ref[...], gm).astype(BF)
    go_out[...] = dot_nt(wo_ref[...], gm).astype(BF)
    sums = jnp.concatenate(
        [jnp.sum(v, axis=0, keepdims=True) for v in (gh * n2, gh, gx, gy)]
        + [jnp.zeros((4, gy.shape[1]), F32)],
        axis=0,
    )

    @pl.when(step == 0)
    def _():
        m_sum[...] = jnp.zeros_like(m_sum)
        o_sum[...] = jnp.zeros_like(o_sum)
        sum_ref[...] = jnp.zeros_like(sum_ref)

    m_sum[...] += dot_nn(cm, gm)
    o_sum[...] += dot_nn(co, gm)
    sum_ref[...] += sums

    @pl.when(step == pl.num_programs(0) - 1)
    def _():
        goutm_ref[...] = m_sum[...].astype(BF)
        gouto_ref[...] = o_sum[...].astype(BF)


def mid_call(x1, gy, gh_a, gh_b, ctx_m, ctx_o, w_m, w_o, norms, ffn, deps=()):
    tok, width = x1.shape
    head = w_m.shape[0]
    anywhere = pl.BlockSpec(memory_space=pl.ANY)
    args = (x1, gy, gh_a, gh_b, *ctx_m, *ctx_o, w_m, w_o, norms, ffn)
    return call(
        functools.partial(mid_kernel, len(ctx_m)),
        args,
        [rows(width)] * 4
        + [cols(part.shape[0]) for part in (*ctx_m, *ctx_o)]
        + [whole(w_m.shape), whole(w_o.shape), whole(norms.shape), anywhere],
        [rows(width), cols(head), cols(head)]
        + [whole((head, width))] * 2
        + [whole((8, width)), anywhere],
        [shaped((tok, width), F32)]
        + [shaped((head, tok), BF)] * 2
        + [shaped((head, width), BF)] * 2
        + [shaped((8, width), F32), shaped(ffn.shape, ffn.dtype)],
        "mid_back",
        deps,
        scratch=[pltpu.VMEM((head, width), F32)] * 2,
        grid=(tok // TILE,),
        cost_estimate=cost(8 * tok * width * head * 2, 1.5e7),
        input_output_aliases={len(args) - 1: 6},
    )


def in_grads_kernel(
    groups, *refs,
):
    gm_refs, go_refs, refs = refs[:groups], refs[groups : 2 * groups], refs[2 * groups :]
    (
        a1_ref, x_ref, wm_ref, wo_ref, outm_ref, outo_ref,
        mine_ref, other_ref, gh_ref, gbm_ref, gbo_ref, sum_ref, m_sum, o_sum,
    ) = refs
    step = pl.program_id(0)
    count = wm_ref.shape[0]
    a1 = a1_ref[...]
    gm, go = (
        jnp.concatenate([ref[j] for j in range(3) for ref in some], axis=0)
        for some in (gm_refs, go_refs)
    )

    @pl.when(step == 0)
    def _():
        m_sum[...] = jnp.zeros_like(m_sum)
        o_sum[...] = jnp.zeros_like(o_sum)
        gbm_ref[...] = jnp.zeros_like(gbm_ref)
        gbo_ref[...] = jnp.zeros_like(gbo_ref)
        sum_ref[...] = jnp.zeros_like(sum_ref)

    m_sum[...] += dot_nn(gm, a1)
    o_sum[...] += dot_nn(go, a1)
    gbm_ref[...] += jnp.sum(gm.astype(F32), axis=1, keepdims=True)
    gbo_ref[...] += jnp.sum(go.astype(F32), axis=1, keepdims=True)
    gh = dot_tn(gm, wm_ref[...]) + dot_tn(go, wo_ref[...])
    gh_ref[...] = gh.astype(BF)
    n1, _ = normalized(x_ref[...].astype(F32))
    sum_ref[...] += jnp.concatenate(
        [jnp.sum(gh * n1, axis=0, keepdims=True), jnp.sum(gh, axis=0, keepdims=True)]
        + [jnp.zeros((6, gh.shape[1]), F32)],
        axis=0,
    )

    @pl.when(step == pl.num_programs(0) - 1)
    def _():
        mine_ref[:count, :] = m_sum[...].astype(BF)
        mine_ref[count:, :] = outm_ref[...]
        other_ref[:count, :] = o_sum[...].astype(BF)
        other_ref[count:, :] = outo_ref[...]


def in_grads_call(g_m, g_o, a1, x, w_m, w_o, gout_m, gout_o, deps=()):
    tok, width = a1.shape
    count, more = w_m.shape[0], gout_m.shape[0]
    thirds = [pl.BlockSpec(part.shape[:2] + (TILE,), lambda t: (0, 0, t)) for part in (*g_m, *g_o)]
    return call(
        functools.partial(in_grads_kernel, len(g_m)),
        (*g_m, *g_o, a1, x, w_m, w_o, gout_m, gout_o),
        thirds
        + [rows(width), rows(width)]
        + [whole((count, width))] * 2
        + [whole((more, width))] * 2,
        [whole((count + more, width))] * 2 + [rows(width)] + [whole((count, 1))] * 2 + [whole((8, width))],
        [shaped((count + more, width), BF)] * 2
        + [shaped((tok, width), BF)]
        + [shaped((count, 1), F32)] * 2
        + [shaped((8, width), F32)],
        "in_grads",
        deps,
        scratch=[pltpu.VMEM((count, width), F32)] * 2,
        grid=(tok // TILE,),
        cost_estimate=cost(8 * tok * width * count * 1.3, 1e7),
    )


def last_kernel(x_ref, gx_ref, gh_a, gh_b, norm_ref, out_ref):
    n1, inv = normalized(x_ref[...].astype(F32))
    e = (gh_a[...].astype(F32) + gh_b[...].astype(F32)) * norm_ref[0:1]
    out_ref[...] = gx_ref[...] + inv * (
        e - jnp.mean(e, axis=-1, keepdims=True) - n1 * jnp.mean(e * n1, axis=-1, keepdims=True)
    )


def last_call(x, gx, gh_a, gh_b, norms):
    tok, width = x.shape
    return call(
        last_kernel,
        (x, gx, gh_a, gh_b, norms),
        [rows(width)] * 4 + [whole(norms.shape)],
        rows(width),
        shaped((tok, width), F32),
        "last_back",
        grid=(tok // TILE,),
        cost_estimate=cost(1e6, 1.2e7),
    )


def attend_kernel(seg_row, seg_col, m_ref, o_ref, cm_ref, co_ref, log_ref):
    tok = m_ref.shape[2]
    rest = tok - LONGEST
    q_t, k_t, v_t = (jnp.concatenate([m_ref[j], o_ref[j]], axis=0) for j in range(3))
    qs = q_t.astype(F32) * SCALE_LOG2
    hi, lo = split_two(qs)
    qx = jnp.transpose(jnp.concatenate([hi, lo], axis=0)).astype(BF)
    kx = jnp.concatenate([k_t, k_t], axis=0)
    v_f = v_t.astype(F32)
    vx = jnp.transpose(jnp.concatenate([v_f, jnp.ones((8, tok), F32)], axis=0)).astype(BF)
    k_f = k_t.astype(F32)
    q_top = jnp.max(jnp.sum(qs * qs, axis=0, keepdims=True))
    k_top = jnp.max(jnp.sum(k_f * k_f, axis=0, keepdims=True))
    safe = q_top * k_top < SAFE_EXP * SAFE_EXP
    same = seg_col[...] == seg_row[...]

    def finish(sums, shift, at, count):
        turned = jnp.transpose(sums)
        total = turned[HEAD_DIM : HEAD_DIM + 1]
        ctx = (turned[0:HEAD_DIM] / total).astype(BF)
        cm_ref[:, at : at + count] = ctx[:HALF]
        co_ref[:, at : at + count] = ctx[HALF:]
        log_total = jnp.log2(total)
        if shift is not None:
            log_total = log_total + jnp.transpose(jnp.broadcast_to(shift, (count, LANES)))[0:1]
        log_ref[0, :, at : at + count] = log_total

    def run(exact):
        for at in range(0, LONGEST, TILE):
            scores = dot_nn(qx[at : at + TILE], kx[:, :LONGEST])
            shift = None
            if exact:
                shift = jnp.max(scores, axis=1, keepdims=True)
                scores = scores - shift
            finish(dot_nn(jnp.exp2(scores).astype(BF), vx[:LONGEST]), shift, at, TILE)
        if rest:
            scores = jnp.where(same, dot_nn(qx[LONGEST:], kx[:, LONGEST:]), NEG_FILL)
            shift = None
            if exact:
                shift = jnp.max(scores, axis=1, keepdims=True)
                scores = scores - shift
            finish(dot_nn(jnp.exp2(scores).astype(BF), vx[LONGEST:]), shift, LONGEST, rest)

    @pl.when(safe)
    def _():
        run(False)

    @pl.when(jnp.logical_not(safe))
    def _():
        run(True)


def attend_call(seg, qkv_m, qkv_o, first, count, deps=()):
    tok = qkv_m.shape[2]
    rest = seg.shape[0]
    part = pl.BlockSpec((3, HALF, tok), lambda h: (0, first + h, 0))
    out = pl.BlockSpec((HALF, tok), lambda h: (h, 0))
    return call(
        attend_kernel,
        (seg[None, :], seg[:, None], qkv_m, qkv_o),
        [whole((1, rest)), whole((rest, 1)), part, part],
        [out, out, pl.BlockSpec((1, 1, tok), lambda h: (h, 0, 0))],
        [shaped((count * HALF, tok), BF)] * 2 + [shaped((count, 1, tok), F32)],
        "attend",
        deps,
        grid=(count,),
        cost_estimate=cost(count * 2.5e9, 3e6),
    )


def attend_back_kernel(
    seg_row, seg_col, cos_ref, sin_ref, m_ref, o_ref, gm_ref, go_ref, cm_ref, co_ref, log_ref,
    outm_ref, outo_ref,
):
    tok = m_ref.shape[2]
    rest = tok - LONGEST
    q_t, k_t, v_t = (jnp.concatenate([m_ref[j], o_ref[j]], axis=0) for j in range(3))
    ctx = jnp.concatenate([cm_ref[...], co_ref[...]], axis=0).astype(F32)
    q_f = q_t.astype(F32)
    g_f = jnp.concatenate([gm_ref[...], go_ref[...]], axis=0).astype(F32)
    hi, lo = split_two(q_f * SCALE_LOG2)
    weighted = jnp.sum(g_f * ctx, axis=0, keepdims=True)
    pad = jnp.zeros((13, tok), F32)
    qx = jnp.concatenate([hi, lo, *split_three(log_ref[0]), pad], axis=0).astype(BF)
    minus = jnp.concatenate([jnp.full((3, tok), -1.0, F32), pad], axis=0)
    k_f = k_t.astype(F32)
    kx = jnp.transpose(jnp.concatenate([k_f, k_f, minus], axis=0)).astype(BF)
    gx = jnp.concatenate([g_f, *split_three(weighted), pad], axis=0).astype(BF)
    vx = jnp.transpose(jnp.concatenate([v_t.astype(F32), minus], axis=0)).astype(BF)
    qn = jnp.transpose(q_f).astype(BF)
    gn = jnp.transpose(g_f).astype(BF)
    same = seg_col[...] == seg_row[...]

    def turn_back(which, grad, at, count):
        cos, sin = cos_ref[:, at : at + count], sin_ref[:, at : at + count]
        mine, other = grad[0:HALF] * SCALE, grad[HALF:] * SCALE
        outm_ref[which, :, at : at + count] = (mine * cos + other * sin).astype(BF)
        outo_ref[which, :, at : at + count] = (other * cos - mine * sin).astype(BF)

    def block(k_at, k_count, q_at, q_count, mask):
        scores = dot_nn(kx[k_at : k_at + k_count], qx[:, q_at : q_at + q_count])
        if mask is not None:
            scores = jnp.where(mask, scores, NEG_FILL)
        prob = jnp.exp2(scores)
        grad_prob = dot_nn(vx[k_at : k_at + k_count], gx[:, q_at : q_at + q_count])
        grad_score = (prob * grad_prob).astype(BF)
        grad_v = dot_nn(prob.astype(BF), gn[q_at : q_at + q_count])
        grad_k = dot_nn(grad_score, qn[q_at : q_at + q_count])
        turned = jnp.transpose(grad_v).astype(BF)
        outm_ref[2, :, k_at : k_at + k_count] = turned[:HALF]
        outo_ref[2, :, k_at : k_at + k_count] = turned[HALF:]
        turn_back(1, jnp.transpose(grad_k), k_at, k_count)
        return dot_nn(k_t[:, k_at : k_at + k_count], grad_score)

    grad_q = None
    for at in range(0, LONGEST, TILE):
        piece = block(at, TILE, 0, LONGEST, None)
        grad_q = piece if grad_q is None else grad_q + piece
    turn_back(0, grad_q, 0, LONGEST)
    if rest:
        turn_back(0, block(LONGEST, rest, LONGEST, rest, same), LONGEST, rest)


def attend_back_call(seg, cos, sin, qkv_m, qkv_o, g_m, g_o, ctx_m, ctx_o, logs, first, count, deps=()):
    tok = qkv_m.shape[2]
    rest = seg.shape[0]
    part = pl.BlockSpec((3, HALF, tok), lambda h: (0, first + h, 0))
    flat = pl.BlockSpec((HALF, tok), lambda h: (first + h, 0))
    here = pl.BlockSpec((HALF, tok), lambda h: (h, 0))
    out = pl.BlockSpec((3, HALF, tok), lambda h: (0, h, 0))
    table = whole((HALF, tok))
    return call(
        attend_back_kernel,
        (seg[None, :], seg[:, None], cos, sin, qkv_m, qkv_o, g_m, g_o, ctx_m, ctx_o, logs),
        [
            whole((1, rest)), whole((rest, 1)), table, table, part, part, flat, flat, here, here,
            pl.BlockSpec((1, 1, tok), lambda h: (h, 0, 0)),
        ],
        [out, out],
        [shaped((3, count * HALF, tok), BF)] * 2,
        "attend_back",
        deps,
        grid=(count,),
        cost_estimate=cost(count * 4.2e9, 6e6),
    )


class Routes:
    def __init__(self, dp_size, slot_cap, pieces, ready, spans):
        self.dp = dp_size
        self.cap = slot_cap
        self.chips = dp_size // 2
        self.pieces = pieces
        self.ready = ready
        self.spans = spans
        if self.chips == 8:
            self.stages = ((2, 4), (1, 2))
        elif self.chips == 64:
            self.stages = ((1, 8), (8, 2), (16, 4))
        else:
            self.stages = ((1, self.chips),)
        self.depth = len(self.stages)
        self.fill = [self.limit(last, self.chips) for last in ready]
        self.begins = [0] + self.fill[:-1]

    def limit(self, count, groups):
        worst = min(count, self.dp // groups * self.cap)
        if self.chips != 8:
            return worst
        typical = count * 11 // 20 + 8 if groups == 2 else (count * 9 + 25) // 50 + 6
        return min(worst, typical)

    def span_limit(self, span, level):
        groups = 1
        for _, size in self.stages[self.depth - level :]:
            groups *= size
        return self.limit(span[1] - span[0], groups)

    def move(self, array, stage, shift):
        stride, size = self.stages[stage]
        pairs = []
        for device in range(self.dp):
            chip, core = device // 2, device % 2
            at = (chip // stride) % size
            pairs.append((device, 2 * (chip + ((at + shift) % size - at) * stride) + core))
        return lax.ppermute(array, "dp", pairs)

    def swap_cores(self, array):
        return lax.ppermute(array, "dp", [(d, d ^ 1) for d in range(self.dp)])

    def spread(self, array):
        buffers, first = [array], None
        for stage, (_, size) in enumerate(self.stages):
            buffers = buffers + [
                self.move(buffer, stage, shift) for shift in range(1, size) for buffer in buffers
            ]
            first = first or buffers
        return first, buffers

    def tables(self, owners, me):
        own_row = jnp.pad(owners, (0, LANES - self.pieces), constant_values=-2)[None, :]
        place = {}

        def kernel(me_ref, row_ref, col_ref, out_ref):
            here = me_ref[0]
            my_chip, my_core = here // 2, here % 2
            row, col = row_ref[...], col_ref[...]
            id_row = lax.broadcasted_iota(I32, (1, LANES), 1)
            id_col = lax.broadcasted_iota(I32, (LANES, 1), 0)
            lane = lax.broadcasted_iota(I32, (LANES, LANES), 1)
            sub = lax.broadcasted_iota(I32, (LANES, LANES), 0)

            def rank_col(key_row, key_col):
                hit = (key_row == key_col) & (lane < sub)
                return jnp.sum(hit.astype(F32), axis=1, keepdims=True).astype(I32)

            def rank_row(key_row, key_col):
                hit = (key_row == key_col) & (sub < lane)
                return jnp.sum(hit.astype(F32), axis=0, keepdims=True).astype(I32)

            def gather(valid_col, entry_col, value_col):
                hit = valid_col & (entry_col == lane)
                return jnp.sum(
                    jnp.where(hit, value_col.astype(F32), 0.0), axis=0, keepdims=True
                ).astype(I32)

            def put(name, value):
                at = place.setdefault(name, len(place))
                out_ref[at : at + 1, :] = value

            def coord(chip, stage):
                stride, size = self.stages[stage]
                return (chip // stride) % size

            def group(chip, level):
                key = 0
                for stage in range(self.depth - level, self.depth):
                    key = key * self.stages[stage][1] + coord(chip, stage)
                return key

            def fullest(inside, rank):
                return jnp.max(jnp.where(inside, rank, -1), axis=0, keepdims=True) + 1

            slot_col = rank_col(row, col)
            put("piece", gather(col == here, slot_col, id_col + 1) - 1)
            over = jnp.zeros((1, 1), I32)
            real = id_col < self.pieces
            chip_col, chip_row = col // 2, row // 2
            rank_c, rank_r = rank_col(chip_row, chip_col), rank_row(chip_row, chip_col)
            from_core = jnp.where(col % 2 == my_core, 0, self.cap)
            put("send", gather(real & (chip_col == my_chip), rank_c, from_core + slot_col))
            for last, fill in zip(self.ready, self.fill):
                over = jnp.maximum(over, fullest(id_col < last, rank_c) - fill)
            aways = [
                (coord(my_chip, stage) - coord(chip_row, stage) + size) % size
                for stage, (_, size) in enumerate(self.stages)
            ]
            take = jnp.zeros((1, LANES), I32)
            for begin, end in zip(self.begins, self.fill):
                spot, scale = rank_r - begin, end - begin
                for away, (_, size) in zip(aways, self.stages):
                    spot = spot + away * scale
                    scale = scale * size
                take = jnp.where(rank_r >= begin, begin * self.chips + spot, take)
            put("take", take)
            for number, span in enumerate(self.spans):
                in_col = (id_col >= span[0]) & (id_col < span[1])
                in_row = (id_row >= span[0]) & (id_row < span[1])
                ranks = {}
                for level in range(1, self.depth + 1):
                    key_col = jnp.where(in_col, group(chip_col, level), -1)
                    key_row = jnp.where(in_row, group(chip_row, level), -1)
                    ranks[level] = rank_col(key_row, key_col)
                    over = jnp.maximum(
                        over, fullest(in_col, ranks[level]) - self.span_limit(span, level)
                    )
                value = id_col - span[0]
                for level in range(1, self.depth + 1):
                    stage = self.depth - level
                    size = self.stages[stage][1]
                    inside = in_col
                    if level > 1:
                        inside = inside & (group(chip_col, level - 1) == group(my_chip, level - 1))
                    for shift in range(size):
                        goal = (coord(my_chip, stage) + shift) % size
                        put(
                            ("back", number, level, shift),
                            gather(inside & (coord(chip_col, stage) == goal), ranks[level], value),
                        )
                    value = ranks[level]
                for which in range(2):
                    goal = my_chip * 2 + (my_core + which) % 2
                    put(
                        ("slot", number, which),
                        gather(in_col & (col == goal), slot_col, ranks[self.depth]),
                    )
            put("over", jnp.broadcast_to(over, (1, LANES)))

        count = 4 + len(self.spans) * (2 + sum(size for _, size in self.stages))
        height = -(-count // 8) * 8
        table = pl.pallas_call(
            kernel,
            in_specs=[pl.BlockSpec(memory_space=pltpu.SMEM), whole((1, LANES)), whole((LANES, 1))],
            out_specs=whole((height, LANES)),
            out_shape=shaped((height, LANES), I32),
            compiler_params=params(),
            name="routes",
        )(me[None], own_row, own_row.reshape(LANES, 1))
        return table, place


SMEM = pl.BlockSpec(memory_space=pltpu.SMEM)


def pick_call(table, picks, parts, sizes, name, deps=()):
    rows_each = [part.shape[0] for part in parts]
    shape = parts[0].shape[1:]

    def kernel(table_ref, *refs):
        ins, outs, source = refs[: len(parts)], refs[len(parts) : -1], refs[-1]
        at = 0
        for ref, count in zip(ins, rows_each):
            source[at : at + count] = ref[...]
            at += count
        for (row, start), size, out in zip(picks, sizes, outs):
            for j in range(size):
                out[j] = source[table_ref[row, start + j]]

    return call(
        kernel,
        (table, *parts),
        [SMEM] + [whole(part.shape) for part in parts],
        [whole((size,) + shape) for size in sizes],
        [shaped((size,) + shape, BF) for size in sizes],
        name,
        deps,
        scratch=[pltpu.VMEM((sum(rows_each),) + shape, BF)],
    )


def add_pick_call(table, picks, parts, sizes, dtype=BF, name="add_pick", deps=()):
    shape = parts[0].shape[1:]

    def kernel(table_ref, *refs):
        ins, outs = refs[: len(parts)], refs[len(parts) :]
        for (row, start), size, out in zip(picks, sizes, outs):
            for j in range(size):
                at = table_ref[row, start + j]
                total = ins[0][at].astype(F32)
                for ref in ins[1:]:
                    total = total + ref[at].astype(F32)
                out[j] = total.astype(dtype)

    return call(
        kernel,
        (table, *parts),
        [SMEM] + [whole(part.shape) for part in parts],
        [whole((size,) + shape) for size in sizes],
        [shaped((size,) + shape, dtype) for size in sizes],
        name,
        deps,
    )


def adam_step(weights, first_mom, second_mom, gradient, rate_arr, decay_rate):
    first_new = BETA_ONE * first_mom + (1.0 - BETA_ONE) * gradient
    second_new = BETA_TWO * second_mom + (1.0 - BETA_TWO) * gradient * gradient
    first_fix = first_new / (1.0 - BETA_ONE**STEP)
    second_fix = second_new / (1.0 - BETA_TWO**STEP)
    weights_new = weights * (1.0 - rate_arr * decay_rate) - rate_arr * first_fix / (
        jnp.sqrt(second_fix) + ADAM_EPS
    )
    return (weights_new, first_new, second_new)


def swap_mp(array):
    return lax.ppermute(array, "mp", [(0, 1), (1, 0)])


def swap_both(array):
    dp_size = lax.axis_size("dp")
    pairs = [(2 * d + m, 2 * (d ^ 1) + 1 - m) for d in range(dp_size) for m in range(2)]
    return lax.ppermute(array, ("dp", "mp"), pairs)


def roll_rows(array, start):
    return lax.dynamic_slice_in_dim(
        jnp.concatenate([array, array], axis=0), start, array.shape[0], axis=0
    )


def body(
    tokens, cotangent, lengths, owners, weight_table, moment_table, square_table,
    norm_params, norm_moment, norm_square, bias_params, bias_moment, bias_square,
):
    dp_size = lax.axis_size("dp")
    mp_size = lax.axis_size("mp")
    heads = HEADS // mp_size
    head_width = heads * HEAD_DIM
    hidden = FF // mp_size
    tok, width = tokens.shape
    slot_cap, piece_len = weight_table.shape[1:3]
    half_len = piece_len // 2
    piece_total = owners.shape[0]
    me = lax.axis_index("dp").astype(I32)
    core = me % 2
    first_core = core == 0

    n_qkv, n_out = 3 * head_width // piece_len, head_width // piece_len
    n_up = hidden // piece_len
    ready = (n_qkv, n_qkv + n_out + n_up, piece_total)
    spans = ((0, n_qkv + n_out), (n_qkv + n_out, piece_total))
    routes = Routes(dp_size, slot_cap, piece_total, ready, spans)
    table, place = routes.tables(owners, me)
    fits = table[place["over"], 0] <= 0

    low_table = weight_table[0].astype(BF).reshape(slot_cap, 2, half_len, width)

    def half(array, which):
        return lax.dynamic_index_in_dim(array, which, axis=1, keepdims=False)

    chip_slots = [half(low_table, core), routes.swap_cores(half(low_table, 1 - core))]

    def slow_gather(low, high):
        everyone = lax.all_gather(weight_table[0].astype(BF), "dp", axis=0, tiled=True)
        earlier = (owners[None, :] == owners[:, None]) & (
            jnp.arange(piece_total)[None, :] < jnp.arange(piece_total)[:, None]
        )
        at = owners * slot_cap + jnp.sum(earlier.astype(I32), axis=1)
        return half(everyone[at[low:high]].reshape(high - low, 2, half_len, width), core)

    def own_chunk(number, deps):
        begin, end = routes.begins[number], routes.fill[number]
        if begin == end:
            return None, []
        (chunk,) = pick_call(
            table, [(place["send"], begin)], chip_slots, [end - begin], "pick_owned", deps
        )
        first, buffers = routes.spread(chunk)
        return first, buffers

    def collect(buffers, cuts, deps=()):
        sizes = [high - low for low, high in zip(cuts[:-1], cuts[1:])]

        def fast():
            return tuple(
                pick_call(
                    table, [(place["take"], low) for low in cuts[:-1]], buffers, sizes, "pick_all", deps
                )
            )

        def slow():
            return tuple(slow_gather(low, high) for low, high in zip(cuts[:-1], cuts[1:]))

        return lax.cond(fits, fast, slow)

    def flat(array):
        return array.reshape(-1, width)

    sizes = lengths[0]
    ends = jnp.cumsum(sizes)
    starts = ends - sizes
    start = jnp.sum(jnp.where(jnp.arange(sizes.shape[0]) == jnp.argmax(sizes), starts, 0))
    origin = lax.rem(jnp.arange(tok, dtype=I32) + start, tok)
    document = jnp.sum((origin[:, None] >= ends[None, :]).astype(I32), axis=1)
    first = jnp.sum(
        jnp.where(document[:, None] == jnp.arange(sizes.shape[0])[None, :], starts[None, :], 0), axis=1
    )
    seg = document[LONGEST:]
    frequency = 10000.0 ** (-(jnp.arange(0, HEAD_DIM, 2).astype(F32) / HEAD_DIM))
    angles = frequency[:, None] * (origin - first).astype(F32)[None, :]
    cos = jnp.cos(angles)
    sin = jnp.where(first_core, jnp.sin(angles), -jnp.sin(angles))
    x = roll_rows(tokens, start)
    gy = roll_rows(cotangent, start)
    bias_halves = bias_params[0].reshape(-1, 2, half_len)
    b_mine, b_other = half(bias_halves, core), half(bias_halves, 1 - core)
    b_qkv = [part[:n_qkv].reshape(-1, 1) for part in (b_mine, b_other)]
    b_up = jnp.concatenate([part[n_qkv:].reshape(1, -1) for part in (b_mine, b_other)], axis=1)

    stage_a, buffers_a = own_chunk(0, ())
    stage_b, buffers_b = own_chunk(1, stage_a[1:])
    (w_qkv_m,) = collect(buffers_a, (0, n_qkv), (x, gy, cos, sin, *b_qkv))
    w_qkv_o = routes.swap_cores(w_qkv_m)
    qkv_m, qkv_o, a1 = qkv_call(x, norm_params, flat(w_qkv_m), flat(w_qkv_o), *b_qkv, cos, sin)
    stage_c, buffers_c = own_chunk(2, (qkv_m, *(stage_b or ())[1:]))
    cut = heads * 6 // 10
    groups = ((0, cut), (cut, heads - cut))
    ctx_one = attend_call(seg, qkv_m, qkv_o, *groups[0], (stage_c or (qkv_m,))[:1])
    w_out_m, w_up_m = collect(
        buffers_a + buffers_b, (n_qkv, n_qkv + n_out, n_qkv + n_out + n_up), (ctx_one[0],)
    )
    ctx_two = attend_call(seg, qkv_m, qkv_o, *groups[1], (w_out_m, *(stage_c or ())[1:]))
    (w_down_m,) = collect(
        buffers_a + buffers_b + buffers_c, (n_qkv + n_out + n_up, piece_total), (ctx_two[0],)
    )
    w_out_o, w_up_o, w_down_o = (routes.swap_cores(w) for w in (w_out_m, w_up_m, w_down_m))
    w_out_x = [swap_mp(w_out_m), swap_both(w_out_m)]
    ctx_m, ctx_o = (ctx_one[0], ctx_two[0]), (ctx_one[1], ctx_two[1])
    ctx_x = [swap_mp(part) for part in (ctx_one[0], ctx_one[1], ctx_two[0], ctx_two[1])]
    x1, a2, act, g_pre, ffn, g_h2, gb_up = mlp_call(
        x, gy, (*ctx_m, *ctx_o, ctx_x[0], ctx_x[2], ctx_x[1], ctx_x[3]),
        [flat(w) for w in (w_out_m, w_out_o, *w_out_x)],
        [flat(w_up_m), flat(w_up_o)], [flat(w_down_m), flat(w_down_o)], b_up, norm_params,
    )
    g_h2_other = swap_mp(g_h2)
    g_mlp_m, g_mlp_o = mlp_grads_call(act, g_pre, a2, gy)

    def pieces(array):
        return array.reshape(-1, half_len, width)

    def sort_out(number, level, parts, deps=()):
        stage = routes.depth - level
        size = routes.stages[stage][1]
        lists = add_pick_call(
            table,
            [(place[("back", number, level, shift)], 0) for shift in range(size)],
            parts,
            [routes.span_limit(spans[number], level)] * size,
            deps=deps,
        )
        return lists, [lists[0]] + [
            routes.move(lists[shift], stage, shift) for shift in range(1, size)
        ]

    lists, parts_mlp = sort_out(1, 1, [pieces(g_mlp_m), routes.swap_cores(pieces(g_mlp_o))])
    gx1, g_ctx_m, g_ctx_o, g_out_m, g_out_o, mid_sums, ffn = mid_call(
        x1, gy, g_h2, g_h2_other, ctx_m, ctx_o, flat(w_out_m), flat(w_out_o), norm_params, ffn,
        (lists[0],),
    )
    ffn_other = swap_mp(ffn)

    back_one = attend_back_call(
        seg, cos, sin, qkv_m, qkv_o, g_ctx_m, g_ctx_o, *ctx_one, *groups[0]
    )
    for level in range(2, routes.depth + 1):
        lists, parts_mlp = sort_out(1, level, parts_mlp, (back_one[0],))
    back_two = attend_back_call(
        seg, cos, sin, qkv_m, qkv_o, g_ctx_m, g_ctx_o, *ctx_two, *groups[1], (lists[0],)
    )
    g_in_m, g_in_o, g_h1, gb_m, gb_o, in_sums = in_grads_call(
        (back_one[0], back_two[0]), (back_one[1], back_two[1]), a1, x,
        flat(w_qkv_m), flat(w_qkv_o), g_out_m, g_out_o,
    )
    g_h1_other = swap_mp(g_h1)
    parts_in = [pieces(g_in_m), routes.swap_cores(pieces(g_in_o))]
    for level in range(1, routes.depth + 1):
        _, parts_in = sort_out(0, level, parts_in)

    out_roll = x1 + (ffn.astype(F32) + ffn_other.astype(F32)) + norm_params[5]
    block_out = roll_rows(out_roll, tok - start)
    grad_roll = last_call(x, gx1, g_h1, g_h1_other, norm_params)
    grad_tokens = roll_rows(grad_roll, tok - start)

    def owned(number, parts):
        return add_pick_call(
            table,
            [(place[("slot", number, which)], 0) for which in range(2)],
            parts,
            [slot_cap] * 2,
            dtype=F32,
            name="owned",
        )

    owned_in, owned_mlp = owned(0, parts_in), owned(1, parts_mlp)
    piece_ids = table[place["piece"], :slot_cap]
    other_ids = routes.swap_cores(piece_ids)
    kept, sent = (
        jnp.where(ids[:, None, None] >= spans[1][0], owned_mlp[which], owned_in[which])
        for which, ids in enumerate((piece_ids, other_ids))
    )
    arrived = routes.swap_cores(sent)
    ids = piece_ids[:, None, None]

    def fast_grad():
        return jnp.where(
            first_core, jnp.concatenate([kept, arrived], 1), jnp.concatenate([arrived, kept], 1)
        )

    def slow_grad():
        def stack(in_part, mlp_part):
            return jnp.concatenate([pieces(in_part), pieces(mlp_part)], axis=0).astype(F32)

        mine, other = stack(g_in_m, g_mlp_m), stack(g_in_o, g_mlp_o)
        both = jnp.where(first_core, jnp.stack([mine, other], 1), jnp.stack([other, mine], 1))
        total = lax.psum(both.reshape(piece_total, piece_len, width), "dp")
        return total[jnp.maximum(piece_ids, 0)]

    owned_grad = lax.cond(fits, fast_grad, slow_grad)
    begins = ids * piece_len
    rate = jnp.where(begins < 4 * head_width + hidden, 0.03, 0.015)
    rate = jnp.where(
        begins < 3 * head_width, 0.03, jnp.where(begins < 4 * head_width, 0.2, rate)
    ).astype(F32)
    updated = adam_step(
        weight_table[0], moment_table[0], square_table[0], owned_grad, rate, DECAY_RATE
    )
    tables_next = tuple(jnp.where(ids >= 0, part, 0.0)[None] for part in updated)

    def natural(mine, other):
        mine, other = mine.reshape(-1, half_len), other.reshape(-1, half_len)
        return jnp.where(
            first_core, jnp.stack([mine, other], 1), jnp.stack([other, mine], 1)
        ).reshape(1, -1)

    in_total = in_sums[0:2] + swap_mp(in_sums[0:2])
    norm_total = jnp.concatenate([in_total, mid_sums[0:4]], axis=0)
    bias_total = jnp.concatenate(
        [natural(gb_m, gb_o), natural(gb_up[:, : hidden // 2], gb_up[:, hidden // 2 :])], axis=1
    )
    bit = 1
    while bit < dp_size:
        pairs = [(d, d ^ bit) for d in range(dp_size)]
        norm_total = norm_total + lax.ppermute(norm_total, "dp", pairs)
        bias_total = bias_total + lax.ppermute(bias_total, "dp", pairs)
        bit *= 2
    norm_rate = jnp.array(NORM_RATES, F32)[:, None]
    norms_out = adam_step(norm_params, norm_moment, norm_square, norm_total, norm_rate, 0.0)
    biases_out = adam_step(bias_params, bias_moment, bias_square, bias_total, BIAS_RATE, 0.0)
    return (block_out, grad_tokens, *tables_next, *norms_out, *biases_out)


def solution(mesh):
    flat = P("dp", None)
    pieces = P("mp", "dp", None, None)
    bias = P("mp", None)
    return jax.shard_map(
        body,
        mesh=mesh,
        in_specs=(flat, flat, flat, P(), pieces, pieces, pieces, P(), P(), P(), bias, bias, bias),
        out_specs=(flat, flat, pieces, pieces, pieces, P(), P(), P(), bias, bias, bias),
        check_vma=False,
    )
```

```python
import functools

import jax
import jax.numpy as jnp
import numpy as np
from jax import lax
from jax.experimental import pallas as pl
from jax.experimental.pallas import tpu as pltpu
from jax.sharding import PartitionSpec as P

HEADS = 20
HEAD_DIM = 32
HALF = HEAD_DIM // 2
FF = 2560
LONGEST = 1024
STEP = 10

EPS_NORM = 1e-05
BETA_ONE = 0.5
BETA_TWO = 0.5
ADAM_EPS = 1e-08
DECAY_RATE = 0.01
NEG_FILL = -1e30
NORM_RATES = (0.5, 0.1, 0.5, 0.1, 0.1, 0.1)
BIAS_RATE = 0.1
SCALE = HEAD_DIM**-0.5
SCALE_LOG2 = SCALE * 1.4426950408889634
SAFE_EXP = 100.0

BF = jnp.bfloat16
F32 = jnp.float32
I32 = jnp.int32
TILE = 256
LANES = 128
VMEM_LIMIT = 56 << 20
SHRINK = 0.1


def params(*kinds):
    return pltpu.CompilerParams(dimension_semantics=kinds or None, vmem_limit_bytes=VMEM_LIMIT)


def cost(flops, moved):
    return pl.CostEstimate(flops=int(flops / SHRINK), bytes_accessed=int(moved / SHRINK), transcendentals=0)


def dot_nn(a, b):
    return lax.dot_general(a, b, (((1,), (0,)), ((), ())), preferred_element_type=F32)


def dot_nt(a, b):
    return lax.dot_general(a, b, (((1,), (1,)), ((), ())), preferred_element_type=F32)


def dot_tn(a, b):
    return lax.dot_general(a, b, (((0,), (0,)), ((), ())), preferred_element_type=F32)


def split_two(v):
    hi = v.astype(BF).astype(F32)
    return hi, v - hi


def split_three(v):
    hi = v.astype(BF).astype(F32)
    mid = (v - hi).astype(BF).astype(F32)
    return hi, mid, v - hi - mid


def normalized(v):
    centred = v - jnp.mean(v, axis=-1, keepdims=True)
    inv = lax.rsqrt(jnp.mean(centred * centred, axis=-1, keepdims=True) + EPS_NORM)
    return centred * inv, inv


SMEM = pl.BlockSpec(memory_space=pltpu.SMEM)


def whole(shape):
    return pl.BlockSpec(shape, lambda *_: (0,) * len(shape))


ANYWHERE = pl.BlockSpec(memory_space=pl.ANY)


def rows(width, begin=0):
    return pl.BlockSpec((TILE, width), lambda t: (begin + t, 0))


def cols(height, begin=0):
    return pl.BlockSpec((height, TILE), lambda t: (0, begin + t))


def both(height, begin=0):
    return pl.BlockSpec((2, height, TILE), lambda t: (0, 0, begin + t))


def shaped(shape, dtype):
    return jax.ShapeDtypeStruct(shape, dtype)


def call(kernel, args, in_specs, out_specs, out_shape, name, deps=(), scratch=(), **more):
    count = len(args)

    def wrapped(*refs):
        kernel(*refs[:count], *refs[count + len(deps) :])

    return pl.pallas_call(
        wrapped,
        in_specs=list(in_specs) + [ANYWHERE] * len(deps),
        out_specs=out_specs,
        out_shape=out_shape,
        scratch_shapes=list(scratch),
        compiler_params=params(*(("arbitrary",) if "grid" in more else ())),
        name=name,
        **more,
    )(*args, *deps)


def qkv_kernel(x_ref, norm_ref, wm_ref, wo_ref, bm_ref, bo_ref, cos_ref, sin_ref, m_ref, o_ref, a_ref):
    n1, _ = normalized(x_ref[...].astype(F32))
    a1 = (n1 * norm_ref[0:1] + norm_ref[1:2]).astype(BF)
    a_ref[...] = a1
    mine = dot_nt(wm_ref[...], a1) + bm_ref[...]
    other = dot_nt(wo_ref[...], a1) + bo_ref[...]
    width = m_ref.shape[1]
    cos, sin = cos_ref[...], sin_ref[...]
    for which in range(2):
        for at in range(0, width, HALF):
            here = which * width + at
            p, r = mine[here : here + HALF], other[here : here + HALF]
            m_ref[which, at : at + HALF, :] = (p * cos - r * sin).astype(BF)
            o_ref[which, at : at + HALF, :] = (r * cos + p * sin).astype(BF)
    m_ref[2] = mine[2 * width :].astype(BF)
    o_ref[2] = other[2 * width :].astype(BF)


def qkv_call(x, norms, w_mine, w_other, b_mine, b_other, cos, sin, deps=()):
    tok, width = x.shape
    out = w_mine.shape[0]
    third = pl.BlockSpec((3, out // 3, TILE), lambda t: (0, 0, t))
    return call(
        qkv_kernel,
        (x, norms, w_mine, w_other, b_mine, b_other, cos, sin),
        [
            rows(width), whole(norms.shape), whole(w_mine.shape), whole(w_mine.shape),
            whole(b_mine.shape), whole(b_mine.shape), cols(HALF), cols(HALF),
        ],
        [third, third, rows(width)],
        [shaped((3, out // 3, tok), BF)] * 2 + [shaped((tok, width), BF)],
        "ln_qkv",
        deps,
        grid=(tok // TILE,),
        cost_estimate=cost(4 * tok * width * out, 8e6),
    )


def mlp_kernel(
    groups, chained, x_ref, gy_ref, *refs,
):
    ctx_refs, refs = refs[: 2 * groups], refs[2 * groups :]
    w_mine, w_other, wx_mine, wx_other, bup_ref, norm_ref = refs[:6]
    refs = refs[6 + chained :]
    x1_ref, a2_ref, act_ref, gpre_ref, ffn_ref, gh_ref, gbup_ref, out_w, up_w, down_w = refs

    @pl.when(pl.program_id(0) == 0)
    def _():
        quarter, half = wx_mine.shape[0], up_w.shape[0] // 2
        for at, ref in enumerate((w_mine, w_other, wx_mine, wx_other)):
            out_w[at * quarter : (at + 1) * quarter, :] = ref[:quarter, :]
        for at, ref in enumerate((w_mine, w_other)):
            up_w[at * half : (at + 1) * half, :] = ref[quarter : quarter + half, :]
            down_w[at * half : (at + 1) * half, :] = ref[quarter + half :, :]

    gy = gy_ref[...]
    own, far = ctx_refs[:groups], ctx_refs[groups:]
    ctx = jnp.concatenate([ref[j] for some in (own, far) for j in range(2) for ref in some], axis=0)
    x1 = x_ref[...].astype(F32) + dot_tn(ctx, out_w[...]) + norm_ref[4:5]
    x1_ref[...] = x1
    n2, _ = normalized(x1)
    a2 = (n2 * norm_ref[2:3] + norm_ref[3:4]).astype(BF)
    a2_ref[...] = a2
    pre = dot_nt(a2, up_w[...]) + bup_ref[...]
    cdf = 0.5 * (1.0 + lax.erf(pre * 0.7071067811865476))
    act = (pre * cdf).astype(BF)
    act_ref[...] = act
    slope = cdf + pre * (jnp.exp(-0.5 * pre * pre) * 0.3989422804014327)
    gpre = (slope * dot_nt(gy, down_w[...])).astype(BF)
    gpre_ref[...] = gpre
    ffn_ref[...] = dot_nn(act, down_w[...]).astype(BF)
    gh_ref[...] = dot_nn(gpre, up_w[...]).astype(BF)
    part = jnp.sum(gpre.astype(F32), axis=0, keepdims=True)

    @pl.when(pl.program_id(0) == 0)
    def _():
        gbup_ref[...] = part

    @pl.when(pl.program_id(0) > 0)
    def _():
        gbup_ref[...] += part


def mlp_call(span, x, gy, ctx, w_mine, w_other, wx, b_up, norms, before=(), deps=()):
    tok, width = x.shape
    hidden = b_up.shape[1]
    quarter = wx[0].shape[0]
    begin, count = span[0], span[1] - span[0]
    args = (x, gy, *ctx, w_mine, w_other, *wx, b_up, norms, *before)
    return call(
        functools.partial(mlp_kernel, len(ctx) // 2, len(before)),
        args,
        [rows(width, begin)] * 2
        + [both(part.shape[1], begin) for part in ctx]
        + [whole(w_mine.shape)] * 2
        + [whole((quarter, width))] * 2
        + [whole(b_up.shape), whole(norms.shape)]
        + [ANYWHERE] * len(before),
        [
            rows(width, begin), rows(width, begin), rows(hidden, begin), rows(hidden, begin),
            rows(width, begin), rows(width), whole((1, hidden)),
        ],
        [
            shaped((tok, width), F32), shaped((tok, width), BF), shaped((tok, hidden), BF),
            shaped((tok, hidden), BF), shaped((tok, width), BF), shaped((count * TILE, width), BF),
            shaped((1, hidden), F32),
        ],
        "mlp",
        deps,
        scratch=[
            pltpu.VMEM((4 * quarter, width), BF), pltpu.VMEM((hidden, width), BF),
            pltpu.VMEM((hidden, width), BF),
        ],
        grid=(count,),
        cost_estimate=cost(2 * count * TILE * width * (hidden * 4 + 4 * quarter) * 1.6, 2e7),
        input_output_aliases={len(args) - len(before) + j: j for j in range(len(before))},
    )


def mlp_grads_kernel(act_ref, gpre_ref, a2_ref, gy_ref, mine_ref, other_ref, down_sum, up_sum):
    step = pl.program_id(0)
    down = dot_tn(act_ref[...], gy_ref[...])
    up = dot_tn(gpre_ref[...], a2_ref[...])

    @pl.when(step == 0)
    def _():
        down_sum[...] = down
        up_sum[...] = up

    @pl.when(step > 0)
    def _():
        down_sum[...] += down
        up_sum[...] += up

    @pl.when(step == pl.num_programs(0) - 1)
    def _():
        half = down_sum.shape[0] // 2
        for which, out_ref in enumerate((mine_ref, other_ref)):
            here = pl.ds(which * half, half)
            out_ref[:half, :] = up_sum[here, :].astype(BF)
            out_ref[half:, :] = down_sum[here, :].astype(BF)


def mlp_grads_call(act, gpre, a2, gy, deps=()):
    tok, hidden = act.shape
    width = a2.shape[1]
    return call(
        mlp_grads_kernel,
        (act, gpre, a2, gy),
        [rows(hidden), rows(hidden), rows(width), rows(width)],
        [whole((hidden, width))] * 2,
        [shaped((hidden, width), BF)] * 2,
        "mlp_grads",
        deps,
        scratch=[pltpu.VMEM((hidden, width), F32)] * 2,
        grid=(tok // TILE,),
        cost_estimate=cost(4 * tok * width * hidden * 1.3, 1.4e7),
    )


def mid_kernel(
    groups, chained, handed, x1_ref, gy_ref, gh_a, gh_b, *refs,
):
    ctx_refs, refs = refs[:groups], refs[groups:]
    wm_ref, wo_ref, norm_ref = refs[:3]
    refs = refs[3 + chained + handed :]
    gx_ref, g_out, gout_ref, sum_ref = refs[:4]
    cm, co = (jnp.concatenate([ref[j] for ref in ctx_refs], axis=0) for j in range(2))
    step = pl.program_id(0)
    gy = gy_ref[...].astype(F32)
    gh = gh_a[...].astype(F32) + gh_b[...].astype(F32)
    n2, inv = normalized(x1_ref[...])
    e = gh * norm_ref[2:3]
    gx = gy + inv * (
        e - jnp.mean(e, axis=-1, keepdims=True) - n2 * jnp.mean(e * n2, axis=-1, keepdims=True)
    )
    gx_ref[...] = gx
    gm = gx.astype(BF)
    g_out[0] = dot_nt(wm_ref[...], gm).astype(BF)
    g_out[1] = dot_nt(wo_ref[...], gm).astype(BF)

    @pl.when(step == 0)
    def _():
        gout_ref[...] = jnp.zeros_like(gout_ref)
        sum_ref[...] = jnp.zeros_like(sum_ref)

    gout_ref[0] += dot_nn(cm, gm)
    gout_ref[1] += dot_nn(co, gm)
    for at, value in enumerate((gh * n2, gh, gx, gy)):
        sum_ref[at : at + 1, :] += jnp.sum(value, axis=0, keepdims=True)


def mid_call(span, x1, gy, gh, gh_other, ctx, w_m, w_o, norms, before=(), hand=(), deps=()):
    tok, width = x1.shape
    head = sum(part.shape[1] for part in ctx)
    begin, count = span[0], span[1] - span[0]
    args = (x1, gy, gh, gh_other, *ctx, w_m, w_o, norms, *before, *hand)
    fixed = len(args) - len(before) - len(hand)
    aliases = {fixed + j: j for j in range(len(before))}
    aliases.update({fixed + len(before) + j: 4 + j for j in range(len(hand))})
    return call(
        functools.partial(mid_kernel, len(ctx), len(before), len(hand)),
        args,
        [rows(width, begin)] * 2
        + [rows(width)] * 2
        + [both(part.shape[1], begin) for part in ctx]
        + [whole((head, width))] * 2
        + [whole(norms.shape)]
        + [ANYWHERE] * (len(before) + len(hand)),
        [rows(width, begin), both(head), whole((2, head, width)), whole((8, width))]
        + [ANYWHERE] * len(hand),
        [
            shaped((tok, width), F32), shaped((2, head, count * TILE), BF),
            shaped((2, head, width), F32), shaped((8, width), F32),
        ]
        + [shaped(part.shape, part.dtype) for part in hand],
        "mid_back",
        deps,
        grid=(count,),
        cost_estimate=cost(8 * count * TILE * width * head * 2, 1e7),
        input_output_aliases=aliases,
    )


def split_small(value):
    hi = value.astype(BF)
    lo = (value - hi.astype(F32)).astype(BF)
    return hi, lo, hi.astype(F32) + lo.astype(F32)


def in_grads_kernel(groups, gouts, *refs):
    g_refs, refs = refs[:groups], refs[groups:]
    out_refs, mid_refs, up_refs, refs = (
        refs[:gouts], refs[gouts : 2 * gouts], refs[2 * gouts : 3 * gouts], refs[3 * gouts :]
    )
    core_ref, a1_ref, x_ref, wm_ref, wo_ref, mine_ref, other_ref, gh_ref, sum_ref = refs[:9]
    m_sum, o_sum, gbm_ref, gbo_ref = refs[9:]
    step = pl.program_id(0)
    count = wm_ref.shape[0]
    a1 = a1_ref[...]
    gm, go = (
        jnp.concatenate([ref[half, j] for j in range(3) for ref in g_refs], axis=0)
        for half in range(2)
    )

    @pl.when(step == 0)
    def _():
        m_sum[...] = jnp.zeros_like(m_sum)
        o_sum[...] = jnp.zeros_like(o_sum)
        gbm_ref[...] = jnp.zeros_like(gbm_ref)
        gbo_ref[...] = jnp.zeros_like(gbo_ref)
        sum_ref[...] = jnp.zeros_like(sum_ref)

    m_sum[...] += dot_nn(gm, a1)
    o_sum[...] += dot_nn(go, a1)
    gbm_ref[...] += jnp.sum(gm.astype(F32), axis=1, keepdims=True)
    gbo_ref[...] += jnp.sum(go.astype(F32), axis=1, keepdims=True)
    gh = dot_tn(gm, wm_ref[...]) + dot_tn(go, wo_ref[...])
    gh_ref[...] = gh.astype(BF)
    n1, _ = normalized(x_ref[...].astype(F32))
    sum_ref[0:1, :] += jnp.sum(gh * n1, axis=0, keepdims=True)
    sum_ref[1:2, :] += jnp.sum(gh, axis=0, keepdims=True)

    @pl.when(step == pl.num_programs(0) - 1)
    def _():
        width = gh.shape[1]
        up = sum((ref[...] for ref in up_refs[1:]), up_refs[0][...])
        pairs = (
            [jnp.transpose(jnp.broadcast_to(ref[...], (count, LANES)))[0:1] for ref in (gbm_ref, gbo_ref)],
            [up[:, :width], up[:, width:]],
        )
        sum_ref[2:6, :] = sum((ref[0:4, :] for ref in mid_refs[1:]), mid_refs[0][0:4, :])
        for at, (first, second) in zip((6, 8), pairs):
            swapped = core_ref[0] == 1
            sum_ref[at : at + 1, : first.shape[1]] = jnp.where(swapped, second, first)
            sum_ref[at + 1 : at + 2, : first.shape[1]] = jnp.where(swapped, first, second)
        hi, lo, kept = split_small(sum_ref[...])
        sum_ref[...] = kept
        more = count + out_refs[0].shape[1]
        for ref, total, half in ((mine_ref, m_sum, 0), (other_ref, o_sum, 1)):
            ref[:count, :] = total[...].astype(BF)
            ref[count:more, :] = sum((out[half] for out in out_refs[1:]), out_refs[0][half]).astype(BF)
        other_ref[more : more + 16, :] = hi
        other_ref[more + 16 :, :] = lo


def in_grads_call(grads, core, a1, x, w_m, w_o, gouts, mid_sums, gb_ups, deps=()):
    tok, width = a1.shape
    count, more = w_m.shape[0], gouts[0].shape[1]
    parts = [
        pl.BlockSpec(part.shape[:3] + (TILE,), lambda t: (0, 0, 0, t)) for part in grads
    ]
    return call(
        functools.partial(in_grads_kernel, len(grads), len(gouts)),
        (*grads, *gouts, *mid_sums, *gb_ups, core[None], a1, x, w_m, w_o),
        parts
        + [whole(part.shape) for part in (*gouts, *mid_sums, *gb_ups)]
        + [SMEM, rows(width), rows(width)]
        + [whole((count, width))] * 2,
        [whole((count + more, width)), whole((count + more + 32, width)), rows(width), whole((16, width))],
        [
            shaped((count + more, width), BF), shaped((count + more + 32, width), BF),
            shaped((tok, width), BF), shaped((16, width), F32),
        ],
        "in_grads",
        deps,
        scratch=[pltpu.VMEM((count, width), F32)] * 2 + [pltpu.VMEM((count, 1), F32)] * 2,
        grid=(tok // TILE,),
        cost_estimate=cost(8 * tok * width * count * 1.3, 1e7),
    )


def out_kernel(x1_ref, a_ref, b_ref, norm_ref, out_ref):
    out_ref[...] = x1_ref[...] + (a_ref[...].astype(F32) + b_ref[...].astype(F32)) + norm_ref[5:6]


def out_call(x1, ffn_a, ffn_b, norms):
    tok, width = x1.shape
    return call(
        out_kernel,
        (x1, ffn_a, ffn_b, norms),
        [rows(width)] * 3 + [whole(norms.shape)],
        rows(width),
        shaped((tok, width), F32),
        "layer_out",
        grid=(tok // TILE,),
        cost_estimate=cost(4e9, 1e7),
    )


def keep_kernel(*refs):
    half = len(refs) // 2
    for source, target in zip(refs[:half], refs[half:]):
        target[...] = source[...]


def keep_call(arrays, deps=()):
    specs = [whole(array.shape) for array in arrays]
    return call(
        keep_kernel, arrays, specs, specs, [shaped(a.shape, a.dtype) for a in arrays], "keep", deps,
        cost_estimate=cost(4e9, 1e7),
    )


def last_kernel(x_ref, gx_ref, gh_a, gh_b, norm_ref, out_ref):
    n1, inv = normalized(x_ref[...].astype(F32))
    e = (gh_a[...].astype(F32) + gh_b[...].astype(F32)) * norm_ref[0:1]
    out_ref[...] = gx_ref[...] + inv * (
        e - jnp.mean(e, axis=-1, keepdims=True) - n1 * jnp.mean(e * n1, axis=-1, keepdims=True)
    )


def last_call(x, gx, gh_a, gh_b, norms):
    tok, width = x.shape
    return call(
        last_kernel,
        (x, gx, gh_a, gh_b, norms),
        [rows(width)] * 4 + [whole(norms.shape)],
        rows(width),
        shaped((tok, width), F32),
        "last_back",
        grid=(tok // TILE,),
        cost_estimate=cost(1e6, 1.2e7),
    )


def layout_kernel(core_ref, len_ref, freq_ref, cos_ref, sin_ref, row_ref, col_ref, start_ref):
    tok = cos_ref.shape[1]
    docs = len_ref.shape[1]
    begin, best, start = 0, len_ref[0, 0], 0
    begins, ends = [], []
    for doc in range(docs):
        size = len_ref[0, doc]
        if doc:
            start = jnp.where(size > best, begin, start)
            best = jnp.maximum(size, best)
        begins.append(begin)
        begin = begin + size
        ends.append(begin)
    start_ref[0] = start + jnp.zeros((), I32)

    def origin(places):
        at = places + start
        return jnp.where(at >= tok, at - tok, at)

    def document(at):
        return sum(((at >= end).astype(I32) for end in ends), jnp.zeros(at.shape, I32))

    row = origin(lax.broadcasted_iota(I32, (1, tok), 1))
    first = jnp.zeros((1, tok), I32)
    for begin in begins[1:]:
        first = jnp.where(row >= begin, begin, first)
    angles = freq_ref[...] * (row - first).astype(F32)
    cos_ref[...] = jnp.cos(angles)
    sine = jnp.sin(angles)
    sin_ref[...] = jnp.where(core_ref[0] == 0, sine, -sine)
    rest = row_ref.shape[1]
    row_ref[...] = document(row[:, tok - rest :])
    col_ref[...] = document(origin(lax.broadcasted_iota(I32, (rest, 1), 0) + (tok - rest)))


def layout_call(core, lengths, tok, deps=()):
    rest = tok - LONGEST
    freq = np.float32(10000.0) ** -(np.arange(0, HEAD_DIM, 2).astype(np.float32) / HEAD_DIM)
    return call(
        layout_kernel,
        (core[None], lengths, jnp.asarray(freq[:, None], F32)),
        [SMEM, SMEM, whole((HALF, 1))],
        [whole((HALF, tok))] * 2 + [whole((1, rest)), whole((rest, 1)), SMEM],
        [shaped((HALF, tok), F32)] * 2
        + [shaped((1, rest), I32), shaped((rest, 1), I32), shaped((1,), I32)],
        "layout",
        deps,
    )


def halves_kernel(core_ref, table_ref, mine_ref, other_ref):
    first = core_ref[0] == 0
    count = mine_ref.shape[1]
    upper, lower = table_ref[:, :count, :], table_ref[:, count:, :]
    mine_ref[...] = jnp.where(first, upper, lower).astype(BF)
    other_ref[...] = jnp.where(first, lower, upper).astype(BF)


def halves_call(core, table):
    cap, count, width = table.shape
    half = (cap, count // 2, width)
    return call(
        halves_kernel,
        (core[None], table),
        [SMEM, whole(table.shape)],
        [whole(half)] * 2,
        [shaped(half, BF)] * 2,
        "halves",
    )


def attend_kernel(seg_row, seg_col, m_ref, o_ref, ctx_ref, log_ref):
    tok = m_ref.shape[2]
    rest = tok - LONGEST
    q_t, k_t, v_t = (jnp.concatenate([m_ref[j], o_ref[j]], axis=0) for j in range(3))
    qs = q_t.astype(F32) * SCALE_LOG2
    hi, lo = split_two(qs)
    qx = jnp.transpose(jnp.concatenate([hi, lo], axis=0)).astype(BF)
    kx = jnp.concatenate([k_t, k_t], axis=0)
    v_f = v_t.astype(F32)
    vx = jnp.transpose(jnp.concatenate([v_f, jnp.ones((8, tok), F32)], axis=0)).astype(BF)
    k_f = k_t.astype(F32)
    q_top = jnp.max(jnp.sum(qs * qs, axis=0, keepdims=True))
    k_top = jnp.max(jnp.sum(k_f * k_f, axis=0, keepdims=True))
    safe = q_top * k_top < SAFE_EXP * SAFE_EXP
    same = seg_col[...] == seg_row[...]

    def finish(sums, shift, at, count):
        turned = jnp.transpose(sums)
        total = turned[HEAD_DIM : HEAD_DIM + 1]
        ctx = (turned[0:HEAD_DIM] / total).astype(BF)
        ctx_ref[0, :, at : at + count] = ctx[:HALF]
        ctx_ref[1, :, at : at + count] = ctx[HALF:]
        log_total = jnp.log2(total)
        if shift is not None:
            log_total = log_total + jnp.transpose(jnp.broadcast_to(shift, (count, LANES)))[0:1]
        log_ref[0, :, at : at + count] = log_total

    def run(exact):
        for at in range(0, LONGEST, TILE):
            scores = dot_nn(qx[at : at + TILE], kx[:, :LONGEST])
            shift = None
            if exact:
                shift = jnp.max(scores, axis=1, keepdims=True)
                scores = scores - shift
            finish(dot_nn(jnp.exp2(scores).astype(BF), vx[:LONGEST]), shift, at, TILE)
        if rest:
            scores = jnp.where(same, dot_nn(qx[LONGEST:], kx[:, LONGEST:]), NEG_FILL)
            shift = None
            if exact:
                shift = jnp.max(scores, axis=1, keepdims=True)
                scores = scores - shift
            finish(dot_nn(jnp.exp2(scores).astype(BF), vx[LONGEST:]), shift, LONGEST, rest)

    @pl.when(safe)
    def _():
        run(False)

    @pl.when(jnp.logical_not(safe))
    def _():
        run(True)


def attend_call(segs, qkv_m, qkv_o, first, count, deps=()):
    tok = qkv_m.shape[2]
    rest = segs[0].shape[1]
    part = pl.BlockSpec((3, HALF, tok), lambda h: (0, first + h, 0))
    out = pl.BlockSpec((2, HALF, tok), lambda h: (0, h, 0))
    return call(
        attend_kernel,
        (*segs, qkv_m, qkv_o),
        [whole((1, rest)), whole((rest, 1)), part, part],
        [out, pl.BlockSpec((1, 1, tok), lambda h: (h, 0, 0))],
        [shaped((2, count * HALF, tok), BF), shaped((count, 1, tok), F32)],
        "attend",
        deps,
        grid=(count,),
        cost_estimate=cost(count * 2.5e9, 3e6),
    )


def attend_back_kernel(
    q_begin, q_end, last, seg_row, seg_col, cos_ref, sin_ref, m_ref, o_ref, g_ref, ctx_ref, log_ref,
    *refs,
):
    tok = m_ref.shape[2]
    rest = tok - LONGEST
    end = tok if last else q_end
    span = slice(q_begin, end)
    q_t, k_t, v_t = (jnp.concatenate([m_ref[j], o_ref[j]], axis=0) for j in range(3))
    q_f = q_t[:, span].astype(F32)
    ctx = jnp.concatenate([ctx_ref[0, :, span], ctx_ref[1, :, span]], axis=0).astype(F32)
    g_f = jnp.concatenate([g_ref[0], g_ref[1]], axis=0).astype(F32)
    hi, lo = split_two(q_f * SCALE_LOG2)
    weighted = jnp.sum(g_f * ctx, axis=0, keepdims=True)
    pad = jnp.zeros((13, end - q_begin), F32)
    qx = jnp.concatenate([hi, lo, *split_three(log_ref[0, :, span]), pad], axis=0).astype(BF)
    keys = tok if last else LONGEST
    k_f, v_f = k_t[:, :keys].astype(F32), v_t[:, :keys].astype(F32)
    minus = jnp.concatenate([jnp.full((3, keys), -1.0, F32), jnp.zeros((13, keys), F32)], axis=0)
    kx = jnp.transpose(jnp.concatenate([k_f, k_f, minus], axis=0)).astype(BF)
    gx = jnp.concatenate([g_f, *split_three(weighted), pad], axis=0).astype(BF)
    vx = jnp.transpose(jnp.concatenate([v_f, minus], axis=0)).astype(BF)
    qn = jnp.transpose(q_f).astype(BF)
    gn = jnp.transpose(g_f).astype(BF)

    if last:
        early_q, early_kv, out_ref = refs
    else:
        out_q, out_kv = refs

    def turned_back(grad, at, count):
        cos, sin = cos_ref[:, at : at + count], sin_ref[:, at : at + count]
        mine, other = grad[0:HALF] * SCALE, grad[HALF:] * SCALE
        return (mine * cos + other * sin).astype(BF), (other * cos - mine * sin).astype(BF)

    def block(k_at, k_count, q_at, q_count, mask, early):
        scores = dot_nn(kx[k_at : k_at + k_count], qx[:, q_at : q_at + q_count])
        if mask is not None:
            scores = jnp.where(mask, scores, NEG_FILL)
        prob = jnp.exp2(scores)
        grad_prob = dot_nn(vx[k_at : k_at + k_count], gx[:, q_at : q_at + q_count])
        grad_score = (prob * grad_prob).astype(BF)
        grad_v = jnp.transpose(dot_nn(prob.astype(BF), gn[q_at : q_at + q_count]))
        grad_k = jnp.transpose(dot_nn(grad_score, qn[q_at : q_at + q_count]))
        here = slice(k_at, k_at + k_count)
        if not last:
            out_kv[0, 0, :, here] = grad_k
            out_kv[1, 0, :, here] = grad_v
        else:
            if early:
                grad_k = grad_k + early_kv[0, 0, :, here]
                grad_v = grad_v + early_kv[1, 0, :, here]
            out_ref[0, 1, :, here], out_ref[1, 1, :, here] = turned_back(grad_k, k_at, k_count)
            out_ref[0, 2, :, here] = grad_v[:HALF].astype(BF)
            out_ref[1, 2, :, here] = grad_v[HALF:].astype(BF)
        return dot_nn(k_t[:, k_at : k_at + k_count], grad_score)

    grad_q = None
    for at in range(0, LONGEST, TILE):
        piece = block(at, TILE, 0, q_end - q_begin, None, True)
        grad_q = piece if grad_q is None else grad_q + piece
    mine, other = turned_back(grad_q, q_begin, q_end - q_begin)
    if not last:
        out_q[0], out_q[1] = mine, other
        return
    out_ref[0, 0, :, :q_begin] = early_q[0]
    out_ref[1, 0, :, :q_begin] = early_q[1]
    out_ref[0, 0, :, q_begin:q_end] = mine
    out_ref[1, 0, :, q_begin:q_end] = other
    if rest:
        same = seg_col[...] == seg_row[...]
        piece = block(LONGEST, rest, LONGEST - q_begin, rest, same, False)
        out_ref[0, 0, :, LONGEST:], out_ref[1, 0, :, LONGEST:] = turned_back(piece, LONGEST, rest)


def attend_back_call(
    q_begin, q_end, segs, cos, sin, qkv_m, qkv_o, g_ctx, ctx, logs, first, count, early=(), deps=()
):
    tok = qkv_m.shape[2]
    last = len(early) > 0
    rest = segs[0].shape[1]
    part = pl.BlockSpec((3, HALF, tok), lambda h: (0, first + h, 0))
    table = whole((HALF, tok))

    def by_head(length, offset=0):
        return pl.BlockSpec((2, HALF, length), lambda h: (0, offset + h, 0))

    pair = pl.BlockSpec((2, 1, HEAD_DIM, LONGEST), lambda h: (0, h, 0, 0))
    if last:
        out_specs = [pl.BlockSpec((2, 3, HALF, tok), lambda h: (0, 0, h, 0))]
        out_shape = [shaped((2, 3, count * HALF, tok), BF)]
    else:
        out_specs = [by_head(q_end), pair]
        out_shape = [
            shaped((2, count * HALF, q_end), BF), shaped((2, count, HEAD_DIM, LONGEST), F32)
        ]
    return call(
        functools.partial(attend_back_kernel, q_begin, q_end, last),
        (*segs, cos, sin, qkv_m, qkv_o, g_ctx, ctx, logs, *early),
        [
            whole((1, rest)), whole((rest, 1)), table, table, part, part,
            by_head(g_ctx.shape[2], first), by_head(tok), pl.BlockSpec((1, 1, tok), lambda h: (h, 0, 0)),
        ]
        + ([by_head(q_begin), pair] if last else []),
        out_specs,
        out_shape,
        "attend_back",
        deps,
        grid=(count,),
        cost_estimate=cost(count * 2.1e9, 6e6),
    )


class Routes:
    def __init__(self, dp_size, slot_cap, pieces, ready, spans):
        self.dp = dp_size
        self.cap = slot_cap
        self.chips = dp_size // 2
        self.pieces = pieces
        self.ready = ready
        self.spans = spans
        if self.chips == 8:
            self.stages = ((2, 4), (1, 2))
        elif self.chips == 64:
            self.stages = ((1, 8), (8, 2), (16, 4))
        else:
            self.stages = ((1, self.chips),)
        self.depth = len(self.stages)
        straight = self.stages[::-1]
        paired = ((1, 2), (4, 2), (2, 2)) if self.chips == 8 else straight
        self.back = (straight, paired)
        self.out = (self.stages, ((4, 2), (2, 2), (1, 2)) if self.chips == 8 else self.stages)
        self.fill = [self.limit(last, self.chips) for last in ready]
        self.begins = [0] + self.fill[:-1]

    def limit(self, count, groups):
        worst = min(count, self.dp // groups * self.cap)
        if self.chips != 8:
            return worst
        typical = {
            2: count * 11 // 20 + 8, 4: count * 3 // 10 + 10, 8: (count * 9 + 25) // 50 + 6
        }[groups]
        return worst if count == self.pieces else min(worst, typical)

    def span_limit(self, number, level):
        groups = 1
        for _, size in self.back[number][:level]:
            groups *= size
        return self.limit(self.spans[number][1] - self.spans[number][0], groups)

    def move(self, array, stage, shift):
        stride, size = stage
        pairs = []
        for device in range(self.dp):
            chip, core = device // 2, device % 2
            at = (chip // stride) % size
            pairs.append((device, 2 * (chip + ((at + shift) % size - at) * stride) + core))
        return lax.ppermute(array, "dp", pairs)

    def swap_cores(self, array):
        return lax.ppermute(array, "dp", [(d, d ^ 1) for d in range(self.dp)])

    def around(self, array, stage):
        return [array] + [self.move(array, stage, shift) for shift in range(1, stage[1])]

    def onward(self, buffers, stage):
        return buffers + [
            self.move(buffer, stage, shift) for shift in range(1, stage[1]) for buffer in buffers
        ]

    def tables(self, owners, me):
        place = {}

        def kernel(me_ref, own_ref, out_ref, row_ref):
            here = me_ref[0]
            my_chip, my_core = here // 2, here % 2
            row_ref[...] = jnp.full((1, LANES), -2, I32)
            row_ref[:, : self.pieces] = own_ref[...]
            row = row_ref[...]
            col = jnp.transpose(jnp.broadcast_to(row, (LANES, LANES)))[:, 0:1]
            id_row = lax.broadcasted_iota(I32, (1, LANES), 1)
            id_col = lax.broadcasted_iota(I32, (LANES, 1), 0)
            lane = lax.broadcasted_iota(I32, (LANES, LANES), 1)
            sub = lax.broadcasted_iota(I32, (LANES, LANES), 0)

            def rank_col(key_row, key_col):
                hit = (key_row == key_col) & (lane < sub)
                return jnp.sum(hit.astype(F32), axis=1, keepdims=True).astype(I32)

            def rank_row(key_row, key_col):
                hit = (key_row == key_col) & (sub < lane)
                return jnp.sum(hit.astype(F32), axis=0, keepdims=True).astype(I32)

            def gather(valid_col, entry_col, value_col):
                hit = valid_col & (entry_col == lane)
                return jnp.sum(
                    jnp.where(hit, value_col.astype(F32), 0.0), axis=0, keepdims=True
                ).astype(I32)

            def put(name, value):
                at = place.setdefault(name, len(place))
                out_ref[at : at + 1, :] = value

            def coord(chip, stage):
                return (chip // stage[0]) % stage[1]

            def group(chip, stages):
                key = 0
                for stage in stages:
                    key = key * stage[1] + coord(chip, stage)
                return key

            def fullest(inside, rank):
                return jnp.max(jnp.where(inside, rank, -1), axis=0, keepdims=True) + 1

            slot_col = rank_col(row, col)
            put("piece", gather(col == here, slot_col, id_col + 1) - 1)
            sibling = my_chip * 2 + 1 - my_core
            put("sibling", gather(col == sibling, slot_col, id_col + 1) - 1)
            over = jnp.zeros((1, 1), I32)
            real = id_col < self.pieces
            chip_col, chip_row = col // 2, row // 2
            rank_c, rank_r = rank_col(chip_row, chip_col), rank_row(chip_row, chip_col)
            from_core = jnp.where(col % 2 == my_core, 0, self.cap)
            put("send", gather(real & (chip_col == my_chip), rank_c, from_core + slot_col))
            for last, fill in zip(self.ready, self.fill):
                over = jnp.maximum(over, fullest(id_col < last, rank_c) - fill)
            put("late", jnp.broadcast_to(over, (1, LANES)))
            over = jnp.zeros((1, 1), I32)
            take = jnp.zeros((1, LANES), I32)
            for begin, end, stages in zip(self.begins, self.fill, self.out):
                spot, scale = rank_r - begin, end - begin
                for stage in stages:
                    away = (coord(my_chip, stage) - coord(chip_row, stage) + stage[1]) % stage[1]
                    spot = spot + away * scale
                    scale = scale * stage[1]
                take = jnp.where(rank_r >= begin, begin * self.chips + spot, take)
            put("take", take)
            for number, span in enumerate(self.spans):
                in_col = (id_col >= span[0]) & (id_col < span[1])
                in_row = (id_row >= span[0]) & (id_row < span[1])
                stages = self.back[number]
                ranks = {}
                for level in range(1, len(stages) + 1):
                    key_col = jnp.where(in_col, group(chip_col, stages[:level]), -1)
                    key_row = jnp.where(in_row, group(chip_row, stages[:level]), -1)
                    ranks[level] = rank_col(key_row, key_col)
                    over = jnp.maximum(
                        over, fullest(in_col, ranks[level]) - self.span_limit(number, level)
                    )
                value = id_col - span[0]
                for level, stage in enumerate(stages, 1):
                    size = stage[1]
                    inside = in_col & (
                        group(chip_col, stages[: level - 1]) == group(my_chip, stages[: level - 1])
                    )
                    for shift in range(size):
                        goal = (coord(my_chip, stage) + shift) % size
                        put(
                            ("back", number, level, shift),
                            gather(inside & (coord(chip_col, stage) == goal), ranks[level], value),
                        )
                    value = ranks[level]
                for which in range(2):
                    goal = my_chip * 2 + (my_core + which) % 2
                    put(
                        ("slot", number, which),
                        gather(in_col & (col == goal), slot_col, ranks[len(stages)]),
                    )
            put("over", jnp.broadcast_to(over, (1, LANES)))

        count = 6 + sum(2 + sum(size for _, size in stages) for stages in self.back)
        height = -(-count // 8) * 8
        table = pl.pallas_call(
            kernel,
            in_specs=[SMEM, whole((1, self.pieces))],
            out_specs=whole((height, LANES)),
            out_shape=shaped((height, LANES), I32),
            scratch_shapes=[pltpu.VMEM((1, LANES), I32)],
            compiler_params=params(),
            name="routes",
        )(me[None], owners[None, :])
        return table, place


def pick_call(table, picks, parts, sizes, name, deps=()):
    rows_each = [part.shape[0] for part in parts]
    shape = parts[0].shape[1:]

    def kernel(table_ref, *refs):
        ins, outs, source = refs[: len(parts)], refs[len(parts) : -1], refs[-1]
        at = 0
        for ref, count in zip(ins, rows_each):
            source[at : at + count] = ref[...]
            at += count
        for (row, start), size, out in zip(picks, sizes, outs):
            for j in range(size):
                out[j] = source[table_ref[row, start + j]]

    return call(
        kernel,
        (table, *parts),
        [SMEM] + [whole(part.shape) for part in parts],
        [whole((size,) + shape) for size in sizes],
        [shaped((size,) + shape, BF) for size in sizes],
        name,
        deps,
        scratch=[pltpu.VMEM((sum(rows_each),) + shape, BF)],
    )


def join_call(parts, deps=()):
    counts = [part.shape[0] for part in parts]
    shape = (sum(counts),) + parts[0].shape[1:]

    def kernel(*refs):
        at = 0
        for ref, count in zip(refs, counts):
            refs[-1][at : at + count] = ref[...]
            at += count

    return call(
        kernel, parts, [whole(part.shape) for part in parts], whole(shape), shaped(shape, BF), "join", deps
    )


def add_pick_call(table, picks, parts, sizes, dtype=BF, name="add_pick", small=None, extra=(), deps=()):
    shape = parts[0].shape[1:]
    lengths = [size + 2 * (j in extra) for j, size in enumerate(sizes)]

    def kernel(table_ref, *refs):
        ins, refs = refs[: len(parts)], refs[len(parts) :]
        if small is not None:
            small_ref, refs = refs[0], refs[1:]
            terms = [small_ref[...]] + [
                ref[ref.shape[0] - 2].astype(F32) + ref[ref.shape[0] - 1].astype(F32) for ref in ins[1:]
            ]
            while len(terms) > 1:
                middle = len(terms) // 2
                terms = [a + b for a, b in zip(terms[:middle], terms[middle:])]
            hi, lo, kept = split_small(terms[0])
            refs[len(sizes)][...] = kept
            for j in extra:
                refs[j][sizes[j]] = hi
                refs[j][sizes[j] + 1] = lo
        for (row, start), size, out in zip(picks, sizes, refs):
            for j in range(size):
                at = table_ref[row, start + j]
                total = ins[0][at].astype(F32)
                for ref in ins[1:]:
                    total = total + ref[at].astype(F32)
                out[j] = total.astype(dtype)

    out_specs = [whole((length,) + shape) for length in lengths]
    out_shape = [shaped((length,) + shape, dtype) for length in lengths]
    if small is not None:
        out_specs, out_shape = out_specs + [whole(shape)], out_shape + [shaped(shape, F32)]
    return call(
        kernel,
        (table, *parts) + (() if small is None else (small,)),
        [SMEM] + [whole(part.shape) for part in parts] + ([] if small is None else [whole(shape)]),
        out_specs,
        out_shape,
        name,
        deps,
    )


def adam_step(weights, first_mom, second_mom, gradient, rate_arr, decay_rate):
    first_new = BETA_ONE * first_mom + (1.0 - BETA_ONE) * gradient
    second_new = BETA_TWO * second_mom + (1.0 - BETA_TWO) * gradient * gradient
    first_fix = first_new / (1.0 - BETA_ONE**STEP)
    second_fix = second_new / (1.0 - BETA_TWO**STEP)
    weights_new = weights * (1.0 - rate_arr * decay_rate) - rate_arr * first_fix / (
        jnp.sqrt(second_fix) + ADAM_EPS
    )
    return (weights_new, first_new, second_new)


def swap_mp(array):
    return lax.ppermute(array, "mp", [(0, 1), (1, 0)])


def swap_both(array):
    dp_size = lax.axis_size("dp")
    pairs = [(2 * d + m, 2 * (d ^ 1) + 1 - m) for d in range(dp_size) for m in range(2)]
    return lax.ppermute(array, ("dp", "mp"), pairs)


def roll_rows(array, start):
    return lax.dynamic_slice_in_dim(
        jnp.concatenate([array, array], axis=0), start, array.shape[0], axis=0
    )


def body(
    tokens, cotangent, lengths, owners, weight_table, moment_table, square_table,
    norm_params, norm_moment, norm_square, bias_params, bias_moment, bias_square,
):
    dp_size = lax.axis_size("dp")
    mp_size = lax.axis_size("mp")
    heads = HEADS // mp_size
    head_width = heads * HEAD_DIM
    hidden = FF // mp_size
    tok, width = tokens.shape
    slot_cap, piece_len = weight_table.shape[1:3]
    half_len = piece_len // 2
    piece_total = owners.shape[0]
    me = lax.axis_index("dp").astype(I32)
    core = me % 2
    first_core = core == 0

    n_qkv, n_out = 3 * head_width // piece_len, head_width // piece_len
    n_up = hidden // piece_len
    ready = (n_qkv, piece_total)
    spans = ((0, n_qkv + n_out), (n_qkv + n_out, piece_total))
    routes = Routes(dp_size, slot_cap, piece_total, ready, spans)
    table, place = routes.tables(owners, me)

    own_half, sibling_half = halves_call(core, weight_table[0])
    chip_slots = [own_half, routes.swap_cores(sibling_half)]

    def half(array, which):
        return lax.dynamic_index_in_dim(array, which, axis=1, keepdims=False)

    def unless(bad, usual, other):
        return lax.while_loop(
            lambda state: state[0] > 0, lambda state: (jnp.zeros((), I32), other()), (bad, usual)
        )[1]

    def own_list(number, deps):
        begin, end = routes.begins[number], routes.fill[number]
        (chunk,) = pick_call(
            table, [(place["send"], begin)], chip_slots, [end - begin], "pick_owned", deps
        )
        return routes.around(chunk, routes.out[number][0])

    def collect(buffers, ranges, deps=()):
        sizes = [high - low for low, high in ranges]
        return pick_call(
            table, [(place["take"], low) for low, _ in ranges], buffers, sizes, "pick_all", deps
        )

    def flat(array):
        return array.reshape(-1, width)

    def slow_first():
        everyone = lax.all_gather(weight_table[0].astype(BF), "dp", axis=0, tiled=True)
        earlier = (owners[None, :] == owners[:, None]) & (
            jnp.arange(piece_total)[None, :] < jnp.arange(piece_total)[:, None]
        )
        at = owners * slot_cap + jnp.sum(earlier.astype(I32), axis=1)
        return half(everyone[at[:n_qkv]].reshape(n_qkv, 2, half_len, width), core)

    list_a = own_list(0, ())
    cos, sin, *segs, start = layout_call(core, lengths, tok, (list_a[0],))
    start = start[0]
    x = roll_rows(tokens, start)
    gy = roll_rows(cotangent, start)
    bias_halves = bias_params[0].reshape(-1, 2, half_len)
    b_mine, b_other = half(bias_halves, core), half(bias_halves, 1 - core)
    b_qkv = [part[:n_qkv].reshape(-1, 1) for part in (b_mine, b_other)]
    b_up = jnp.concatenate([part[n_qkv:].reshape(1, -1) for part in (b_mine, b_other)], axis=1)

    buffers_a = list_a
    for stage in routes.out[0][1:]:
        buffers_a = routes.onward(buffers_a, stage)
    many = routes.fill[1] > routes.fill[0]
    list_b = own_list(1, (*list_a[1:], buffers_a[len(list_a)])) if many else []
    (w_qkv_m,) = collect(buffers_a, ((0, n_qkv),), (x, gy, cos, sin, *b_qkv, b_up, *list_b[:1]))
    b_qkv = keep_call(b_qkv, (w_qkv_m,))
    buffers_b = [join_call(list_b, (w_qkv_m,))] if many else []
    w_qkv_m = unless(table[place["late"], 0], w_qkv_m, slow_first)
    w_qkv_o = routes.swap_cores(w_qkv_m)
    qkv_m, qkv_o, a1 = qkv_call(x, norm_params, flat(w_qkv_m), flat(w_qkv_o), *b_qkv, cos, sin, buffers_b[:1])
    for stage in routes.out[1][1:] if many else ():
        buffers_b = routes.onward(buffers_b, stage)
    cut = heads * 6 // 10
    groups = ((0, cut), (cut, heads - cut))
    ctx_one, logs_one = attend_call(segs, qkv_m, qkv_o, *groups[0])
    ctx_two, logs_two = attend_call(segs, qkv_m, qkv_o, *groups[1], (ctx_one, *buffers_b[1:2]))
    ctx = (ctx_one, ctx_two)
    ctx_x = [swap_mp(part) for part in ctx]
    w_out_m, w_mine = collect(buffers_a + buffers_b, ((n_qkv, n_qkv + n_out), (n_qkv, piece_total)), ctx_x)
    w_other = routes.swap_cores(w_mine)
    w_out_x = [flat(swap_mp(w_out_m)), flat(swap_both(w_out_m))]
    w_mine, w_other = flat(w_mine), flat(w_other)
    tiles = tok // TILE
    spans_tok = ((0, 2), (2, tiles))
    mlp_args = (x, gy, (*ctx, *ctx_x), w_mine, w_other, w_out_x, b_up, norm_params)
    *filled, g_h2_a, gb_up_a = mlp_call(spans_tok[0], *mlp_args)
    *filled, g_h2_b, gb_up_b = mlp_call(spans_tok[1], *mlp_args, filled)
    x1, a2, act, g_pre, ffn = filled
    g_h2_ax, g_h2_bx = swap_mp(g_h2_a), swap_mp(g_h2_b)
    g_mlp = mlp_grads_call(act, g_pre, a2, gy)

    def pieces(array):
        return array.reshape(-1, half_len, width)

    def sort_out(number, level, parts, small=None, deps=()):
        stage = routes.back[number][level - 1]
        size = stage[1]
        lists = add_pick_call(
            table,
            [(place[("back", number, level, shift)], 0) for shift in range(size)],
            parts,
            [routes.span_limit(number, level)] * size,
            small=small,
            extra=() if small is None else range(1, size),
            deps=deps,
        )
        moved = [routes.move(lists[shift], stage, shift) for shift in range(1, size)]
        return [lists[0]] + moved, lists[-1]

    gx1, g_ctx_a, g_out_a, mid_a, g_mlp_m, g_mlp_o = mid_call(
        spans_tok[0], x1, gy, g_h2_a, g_h2_ax, ctx, w_mine, w_other, norm_params, (), g_mlp
    )
    back = (segs, cos, sin, qkv_m, qkv_o)
    half_way = spans_tok[0][1] * TILE
    early_one = attend_back_call(0, half_way, *back, g_ctx_a, ctx_one, logs_one, *groups[0])
    parts_mlp, listed = sort_out(
        1, 1, [pieces(g_mlp_m), routes.swap_cores(pieces(g_mlp_o))], deps=early_one[:1]
    )
    early_two = attend_back_call(
        0, half_way, *back, g_ctx_a, ctx_two, logs_two, *groups[1], deps=(listed,)
    )
    gx1, g_ctx_b, g_out_b, mid_b, ffn = mid_call(
        spans_tok[1], x1, gy, g_h2_b, g_h2_bx, ctx, w_mine, w_other, norm_params, (gx1,), (ffn,),
        early_two[:1],
    )
    ffn_other = swap_mp(ffn)

    (grads_one,) = attend_back_call(
        half_way, LONGEST, *back, g_ctx_b, ctx_one, logs_one, *groups[0], early_one
    )
    parts_mlp, listed = sort_out(1, 2, parts_mlp, deps=(grads_one,))
    (grads_two,) = attend_back_call(
        half_way, LONGEST, *back, g_ctx_b, ctx_two, logs_two, *groups[1], early_two, (listed,)
    )
    g_in_m, g_in_o, g_h1, small = in_grads_call(
        (grads_one, grads_two), core, a1, x, flat(w_qkv_m), flat(w_qkv_o),
        (g_out_a, g_out_b), (mid_a, mid_b), (gb_up_a, gb_up_b), (ffn_other,),
    )
    g_h1_other = swap_mp(g_h1)
    out_roll = out_call(x1, ffn, ffn_other, norm_params)
    parts_in = [pieces(g_in_m), routes.swap_cores(pieces(g_in_o))]
    for level in range(1, len(routes.back[0])):
        parts_in, small = sort_out(0, level, parts_in, small, (out_roll,))
    for level in range(3, len(routes.back[1]) + 1):
        parts_mlp, _ = sort_out(1, level, parts_mlp, deps=(small,))
    parts_in, small = sort_out(0, len(routes.back[0]), parts_in, small)

    block_out = roll_rows(out_roll, tok - start)
    grad_roll = last_call(x, gx1, g_h1, g_h1_other, norm_params)
    grad_tokens = roll_rows(grad_roll, tok - start)

    def owned(number, parts, small=None):
        return add_pick_call(
            table,
            [(place[("slot", number, which)], 0) for which in range(2)],
            parts,
            [slot_cap] * 2,
            dtype=F32,
            name="owned",
            small=small,
        )

    owned_in, owned_mlp = owned(0, parts_in, small), owned(1, parts_mlp)
    small = owned_in[2]
    small_x = swap_mp(small[0:2])
    piece_ids = table[place["piece"], :slot_cap]
    other_ids = table[place["sibling"], :slot_cap]
    kept, sent = (
        jnp.where(ids[:, None, None] >= spans[1][0], owned_mlp[which], owned_in[which])
        for which, ids in enumerate((piece_ids, other_ids))
    )
    arrived = routes.swap_cores(sent)
    ids = piece_ids[:, None, None]

    def slow_grad():
        def stack(in_part, mlp_part):
            return jnp.concatenate([pieces(in_part), pieces(mlp_part)], axis=0).astype(F32)

        mine, other = stack(g_in_m, g_mlp_m), stack(g_in_o[: g_in_m.shape[0]], g_mlp_o)
        both = jnp.where(first_core, jnp.stack([mine, other], 1), jnp.stack([other, mine], 1))
        total = lax.psum(both.reshape(piece_total, piece_len, width), "dp")
        return total[jnp.maximum(piece_ids, 0)]

    owned_grad = jnp.where(
        first_core, jnp.concatenate([kept, arrived], 1), jnp.concatenate([arrived, kept], 1)
    )
    owned_grad = unless(table[place["over"], 0], owned_grad, slow_grad)
    begins = ids * piece_len
    rate = jnp.where(begins < 4 * head_width + hidden, 0.03, 0.015)
    rate = jnp.where(
        begins < 3 * head_width, 0.03, jnp.where(begins < 4 * head_width, 0.2, rate)
    ).astype(F32)
    updated = adam_step(
        weight_table[0], moment_table[0], square_table[0], owned_grad, rate, DECAY_RATE
    )
    tables_next = tuple(jnp.where(ids >= 0, part, 0.0)[None] for part in updated)

    norm_total = jnp.concatenate([small[0:2] + small_x, small[2:6]], axis=0)

    def natural(at, count):
        return jnp.stack([part[:count].reshape(-1, half_len) for part in small[at : at + 2]], 1).reshape(1, -1)

    bias_total = jnp.concatenate([natural(6, 3 * head_width // 2), natural(8, hidden // 2)], axis=1)
    norm_rate = jnp.array(NORM_RATES, F32)[:, None]
    norms_out = adam_step(norm_params, norm_moment, norm_square, norm_total, norm_rate, 0.0)
    biases_out = adam_step(bias_params, bias_moment, bias_square, bias_total, BIAS_RATE, 0.0)
    return (block_out, grad_tokens, *tables_next, *norms_out, *biases_out)


def solution(mesh):
    flat = P("dp", None)
    pieces = P("mp", "dp", None, None)
    bias = P("mp", None)
    return jax.shard_map(
        body,
        mesh=mesh,
        in_specs=(flat, flat, flat, P(), pieces, pieces, pieces, P(), P(), P(), bias, bias, bias),
        out_specs=(flat, flat, pieces, pieces, pieces, P(), P(), P(), bias, bias, bias),
        check_vma=False,
    )
```

```python
import functools

import jax
import jax.numpy as jnp
import numpy as np
from jax import lax
from jax.experimental import pallas as pl
from jax.experimental.pallas import tpu as pltpu
from jax.sharding import PartitionSpec as P

HEADS = 20
HEAD_DIM = 32
HALF = HEAD_DIM // 2
FF = 2560
LONGEST = 1024
STEP = 10

EPS_NORM = 1e-05
BETA_ONE = 0.5
BETA_TWO = 0.5
ADAM_EPS = 1e-08
DECAY_RATE = 0.01
NEG_FILL = -1e30
NORM_RATES = (0.5, 0.1, 0.5, 0.1, 0.1, 0.1)
BIAS_RATE = 0.1
SCALE = HEAD_DIM**-0.5
SCALE_LOG2 = SCALE * 1.4426950408889634
SAFE_EXP = 100.0

BF = jnp.bfloat16
F32 = jnp.float32
I32 = jnp.int32
TILE = 256
LANES = 128
VMEM_LIMIT = 16 << 20
SHRINK = 0.1


def params(*kinds):
    return pltpu.CompilerParams(dimension_semantics=kinds or None, vmem_limit_bytes=VMEM_LIMIT)


def cost(flops, moved):
    return pl.CostEstimate(flops=int(flops / SHRINK), bytes_accessed=int(moved / SHRINK), transcendentals=0)


def dot_nn(a, b):
    return lax.dot_general(a, b, (((1,), (0,)), ((), ())), preferred_element_type=F32)


def dot_nt(a, b):
    return lax.dot_general(a, b, (((1,), (1,)), ((), ())), preferred_element_type=F32)


def dot_tn(a, b):
    return lax.dot_general(a, b, (((0,), (0,)), ((), ())), preferred_element_type=F32)


def split_two(v):
    hi = v.astype(BF).astype(F32)
    return hi, v - hi


def split_three(v):
    hi = v.astype(BF).astype(F32)
    mid = (v - hi).astype(BF).astype(F32)
    return hi, mid, v - hi - mid


def normalized(v):
    centred = v - jnp.mean(v, axis=-1, keepdims=True)
    inv = lax.rsqrt(jnp.mean(centred * centred, axis=-1, keepdims=True) + EPS_NORM)
    return centred * inv, inv


SMEM = pl.BlockSpec(memory_space=pltpu.SMEM)


def whole(shape):
    return pl.BlockSpec(shape, lambda *_: (0,) * len(shape))


ANYWHERE = pl.BlockSpec(memory_space=pl.ANY)


def rows(width, begin=0):
    return pl.BlockSpec((TILE, width), lambda t: (begin + t, 0))


def cols(height, begin=0):
    return pl.BlockSpec((height, TILE), lambda t: (0, begin + t))


def both(height, begin=0):
    return pl.BlockSpec((2, height, TILE), lambda t: (0, 0, begin + t))


def shaped(shape, dtype):
    return jax.ShapeDtypeStruct(shape, dtype)


def call(kernel, args, in_specs, out_specs, out_shape, name, deps=(), scratch=(), **more):
    count = len(args)

    def wrapped(*refs):
        kernel(*refs[:count], *refs[count + len(deps) :])

    return pl.pallas_call(
        wrapped,
        in_specs=list(in_specs) + [ANYWHERE] * len(deps),
        out_specs=out_specs,
        out_shape=out_shape,
        scratch_shapes=list(scratch),
        compiler_params=params(*(("arbitrary",) if "grid" in more else ())),
        name=name,
        **more,
    )(*args, *deps)


def qkv_kernel(x_ref, norm_ref, wm_ref, wo_ref, bm_ref, bo_ref, cos_ref, sin_ref, m_ref, o_ref, a_ref):
    n1, _ = normalized(x_ref[...].astype(F32))
    a1 = (n1 * norm_ref[0:1] + norm_ref[1:2]).astype(BF)
    a_ref[...] = a1
    mine = dot_nt(wm_ref[...], a1) + bm_ref[...]
    other = dot_nt(wo_ref[...], a1) + bo_ref[...]
    width = m_ref.shape[1]
    cos, sin = cos_ref[...], sin_ref[...]
    for which in range(2):
        for at in range(0, width, HALF):
            here = which * width + at
            p, r = mine[here : here + HALF], other[here : here + HALF]
            m_ref[which, at : at + HALF, :] = (p * cos - r * sin).astype(BF)
            o_ref[which, at : at + HALF, :] = (r * cos + p * sin).astype(BF)
    m_ref[2] = mine[2 * width :].astype(BF)
    o_ref[2] = other[2 * width :].astype(BF)


def qkv_call(x, norms, w_mine, w_other, b_mine, b_other, cos, sin, deps=()):
    tok, width = x.shape
    out = w_mine.shape[0]
    third = pl.BlockSpec((3, out // 3, TILE), lambda t: (0, 0, t))
    return call(
        qkv_kernel,
        (x, norms, w_mine, w_other, b_mine, b_other, cos, sin),
        [
            rows(width), whole(norms.shape), whole(w_mine.shape), whole(w_mine.shape),
            whole(b_mine.shape), whole(b_mine.shape), cols(HALF), cols(HALF),
        ],
        [third, third, rows(width)],
        [shaped((3, out // 3, tok), BF)] * 2 + [shaped((tok, width), BF)],
        "ln_qkv",
        deps,
        grid=(tok // TILE,),
        cost_estimate=cost(4 * tok * width * out, 8e6),
    )


def mlp_kernel(
    groups, chained, x_ref, gy_ref, *refs,
):
    ctx_refs, refs = refs[: 2 * groups], refs[2 * groups :]
    w_mine, w_other, wx_mine, wx_other, bup_ref, norm_ref = refs[:6]
    refs = refs[6 + chained :]
    x1_ref, a2_ref, act_ref, gpre_ref, ffn_ref, gh_ref, gbup_ref, out_w, up_w, down_w = refs

    @pl.when(pl.program_id(0) == 0)
    def _():
        quarter, half = wx_mine.shape[0], up_w.shape[0] // 2
        for at, ref in enumerate((w_mine, w_other, wx_mine, wx_other)):
            out_w[at * quarter : (at + 1) * quarter, :] = ref[:quarter, :]
        for at, ref in enumerate((w_mine, w_other)):
            up_w[at * half : (at + 1) * half, :] = ref[quarter : quarter + half, :]
            down_w[at * half : (at + 1) * half, :] = ref[quarter + half :, :]

    gy = gy_ref[...]
    own, far = ctx_refs[:groups], ctx_refs[groups:]
    ctx = jnp.concatenate([ref[j] for some in (own, far) for j in range(2) for ref in some], axis=0)
    x1 = x_ref[...].astype(F32) + dot_tn(ctx, out_w[...]) + norm_ref[4:5]
    x1_ref[...] = x1
    n2, _ = normalized(x1)
    a2 = (n2 * norm_ref[2:3] + norm_ref[3:4]).astype(BF)
    a2_ref[...] = a2
    pre = dot_nt(a2, up_w[...]) + bup_ref[...]
    cdf = 0.5 * (1.0 + lax.erf(pre * 0.7071067811865476))
    act = (pre * cdf).astype(BF)
    act_ref[...] = act
    slope = cdf + pre * (jnp.exp(-0.5 * pre * pre) * 0.3989422804014327)
    gpre = (slope * dot_nt(gy, down_w[...])).astype(BF)
    gpre_ref[...] = gpre
    ffn_ref[...] = dot_nn(act, down_w[...]).astype(BF)
    gh_ref[...] = dot_nn(gpre, up_w[...]).astype(BF)
    part = jnp.sum(gpre.astype(F32), axis=0, keepdims=True)

    @pl.when(pl.program_id(0) == 0)
    def _():
        gbup_ref[...] = part

    @pl.when(pl.program_id(0) > 0)
    def _():
        gbup_ref[...] += part


def mlp_call(span, x, gy, ctx, w_mine, w_other, wx, b_up, norms, before=(), deps=()):
    tok, width = x.shape
    hidden = b_up.shape[1]
    quarter = wx[0].shape[0]
    begin, count = span[0], span[1] - span[0]
    args = (x, gy, *ctx, w_mine, w_other, *wx, b_up, norms, *before)
    return call(
        functools.partial(mlp_kernel, len(ctx) // 2, len(before)),
        args,
        [rows(width, begin)] * 2
        + [both(part.shape[1], begin) for part in ctx]
        + [whole(w_mine.shape)] * 2
        + [whole((quarter, width))] * 2
        + [whole(b_up.shape), whole(norms.shape)]
        + [ANYWHERE] * len(before),
        [
            rows(width, begin), rows(width, begin), rows(hidden, begin), rows(hidden, begin),
            rows(width, begin), rows(width), whole((1, hidden)),
        ],
        [
            shaped((tok, width), F32), shaped((tok, width), BF), shaped((tok, hidden), BF),
            shaped((tok, hidden), BF), shaped((tok, width), BF), shaped((count * TILE, width), BF),
            shaped((1, hidden), F32),
        ],
        "mlp",
        deps,
        scratch=[
            pltpu.VMEM((4 * quarter, width), BF), pltpu.VMEM((hidden, width), BF),
            pltpu.VMEM((hidden, width), BF),
        ],
        grid=(count,),
        cost_estimate=cost(2 * count * TILE * width * (hidden * 4 + 4 * quarter) * 1.6, 2e7),
        input_output_aliases={len(args) - len(before) + j: j for j in range(len(before))},
    )


def mlp_grads_kernel(act_ref, gpre_ref, a2_ref, gy_ref, mine_ref, other_ref, down_sum, up_sum):
    step = pl.program_id(0)
    down = dot_tn(act_ref[...], gy_ref[...])
    up = dot_tn(gpre_ref[...], a2_ref[...])

    @pl.when(step == 0)
    def _():
        down_sum[...] = down
        up_sum[...] = up

    @pl.when(step > 0)
    def _():
        down_sum[...] += down
        up_sum[...] += up

    @pl.when(step == pl.num_programs(0) - 1)
    def _():
        half = down_sum.shape[0] // 2
        for which, out_ref in enumerate((mine_ref, other_ref)):
            here = pl.ds(which * half, half)
            out_ref[:half, :] = up_sum[here, :].astype(BF)
            out_ref[half:, :] = down_sum[here, :].astype(BF)


def mlp_grads_call(act, gpre, a2, gy, deps=()):
    tok, hidden = act.shape
    width = a2.shape[1]
    return call(
        mlp_grads_kernel,
        (act, gpre, a2, gy),
        [rows(hidden), rows(hidden), rows(width), rows(width)],
        [whole((hidden, width))] * 2,
        [shaped((hidden, width), BF)] * 2,
        "mlp_grads",
        deps,
        scratch=[pltpu.VMEM((hidden, width), F32)] * 2,
        grid=(tok // TILE,),
        cost_estimate=cost(4 * tok * width * hidden * 1.3, 1.4e7),
    )


def mid_kernel(
    groups, chained, handed, x1_ref, gy_ref, gh_a, gh_b, *refs,
):
    ctx_refs, refs = refs[:groups], refs[groups:]
    wm_ref, wo_ref, norm_ref = refs[:3]
    refs = refs[3 + chained + handed :]
    gx_ref, g_out, gout_ref, sum_ref = refs[:4]
    cm, co = (jnp.concatenate([ref[j] for ref in ctx_refs], axis=0) for j in range(2))
    step = pl.program_id(0)
    gy = gy_ref[...].astype(F32)
    gh = gh_a[...].astype(F32) + gh_b[...].astype(F32)
    n2, inv = normalized(x1_ref[...])
    e = gh * norm_ref[2:3]
    gx = gy + inv * (
        e - jnp.mean(e, axis=-1, keepdims=True) - n2 * jnp.mean(e * n2, axis=-1, keepdims=True)
    )
    gx_ref[...] = gx
    gm = gx.astype(BF)
    g_out[0] = dot_nt(wm_ref[...], gm).astype(BF)
    g_out[1] = dot_nt(wo_ref[...], gm).astype(BF)

    @pl.when(step == 0)
    def _():
        gout_ref[...] = jnp.zeros_like(gout_ref)
        sum_ref[...] = jnp.zeros_like(sum_ref)

    gout_ref[0] += dot_nn(cm, gm)
    gout_ref[1] += dot_nn(co, gm)
    for at, value in enumerate((gh * n2, gh, gx, gy)):
        sum_ref[at : at + 1, :] += jnp.sum(value, axis=0, keepdims=True)


def mid_call(span, x1, gy, gh, gh_other, ctx, w_m, w_o, norms, before=(), hand=(), deps=()):
    tok, width = x1.shape
    head = sum(part.shape[1] for part in ctx)
    begin, count = span[0], span[1] - span[0]
    args = (x1, gy, gh, gh_other, *ctx, w_m, w_o, norms, *before, *hand)
    fixed = len(args) - len(before) - len(hand)
    aliases = {fixed + j: j for j in range(len(before))}
    aliases.update({fixed + len(before) + j: 4 + j for j in range(len(hand))})
    return call(
        functools.partial(mid_kernel, len(ctx), len(before), len(hand)),
        args,
        [rows(width, begin)] * 2
        + [rows(width)] * 2
        + [both(part.shape[1], begin) for part in ctx]
        + [whole((head, width))] * 2
        + [whole(norms.shape)]
        + [ANYWHERE] * (len(before) + len(hand)),
        [rows(width, begin), both(head), whole((2, head, width)), whole((8, width))]
        + [ANYWHERE] * len(hand),
        [
            shaped((tok, width), F32), shaped((2, head, count * TILE), BF),
            shaped((2, head, width), F32), shaped((8, width), F32),
        ]
        + [shaped(part.shape, part.dtype) for part in hand],
        "mid_back",
        deps,
        grid=(count,),
        cost_estimate=cost(8 * count * TILE * width * head * 2, 1e7),
        input_output_aliases=aliases,
    )


def split_small(value):
    hi = value.astype(BF)
    lo = (value - hi.astype(F32)).astype(BF)
    return hi, lo, hi.astype(F32) + lo.astype(F32)


def in_grads_kernel(groups, gouts, *refs):
    g_refs, refs = refs[:groups], refs[groups:]
    out_refs, mid_refs, up_refs, refs = (
        refs[:gouts], refs[gouts : 2 * gouts], refs[2 * gouts : 3 * gouts], refs[3 * gouts :]
    )
    core_ref, a1_ref, x_ref, wm_ref, wo_ref, mine_ref, other_ref, gh_ref, sum_ref = refs[:9]
    m_sum, o_sum, gbm_ref, gbo_ref = refs[9:]
    step = pl.program_id(0)
    count = wm_ref.shape[0]
    a1 = a1_ref[...]
    gm, go = (
        jnp.concatenate([ref[half, j] for j in range(3) for ref in g_refs], axis=0)
        for half in range(2)
    )

    @pl.when(step == 0)
    def _():
        m_sum[...] = jnp.zeros_like(m_sum)
        o_sum[...] = jnp.zeros_like(o_sum)
        gbm_ref[...] = jnp.zeros_like(gbm_ref)
        gbo_ref[...] = jnp.zeros_like(gbo_ref)
        sum_ref[...] = jnp.zeros_like(sum_ref)

    m_sum[...] += dot_nn(gm, a1)
    o_sum[...] += dot_nn(go, a1)
    gbm_ref[...] += jnp.sum(gm.astype(F32), axis=1, keepdims=True)
    gbo_ref[...] += jnp.sum(go.astype(F32), axis=1, keepdims=True)
    gh = dot_tn(gm, wm_ref[...]) + dot_tn(go, wo_ref[...])
    gh_ref[...] = gh.astype(BF)
    n1, _ = normalized(x_ref[...].astype(F32))
    sum_ref[0:1, :] += jnp.sum(gh * n1, axis=0, keepdims=True)
    sum_ref[1:2, :] += jnp.sum(gh, axis=0, keepdims=True)

    @pl.when(step == pl.num_programs(0) - 1)
    def _():
        width = gh.shape[1]
        up = sum((ref[...] for ref in up_refs[1:]), up_refs[0][...])
        pairs = (
            [jnp.transpose(jnp.broadcast_to(ref[...], (count, LANES)))[0:1] for ref in (gbm_ref, gbo_ref)],
            [up[:, :width], up[:, width:]],
        )
        sum_ref[2:6, :] = sum((ref[0:4, :] for ref in mid_refs[1:]), mid_refs[0][0:4, :])
        for at, (first, second) in zip((6, 8), pairs):
            swapped = core_ref[0] == 1
            sum_ref[at : at + 1, : first.shape[1]] = jnp.where(swapped, second, first)
            sum_ref[at + 1 : at + 2, : first.shape[1]] = jnp.where(swapped, first, second)
        hi, lo, kept = split_small(sum_ref[...])
        sum_ref[...] = kept
        more = count + out_refs[0].shape[1]
        for ref, total, half in ((mine_ref, m_sum, 0), (other_ref, o_sum, 1)):
            ref[:count, :] = total[...].astype(BF)
            ref[count:more, :] = sum((out[half] for out in out_refs[1:]), out_refs[0][half]).astype(BF)
        other_ref[more : more + 16, :] = hi
        other_ref[more + 16 :, :] = lo


def in_grads_call(grads, core, a1, x, w_m, w_o, gouts, mid_sums, gb_ups, deps=()):
    tok, width = a1.shape
    count, more = w_m.shape[0], gouts[0].shape[1]
    parts = [
        pl.BlockSpec(part.shape[:3] + (TILE,), lambda t: (0, 0, 0, t)) for part in grads
    ]
    return call(
        functools.partial(in_grads_kernel, len(grads), len(gouts)),
        (*grads, *gouts, *mid_sums, *gb_ups, core[None], a1, x, w_m, w_o),
        parts
        + [whole(part.shape) for part in (*gouts, *mid_sums, *gb_ups)]
        + [SMEM, rows(width), rows(width)]
        + [whole((count, width))] * 2,
        [whole((count + more, width)), whole((count + more + 32, width)), rows(width), whole((16, width))],
        [
            shaped((count + more, width), BF), shaped((count + more + 32, width), BF),
            shaped((tok, width), BF), shaped((16, width), F32),
        ],
        "in_grads",
        deps,
        scratch=[pltpu.VMEM((count, width), F32)] * 2 + [pltpu.VMEM((count, 1), F32)] * 2,
        grid=(tok // TILE,),
        cost_estimate=cost(8 * tok * width * count * 1.3, 1e7),
    )


def out_kernel(x1_ref, a_ref, b_ref, norm_ref, out_ref):
    out_ref[...] = x1_ref[...] + (a_ref[...].astype(F32) + b_ref[...].astype(F32)) + norm_ref[5:6]


def out_call(x1, ffn_a, ffn_b, norms):
    tok, width = x1.shape
    return call(
        out_kernel,
        (x1, ffn_a, ffn_b, norms),
        [rows(width)] * 3 + [whole(norms.shape)],
        rows(width),
        shaped((tok, width), F32),
        "layer_out",
        grid=(tok // TILE,),
        cost_estimate=cost(4e9, 1e7),
    )


def keep_kernel(*refs):
    half = len(refs) // 2
    for source, target in zip(refs[:half], refs[half:]):
        target[...] = source[...]


def keep_call(arrays, deps=()):
    specs = [whole(array.shape) for array in arrays]
    return call(
        keep_kernel, arrays, specs, specs, [shaped(a.shape, a.dtype) for a in arrays], "keep", deps,
        cost_estimate=cost(4e9, 1e7),
    )


def last_kernel(x_ref, gx_ref, gh_a, gh_b, norm_ref, out_ref):
    n1, inv = normalized(x_ref[...].astype(F32))
    e = (gh_a[...].astype(F32) + gh_b[...].astype(F32)) * norm_ref[0:1]
    out_ref[...] = gx_ref[...] + inv * (
        e - jnp.mean(e, axis=-1, keepdims=True) - n1 * jnp.mean(e * n1, axis=-1, keepdims=True)
    )


def last_call(x, gx, gh_a, gh_b, norms):
    tok, width = x.shape
    return call(
        last_kernel,
        (x, gx, gh_a, gh_b, norms),
        [rows(width)] * 4 + [whole(norms.shape)],
        rows(width),
        shaped((tok, width), F32),
        "last_back",
        grid=(tok // TILE,),
        cost_estimate=cost(1e6, 1.2e7),
    )


def layout_kernel(core_ref, len_ref, freq_ref, cos_ref, sin_ref, row_ref, col_ref, start_ref):
    tok = cos_ref.shape[1]
    docs = len_ref.shape[1]
    begin, best, start = 0, len_ref[0, 0], 0
    begins, ends = [], []
    for doc in range(docs):
        size = len_ref[0, doc]
        if doc:
            start = jnp.where(size > best, begin, start)
            best = jnp.maximum(size, best)
        begins.append(begin)
        begin = begin + size
        ends.append(begin)
    start_ref[0] = start + jnp.zeros((), I32)

    def origin(places):
        at = places + start
        return jnp.where(at >= tok, at - tok, at)

    def document(at):
        return sum(((at >= end).astype(I32) for end in ends), jnp.zeros(at.shape, I32))

    row = origin(lax.broadcasted_iota(I32, (1, tok), 1))
    first = jnp.zeros((1, tok), I32)
    for begin in begins[1:]:
        first = jnp.where(row >= begin, begin, first)
    angles = freq_ref[...] * (row - first).astype(F32)
    cos_ref[...] = jnp.cos(angles)
    sine = jnp.sin(angles)
    sin_ref[...] = jnp.where(core_ref[0] == 0, sine, -sine)
    rest = row_ref.shape[1]
    row_ref[...] = document(row[:, tok - rest :])
    col_ref[...] = document(origin(lax.broadcasted_iota(I32, (rest, 1), 0) + (tok - rest)))


def layout_call(core, lengths, tok, deps=()):
    rest = tok - LONGEST
    freq = np.float32(10000.0) ** -(np.arange(0, HEAD_DIM, 2).astype(np.float32) / HEAD_DIM)
    return call(
        layout_kernel,
        (core[None], lengths, jnp.asarray(freq[:, None], F32)),
        [SMEM, SMEM, whole((HALF, 1))],
        [whole((HALF, tok))] * 2 + [whole((1, rest)), whole((rest, 1)), SMEM],
        [shaped((HALF, tok), F32)] * 2
        + [shaped((1, rest), I32), shaped((rest, 1), I32), shaped((1,), I32)],
        "layout",
        deps,
    )


def halves_kernel(core_ref, table_ref, mine_ref, other_ref):
    first = core_ref[0] == 0
    count = mine_ref.shape[1]
    upper, lower = table_ref[:, :count, :], table_ref[:, count:, :]
    mine_ref[...] = jnp.where(first, upper, lower).astype(BF)
    other_ref[...] = jnp.where(first, lower, upper).astype(BF)


def halves_call(core, table):
    cap, count, width = table.shape
    half = (cap, count // 2, width)
    return call(
        halves_kernel,
        (core[None], table),
        [SMEM, whole(table.shape)],
        [whole(half)] * 2,
        [shaped(half, BF)] * 2,
        "halves",
    )


def attend_kernel(seg_row, seg_col, m_ref, o_ref, ctx_ref, log_ref):
    tok = m_ref.shape[2]
    rest = tok - LONGEST
    q_t, k_t, v_t = (jnp.concatenate([m_ref[j], o_ref[j]], axis=0) for j in range(3))
    qs = q_t.astype(F32) * SCALE_LOG2
    hi, lo = split_two(qs)
    qx = jnp.transpose(jnp.concatenate([hi, lo], axis=0)).astype(BF)
    kx = jnp.concatenate([k_t, k_t], axis=0)
    v_f = v_t.astype(F32)
    vx = jnp.transpose(jnp.concatenate([v_f, jnp.ones((8, tok), F32)], axis=0)).astype(BF)
    k_f = k_t.astype(F32)
    q_top = jnp.max(jnp.sum(qs * qs, axis=0, keepdims=True))
    k_top = jnp.max(jnp.sum(k_f * k_f, axis=0, keepdims=True))
    safe = q_top * k_top < SAFE_EXP * SAFE_EXP
    same = seg_col[...] == seg_row[...]

    def finish(sums, shift, at, count):
        turned = jnp.transpose(sums)
        total = turned[HEAD_DIM : HEAD_DIM + 1]
        ctx = (turned[0:HEAD_DIM] / total).astype(BF)
        ctx_ref[0, :, at : at + count] = ctx[:HALF]
        ctx_ref[1, :, at : at + count] = ctx[HALF:]
        log_total = jnp.log2(total)
        if shift is not None:
            log_total = log_total + jnp.transpose(jnp.broadcast_to(shift, (count, LANES)))[0:1]
        log_ref[0, :, at : at + count] = log_total

    def run(exact):
        for at in range(0, LONGEST, TILE):
            scores = dot_nn(qx[at : at + TILE], kx[:, :LONGEST])
            shift = None
            if exact:
                shift = jnp.max(scores, axis=1, keepdims=True)
                scores = scores - shift
            finish(dot_nn(jnp.exp2(scores).astype(BF), vx[:LONGEST]), shift, at, TILE)
        if rest:
            scores = jnp.where(same, dot_nn(qx[LONGEST:], kx[:, LONGEST:]), NEG_FILL)
            shift = None
            if exact:
                shift = jnp.max(scores, axis=1, keepdims=True)
                scores = scores - shift
            finish(dot_nn(jnp.exp2(scores).astype(BF), vx[LONGEST:]), shift, LONGEST, rest)

    @pl.when(safe)
    def _():
        run(False)

    @pl.when(jnp.logical_not(safe))
    def _():
        run(True)


def attend_call(segs, qkv_m, qkv_o, first, count, deps=()):
    tok = qkv_m.shape[2]
    rest = segs[0].shape[1]
    part = pl.BlockSpec((3, HALF, tok), lambda h: (0, first + h, 0))
    out = pl.BlockSpec((2, HALF, tok), lambda h: (0, h, 0))
    return call(
        attend_kernel,
        (*segs, qkv_m, qkv_o),
        [whole((1, rest)), whole((rest, 1)), part, part],
        [out, pl.BlockSpec((1, 1, tok), lambda h: (h, 0, 0))],
        [shaped((2, count * HALF, tok), BF), shaped((count, 1, tok), F32)],
        "attend",
        deps,
        grid=(count,),
        cost_estimate=cost(count * 2.5e9, 3e6),
    )


def attend_back_kernel(
    q_begin, q_end, last, seg_row, seg_col, cos_ref, sin_ref, m_ref, o_ref, g_ref, ctx_ref, log_ref,
    *refs,
):
    tok = m_ref.shape[2]
    rest = tok - LONGEST
    end = tok if last else q_end
    span = slice(q_begin, end)
    q_t, k_t, v_t = (jnp.concatenate([m_ref[j], o_ref[j]], axis=0) for j in range(3))
    q_f = q_t[:, span].astype(F32)
    ctx = jnp.concatenate([ctx_ref[0, :, span], ctx_ref[1, :, span]], axis=0).astype(F32)
    g_f = jnp.concatenate([g_ref[0], g_ref[1]], axis=0).astype(F32)
    hi, lo = split_two(q_f * SCALE_LOG2)
    weighted = jnp.sum(g_f * ctx, axis=0, keepdims=True)
    pad = jnp.zeros((13, end - q_begin), F32)
    qx = jnp.concatenate([hi, lo, *split_three(log_ref[0, :, span]), pad], axis=0).astype(BF)
    keys = tok if last else LONGEST
    k_f, v_f = k_t[:, :keys].astype(F32), v_t[:, :keys].astype(F32)
    minus = jnp.concatenate([jnp.full((3, keys), -1.0, F32), jnp.zeros((13, keys), F32)], axis=0)
    kx = jnp.transpose(jnp.concatenate([k_f, k_f, minus], axis=0)).astype(BF)
    gx = jnp.concatenate([g_f, *split_three(weighted), pad], axis=0).astype(BF)
    vx = jnp.transpose(jnp.concatenate([v_f, minus], axis=0)).astype(BF)
    qn = jnp.transpose(q_f).astype(BF)
    gn = jnp.transpose(g_f).astype(BF)

    if last:
        early_q, early_kv, out_ref = refs
    else:
        out_q, out_kv = refs

    def turned_back(grad, at, count):
        cos, sin = cos_ref[:, at : at + count], sin_ref[:, at : at + count]
        mine, other = grad[0:HALF] * SCALE, grad[HALF:] * SCALE
        return (mine * cos + other * sin).astype(BF), (other * cos - mine * sin).astype(BF)

    def block(k_at, k_count, q_at, q_count, mask, early):
        scores = dot_nn(kx[k_at : k_at + k_count], qx[:, q_at : q_at + q_count])
        if mask is not None:
            scores = jnp.where(mask, scores, NEG_FILL)
        prob = jnp.exp2(scores)
        grad_prob = dot_nn(vx[k_at : k_at + k_count], gx[:, q_at : q_at + q_count])
        grad_score = (prob * grad_prob).astype(BF)
        grad_v = jnp.transpose(dot_nn(prob.astype(BF), gn[q_at : q_at + q_count]))
        grad_k = jnp.transpose(dot_nn(grad_score, qn[q_at : q_at + q_count]))
        here = slice(k_at, k_at + k_count)
        if not last:
            out_kv[0, 0, :, here] = grad_k
            out_kv[1, 0, :, here] = grad_v
        else:
            if early:
                grad_k = grad_k + early_kv[0, 0, :, here]
                grad_v = grad_v + early_kv[1, 0, :, here]
            out_ref[0, 1, :, here], out_ref[1, 1, :, here] = turned_back(grad_k, k_at, k_count)
            out_ref[0, 2, :, here] = grad_v[:HALF].astype(BF)
            out_ref[1, 2, :, here] = grad_v[HALF:].astype(BF)
        return dot_nn(k_t[:, k_at : k_at + k_count], grad_score)

    grad_q = None
    for at in range(0, LONGEST, TILE):
        piece = block(at, TILE, 0, q_end - q_begin, None, True)
        grad_q = piece if grad_q is None else grad_q + piece
    mine, other = turned_back(grad_q, q_begin, q_end - q_begin)
    if not last:
        out_q[0], out_q[1] = mine, other
        return
    out_ref[0, 0, :, :q_begin] = early_q[0]
    out_ref[1, 0, :, :q_begin] = early_q[1]
    out_ref[0, 0, :, q_begin:q_end] = mine
    out_ref[1, 0, :, q_begin:q_end] = other
    if rest:
        same = seg_col[...] == seg_row[...]
        piece = block(LONGEST, rest, LONGEST - q_begin, rest, same, False)
        out_ref[0, 0, :, LONGEST:], out_ref[1, 0, :, LONGEST:] = turned_back(piece, LONGEST, rest)


def attend_back_call(
    q_begin, q_end, segs, cos, sin, qkv_m, qkv_o, g_ctx, ctx, logs, first, count, early=(), deps=()
):
    tok = qkv_m.shape[2]
    last = len(early) > 0
    rest = segs[0].shape[1]
    part = pl.BlockSpec((3, HALF, tok), lambda h: (0, first + h, 0))
    table = whole((HALF, tok))

    def by_head(length, offset=0):
        return pl.BlockSpec((2, HALF, length), lambda h: (0, offset + h, 0))

    pair = pl.BlockSpec((2, 1, HEAD_DIM, LONGEST), lambda h: (0, h, 0, 0))
    if last:
        out_specs = [pl.BlockSpec((2, 3, HALF, tok), lambda h: (0, 0, h, 0))]
        out_shape = [shaped((2, 3, count * HALF, tok), BF)]
    else:
        out_specs = [by_head(q_end), pair]
        out_shape = [
            shaped((2, count * HALF, q_end), BF), shaped((2, count, HEAD_DIM, LONGEST), F32)
        ]
    return call(
        functools.partial(attend_back_kernel, q_begin, q_end, last),
        (*segs, cos, sin, qkv_m, qkv_o, g_ctx, ctx, logs, *early),
        [
            whole((1, rest)), whole((rest, 1)), table, table, part, part,
            by_head(g_ctx.shape[2], first), by_head(tok), pl.BlockSpec((1, 1, tok), lambda h: (h, 0, 0)),
        ]
        + ([by_head(q_begin), pair] if last else []),
        out_specs,
        out_shape,
        "attend_back",
        deps,
        grid=(count,),
        cost_estimate=cost(count * 2.1e9, 6e6),
    )


class Routes:
    def __init__(self, dp_size, slot_cap, pieces, ready, spans):
        self.dp = dp_size
        self.cap = slot_cap
        self.chips = dp_size // 2
        self.pieces = pieces
        self.ready = ready
        self.spans = spans
        if self.chips == 8:
            self.stages = ((2, 4), (1, 2))
        elif self.chips == 64:
            self.stages = ((1, 8), (8, 2), (16, 4))
        else:
            self.stages = ((1, self.chips),)
        self.depth = len(self.stages)
        straight = self.stages[::-1]
        paired = ((1, 2), (4, 2), (2, 2)) if self.chips == 8 else straight
        self.back = (straight, paired)
        self.out = (self.stages, ((4, 2), (2, 2), (1, 2)) if self.chips == 8 else self.stages)
        self.fill = [self.limit(last, self.chips) for last in ready]
        self.begins = [0] + self.fill[:-1]

    def limit(self, count, groups):
        worst = min(count, self.dp // groups * self.cap)
        if self.chips != 8:
            return worst
        typical = {
            2: count * 11 // 20 + 8, 4: count * 3 // 10 + 10, 8: (count * 9 + 25) // 50 + 6
        }[groups]
        return worst if count == self.pieces else min(worst, typical)

    def span_limit(self, number, level):
        groups = 1
        for _, size in self.back[number][:level]:
            groups *= size
        return self.limit(self.spans[number][1] - self.spans[number][0], groups)

    def move(self, array, stage, shift):
        stride, size = stage
        pairs = []
        for device in range(self.dp):
            chip, core = device // 2, device % 2
            at = (chip // stride) % size
            pairs.append((device, 2 * (chip + ((at + shift) % size - at) * stride) + core))
        return lax.ppermute(array, "dp", pairs)

    def swap_cores(self, array):
        return lax.ppermute(array, "dp", [(d, d ^ 1) for d in range(self.dp)])

    def around(self, array, stage):
        return [array] + [self.move(array, stage, shift) for shift in range(1, stage[1])]

    def onward(self, buffers, stage):
        return buffers + [
            self.move(buffer, stage, shift) for shift in range(1, stage[1]) for buffer in buffers
        ]

    def tables(self, owners, me):
        place = {}

        def kernel(me_ref, own_ref, out_ref, row_ref):
            here = me_ref[0]
            my_chip, my_core = here // 2, here % 2
            row_ref[...] = jnp.full((1, LANES), -2, I32)
            row_ref[:, : self.pieces] = own_ref[...]
            row = row_ref[...]
            col = jnp.transpose(jnp.broadcast_to(row, (LANES, LANES)))[:, 0:1]
            id_row = lax.broadcasted_iota(I32, (1, LANES), 1)
            id_col = lax.broadcasted_iota(I32, (LANES, 1), 0)
            lane = lax.broadcasted_iota(I32, (LANES, LANES), 1)
            sub = lax.broadcasted_iota(I32, (LANES, LANES), 0)

            def rank_col(key_row, key_col):
                hit = (key_row == key_col) & (lane < sub)
                return jnp.sum(hit.astype(F32), axis=1, keepdims=True).astype(I32)

            def rank_row(key_row, key_col):
                hit = (key_row == key_col) & (sub < lane)
                return jnp.sum(hit.astype(F32), axis=0, keepdims=True).astype(I32)

            def gather(valid_col, entry_col, value_col):
                hit = valid_col & (entry_col == lane)
                return jnp.sum(
                    jnp.where(hit, value_col.astype(F32), 0.0), axis=0, keepdims=True
                ).astype(I32)

            def put(name, value):
                at = place.setdefault(name, len(place))
                out_ref[at : at + 1, :] = value

            def coord(chip, stage):
                return (chip // stage[0]) % stage[1]

            def group(chip, stages):
                key = 0
                for stage in stages:
                    key = key * stage[1] + coord(chip, stage)
                return key

            def fullest(inside, rank):
                return jnp.max(jnp.where(inside, rank, -1), axis=0, keepdims=True) + 1

            slot_col = rank_col(row, col)
            put("piece", gather(col == here, slot_col, id_col + 1) - 1)
            sibling = my_chip * 2 + 1 - my_core
            put("sibling", gather(col == sibling, slot_col, id_col + 1) - 1)
            over = jnp.zeros((1, 1), I32)
            real = id_col < self.pieces
            chip_col, chip_row = col // 2, row // 2
            rank_c, rank_r = rank_col(chip_row, chip_col), rank_row(chip_row, chip_col)
            from_core = jnp.where(col % 2 == my_core, 0, self.cap)
            put("send", gather(real & (chip_col == my_chip), rank_c, from_core + slot_col))
            for last, fill in zip(self.ready, self.fill):
                over = jnp.maximum(over, fullest(id_col < last, rank_c) - fill)
            put("late", jnp.broadcast_to(over, (1, LANES)))
            over = jnp.zeros((1, 1), I32)
            take = jnp.zeros((1, LANES), I32)
            for begin, end, stages in zip(self.begins, self.fill, self.out):
                spot, scale = rank_r - begin, end - begin
                for stage in stages:
                    away = (coord(my_chip, stage) - coord(chip_row, stage) + stage[1]) % stage[1]
                    spot = spot + away * scale
                    scale = scale * stage[1]
                take = jnp.where(rank_r >= begin, begin * self.chips + spot, take)
            put("take", take)
            for number, span in enumerate(self.spans):
                in_col = (id_col >= span[0]) & (id_col < span[1])
                in_row = (id_row >= span[0]) & (id_row < span[1])
                stages = self.back[number]
                ranks = {}
                for level in range(1, len(stages) + 1):
                    key_col = jnp.where(in_col, group(chip_col, stages[:level]), -1)
                    key_row = jnp.where(in_row, group(chip_row, stages[:level]), -1)
                    ranks[level] = rank_col(key_row, key_col)
                    over = jnp.maximum(
                        over, fullest(in_col, ranks[level]) - self.span_limit(number, level)
                    )
                value = id_col - span[0]
                for level, stage in enumerate(stages, 1):
                    size = stage[1]
                    inside = in_col & (
                        group(chip_col, stages[: level - 1]) == group(my_chip, stages[: level - 1])
                    )
                    for shift in range(size):
                        goal = (coord(my_chip, stage) + shift) % size
                        put(
                            ("back", number, level, shift),
                            gather(inside & (coord(chip_col, stage) == goal), ranks[level], value),
                        )
                    value = ranks[level]
                for which in range(2):
                    goal = my_chip * 2 + (my_core + which) % 2
                    put(
                        ("slot", number, which),
                        gather(in_col & (col == goal), slot_col, ranks[len(stages)]),
                    )
            put("over", jnp.broadcast_to(over, (1, LANES)))

        count = 6 + sum(2 + sum(size for _, size in stages) for stages in self.back)
        height = -(-count // 8) * 8
        table = pl.pallas_call(
            kernel,
            in_specs=[SMEM, whole((1, self.pieces))],
            out_specs=whole((height, LANES)),
            out_shape=shaped((height, LANES), I32),
            scratch_shapes=[pltpu.VMEM((1, LANES), I32)],
            compiler_params=params(),
            name="routes",
        )(me[None], owners[None, :])
        return table, place


def pick_call(table, picks, parts, sizes, name, deps=()):
    rows_each = [part.shape[0] for part in parts]
    shape = parts[0].shape[1:]

    def kernel(table_ref, *refs):
        ins, outs, source = refs[: len(parts)], refs[len(parts) : -1], refs[-1]
        at = 0
        for ref, count in zip(ins, rows_each):
            source[at : at + count] = ref[...]
            at += count
        for (row, start), size, out in zip(picks, sizes, outs):
            for j in range(size):
                out[j] = source[table_ref[row, start + j]]

    return call(
        kernel,
        (table, *parts),
        [SMEM] + [whole(part.shape) for part in parts],
        [whole((size,) + shape) for size in sizes],
        [shaped((size,) + shape, BF) for size in sizes],
        name,
        deps,
        scratch=[pltpu.VMEM((sum(rows_each),) + shape, BF)],
    )


def join_call(parts, deps=()):
    counts = [part.shape[0] for part in parts]
    shape = (sum(counts),) + parts[0].shape[1:]

    def kernel(*refs):
        at = 0
        for ref, count in zip(refs, counts):
            refs[-1][at : at + count] = ref[...]
            at += count

    return call(
        kernel, parts, [whole(part.shape) for part in parts], whole(shape), shaped(shape, BF), "join", deps
    )


def add_pick_call(table, picks, parts, sizes, dtype=BF, name="add_pick", small=None, extra=(), deps=()):
    shape = parts[0].shape[1:]
    lengths = [size + 2 * (j in extra) for j, size in enumerate(sizes)]

    def kernel(table_ref, *refs):
        ins, refs = refs[: len(parts)], refs[len(parts) :]
        if small is not None:
            small_ref, refs = refs[0], refs[1:]
            terms = [small_ref[...]] + [
                ref[ref.shape[0] - 2].astype(F32) + ref[ref.shape[0] - 1].astype(F32) for ref in ins[1:]
            ]
            while len(terms) > 1:
                middle = len(terms) // 2
                terms = [a + b for a, b in zip(terms[:middle], terms[middle:])]
            hi, lo, kept = split_small(terms[0])
            refs[len(sizes)][...] = kept
            for j in extra:
                refs[j][sizes[j]] = hi
                refs[j][sizes[j] + 1] = lo
        for (row, start), size, out in zip(picks, sizes, refs):
            for j in range(size):
                at = table_ref[row, start + j]
                total = ins[0][at].astype(F32)
                for ref in ins[1:]:
                    total = total + ref[at].astype(F32)
                out[j] = total.astype(dtype)

    out_specs = [whole((length,) + shape) for length in lengths]
    out_shape = [shaped((length,) + shape, dtype) for length in lengths]
    if small is not None:
        out_specs, out_shape = out_specs + [whole(shape)], out_shape + [shaped(shape, F32)]
    return call(
        kernel,
        (table, *parts) + (() if small is None else (small,)),
        [SMEM] + [whole(part.shape) for part in parts] + ([] if small is None else [whole(shape)]),
        out_specs,
        out_shape,
        name,
        deps,
    )


def adam_step(weights, first_mom, second_mom, gradient, rate_arr, decay_rate):
    first_new = BETA_ONE * first_mom + (1.0 - BETA_ONE) * gradient
    second_new = BETA_TWO * second_mom + (1.0 - BETA_TWO) * gradient * gradient
    first_fix = first_new / (1.0 - BETA_ONE**STEP)
    second_fix = second_new / (1.0 - BETA_TWO**STEP)
    weights_new = weights * (1.0 - rate_arr * decay_rate) - rate_arr * first_fix / (
        jnp.sqrt(second_fix) + ADAM_EPS
    )
    return (weights_new, first_new, second_new)


def swap_mp(array):
    return lax.ppermute(array, "mp", [(0, 1), (1, 0)])


def swap_both(array):
    dp_size = lax.axis_size("dp")
    pairs = [(2 * d + m, 2 * (d ^ 1) + 1 - m) for d in range(dp_size) for m in range(2)]
    return lax.ppermute(array, ("dp", "mp"), pairs)


def roll_rows(array, start):
    return lax.dynamic_slice_in_dim(
        jnp.concatenate([array, array], axis=0), start, array.shape[0], axis=0
    )


def body(
    tokens, cotangent, lengths, owners, weight_table, moment_table, square_table,
    norm_params, norm_moment, norm_square, bias_params, bias_moment, bias_square,
):
    dp_size = lax.axis_size("dp")
    mp_size = lax.axis_size("mp")
    heads = HEADS // mp_size
    head_width = heads * HEAD_DIM
    hidden = FF // mp_size
    tok, width = tokens.shape
    slot_cap, piece_len = weight_table.shape[1:3]
    half_len = piece_len // 2
    piece_total = owners.shape[0]
    me = lax.axis_index("dp").astype(I32)
    core = me % 2
    first_core = core == 0

    n_qkv, n_out = 3 * head_width // piece_len, head_width // piece_len
    n_up = hidden // piece_len
    ready = (n_qkv, piece_total)
    spans = ((0, n_qkv + n_out), (n_qkv + n_out, piece_total))
    routes = Routes(dp_size, slot_cap, piece_total, ready, spans)
    table, place = routes.tables(owners, me)

    own_half, sibling_half = halves_call(core, weight_table[0])
    chip_slots = [own_half, routes.swap_cores(sibling_half)]

    def half(array, which):
        return lax.dynamic_index_in_dim(array, which, axis=1, keepdims=False)

    def unless(bad, usual, other):
        return lax.while_loop(
            lambda state: state[0] > 0, lambda state: (jnp.zeros((), I32), other()), (bad, usual)
        )[1]

    def own_list(number, deps):
        begin, end = routes.begins[number], routes.fill[number]
        (chunk,) = pick_call(
            table, [(place["send"], begin)], chip_slots, [end - begin], "pick_owned", deps
        )
        return routes.around(chunk, routes.out[number][0])

    def collect(buffers, ranges, deps=()):
        sizes = [high - low for low, high in ranges]
        return pick_call(
            table, [(place["take"], low) for low, _ in ranges], buffers, sizes, "pick_all", deps
        )

    def flat(array):
        return array.reshape(-1, width)

    def slow_first():
        everyone = lax.all_gather(weight_table[0].astype(BF), "dp", axis=0, tiled=True)
        earlier = (owners[None, :] == owners[:, None]) & (
            jnp.arange(piece_total)[None, :] < jnp.arange(piece_total)[:, None]
        )
        at = owners * slot_cap + jnp.sum(earlier.astype(I32), axis=1)
        return half(everyone[at[:n_qkv]].reshape(n_qkv, 2, half_len, width), core)

    list_a = own_list(0, ())
    cos, sin, *segs, start = layout_call(core, lengths, tok, (list_a[0],))
    start = start[0]
    x = roll_rows(tokens, start)
    gy = roll_rows(cotangent, start)
    bias_halves = bias_params[0].reshape(-1, 2, half_len)
    b_mine, b_other = half(bias_halves, core), half(bias_halves, 1 - core)
    b_qkv = [part[:n_qkv].reshape(-1, 1) for part in (b_mine, b_other)]
    b_up = jnp.concatenate([part[n_qkv:].reshape(1, -1) for part in (b_mine, b_other)], axis=1)

    buffers_a = list_a
    for stage in routes.out[0][1:]:
        buffers_a = routes.onward(buffers_a, stage)
    many = routes.fill[1] > routes.fill[0]
    list_b = own_list(1, (*list_a[1:], buffers_a[len(list_a)])) if many else []
    (w_qkv_m,) = collect(buffers_a, ((0, n_qkv),), (x, gy, cos, sin, *b_qkv, b_up, *list_b[:1]))
    b_qkv = keep_call(b_qkv, (w_qkv_m,))
    buffers_b = [join_call(list_b, (w_qkv_m,))] if many else []
    w_qkv_m = unless(table[place["late"], 0], w_qkv_m, slow_first)
    w_qkv_o = routes.swap_cores(w_qkv_m)
    qkv_m, qkv_o, a1 = qkv_call(x, norm_params, flat(w_qkv_m), flat(w_qkv_o), *b_qkv, cos, sin, buffers_b[:1])
    for stage in routes.out[1][1:] if many else ():
        buffers_b = routes.onward(buffers_b, stage)
    cut = heads * 6 // 10
    groups = ((0, cut), (cut, heads - cut))
    ctx_one, logs_one = attend_call(segs, qkv_m, qkv_o, *groups[0])
    ctx_two, logs_two = attend_call(segs, qkv_m, qkv_o, *groups[1], (ctx_one, *buffers_b[1:2]))
    ctx = (ctx_one, ctx_two)
    ctx_x = [swap_mp(part) for part in ctx]
    w_out_m, w_mine = collect(buffers_a + buffers_b, ((n_qkv, n_qkv + n_out), (n_qkv, piece_total)), ctx_x)
    w_other = routes.swap_cores(w_mine)
    w_out_x = [flat(swap_mp(w_out_m)), flat(swap_both(w_out_m))]
    w_mine, w_other = flat(w_mine), flat(w_other)
    tiles = tok // TILE
    spans_tok = ((0, 2), (2, tiles))
    mlp_args = (x, gy, (*ctx, *ctx_x), w_mine, w_other, w_out_x, b_up, norm_params)
    *filled, g_h2_a, gb_up_a = mlp_call(spans_tok[0], *mlp_args)
    *filled, g_h2_b, gb_up_b = mlp_call(spans_tok[1], *mlp_args, filled)
    x1, a2, act, g_pre, ffn = filled
    g_h2_ax, g_h2_bx = swap_mp(g_h2_a), swap_mp(g_h2_b)
    g_mlp = mlp_grads_call(act, g_pre, a2, gy)

    def pieces(array):
        return array.reshape(-1, half_len, width)

    def sort_out(number, level, parts, small=None, deps=()):
        stage = routes.back[number][level - 1]
        size = stage[1]
        lists = add_pick_call(
            table,
            [(place[("back", number, level, shift)], 0) for shift in range(size)],
            parts,
            [routes.span_limit(number, level)] * size,
            small=small,
            extra=() if small is None else range(1, size),
            deps=deps,
        )
        moved = [routes.move(lists[shift], stage, shift) for shift in range(1, size)]
        return [lists[0]] + moved, lists[-1]

    gx1, g_ctx_a, g_out_a, mid_a, g_mlp_m, g_mlp_o = mid_call(
        spans_tok[0], x1, gy, g_h2_a, g_h2_ax, ctx, w_mine, w_other, norm_params, (), g_mlp
    )
    back = (segs, cos, sin, qkv_m, qkv_o)
    half_way = spans_tok[0][1] * TILE
    early_one = attend_back_call(0, half_way, *back, g_ctx_a, ctx_one, logs_one, *groups[0])
    parts_mlp, listed = sort_out(
        1, 1, [pieces(g_mlp_m), routes.swap_cores(pieces(g_mlp_o))], deps=early_one[:1]
    )
    early_two = attend_back_call(
        0, half_way, *back, g_ctx_a, ctx_two, logs_two, *groups[1], deps=(listed,)
    )
    gx1, g_ctx_b, g_out_b, mid_b, ffn = mid_call(
        spans_tok[1], x1, gy, g_h2_b, g_h2_bx, ctx, w_mine, w_other, norm_params, (gx1,), (ffn,),
        early_two[:1],
    )
    ffn_other = swap_mp(ffn)

    (grads_one,) = attend_back_call(
        half_way, LONGEST, *back, g_ctx_b, ctx_one, logs_one, *groups[0], early_one
    )
    parts_mlp, listed = sort_out(1, 2, parts_mlp, deps=(grads_one,))
    (grads_two,) = attend_back_call(
        half_way, LONGEST, *back, g_ctx_b, ctx_two, logs_two, *groups[1], early_two, (listed,)
    )
    g_in_m, g_in_o, g_h1, small = in_grads_call(
        (grads_one, grads_two), core, a1, x, flat(w_qkv_m), flat(w_qkv_o),
        (g_out_a, g_out_b), (mid_a, mid_b), (gb_up_a, gb_up_b), (ffn_other,),
    )
    g_h1_other = swap_mp(g_h1)
    out_roll = out_call(x1, ffn, ffn_other, norm_params)
    parts_in = [pieces(g_in_m), routes.swap_cores(pieces(g_in_o))]
    for level in range(1, len(routes.back[0])):
        parts_in, small = sort_out(0, level, parts_in, small, (out_roll,))
    for level in range(3, len(routes.back[1]) + 1):
        parts_mlp, _ = sort_out(1, level, parts_mlp, deps=(small,))
    parts_in, small = sort_out(0, len(routes.back[0]), parts_in, small)

    block_out = roll_rows(out_roll, tok - start)
    grad_roll = last_call(x, gx1, g_h1, g_h1_other, norm_params)
    grad_tokens = roll_rows(grad_roll, tok - start)

    def owned(number, parts, small=None):
        return add_pick_call(
            table,
            [(place[("slot", number, which)], 0) for which in range(2)],
            parts,
            [slot_cap] * 2,
            dtype=F32,
            name="owned",
            small=small,
        )

    owned_in, owned_mlp = owned(0, parts_in, small), owned(1, parts_mlp)
    small = owned_in[2]
    small_x = swap_mp(small[0:2])
    piece_ids = table[place["piece"], :slot_cap]
    other_ids = table[place["sibling"], :slot_cap]
    kept, sent = (
        jnp.where(ids[:, None, None] >= spans[1][0], owned_mlp[which], owned_in[which])
        for which, ids in enumerate((piece_ids, other_ids))
    )
    arrived = routes.swap_cores(sent)
    ids = piece_ids[:, None, None]

    def slow_grad():
        def stack(in_part, mlp_part):
            return jnp.concatenate([pieces(in_part), pieces(mlp_part)], axis=0).astype(F32)

        mine, other = stack(g_in_m, g_mlp_m), stack(g_in_o[: g_in_m.shape[0]], g_mlp_o)
        both = jnp.where(first_core, jnp.stack([mine, other], 1), jnp.stack([other, mine], 1))
        total = lax.psum(both.reshape(piece_total, piece_len, width), "dp")
        return total[jnp.maximum(piece_ids, 0)]

    owned_grad = jnp.where(
        first_core, jnp.concatenate([kept, arrived], 1), jnp.concatenate([arrived, kept], 1)
    )
    owned_grad = unless(table[place["over"], 0], owned_grad, slow_grad)
    begins = ids * piece_len
    rate = jnp.where(begins < 4 * head_width + hidden, 0.03, 0.015)
    rate = jnp.where(
        begins < 3 * head_width, 0.03, jnp.where(begins < 4 * head_width, 0.2, rate)
    ).astype(F32)
    updated = adam_step(
        weight_table[0], moment_table[0], square_table[0], owned_grad, rate, DECAY_RATE
    )
    tables_next = tuple(jnp.where(ids >= 0, part, 0.0)[None] for part in updated)

    norm_total = jnp.concatenate([small[0:2] + small_x, small[2:6]], axis=0)

    def natural(at, count):
        return jnp.stack([part[:count].reshape(-1, half_len) for part in small[at : at + 2]], 1).reshape(1, -1)

    bias_total = jnp.concatenate([natural(6, 3 * head_width // 2), natural(8, hidden // 2)], axis=1)
    norm_rate = jnp.array(NORM_RATES, F32)[:, None]
    norms_out = adam_step(norm_params, norm_moment, norm_square, norm_total, norm_rate, 0.0)
    biases_out = adam_step(bias_params, bias_moment, bias_square, bias_total, BIAS_RATE, 0.0)
    return (block_out, grad_tokens, *tables_next, *norms_out, *biases_out)


def solution(mesh):
    flat = P("dp", None)
    pieces = P("mp", "dp", None, None)
    bias = P("mp", None)
    return jax.shard_map(
        body,
        mesh=mesh,
        in_specs=(flat, flat, flat, P(), pieces, pieces, pieces, P(), P(), P(), bias, bias, bias),
        out_specs=(flat, flat, pieces, pieces, pieces, P(), P(), P(), bias, bias, bias),
        check_vma=False,
    )
```

```python
import functools

import jax
import jax.numpy as jnp
import numpy as np
from jax import lax
from jax.experimental import pallas as pl
from jax.experimental.pallas import tpu as pltpu
from jax.sharding import PartitionSpec as P

HEADS = 20
HEAD_DIM = 32
HALF = HEAD_DIM // 2
FF = 2560
LONGEST = 1024
STEP = 10

EPS_NORM = 1e-05
BETA_ONE = 0.5
BETA_TWO = 0.5
ADAM_EPS = 1e-08
DECAY_RATE = 0.01
NEG_FILL = -1e30
NORM_RATES = (0.5, 0.1, 0.5, 0.1, 0.1, 0.1)
BIAS_RATE = 0.1
SCALE = HEAD_DIM**-0.5
SCALE_LOG2 = SCALE * 1.4426950408889634
SAFE_EXP = 100.0

BF = jnp.bfloat16
F32 = jnp.float32
I32 = jnp.int32
TILE = 256
LANES = 128
VMEM_LIMIT = 16 << 20
SHRINK = 0.1


def params(*kinds):
    return pltpu.CompilerParams(dimension_semantics=kinds or None, vmem_limit_bytes=VMEM_LIMIT)


def cost(flops, moved):
    return pl.CostEstimate(flops=int(flops / SHRINK), bytes_accessed=int(moved / SHRINK), transcendentals=0)


def dot_nn(a, b):
    return lax.dot_general(a, b, (((1,), (0,)), ((), ())), preferred_element_type=F32)


def dot_nt(a, b):
    return lax.dot_general(a, b, (((1,), (1,)), ((), ())), preferred_element_type=F32)


def dot_tn(a, b):
    return lax.dot_general(a, b, (((0,), (0,)), ((), ())), preferred_element_type=F32)


def split_two(v):
    hi = v.astype(BF).astype(F32)
    return hi, v - hi


def split_three(v):
    hi = v.astype(BF).astype(F32)
    mid = (v - hi).astype(BF).astype(F32)
    return hi, mid, v - hi - mid


def normalized(v):
    centred = v - jnp.mean(v, axis=-1, keepdims=True)
    inv = lax.rsqrt(jnp.mean(centred * centred, axis=-1, keepdims=True) + EPS_NORM)
    return centred * inv, inv


SMEM = pl.BlockSpec(memory_space=pltpu.SMEM)


def whole(shape):
    return pl.BlockSpec(shape, lambda *_: (0,) * len(shape))


ANYWHERE = pl.BlockSpec(memory_space=pl.ANY)


def rows(width, begin=0):
    return pl.BlockSpec((TILE, width), lambda t: (begin + t, 0))


def cols(height, begin=0):
    return pl.BlockSpec((height, TILE), lambda t: (0, begin + t))


def both(height, begin=0):
    return pl.BlockSpec((2, height, TILE), lambda t: (0, 0, begin + t))


def last_rows(array, count):
    return pl.BlockSpec((count, array.shape[1]), lambda *_: (array.shape[0] // count - 1, 0))


def shaped(shape, dtype):
    return jax.ShapeDtypeStruct(shape, dtype)


def call(kernel, args, in_specs, out_specs, out_shape, name, deps=(), scratch=(), **more):
    count = len(args)

    def wrapped(*refs):
        kernel(*refs[:count], *refs[count + len(deps) :])

    return pl.pallas_call(
        wrapped,
        in_specs=list(in_specs) + [ANYWHERE] * len(deps),
        out_specs=out_specs,
        out_shape=out_shape,
        scratch_shapes=list(scratch),
        compiler_params=params(*(("arbitrary",) if "grid" in more else ())),
        name=name,
        **more,
    )(*args, *deps)


def norm_kernel(x_ref, norm_ref, a_ref):
    n1, _ = normalized(x_ref[...].astype(F32))
    a_ref[...] = (n1 * norm_ref[0:1] + norm_ref[1:2]).astype(BF)


def norm_call(x, norms):
    tok, width = x.shape
    return call(
        norm_kernel,
        (x, norms),
        [rows(width), whole(norms.shape)],
        rows(width),
        shaped((tok, width), BF),
        "first_norm",
        grid=(tok // TILE,),
        cost_estimate=cost(1e9, 3e6),
    )


def qkv_kernel(a_ref, wm_ref, wo_ref, bm_ref, bo_ref, cos_ref, sin_ref, m_ref, o_ref):
    a1 = a_ref[...]
    mine = dot_nt(wm_ref[...], a1) + bm_ref[...]
    other = dot_nt(wo_ref[...], a1) + bo_ref[...]
    width = m_ref.shape[1]
    cos, sin = cos_ref[...], sin_ref[...]
    for which in range(2):
        for at in range(0, width, HALF):
            here = which * width + at
            p, r = mine[here : here + HALF], other[here : here + HALF]
            m_ref[which, at : at + HALF, :] = (p * cos - r * sin).astype(BF)
            o_ref[which, at : at + HALF, :] = (r * cos + p * sin).astype(BF)
    m_ref[2] = mine[2 * width :].astype(BF)
    o_ref[2] = other[2 * width :].astype(BF)


def qkv_call(a1, w_mine, w_other, b_mine, b_other, cos, sin, deps=()):
    tok, width = a1.shape
    out = b_mine.shape[0]
    third = pl.BlockSpec((3, out // 3, TILE), lambda t: (0, 0, t))
    return call(
        qkv_kernel,
        (a1, w_mine, w_other, b_mine, b_other, cos, sin),
        [
            rows(width), whole((out, width)), whole((out, width)),
            whole(b_mine.shape), whole(b_mine.shape), cols(HALF), cols(HALF),
        ],
        [third, third],
        [shaped((3, out // 3, tok), BF)] * 2,
        "qkv",
        deps,
        grid=(tok // TILE,),
        cost_estimate=cost(4 * tok * width * out, 8e6),
    )


def mlp_kernel(
    groups, chained, x_ref, gy_ref, *refs,
):
    ctx_refs, refs = refs[: 2 * groups], refs[2 * groups :]
    wp_mine, wp_other, wx_mine, wx_other, w_mine, w_other, bup_ref, norm_ref = refs[:8]
    refs = refs[8 + chained :]
    x1_ref, a2_ref, act_ref, gpre_ref, ffn_ref, gh_ref, gbup_ref, out_w, up_w, down_w = refs

    @pl.when(pl.program_id(0) == 0)
    def _():
        quarter, half = wx_mine.shape[0], up_w.shape[0] // 2
        for at, ref in enumerate((wp_mine, wp_other, wx_mine, wx_other)):
            out_w[at * quarter : (at + 1) * quarter, :] = ref[...]
        for at, ref in enumerate((w_mine, w_other)):
            up_w[at * half : (at + 1) * half, :] = ref[:half, :]
            down_w[at * half : (at + 1) * half, :] = ref[half:, :]

    gy = gy_ref[...]
    own, far = ctx_refs[:groups], ctx_refs[groups:]
    ctx = jnp.concatenate([ref[j] for some in (own, far) for j in range(2) for ref in some], axis=0)
    x1 = x_ref[...].astype(F32) + dot_tn(ctx, out_w[...]) + norm_ref[4:5]
    x1_ref[...] = x1
    n2, _ = normalized(x1)
    a2 = (n2 * norm_ref[2:3] + norm_ref[3:4]).astype(BF)
    a2_ref[...] = a2
    pre = dot_nt(a2, up_w[...]) + bup_ref[...]
    cdf = 0.5 * (1.0 + lax.erf(pre * 0.7071067811865476))
    act = (pre * cdf).astype(BF)
    act_ref[...] = act
    slope = cdf + pre * (jnp.exp(-0.5 * pre * pre) * 0.3989422804014327)
    gpre = (slope * dot_nt(gy, down_w[...])).astype(BF)
    gpre_ref[...] = gpre
    ffn_ref[...] = dot_nn(act, down_w[...]).astype(BF)
    gh_ref[...] = dot_nn(gpre, up_w[...]).astype(BF)
    part = jnp.sum(gpre.astype(F32), axis=0, keepdims=True)

    @pl.when(pl.program_id(0) == 0)
    def _():
        gbup_ref[...] = part

    @pl.when(pl.program_id(0) > 0)
    def _():
        gbup_ref[...] += part


def mlp_call(span, x, gy, ctx, wp, wx, w_mine, w_other, b_up, norms, before=(), deps=()):
    tok, width = x.shape
    hidden = b_up.shape[1]
    quarter = wx[0].shape[0]
    begin, count = span[0], span[1] - span[0]
    args = (x, gy, *ctx, *wp, *wx, w_mine, w_other, b_up, norms, *before)
    return call(
        functools.partial(mlp_kernel, len(ctx) // 2, len(before)),
        args,
        [rows(width, begin)] * 2
        + [both(part.shape[1], begin) for part in ctx]
        + [last_rows(wp[0], quarter)] * 2
        + [whole((quarter, width))] * 2
        + [whole(w_mine.shape)] * 2
        + [whole(b_up.shape), whole(norms.shape)]
        + [ANYWHERE] * len(before),
        [
            rows(width, begin), rows(width, begin), rows(hidden, begin), rows(hidden, begin),
            rows(width, begin), rows(width), whole((1, hidden)),
        ],
        [
            shaped((tok, width), F32), shaped((tok, width), BF), shaped((tok, hidden), BF),
            shaped((tok, hidden), BF), shaped((tok, width), BF), shaped((count * TILE, width), BF),
            shaped((1, hidden), F32),
        ],
        "mlp",
        deps,
        scratch=[
            pltpu.VMEM((4 * quarter, width), BF), pltpu.VMEM((hidden, width), BF),
            pltpu.VMEM((hidden, width), BF),
        ],
        grid=(count,),
        cost_estimate=cost(2 * count * TILE * width * (hidden * 4 + 4 * quarter) * 1.6, 2e7),
        input_output_aliases={len(args) - len(before) + j: j for j in range(len(before))},
    )


def mlp_grads_kernel(act_ref, gpre_ref, a2_ref, gy_ref, mine_ref, other_ref, down_sum, up_sum):
    step = pl.program_id(0)
    down = dot_tn(act_ref[...], gy_ref[...])
    up = dot_tn(gpre_ref[...], a2_ref[...])

    @pl.when(step == 0)
    def _():
        down_sum[...] = down
        up_sum[...] = up

    @pl.when(step > 0)
    def _():
        down_sum[...] += down
        up_sum[...] += up

    @pl.when(step == pl.num_programs(0) - 1)
    def _():
        half = down_sum.shape[0] // 2
        for which, out_ref in enumerate((mine_ref, other_ref)):
            here = pl.ds(which * half, half)
            out_ref[:half, :] = up_sum[here, :].astype(BF)
            out_ref[half:, :] = down_sum[here, :].astype(BF)


def mlp_grads_call(act, gpre, a2, gy, deps=()):
    tok, hidden = act.shape
    width = a2.shape[1]
    return call(
        mlp_grads_kernel,
        (act, gpre, a2, gy),
        [rows(hidden), rows(hidden), rows(width), rows(width)],
        [whole((hidden, width))] * 2,
        [shaped((hidden, width), BF)] * 2,
        "mlp_grads",
        deps,
        scratch=[pltpu.VMEM((hidden, width), F32)] * 2,
        grid=(tok // TILE,),
        cost_estimate=cost(4 * tok * width * hidden * 1.3, 1.4e7),
    )


def mid_kernel(
    groups, chained, handed, x1_ref, gy_ref, gh_a, gh_b, *refs,
):
    ctx_refs, refs = refs[:groups], refs[groups:]
    wm_ref, wo_ref, norm_ref = refs[:3]
    refs = refs[3 + chained + handed :]
    gx_ref, g_out, gout_ref, sum_ref = refs[:4]
    cm, co = (jnp.concatenate([ref[j] for ref in ctx_refs], axis=0) for j in range(2))
    step = pl.program_id(0)
    gy = gy_ref[...].astype(F32)
    gh = gh_a[...].astype(F32) + gh_b[...].astype(F32)
    n2, inv = normalized(x1_ref[...])
    e = gh * norm_ref[2:3]
    gx = gy + inv * (
        e - jnp.mean(e, axis=-1, keepdims=True) - n2 * jnp.mean(e * n2, axis=-1, keepdims=True)
    )
    gx_ref[...] = gx
    gm = gx.astype(BF)
    g_out[0] = dot_nt(wm_ref[...], gm).astype(BF)
    g_out[1] = dot_nt(wo_ref[...], gm).astype(BF)

    @pl.when(step == 0)
    def _():
        gout_ref[...] = jnp.zeros_like(gout_ref)
        sum_ref[...] = jnp.zeros_like(sum_ref)

    gout_ref[0] += dot_nn(cm, gm)
    gout_ref[1] += dot_nn(co, gm)
    for at, value in enumerate((gh * n2, gh, gx, gy)):
        sum_ref[at : at + 1, :] += jnp.sum(value, axis=0, keepdims=True)


def mid_call(span, x1, gy, gh, gh_other, ctx, w_m, w_o, norms, before=(), hand=(), deps=()):
    tok, width = x1.shape
    head = sum(part.shape[1] for part in ctx)
    begin, count = span[0], span[1] - span[0]
    args = (x1, gy, gh, gh_other, *ctx, w_m, w_o, norms, *before, *hand)
    fixed = len(args) - len(before) - len(hand)
    aliases = {fixed + j: j for j in range(len(before))}
    aliases.update({fixed + len(before) + j: 4 + j for j in range(len(hand))})
    return call(
        functools.partial(mid_kernel, len(ctx), len(before), len(hand)),
        args,
        [rows(width, begin)] * 2
        + [rows(width)] * 2
        + [both(part.shape[1], begin) for part in ctx]
        + [last_rows(w_m, head)] * 2
        + [whole(norms.shape)]
        + [ANYWHERE] * (len(before) + len(hand)),
        [rows(width, begin), both(head), whole((2, head, width)), whole((8, width))]
        + [ANYWHERE] * len(hand),
        [
            shaped((tok, width), F32), shaped((2, head, count * TILE), BF),
            shaped((2, head, width), F32), shaped((8, width), F32),
        ]
        + [shaped(part.shape, part.dtype) for part in hand],
        "mid_back",
        deps,
        grid=(count,),
        cost_estimate=cost(8 * count * TILE * width * head * 2, 1e7),
        input_output_aliases=aliases,
    )


def split_small(value):
    hi = value.astype(BF)
    lo = (value - hi.astype(F32)).astype(BF)
    return hi, lo, hi.astype(F32) + lo.astype(F32)


def in_grads_kernel(groups, gouts, *refs):
    g_refs, refs = refs[:groups], refs[groups:]
    out_refs, mid_refs, up_refs, refs = (
        refs[:gouts], refs[gouts : 2 * gouts], refs[2 * gouts : 3 * gouts], refs[3 * gouts :]
    )
    core_ref, a1_ref, x_ref, wm_ref, wo_ref, mine_ref, other_ref, gh_ref, sum_ref = refs[:9]
    m_sum, o_sum, gbm_ref, gbo_ref = refs[9:]
    step = pl.program_id(0)
    count = wm_ref.shape[0]
    a1 = a1_ref[...]
    gm, go = (
        jnp.concatenate([ref[half, j] for j in range(3) for ref in g_refs], axis=0)
        for half in range(2)
    )

    @pl.when(step == 0)
    def _():
        m_sum[...] = jnp.zeros_like(m_sum)
        o_sum[...] = jnp.zeros_like(o_sum)
        gbm_ref[...] = jnp.zeros_like(gbm_ref)
        gbo_ref[...] = jnp.zeros_like(gbo_ref)
        sum_ref[...] = jnp.zeros_like(sum_ref)

    m_sum[...] += dot_nn(gm, a1)
    o_sum[...] += dot_nn(go, a1)
    gbm_ref[...] += jnp.sum(gm.astype(F32), axis=1, keepdims=True)
    gbo_ref[...] += jnp.sum(go.astype(F32), axis=1, keepdims=True)
    gh = dot_tn(gm, wm_ref[...]) + dot_tn(go, wo_ref[...])
    gh_ref[...] = gh.astype(BF)
    n1, _ = normalized(x_ref[...].astype(F32))
    sum_ref[0:1, :] += jnp.sum(gh * n1, axis=0, keepdims=True)
    sum_ref[1:2, :] += jnp.sum(gh, axis=0, keepdims=True)

    @pl.when(step == pl.num_programs(0) - 1)
    def _():
        width = gh.shape[1]
        up = sum((ref[...] for ref in up_refs[1:]), up_refs[0][...])
        sum_ref[2:6, :] = sum((ref[0:4, :] for ref in mid_refs[1:]), mid_refs[0][0:4, :])

        def column(row):
            return jnp.transpose(jnp.broadcast_to(row, (LANES, row.shape[1])))[:, 0:1]

        swapped = core_ref[0] == 1
        mixed = []
        for mine, other in ((gbm_ref[...], gbo_ref[...]), (column(up[:, :width]), column(up[:, width:]))):
            lower, upper = jnp.where(swapped, other, mine), jnp.where(swapped, mine, other)
            for at in range(0, mine.shape[0], HALF):
                mixed += [lower[at : at + HALF], upper[at : at + HALF]]
        natural = jnp.concatenate(mixed, axis=0)
        natural = jnp.transpose(jnp.broadcast_to(natural, (natural.shape[0], LANES)))[0:1]
        for at in range(0, natural.shape[1], width):
            part = natural[:, at : at + width]
            sum_ref[6 + at // width : 7 + at // width, : part.shape[1]] = part
        hi, lo, kept = split_small(sum_ref[...])
        sum_ref[...] = kept
        more = count + out_refs[0].shape[1]
        for ref, total, half in ((mine_ref, m_sum, 0), (other_ref, o_sum, 1)):
            ref[:count, :] = total[...].astype(BF)
            ref[count:more, :] = sum((out[half] for out in out_refs[1:]), out_refs[0][half]).astype(BF)
        other_ref[more : more + 16, :] = hi
        other_ref[more + 16 :, :] = lo


def in_grads_call(grads, core, a1, x, w_m, w_o, gouts, mid_sums, gb_ups, deps=()):
    tok, width = a1.shape
    more = gouts[0].shape[1]
    count = w_m.shape[0] - more
    parts = [
        pl.BlockSpec(part.shape[:3] + (TILE,), lambda t: (0, 0, 0, t)) for part in grads
    ]
    return call(
        functools.partial(in_grads_kernel, len(grads), len(gouts)),
        (*grads, *gouts, *mid_sums, *gb_ups, core[None], a1, x, w_m, w_o),
        parts
        + [whole(part.shape) for part in (*gouts, *mid_sums, *gb_ups)]
        + [SMEM, rows(width), rows(width)]
        + [whole((count, width))] * 2,
        [whole((count + more, width)), whole((count + more + 32, width)), rows(width), whole((16, width))],
        [
            shaped((count + more, width), BF), shaped((count + more + 32, width), BF),
            shaped((tok, width), BF), shaped((16, width), F32),
        ],
        "in_grads",
        deps,
        scratch=[pltpu.VMEM((count, width), F32)] * 2 + [pltpu.VMEM((count, 1), F32)] * 2,
        grid=(tok // TILE,),
        cost_estimate=cost(8 * tok * width * count * 1.3, 1e7),
    )


def out_kernel(x1_ref, a_ref, b_ref, norm_ref, out_ref):
    out_ref[...] = x1_ref[...] + (a_ref[...].astype(F32) + b_ref[...].astype(F32)) + norm_ref[5:6]


def out_call(x1, ffn_a, ffn_b, norms):
    tok, width = x1.shape
    return call(
        out_kernel,
        (x1, ffn_a, ffn_b, norms),
        [rows(width)] * 3 + [whole(norms.shape)],
        rows(width),
        shaped((tok, width), F32),
        "layer_out",
        grid=(tok // TILE,),
        cost_estimate=cost(4e9, 1e7),
    )


def nothing_kernel(*refs):
    pass


def hand_call(arrays, deps):
    return call(
        nothing_kernel, arrays, [ANYWHERE] * len(arrays), [ANYWHERE] * len(arrays),
        [shaped(array.shape, array.dtype) for array in arrays], "hand", deps,
        input_output_aliases={at: at for at in range(len(arrays))},
    )


def keep_kernel(*refs):
    half = len(refs) // 2
    for source, target in zip(refs[:half], refs[half:]):
        target[...] = source[...]


def keep_call(arrays, deps=()):
    specs = [whole(array.shape) for array in arrays]
    return call(
        keep_kernel, arrays, specs, specs, [shaped(a.shape, a.dtype) for a in arrays], "keep", deps,
        cost_estimate=cost(4e9, 1e7),
    )


def last_kernel(x_ref, gx_ref, gh_a, gh_b, norm_ref, out_ref):
    n1, inv = normalized(x_ref[...].astype(F32))
    e = (gh_a[...].astype(F32) + gh_b[...].astype(F32)) * norm_ref[0:1]
    out_ref[...] = gx_ref[...] + inv * (
        e - jnp.mean(e, axis=-1, keepdims=True) - n1 * jnp.mean(e * n1, axis=-1, keepdims=True)
    )


def last_call(x, gx, gh_a, gh_b, norms):
    tok, width = x.shape
    return call(
        last_kernel,
        (x, gx, gh_a, gh_b, norms),
        [rows(width)] * 4 + [whole(norms.shape)],
        rows(width),
        shaped((tok, width), F32),
        "last_back",
        grid=(tok // TILE,),
        cost_estimate=cost(1e6, 1.2e7),
    )


def layout_kernel(core_ref, len_ref, freq_ref, bias_ref, cos_ref, sin_ref, row_ref, col_ref, kept_ref, start_ref):
    kept_ref[...] = bias_ref[...]
    tok = cos_ref.shape[1]
    docs = len_ref.shape[1]
    begin, best, start = 0, len_ref[0, 0], 0
    begins, ends = [], []
    for doc in range(docs):
        size = len_ref[0, doc]
        if doc:
            start = jnp.where(size > best, begin, start)
            best = jnp.maximum(size, best)
        begins.append(begin)
        begin = begin + size
        ends.append(begin)
    start_ref[0] = start + jnp.zeros((), I32)

    def origin(places):
        at = places + start
        return jnp.where(at >= tok, at - tok, at)

    def document(at):
        return sum(((at >= end).astype(I32) for end in ends), jnp.zeros(at.shape, I32))

    row = origin(lax.broadcasted_iota(I32, (1, tok), 1))
    first = jnp.zeros((1, tok), I32)
    for begin in begins[1:]:
        first = jnp.where(row >= begin, begin, first)
    angles = freq_ref[...] * (row - first).astype(F32)
    cos_ref[...] = jnp.cos(angles)
    sine = jnp.sin(angles)
    sin_ref[...] = jnp.where(core_ref[0] == 0, sine, -sine)
    rest = row_ref.shape[1]
    row_ref[...] = document(row[:, tok - rest :])
    col_ref[...] = document(origin(lax.broadcasted_iota(I32, (rest, 1), 0) + (tok - rest)))


def layout_call(core, lengths, biases, tok, deps=()):
    rest = tok - LONGEST
    freq = np.float32(10000.0) ** -(np.arange(0, HEAD_DIM, 2).astype(np.float32) / HEAD_DIM)
    return call(
        layout_kernel,
        (core[None], lengths, jnp.asarray(freq[:, None], F32), biases),
        [SMEM, SMEM, whole((HALF, 1)), whole(biases.shape)],
        [whole((HALF, tok))] * 2 + [whole((1, rest)), whole((rest, 1)), whole(biases.shape), SMEM],
        [shaped((HALF, tok), F32)] * 2
        + [
            shaped((1, rest), I32), shaped((rest, 1), I32), shaped(biases.shape, F32),
            shaped((1,), I32),
        ],
        "layout",
        deps,
    )


def halves_kernel(core_ref, table_ref, mine_ref, other_ref):
    first = core_ref[0] == 0
    count = mine_ref.shape[1]
    upper, lower = table_ref[:, :count, :], table_ref[:, count:, :]
    mine_ref[...] = jnp.where(first, upper, lower).astype(BF)
    other_ref[...] = jnp.where(first, lower, upper).astype(BF)


def halves_call(core, table):
    cap, count, width = table.shape
    half = (cap, count // 2, width)
    return call(
        halves_kernel,
        (core[None], table),
        [SMEM, whole(table.shape)],
        [whole(half)] * 2,
        [shaped(half, BF)] * 2,
        "halves",
    )


def attend_kernel(seg_row, seg_col, m_ref, o_ref, ctx_ref, log_ref):
    tok = m_ref.shape[2]
    rest = tok - LONGEST
    q_t, k_t, v_t = (jnp.concatenate([m_ref[j], o_ref[j]], axis=0) for j in range(3))
    qs = q_t.astype(F32) * SCALE_LOG2
    hi, lo = split_two(qs)
    qx = jnp.transpose(jnp.concatenate([hi, lo], axis=0)).astype(BF)
    kx = jnp.concatenate([k_t, k_t], axis=0)
    v_f = v_t.astype(F32)
    vx = jnp.transpose(jnp.concatenate([v_f, jnp.ones((8, tok), F32)], axis=0)).astype(BF)
    k_f = k_t.astype(F32)
    q_top = jnp.max(jnp.sum(qs * qs, axis=0, keepdims=True))
    k_top = jnp.max(jnp.sum(k_f * k_f, axis=0, keepdims=True))
    safe = q_top * k_top < SAFE_EXP * SAFE_EXP
    same = seg_col[...] == seg_row[...]

    def finish(sums, shift, at, count):
        turned = jnp.transpose(sums)
        total = turned[HEAD_DIM : HEAD_DIM + 1]
        ctx = (turned[0:HEAD_DIM] / total).astype(BF)
        ctx_ref[0, :, at : at + count] = ctx[:HALF]
        ctx_ref[1, :, at : at + count] = ctx[HALF:]
        log_total = jnp.log2(total)
        if shift is not None:
            log_total = log_total + jnp.transpose(jnp.broadcast_to(shift, (count, LANES)))[0:1]
        log_ref[0, :, at : at + count] = log_total

    def run(exact):
        for at in range(0, LONGEST, TILE):
            scores = dot_nn(qx[at : at + TILE], kx[:, :LONGEST])
            shift = None
            if exact:
                shift = jnp.max(scores, axis=1, keepdims=True)
                scores = scores - shift
            finish(dot_nn(jnp.exp2(scores).astype(BF), vx[:LONGEST]), shift, at, TILE)
        if rest:
            scores = jnp.where(same, dot_nn(qx[LONGEST:], kx[:, LONGEST:]), NEG_FILL)
            shift = None
            if exact:
                shift = jnp.max(scores, axis=1, keepdims=True)
                scores = scores - shift
            finish(dot_nn(jnp.exp2(scores).astype(BF), vx[LONGEST:]), shift, LONGEST, rest)

    @pl.when(safe)
    def _():
        run(False)

    @pl.when(jnp.logical_not(safe))
    def _():
        run(True)


def attend_call(segs, qkv_m, qkv_o, first, count, deps=()):
    tok = qkv_m.shape[2]
    rest = segs[0].shape[1]
    part = pl.BlockSpec((3, HALF, tok), lambda h: (0, first + h, 0))
    out = pl.BlockSpec((2, HALF, tok), lambda h: (0, h, 0))
    return call(
        attend_kernel,
        (*segs, qkv_m, qkv_o),
        [whole((1, rest)), whole((rest, 1)), part, part],
        [out, pl.BlockSpec((1, 1, tok), lambda h: (h, 0, 0))],
        [shaped((2, count * HALF, tok), BF), shaped((count, 1, tok), F32)],
        "attend",
        deps,
        grid=(count,),
        cost_estimate=cost(count * 2.5e9, 3e6),
    )


def attend_back_kernel(
    q_begin, q_end, last, seg_row, seg_col, cos_ref, sin_ref, m_ref, o_ref, g_ref, ctx_ref, log_ref,
    *refs,
):
    tok = m_ref.shape[2]
    rest = tok - LONGEST
    end = tok if last else q_end
    span = slice(q_begin, end)
    q_t, k_t, v_t = (jnp.concatenate([m_ref[j], o_ref[j]], axis=0) for j in range(3))
    q_f = q_t[:, span].astype(F32)
    ctx = jnp.concatenate([ctx_ref[0, :, span], ctx_ref[1, :, span]], axis=0).astype(F32)
    g_f = jnp.concatenate([g_ref[0], g_ref[1]], axis=0).astype(F32)
    hi, lo = split_two(q_f * SCALE_LOG2)
    weighted = jnp.sum(g_f * ctx, axis=0, keepdims=True)
    pad = jnp.zeros((13, end - q_begin), F32)
    qx = jnp.concatenate([hi, lo, *split_three(log_ref[0, :, span]), pad], axis=0).astype(BF)
    keys = tok if last else LONGEST
    k_f, v_f = k_t[:, :keys].astype(F32), v_t[:, :keys].astype(F32)
    minus = jnp.concatenate([jnp.full((3, keys), -1.0, F32), jnp.zeros((13, keys), F32)], axis=0)
    kx = jnp.transpose(jnp.concatenate([k_f, k_f, minus], axis=0)).astype(BF)
    gx = jnp.concatenate([g_f, *split_three(weighted), pad], axis=0).astype(BF)
    vx = jnp.transpose(jnp.concatenate([v_f, minus], axis=0)).astype(BF)
    qn = jnp.transpose(q_f).astype(BF)
    gn = jnp.transpose(g_f).astype(BF)

    if last:
        early_q, early_kv, out_ref = refs
    else:
        out_q, out_kv = refs

    def turned_back(grad, at, count):
        cos, sin = cos_ref[:, at : at + count], sin_ref[:, at : at + count]
        mine, other = grad[0:HALF] * SCALE, grad[HALF:] * SCALE
        return (mine * cos + other * sin).astype(BF), (other * cos - mine * sin).astype(BF)

    def block(k_at, k_count, q_at, q_count, mask, early):
        scores = dot_nn(kx[k_at : k_at + k_count], qx[:, q_at : q_at + q_count])
        if mask is not None:
            scores = jnp.where(mask, scores, NEG_FILL)
        prob = jnp.exp2(scores)
        grad_prob = dot_nn(vx[k_at : k_at + k_count], gx[:, q_at : q_at + q_count])
        grad_score = (prob * grad_prob).astype(BF)
        grad_v = jnp.transpose(dot_nn(prob.astype(BF), gn[q_at : q_at + q_count]))
        grad_k = jnp.transpose(dot_nn(grad_score, qn[q_at : q_at + q_count]))
        here = slice(k_at, k_at + k_count)
        if not last:
            out_kv[0, 0, :, here] = grad_k
            out_kv[1, 0, :, here] = grad_v
        else:
            if early:
                grad_k = grad_k + early_kv[0, 0, :, here]
                grad_v = grad_v + early_kv[1, 0, :, here]
            out_ref[0, 1, :, here], out_ref[1, 1, :, here] = turned_back(grad_k, k_at, k_count)
            out_ref[0, 2, :, here] = grad_v[:HALF].astype(BF)
            out_ref[1, 2, :, here] = grad_v[HALF:].astype(BF)
        return dot_nn(k_t[:, k_at : k_at + k_count], grad_score)

    grad_q = None
    for at in range(0, LONGEST, TILE):
        piece = block(at, TILE, 0, q_end - q_begin, None, True)
        grad_q = piece if grad_q is None else grad_q + piece
    mine, other = turned_back(grad_q, q_begin, q_end - q_begin)
    if not last:
        out_q[0], out_q[1] = mine, other
        return
    out_ref[0, 0, :, :q_begin] = early_q[0]
    out_ref[1, 0, :, :q_begin] = early_q[1]
    out_ref[0, 0, :, q_begin:q_end] = mine
    out_ref[1, 0, :, q_begin:q_end] = other
    if rest:
        same = seg_col[...] == seg_row[...]
        piece = block(LONGEST, rest, LONGEST - q_begin, rest, same, False)
        out_ref[0, 0, :, LONGEST:], out_ref[1, 0, :, LONGEST:] = turned_back(piece, LONGEST, rest)


def attend_back_call(
    q_begin, q_end, segs, cos, sin, qkv_m, qkv_o, g_ctx, ctx, logs, first, count, early=(), deps=()
):
    tok = qkv_m.shape[2]
    last = len(early) > 0
    rest = segs[0].shape[1]
    part = pl.BlockSpec((3, HALF, tok), lambda h: (0, first + h, 0))
    table = whole((HALF, tok))

    def by_head(length, offset=0):
        return pl.BlockSpec((2, HALF, length), lambda h: (0, offset + h, 0))

    pair = pl.BlockSpec((2, 1, HEAD_DIM, LONGEST), lambda h: (0, h, 0, 0))
    if last:
        out_specs = [pl.BlockSpec((2, 3, HALF, tok), lambda h: (0, 0, h, 0))]
        out_shape = [shaped((2, 3, count * HALF, tok), BF)]
    else:
        out_specs = [by_head(q_end), pair]
        out_shape = [
            shaped((2, count * HALF, q_end), BF), shaped((2, count, HEAD_DIM, LONGEST), F32)
        ]
    return call(
        functools.partial(attend_back_kernel, q_begin, q_end, last),
        (*segs, cos, sin, qkv_m, qkv_o, g_ctx, ctx, logs, *early),
        [
            whole((1, rest)), whole((rest, 1)), table, table, part, part,
            by_head(g_ctx.shape[2], first), by_head(tok), pl.BlockSpec((1, 1, tok), lambda h: (h, 0, 0)),
        ]
        + ([by_head(q_begin), pair] if last else []),
        out_specs,
        out_shape,
        "attend_back",
        deps,
        grid=(count,),
        cost_estimate=cost(count * 2.1e9, 6e6),
    )


class Routes:
    def __init__(self, dp_size, slot_cap, pieces, ready, spans):
        self.dp = dp_size
        self.cap = slot_cap
        self.chips = dp_size // 2
        self.pieces = pieces
        self.ready = ready
        self.spans = spans
        if self.chips == 8:
            self.stages = ((2, 4), (1, 2))
        elif self.chips == 64:
            self.stages = ((1, 8), (8, 2), (16, 4))
        else:
            self.stages = ((1, self.chips),)
        self.depth = len(self.stages)
        straight = self.stages[::-1]
        paired = ((1, 2), (4, 2), (2, 2)) if self.chips == 8 else straight
        self.back = (straight, paired)
        self.out = (self.stages, ((4, 2), (2, 2), (1, 2)) if self.chips == 8 else self.stages)
        self.fill = [self.limit(last, self.chips) for last in ready]
        self.begins = [0] + self.fill[:-1]
        early, late = self.fill[0], self.fill[1] - self.fill[0]
        if self.chips == 8:
            self.bases = (
                [at * early for at in range(4)]
                + [4 * early]
                + [4 * early + self.fill[1] + at * early for at in range(3)],
                [7 * early + self.fill[1] + at * late for at in range(4)]
                + [5 * early]
                + [7 * early + self.fill[1] + at * late for at in range(4, 7)],
            )
        else:
            self.bases = tuple(
                [begin * self.chips + at * (end - begin) for at in range(self.chips)]
                for begin, end in zip(self.begins, self.fill)
            )

    def limit(self, count, groups):
        worst = min(count, self.dp // groups * self.cap)
        if self.chips != 8:
            return worst
        typical = {
            2: count * 11 // 20 + 8, 4: count * 3 // 10 + 10, 8: count // 5 + 5
        }[groups]
        return worst if count == self.pieces else min(worst, typical)

    def span_limit(self, number, level):
        groups = 1
        for _, size in self.back[number][:level]:
            groups *= size
        return self.limit(self.spans[number][1] - self.spans[number][0], groups)

    def move(self, array, stage, shift):
        stride, size = stage
        pairs = []
        for device in range(self.dp):
            chip, core = device // 2, device % 2
            at = (chip // stride) % size
            pairs.append((device, 2 * (chip + ((at + shift) % size - at) * stride) + core))
        return lax.ppermute(array, "dp", pairs)

    def swap_cores(self, array):
        return lax.ppermute(array, "dp", [(d, d ^ 1) for d in range(self.dp)])

    def around(self, array, stage):
        return [array] + [self.move(array, stage, shift) for shift in range(1, stage[1])]

    def onward(self, buffers, stage):
        return buffers + [
            self.move(buffer, stage, shift) for shift in range(1, stage[1]) for buffer in buffers
        ]

    def tables(self, owners, me):
        place = {}

        def kernel(me_ref, own_ref, out_ref, row_ref):
            here = me_ref[0]
            my_chip, my_core = here // 2, here % 2
            row_ref[...] = jnp.full((1, LANES), -2, I32)
            row_ref[:, : self.pieces] = own_ref[...]
            row = row_ref[...]
            col = jnp.transpose(jnp.broadcast_to(row, (LANES, LANES)))[:, 0:1]
            id_row = lax.broadcasted_iota(I32, (1, LANES), 1)
            id_col = lax.broadcasted_iota(I32, (LANES, 1), 0)
            lane = lax.broadcasted_iota(I32, (LANES, LANES), 1)
            sub = lax.broadcasted_iota(I32, (LANES, LANES), 0)

            def rank_col(key_row, key_col):
                hit = (key_row == key_col) & (lane < sub)
                return jnp.sum(hit.astype(F32), axis=1, keepdims=True).astype(I32)

            def rank_row(key_row, key_col):
                hit = (key_row == key_col) & (sub < lane)
                return jnp.sum(hit.astype(F32), axis=0, keepdims=True).astype(I32)

            def gather(valid_col, entry_col, value_col):
                hit = valid_col & (entry_col == lane)
                return jnp.sum(
                    jnp.where(hit, value_col.astype(F32), 0.0), axis=0, keepdims=True
                ).astype(I32)

            def put(name, value):
                at = place.setdefault(name, len(place))
                out_ref[at : at + 1, :] = value

            def coord(chip, stage):
                return (chip // stage[0]) % stage[1]

            def group(chip, stages):
                key = 0
                for stage in stages:
                    key = key * stage[1] + coord(chip, stage)
                return key

            def fullest(inside, rank):
                return jnp.max(jnp.where(inside, rank, -1), axis=0, keepdims=True) + 1

            slot_col = rank_col(row, col)
            put("piece", gather(col == here, slot_col, id_col + 1) - 1)
            sibling = my_chip * 2 + 1 - my_core
            put("sibling", gather(col == sibling, slot_col, id_col + 1) - 1)
            over = jnp.zeros((1, 1), I32)
            real = id_col < self.pieces
            chip_col, chip_row = col // 2, row // 2
            rank_c, rank_r = rank_col(chip_row, chip_col), rank_row(chip_row, chip_col)
            from_core = jnp.where(col % 2 == my_core, 0, self.cap)
            put("send", gather(real & (chip_col == my_chip), rank_c, from_core + slot_col))
            for last, fill in zip(self.ready, self.fill):
                over = jnp.maximum(over, fullest(id_col < last, rank_c) - fill)
            put("late", jnp.broadcast_to(over, (1, LANES)))
            over = jnp.zeros((1, 1), I32)
            take = jnp.zeros((1, LANES), I32)
            for begin, bases, stages in zip(self.begins, self.bases, self.out):
                way, scale = jnp.zeros((1, LANES), I32), 1
                for stage in stages:
                    away = (coord(my_chip, stage) - coord(chip_row, stage) + stage[1]) % stage[1]
                    way = way + away * scale
                    scale = scale * stage[1]
                spot = rank_r - begin
                for at, base in enumerate(bases):
                    spot = spot + jnp.where(way == at, base, 0)
                take = jnp.where(rank_r >= begin, spot, take)
            put("take", take)
            for number, span in enumerate(self.spans):
                in_col = (id_col >= span[0]) & (id_col < span[1])
                in_row = (id_row >= span[0]) & (id_row < span[1])
                stages = self.back[number]
                ranks = {}
                for level in range(1, len(stages) + 1):
                    key_col = jnp.where(in_col, group(chip_col, stages[:level]), -1)
                    key_row = jnp.where(in_row, group(chip_row, stages[:level]), -1)
                    ranks[level] = rank_col(key_row, key_col)
                    over = jnp.maximum(
                        over, fullest(in_col, ranks[level]) - self.span_limit(number, level)
                    )
                value = id_col - span[0]
                for level, stage in enumerate(stages, 1):
                    size = stage[1]
                    inside = in_col & (
                        group(chip_col, stages[: level - 1]) == group(my_chip, stages[: level - 1])
                    )
                    for shift in range(size):
                        goal = (coord(my_chip, stage) + shift) % size
                        put(
                            ("back", number, level, shift),
                            gather(inside & (coord(chip_col, stage) == goal), ranks[level], value),
                        )
                    value = ranks[level]
                for which in range(2):
                    goal = my_chip * 2 + (my_core + which) % 2
                    put(
                        ("slot", number, which),
                        gather(in_col & (col == goal), slot_col, ranks[len(stages)]),
                    )
            put("over", jnp.broadcast_to(over, (1, LANES)))

        count = 6 + sum(2 + sum(size for _, size in stages) for stages in self.back)
        height = -(-count // 8) * 8
        table = pl.pallas_call(
            kernel,
            in_specs=[SMEM, whole((1, self.pieces))],
            out_specs=whole((height, LANES)),
            out_shape=shaped((height, LANES), I32),
            scratch_shapes=[pltpu.VMEM((1, LANES), I32)],
            compiler_params=params(),
            name="routes",
        )(me[None], owners[None, :])
        return table, place


def pick_call(table, picks, parts, sizes, name, deps=()):
    rows_each = [part.shape[0] for part in parts]
    shape = parts[0].shape[1:]

    def kernel(table_ref, *refs):
        ins, outs, source = refs[: len(parts)], refs[len(parts) : -1], refs[-1]
        at = 0
        for ref, count in zip(ins, rows_each):
            source[at : at + count] = ref[...]
            at += count
        for (row, start), size, out in zip(picks, sizes, outs):
            for j in range(size):
                out[j] = source[table_ref[row, start + j]]

    return call(
        kernel,
        (table, *parts),
        [SMEM] + [whole(part.shape) for part in parts],
        [whole((size,) + shape) for size in sizes],
        [shaped((size,) + shape, BF) for size in sizes],
        name,
        deps,
        scratch=[pltpu.VMEM((sum(rows_each),) + shape, BF)],
    )


def join_call(parts, deps=()):
    counts = [part.shape[0] for part in parts]
    shape = (sum(counts),) + parts[0].shape[1:]

    def kernel(*refs):
        at = 0
        for ref, count in zip(refs, counts):
            refs[-1][at : at + count] = ref[...]
            at += count

    return call(
        kernel, parts, [whole(part.shape) for part in parts], whole(shape), shaped(shape, BF), "join", deps
    )


def add_pick_call(table, picks, parts, sizes, dtype=BF, name="add_pick", small=None, extra=(), deps=()):
    shape = parts[0].shape[1:]
    lengths = [size + 2 * (j in extra) for j, size in enumerate(sizes)]

    def kernel(table_ref, *refs):
        ins, refs = refs[: len(parts)], refs[len(parts) :]
        if small is not None:
            small_ref, refs = refs[0], refs[1:]
            terms = [small_ref[...]] + [
                ref[ref.shape[0] - 2].astype(F32) + ref[ref.shape[0] - 1].astype(F32) for ref in ins[1:]
            ]
            while len(terms) > 1:
                middle = len(terms) // 2
                terms = [a + b for a, b in zip(terms[:middle], terms[middle:])]
            hi, lo, kept = split_small(terms[0])
            refs[len(sizes)][...] = kept
            for j in extra:
                refs[j][sizes[j]] = hi
                refs[j][sizes[j] + 1] = lo
        for (row, start), size, out in zip(picks, sizes, refs):
            for j in range(size):
                at = table_ref[row, start + j]
                total = ins[0][at].astype(F32)
                for ref in ins[1:]:
                    total = total + ref[at].astype(F32)
                out[j] = total.astype(dtype)

    out_specs = [whole((length,) + shape) for length in lengths]
    out_shape = [shaped((length,) + shape, dtype) for length in lengths]
    if small is not None:
        out_specs, out_shape = out_specs + [whole(shape)], out_shape + [shaped(shape, F32)]
    return call(
        kernel,
        (table, *parts) + (() if small is None else (small,)),
        [SMEM] + [whole(part.shape) for part in parts] + ([] if small is None else [whole(shape)]),
        out_specs,
        out_shape,
        name,
        deps,
    )


def owned_call(table, place, routes, parts, small, deps=()):
    (parts_in, parts_mlp), cap = parts, routes.cap
    shape = parts_in[0].shape[1:]
    border = routes.spans[1][0]

    def kernel(table_ref, *refs):
        ins, refs = refs[: len(parts_in)], refs[len(parts_in) :]
        mlps, refs = refs[: len(parts_mlp)], refs[len(parts_mlp) :]
        small_ref, kept_ref, sent_ref, total_ref = refs
        terms = [small_ref[...]] + [
            ref[ref.shape[0] - 2].astype(F32) + ref[ref.shape[0] - 1].astype(F32) for ref in ins[1:]
        ]
        while len(terms) > 1:
            middle = len(terms) // 2
            terms = [a + b for a, b in zip(terms[:middle], terms[middle:])]
        total_ref[...] = terms[0]
        for which, (name, out) in enumerate((("piece", kept_ref), ("sibling", sent_ref))):
            for j in range(cap):
                sums = []
                for number, some in enumerate((ins, mlps)):
                    at = table_ref[place[("slot", number, which)], j]
                    total = some[0][at].astype(F32)
                    for ref in some[1:]:
                        total = total + ref[at].astype(F32)
                    sums.append(total)
                out[j] = jnp.where(table_ref[place[name], j] >= border, sums[1], sums[0])

    args = (table, *parts_in, *parts_mlp, small)
    return call(
        kernel,
        args,
        [SMEM] + [whole(arg.shape) for arg in args[1:]],
        [whole((cap,) + shape)] * 2 + [whole(shape)],
        [shaped((cap,) + shape, F32)] * 2 + [shaped(shape, F32)],
        "owned",
        deps,
    )


def adam_step(weights, first_mom, second_mom, gradient, rate, decay_rate):
    first_new = BETA_ONE * first_mom + (1.0 - BETA_ONE) * gradient
    second_new = BETA_TWO * second_mom + (1.0 - BETA_TWO) * gradient * gradient
    first_fix = first_new / (1.0 - BETA_ONE**STEP)
    second_fix = second_new / (1.0 - BETA_TWO**STEP)
    weights_new = weights * (1.0 - rate * decay_rate) - rate * first_fix / (
        jnp.sqrt(second_fix) + ADAM_EPS
    )
    return (weights_new, first_new, second_new)


def adam_call(table, row, core, borders, kept, arrived, tables):
    cap, count, width = tables[0].shape
    half = count // 2
    group = max(g for g in range(1, 6) if cap % g == 0)

    def kernel(table_ref, core_ref, kept_ref, arrived_ref, w_ref, m_ref, v_ref, *outs):
        step = pl.program_id(0)
        swapped = core_ref[0] == 1
        for j in range(group):
            piece = table_ref[row, step * group + j]
            rate = jnp.where(piece < borders[2], 0.03, 0.015)
            rate = jnp.where(piece < borders[1], 0.2, rate)
            rate = jnp.where(piece < borders[0], 0.03, rate).astype(F32)
            halves = (kept_ref[j], arrived_ref[j])
            for at in range(2):
                here = pl.ds(at * half, half)
                grad = jnp.where(swapped, halves[1 - at], halves[at])
                new = adam_step(w_ref[j, here], m_ref[j, here], v_ref[j, here], grad, rate, DECAY_RATE)
                for out, value in zip(outs, new):
                    out[j, here] = jnp.where(piece >= 0, value, 0.0)

    def block(rows_each):
        return pl.BlockSpec((group, rows_each, width), lambda t: (t, 0, 0))

    return call(
        kernel,
        (table, core[None], kept, arrived, *tables),
        [SMEM, SMEM, block(half), block(half)] + [block(count)] * 3,
        [block(count)] * 3,
        [shaped((cap, count, width), F32)] * 3,
        "adam",
        grid=(cap // group,),
        cost_estimate=cost(1e7, 8e6),
    )


def small_kernel(total_ref, far_ref, norm_ref, nm_ref, nv_ref, bias_ref, bm_ref, bv_ref, *outs):
    gains = total_ref[0:2, :] + far_ref[0:2, :]
    for at, rate in enumerate(NORM_RATES):
        here = slice(at, at + 1)
        grad = gains[here] if at < 2 else total_ref[here, :]
        new = adam_step(norm_ref[here, :], nm_ref[here, :], nv_ref[here, :], grad, rate, 0.0)
        for out, value in zip(outs[:3], new):
            out[here, :] = value
    width = total_ref.shape[1]
    for at in range(0, bias_ref.shape[1], width):
        here = slice(at, min(at + width, bias_ref.shape[1]))
        row = 6 + at // width
        grad = total_ref[row : row + 1, : here.stop - at]
        new = adam_step(bias_ref[:, here], bm_ref[:, here], bv_ref[:, here], grad, BIAS_RATE, 0.0)
        for out, value in zip(outs[3:], new):
            out[:, here] = value


def small_call(total, far, norms, biases):
    args = (total, far, *norms, *biases)
    kept = [shaped(part.shape, F32) for part in (*norms, *biases)]
    return call(
        small_kernel, args, [whole(arg.shape) for arg in args], [whole(k.shape) for k in kept], kept, "small_update"
    )


def swap_mp(array):
    return lax.ppermute(array, "mp", [(0, 1), (1, 0)])


def swap_both(array):
    dp_size = lax.axis_size("dp")
    pairs = [(2 * d + m, 2 * (d ^ 1) + 1 - m) for d in range(dp_size) for m in range(2)]
    return lax.ppermute(array, ("dp", "mp"), pairs)


def roll_rows(array, start):
    return lax.dynamic_slice_in_dim(
        jnp.concatenate([array, array], axis=0), start, array.shape[0], axis=0
    )


def body(
    tokens, cotangent, lengths, owners, weight_table, moment_table, square_table,
    norm_params, norm_moment, norm_square, bias_params, bias_moment, bias_square,
):
    dp_size = lax.axis_size("dp")
    mp_size = lax.axis_size("mp")
    heads = HEADS // mp_size
    head_width = heads * HEAD_DIM
    hidden = FF // mp_size
    tok, width = tokens.shape
    slot_cap, piece_len = weight_table.shape[1:3]
    half_len = piece_len // 2
    piece_total = owners.shape[0]
    me = lax.axis_index("dp").astype(I32)
    core = me % 2
    first_core = core == 0

    n_qkv, n_out = 3 * head_width // piece_len, head_width // piece_len
    n_up = hidden // piece_len
    n_first = n_qkv + n_out
    ready = (n_first, piece_total)
    spans = ((0, n_first), (n_first, piece_total))
    routes = Routes(dp_size, slot_cap, piece_total, ready, spans)
    table, place = routes.tables(owners, me)

    own_half, sibling_half = halves_call(core, weight_table[0])
    chip_slots = [own_half, routes.swap_cores(sibling_half)]

    def half(array, which):
        return lax.dynamic_index_in_dim(array, which, axis=1, keepdims=False)

    def unless(bad, usual, other):
        return lax.while_loop(
            lambda state: state[0] > 0, lambda state: (jnp.zeros((), I32), other()), (bad, usual)
        )[1]

    def own_lists(ranges, deps=()):
        return pick_call(
            table, [(place["send"], begin) for begin, _ in ranges], chip_slots,
            [end - begin for begin, end in ranges], "pick_owned", deps,
        )

    def collect(buffers, ranges, deps=()):
        sizes = [high - low for low, high in ranges]
        return pick_call(
            table, [(place["take"], low) for low, _ in ranges], buffers, sizes, "pick_all", deps
        )

    def flat(array):
        return array.reshape(-1, width)

    def pairs_apart(bit):
        return [(device, device ^ bit) for device in range(dp_size)]

    def slow_first():
        everyone, bit = weight_table[0].astype(BF), 1
        while bit < dp_size:
            everyone = jnp.concatenate([everyone, lax.ppermute(everyone, "dp", pairs_apart(bit))], 0)
            bit *= 2
        earlier = (owners[None, :] == owners[:, None]) & (
            jnp.arange(piece_total)[None, :] < jnp.arange(piece_total)[:, None]
        )
        at = (owners ^ me) * slot_cap + jnp.sum(earlier.astype(I32), axis=1)
        return half(everyone[at[:n_first]].reshape(n_first, 2, half_len, width), core)

    stages = routes.out
    chunks = tuple(zip(routes.begins, routes.fill))
    relayed = routes.chips == 8
    if relayed:
        list_a, list_all = own_lists((chunks[0], (0, routes.fill[1])))
    else:
        list_a, list_b = own_lists([chunk for chunk in chunks if chunk[0] < chunk[1]] * 2)[:2]
    list_a = routes.around(list_a, stages[0][0])
    cos, sin, *segs, biases, start = layout_call(core, lengths, bias_params, tok, (list_a[0],))
    start = start[0]
    x = roll_rows(tokens, start)
    gy = roll_rows(cotangent, start)
    a1 = norm_call(x, norm_params)
    bias_halves = biases[0].reshape(-1, 2, half_len)
    b_mine, b_other = half(bias_halves, core), half(bias_halves, 1 - core)
    b_qkv = [part[:n_qkv].reshape(-1, 1) for part in (b_mine, b_other)]
    b_up = jnp.concatenate([part[n_qkv:].reshape(1, -1) for part in (b_mine, b_other)], axis=1)

    if relayed:
        own_y = routes.move(list_all, stages[0][1], 1)
        buffers_a = list_a + [own_y] + [routes.move(part, stages[0][1], 1) for part in list_a[1:]]
        (list_b,) = own_lists(chunks[1:], (*list_a[1:], own_y))
        from_two, from_one = (routes.move(list_b, stage, 1) for stage in stages[1][:2])
    else:
        buffers_a, buffers_b = list_a, [list_b]
        for stage in stages[0][1:]:
            buffers_a = routes.onward(buffers_a, stage)
    (w_first_m,) = collect(buffers_a, ((0, n_first),), (a1, gy, cos, sin, *b_qkv, b_up, list_b))
    w_first_m = unless(table[place["late"], 0], w_first_m, slow_first)
    b_qkv = keep_call(b_qkv, (w_first_m,))
    w_first_o = routes.swap_cores(w_first_m)
    qkv_m, qkv_o = qkv_call(a1, flat(w_first_m), flat(w_first_o), *b_qkv, cos, sin)
    w_out_m = w_first_m[n_qkv:]
    w_out_x = [flat(swap_mp(w_out_m)), flat(swap_both(w_out_m))]
    if relayed:
        joined = join_call([from_two, from_one], (qkv_m,))
        (held,) = hand_call((from_two,), (qkv_m,))
        relay = routes.move(held, stages[1][1], 1)
        y_joined = routes.move(joined, stages[1][2], 1)
    cut = heads * 6 // 10
    groups = ((0, cut), (cut, heads - cut))
    ctx_one, logs_one = attend_call(segs, qkv_m, qkv_o, *groups[0], (joined, *w_out_x) if relayed else ())
    if relayed:
        (held,) = hand_call((relay,), (ctx_one,))
        buffers_b = [list_b, from_two, from_one, relay, y_joined, routes.move(held, stages[1][2], 1)]
    elif chunks[1][0] < chunks[1][1]:
        for stage in stages[1]:
            buffers_b = routes.onward(buffers_b, stage)
    else:
        buffers_b = []
    ctx_two, logs_two = attend_call(segs, qkv_m, qkv_o, *groups[1], (ctx_one, held) if relayed else (ctx_one,))
    ctx = (ctx_one, ctx_two)
    ctx_x = [swap_mp(part) for part in ctx]
    (w_mine,) = collect(buffers_a + buffers_b, ((n_first, piece_total),), ctx_x)
    w_mine, w_other = flat(w_mine), flat(routes.swap_cores(w_mine))
    w_first = [flat(w_first_m), flat(w_first_o)]
    tiles = tok // TILE
    spans_tok = ((0, 2), (2, tiles))
    mlp_args = (x, gy, (*ctx, *ctx_x), w_first, w_out_x, w_mine, w_other, b_up, norm_params)
    *filled, g_h2_a, gb_up_a = mlp_call(spans_tok[0], *mlp_args)
    *filled, g_h2_b, gb_up_b = mlp_call(spans_tok[1], *mlp_args, filled)
    x1, a2, act, g_pre, ffn = filled
    g_h2_ax, g_h2_bx = swap_mp(g_h2_a), swap_mp(g_h2_b)
    g_mlp = mlp_grads_call(act, g_pre, a2, gy)

    def pieces(array):
        return array.reshape(-1, half_len, width)

    def sort_out(number, level, parts, small=None, deps=()):
        stage = routes.back[number][level - 1]
        size = stage[1]
        lists = add_pick_call(
            table,
            [(place[("back", number, level, shift)], 0) for shift in range(size)],
            parts,
            [routes.span_limit(number, level)] * size,
            small=small,
            extra=() if small is None else range(1, size),
            deps=deps,
        )
        moved = [routes.move(lists[shift], stage, shift) for shift in range(1, size)]
        return [lists[0]] + moved, lists[-1]

    gx1, g_ctx_a, g_out_a, mid_a, g_mlp_m, g_mlp_o = mid_call(
        spans_tok[0], x1, gy, g_h2_a, g_h2_ax, ctx, *w_first, norm_params, (), g_mlp
    )
    back = (segs, cos, sin, qkv_m, qkv_o)
    half_way = spans_tok[0][1] * TILE
    early_one = attend_back_call(0, half_way, *back, g_ctx_a, ctx_one, logs_one, *groups[0])
    parts_mlp, listed = sort_out(
        1, 1, [pieces(g_mlp_m), routes.swap_cores(pieces(g_mlp_o))], deps=early_one[:1]
    )
    (ffn,) = hand_call((ffn,), (early_one[0], listed))
    ffn_other = swap_mp(ffn)
    early_two = attend_back_call(
        0, half_way, *back, g_ctx_a, ctx_two, logs_two, *groups[1], deps=(listed, ffn)
    )
    gx1, g_ctx_b, g_out_b, mid_b = mid_call(
        spans_tok[1], x1, gy, g_h2_b, g_h2_bx, ctx, *w_first, norm_params, (gx1,), (), early_two[:1]
    )

    (grads_one,) = attend_back_call(
        half_way, LONGEST, *back, g_ctx_b, ctx_one, logs_one, *groups[0], early_one
    )
    parts_mlp, listed = sort_out(1, 2, parts_mlp, deps=(grads_one,))
    (grads_two,) = attend_back_call(
        half_way, LONGEST, *back, g_ctx_b, ctx_two, logs_two, *groups[1], early_two, (listed,)
    )
    g_in_m, g_in_o, g_h1, small = in_grads_call(
        (grads_one, grads_two), core, a1, x, *w_first,
        (g_out_a, g_out_b), (mid_a, mid_b), (gb_up_a, gb_up_b),
    )
    g_h1_other = swap_mp(g_h1)
    out_roll = out_call(x1, ffn, ffn_other, norm_params)
    parts_in = [pieces(g_in_m), routes.swap_cores(pieces(g_in_o))]
    for level in range(1, len(routes.back[0])):
        parts_in, small = sort_out(0, level, parts_in, small, (out_roll,))
    for level in range(3, len(routes.back[1]) + 1):
        parts_mlp, _ = sort_out(1, level, parts_mlp, deps=(small,))
    parts_in, small = sort_out(0, len(routes.back[0]), parts_in, small)

    block_out = roll_rows(out_roll, tok - start)
    grad_roll = last_call(x, gx1, g_h1, g_h1_other, norm_params)
    grad_tokens = roll_rows(grad_roll, tok - start)

    kept, sent, small = owned_call(table, place, routes, (parts_in, parts_mlp), small)
    small_x = swap_mp(small[0:8])
    arrived = routes.swap_cores(sent)

    def slow_grads():
        def stack(in_part, mlp_part):
            return jnp.concatenate([pieces(in_part), pieces(mlp_part)], axis=0).astype(F32)

        mine, other = stack(g_in_m, g_mlp_m), stack(g_in_o[: g_in_m.shape[0]], g_mlp_o)
        both = jnp.where(first_core, jnp.stack([mine, other], 1), jnp.stack([other, mine], 1))
        total, bit = both, 1
        while bit < dp_size:
            total = total + lax.ppermute(total, "dp", pairs_apart(bit))
            bit *= 2
        total = total[jnp.maximum(table[place["piece"], :slot_cap], 0)]
        return half(total, core), half(total, 1 - core)

    kept, arrived = unless(table[place["over"], 0], (kept, arrived), slow_grads)
    tables_next = adam_call(
        table, place["piece"], core, (n_qkv, n_first, n_first + n_up), kept, arrived,
        (weight_table[0], moment_table[0], square_table[0]),
    )
    small_out = small_call(
        small, small_x,
        (norm_params, norm_moment, norm_square), (bias_params, bias_moment, bias_square),
    )
    return (block_out, grad_tokens, *(part[None] for part in tables_next), *small_out)


def solution(mesh):
    flat = P("dp", None)
    pieces = P("mp", "dp", None, None)
    bias = P("mp", None)
    return jax.shard_map(
        body,
        mesh=mesh,
        in_specs=(flat, flat, flat, P(), pieces, pieces, pieces, P(), P(), P(), bias, bias, bias),
        out_specs=(flat, flat, pieces, pieces, pieces, P(), P(), P(), bias, bias, bias),
        check_vma=False,
    )
```

```python
import functools

import jax
import jax.numpy as jnp
import numpy as np
from jax import lax
from jax.experimental import pallas as pl
from jax.experimental.pallas import tpu as pltpu
from jax.sharding import PartitionSpec as P

HEADS = 20
HEAD_DIM = 32
HALF = HEAD_DIM // 2
FF = 2560
LONGEST = 1024
STEP = 10

EPS_NORM = 1e-05
BETA_ONE = 0.5
BETA_TWO = 0.5
ADAM_EPS = 1e-08
DECAY_RATE = 0.01
NEG_FILL = -1e30
NORM_RATES = (0.5, 0.1, 0.5, 0.1, 0.1, 0.1)
BIAS_RATE = 0.1
SCALE = HEAD_DIM**-0.5
LOG2_E = 1.4426950408889634
SCALE_LOG2 = SCALE * LOG2_E
SAFE_EXP = 100.0

BF = jnp.bfloat16
F32 = jnp.float32
I32 = jnp.int32
TILE = 256
LANES = 128
TICK = (8, 128)
HEADS_EACH = 2
VMEM_LIMIT = 16 << 20
SHRINK = 0.1


def params(*kinds):
    return pltpu.CompilerParams(dimension_semantics=kinds or None, vmem_limit_bytes=VMEM_LIMIT)


def cost(flops, moved):
    return pl.CostEstimate(flops=int(flops / SHRINK), bytes_accessed=int(moved / SHRINK), transcendentals=0)


def dot_nn(a, b):
    return lax.dot_general(a, b, (((1,), (0,)), ((), ())), preferred_element_type=F32)


def dot_nt(a, b):
    return lax.dot_general(a, b, (((1,), (1,)), ((), ())), preferred_element_type=F32)


def dot_tn(a, b):
    return lax.dot_general(a, b, (((0,), (0,)), ((), ())), preferred_element_type=F32)


def split_two(v):
    hi = v.astype(BF).astype(F32)
    return hi, v - hi


def split_three(v):
    hi = v.astype(BF).astype(F32)
    mid = (v - hi).astype(BF).astype(F32)
    return hi, mid, v - hi - mid


def normalized(v):
    centred = v - jnp.mean(v, axis=-1, keepdims=True)
    inv = lax.rsqrt(jnp.mean(centred * centred, axis=-1, keepdims=True) + EPS_NORM)
    return centred * inv, inv


ANYWHERE = pl.BlockSpec(memory_space=pl.ANY)
SMEM = pl.BlockSpec(memory_space=pltpu.SMEM)
HBM = pl.BlockSpec(memory_space=pltpu.HBM)


def whole(shape):
    return pl.BlockSpec(shape, lambda *_: (0,) * len(shape))


def rows(width, begin=0):
    return pl.BlockSpec((TILE, width), lambda t: (begin + t, 0))


def cols(height, begin=0):
    return pl.BlockSpec((height, TILE), lambda t: (0, begin + t))


def both(height, begin=0):
    return pl.BlockSpec((2, height, TILE), lambda t: (0, 0, begin + t))


def last_rows(array, count):
    return pl.BlockSpec((count, array.shape[1]), lambda *_: (array.shape[0] // count - 1, 0))


def shaped(shape, dtype):
    return jax.ShapeDtypeStruct(shape, dtype)


class Clock:
    wanted = False
    tick = None


def ticked(function, *args, **named):
    Clock.wanted = True
    results = function(*args, **named)
    Clock.wanted = False
    return results


def call(kernel, args, in_specs, out_specs, out_shape, name, deps=(), scratch=(), limit=VMEM_LIMIT, late=(), **more):
    count = len(args)
    single = not isinstance(out_shape, (list, tuple))
    out_specs, out_shape = ([out_specs], [out_shape]) if single else (list(out_specs), list(out_shape))
    if any(spec is not ANYWHERE for spec in in_specs):
        more.setdefault("grid", (1,))

    if "input_output_aliases" in more:
        aliases = more["input_output_aliases"]
        more["input_output_aliases"] = {len(deps) + at: to for at, to in aliases.items()}
    real, ticks = len(out_shape), Clock.wanted
    if ticks:
        out_specs, out_shape = out_specs + [whole(TICK)], out_shape + [shaped(TICK, F32)]

    def wrapped(*refs):
        ins, outs = refs[len(deps) : len(deps) + count], refs[len(deps) + count + len(late) :]
        if ticks:
            outs[real][...] = jnp.zeros(TICK, F32)
        kernel(*ins, *outs[:real], *outs[real + ticks :])

    results = pl.pallas_call(
        wrapped,
        in_specs=[ANYWHERE] * len(deps) + list(in_specs) + [ANYWHERE] * len(late),
        out_specs=out_specs,
        out_shape=out_shape,
        scratch_shapes=list(scratch),
        compiler_params=pltpu.CompilerParams(
            dimension_semantics=("arbitrary",) * len(more.get("grid", ())) or None,
            vmem_limit_bytes=limit,
        ),
        name=name,
        **more,
    )(*deps, *args, *late)
    if ticks:
        Clock.tick = results[-1]
        results = results[:-1]
    return results[0] if single else results


def rolled(array, start):
    tok = array.shape[0]
    shift = jnp.where(start == 0, 0, tok - start)
    return pltpu.roll(array.astype(F32), shift, 0)


def roll_kernel(start_ref, array_ref, out_ref):
    out_ref[...] = rolled(array_ref[...], start_ref[0]).astype(BF)


def roll_call(start, array, deps=()):
    return call(
        roll_kernel, (start, array), [SMEM, whole(array.shape)], whole(array.shape),
        shaped(array.shape, BF), "roll", deps,
    )


def norm_kernel(start_ref, x_ref, norm_ref, out_ref, a_ref, turned):
    turned[...] = rolled(x_ref[...], start_ref[0])
    for at in range(0, x_ref.shape[0], LANES):
        here = slice(at, at + LANES)
        value = turned[here, :]
        out_ref[here, :] = value.astype(BF)
        n1, _ = normalized(value)
        a_ref[here, :] = (n1 * norm_ref[0:1] + norm_ref[1:2]).astype(BF)


def norm_call(start, x, norms):
    return call(
        norm_kernel,
        (start, x, norms),
        [SMEM, whole(x.shape), whole(norms.shape)],
        [whole(x.shape)] * 2,
        [shaped(x.shape, BF)] * 2,
        "first_norm",
        scratch=[pltpu.VMEM(x.shape, F32)],
        limit=2 * VMEM_LIMIT,
    )


def qkv_kernel(a_ref, wm_ref, wo_ref, bm_ref, bo_ref, cos_ref, sin_ref, m_ref, o_ref, safe_ref, top):
    a1 = a_ref[...]
    mine = dot_nt(wm_ref[...], a1) + bm_ref[...]
    other = dot_nt(wo_ref[...], a1) + bo_ref[...]
    width = m_ref.shape[1]
    cos, sin = cos_ref[...], sin_ref[...]
    step = pl.program_id(0)

    @pl.when(step == 0)
    def _():
        top[...] = jnp.zeros_like(top)

    for which in range(2):
        for at in range(0, width, HALF):
            here = which * width + at
            p, r = mine[here : here + HALF], other[here : here + HALF]
            length = jnp.sum(p * p + r * r, axis=0, keepdims=True)
            top[which : which + 1, :] = jnp.maximum(top[which : which + 1, :], length)
            m_ref[which, at : at + HALF, :] = (p * cos - r * sin).astype(BF)
            o_ref[which, at : at + HALF, :] = (r * cos + p * sin).astype(BF)
    m_ref[2] = mine[2 * width :].astype(BF)
    o_ref[2] = other[2 * width :].astype(BF)

    @pl.when(step == pl.num_programs(0) - 1)
    def _():
        bound = jnp.max(top[0:1, :]) * jnp.max(top[1:2, :]) * SCALE_LOG2**2
        safe_ref[0] = (bound < SAFE_EXP**2).astype(I32)


def qkv_call(a1, w_mine, w_other, b_mine, b_other, cos, sin, deps=()):
    tok, width = a1.shape
    out = b_mine.shape[0]
    third = pl.BlockSpec((3, out // 3, TILE), lambda t: (0, 0, t))
    return call(
        qkv_kernel,
        (a1, w_mine, w_other, b_mine, b_other, cos, sin),
        [
            rows(width), whole((out, width)), whole((out, width)),
            whole(b_mine.shape), whole(b_mine.shape), cols(HALF), cols(HALF),
        ],
        [third, third, SMEM],
        [shaped((3, out // 3, tok), BF)] * 2 + [shaped((1,), I32)],
        "qkv",
        deps,
        scratch=[pltpu.VMEM((8, TILE), F32)],
        grid=(tok // TILE,),
        cost_estimate=cost(4 * tok * width * out, 8e6),
    )


def normal_tables(u):
    return 0.5 * (1.0 + lax.erf(u * 0.7071067811865476)), jnp.exp(-0.5 * u * u)


def mlp_kernel(
    groups, chained, x_ref, gy_ref, *refs,
):
    ctx_refs, refs = refs[: 2 * groups], refs[2 * groups :]
    wp_mine, wp_other, wx_mine, wx_other, w_mine, w_other, bup_ref, norm_ref = refs[:8]
    refs = refs[8 + chained :]
    x1_ref, a2_ref, act_ref, gpre_ref, ffn_ref, gh_ref, gbup_ref, out_w, up_w, down_w = refs

    @pl.when(pl.program_id(0) == 0)
    def _():
        quarter, half = wx_mine.shape[0], up_w.shape[0] // 2
        for at, ref in enumerate((wp_mine, wp_other, wx_mine, wx_other)):
            out_w[at * quarter : (at + 1) * quarter, :] = ref[...]
        for at, ref in enumerate((w_mine, w_other)):
            up_w[at * half : (at + 1) * half, :] = ref[:half, :]
            down_w[at * half : (at + 1) * half, :] = ref[half:, :]

    gy = gy_ref[...]
    own, far = ctx_refs[:groups], ctx_refs[groups:]
    ctx = jnp.concatenate([ref[j] for some in (own, far) for j in range(2) for ref in some], axis=0)
    x1 = x_ref[...].astype(F32) + dot_tn(ctx, out_w[...]) + norm_ref[4:5]
    x1_ref[...] = x1
    n2, _ = normalized(x1)
    a2 = (n2 * norm_ref[2:3] + norm_ref[3:4]).astype(BF)
    a2_ref[...] = a2
    pre = dot_nt(a2, up_w[...]) + bup_ref[...]
    cdf, bell = normal_tables(pre)
    act = (pre * cdf).astype(BF)
    act_ref[...] = act
    slope = cdf + pre * (bell * 0.3989422804014327)
    gpre = (slope * dot_nt(gy, down_w[...])).astype(BF)
    gpre_ref[...] = gpre
    ffn_ref[...] = dot_nn(act, down_w[...]).astype(BF)
    gh_ref[...] = dot_nn(gpre, up_w[...]).astype(BF)
    part = jnp.sum(gpre.astype(F32), axis=0, keepdims=True)

    @pl.when(pl.program_id(0) == 0)
    def _():
        gbup_ref[...] = part

    @pl.when(pl.program_id(0) > 0)
    def _():
        gbup_ref[...] += part


def mlp_call(span, x, gy, ctx, wp, wx, w_mine, w_other, b_up, norms, before=(), deps=()):
    tok, width = x.shape
    hidden = b_up.shape[1]
    quarter = wx[0].shape[0]
    begin, count = span[0], span[1] - span[0]
    args = (x, gy, *ctx, *wp, *wx, w_mine, w_other, b_up, norms, *before)
    return call(
        functools.partial(mlp_kernel, len(ctx) // 2, len(before)),
        args,
        [rows(width, begin)] * 2
        + [both(part.shape[1]) for part in ctx]
        + [last_rows(wp[0], quarter)] * 2
        + [whole((quarter, width))] * 2
        + [whole(w_mine.shape)] * 2
        + [whole(b_up.shape), whole(norms.shape)]
        + [ANYWHERE] * len(before),
        [
            rows(width, begin), rows(width, begin), rows(hidden, begin), rows(hidden, begin),
            rows(width, begin), rows(width), whole((1, hidden)),
        ],
        [
            shaped((tok, width), F32), shaped((tok, width), BF), shaped((tok, hidden), BF),
            shaped((tok, hidden), BF), shaped((tok, width), BF), shaped((count * TILE, width), BF),
            shaped((1, hidden), F32),
        ],
        "mlp",
        deps,
        scratch=[
            pltpu.VMEM((4 * quarter, width), BF), pltpu.VMEM((hidden, width), BF),
            pltpu.VMEM((hidden, width), BF),
        ],
        grid=(count,),
        cost_estimate=cost(2 * count * TILE * width * (hidden * 4 + 4 * quarter) * 1.6, 2e7),
        input_output_aliases={len(args) - len(before) + j: j for j in range(len(before))},
    )


def mlp_grads_kernel(act_ref, gpre_ref, a2_ref, gy_ref, mine_ref, other_ref, down_sum, up_sum):
    step = pl.program_id(0)
    down = dot_tn(act_ref[...], gy_ref[...])
    up = dot_tn(gpre_ref[...], a2_ref[...])

    @pl.when(step == 0)
    def _():
        down_sum[...] = down
        up_sum[...] = up

    @pl.when(step > 0)
    def _():
        down_sum[...] += down
        up_sum[...] += up

    @pl.when(step == pl.num_programs(0) - 1)
    def _():
        half = down_sum.shape[0] // 2
        for which, out_ref in enumerate((mine_ref, other_ref)):
            here = pl.ds(which * half, half)
            out_ref[:half, :] = up_sum[here, :].astype(BF)
            out_ref[half:, :] = down_sum[here, :].astype(BF)


def mlp_grads_call(act, gpre, a2, gy, deps=()):
    tok, hidden = act.shape
    width = a2.shape[1]
    return call(
        mlp_grads_kernel,
        (act, gpre, a2, gy),
        [rows(hidden), rows(hidden), rows(width), rows(width)],
        [whole((hidden, width))] * 2,
        [shaped((hidden, width), BF)] * 2,
        "mlp_grads",
        deps,
        scratch=[pltpu.VMEM((hidden, width), F32)] * 2,
        grid=(tok // TILE,),
        cost_estimate=cost(4 * tok * width * hidden * 1.3, 1.4e7),
    )


def mid_kernel(
    groups, chained, handed, x1_ref, gy_ref, gh_a, gh_b, *refs,
):
    ctx_refs, refs = refs[:groups], refs[groups:]
    wm_ref, wo_ref, norm_ref = refs[:3]
    refs = refs[3 + chained + handed :]
    gx_ref, g_out, gout_ref, sum_ref = refs[:4]
    cm, co = (jnp.concatenate([ref[j] for ref in ctx_refs], axis=0) for j in range(2))
    step = pl.program_id(0)
    gy = gy_ref[...].astype(F32)
    gh = gh_a[...].astype(F32) + gh_b[...].astype(F32)
    n2, inv = normalized(x1_ref[...])
    e = gh * norm_ref[2:3]
    gx = gy + inv * (
        e - jnp.mean(e, axis=-1, keepdims=True) - n2 * jnp.mean(e * n2, axis=-1, keepdims=True)
    )
    gx_ref[...] = gx
    gm = gx.astype(BF)
    g_out[0] = dot_nt(wm_ref[...], gm).astype(BF)
    g_out[1] = dot_nt(wo_ref[...], gm).astype(BF)

    @pl.when(step == 0)
    def _():
        gout_ref[...] = jnp.zeros_like(gout_ref)
        sum_ref[...] = jnp.zeros_like(sum_ref)

    gout_ref[0] += dot_nn(cm, gm)
    gout_ref[1] += dot_nn(co, gm)
    for at, value in enumerate((gh * n2, gh, gx, gy)):
        sum_ref[at : at + 1, :] += jnp.sum(value, axis=0, keepdims=True)


def mid_call(span, x1, gy, gh, gh_other, ctx, w_m, w_o, norms, before=(), hand=(), deps=()):
    tok, width = x1.shape
    head = sum(part.shape[1] for part in ctx)
    begin, count = span[0], span[1] - span[0]
    args = (x1, gy, gh, gh_other, *ctx, w_m, w_o, norms, *before, *hand)
    fixed = len(args) - len(before) - len(hand)
    aliases = {fixed + j: j for j in range(len(before))}
    aliases.update({fixed + len(before) + j: 4 + j for j in range(len(hand))})
    return call(
        functools.partial(mid_kernel, len(ctx), len(before), len(hand)),
        args,
        [rows(width, begin)] * 2
        + [rows(width)] * 2
        + [both(part.shape[1]) for part in ctx]
        + [last_rows(w_m, head)] * 2
        + [whole(norms.shape)]
        + [ANYWHERE] * (len(before) + len(hand)),
        [rows(width, begin), both(head), whole((2, head, width)), whole((8, width))]
        + [ANYWHERE] * len(hand),
        [
            shaped((tok, width), F32), shaped((2, head, count * TILE), BF),
            shaped((2, head, width), F32), shaped((8, width), F32),
        ]
        + [shaped(part.shape, part.dtype) for part in hand],
        "mid_back",
        deps,
        grid=(count,),
        cost_estimate=cost(8 * count * TILE * width * head * 2, 1e7),
        input_output_aliases=aliases,
    )


def split_small(value):
    hi = value.astype(BF)
    lo = (value - hi.astype(F32)).astype(BF)
    return hi, lo, hi.astype(F32) + lo.astype(F32)


def in_grads_kernel(groups, gouts, *refs):
    g_refs, refs = refs[:groups], refs[groups:]
    out_refs, mid_refs, up_refs, refs = (
        refs[:gouts], refs[gouts : 2 * gouts], refs[2 * gouts : 3 * gouts], refs[3 * gouts :]
    )
    core_ref, a1_ref, x_ref, wm_ref, wo_ref, mine_ref, other_ref, gh_ref, sum_ref = refs[:9]
    m_sum, o_sum, gbm_ref, gbo_ref = refs[9:]
    step = pl.program_id(0)
    count = wm_ref.shape[0]
    a1 = a1_ref[...]
    gm, go = (
        jnp.concatenate([ref[half, j] for j in range(3) for ref in g_refs], axis=0)
        for half in range(2)
    )

    @pl.when(step == 0)
    def _():
        m_sum[...] = jnp.zeros_like(m_sum)
        o_sum[...] = jnp.zeros_like(o_sum)
        gbm_ref[...] = jnp.zeros_like(gbm_ref)
        gbo_ref[...] = jnp.zeros_like(gbo_ref)
        sum_ref[...] = jnp.zeros_like(sum_ref)

    m_sum[...] += dot_nn(gm, a1)
    o_sum[...] += dot_nn(go, a1)
    gbm_ref[...] += jnp.sum(gm.astype(F32), axis=1, keepdims=True)
    gbo_ref[...] += jnp.sum(go.astype(F32), axis=1, keepdims=True)
    gh = dot_tn(gm, wm_ref[...]) + dot_tn(go, wo_ref[...])
    gh_ref[...] = gh.astype(BF)
    n1, _ = normalized(x_ref[...].astype(F32))
    sum_ref[0:1, :] += jnp.sum(gh * n1, axis=0, keepdims=True)
    sum_ref[1:2, :] += jnp.sum(gh, axis=0, keepdims=True)

    @pl.when(step == pl.num_programs(0) - 1)
    def _():
        width = gh.shape[1]
        up = sum((ref[...] for ref in up_refs[1:]), up_refs[0][...])
        sum_ref[2:6, :] = sum((ref[0:4, :] for ref in mid_refs[1:]), mid_refs[0][0:4, :])

        def column(row):
            return jnp.transpose(jnp.broadcast_to(row, (LANES, row.shape[1])))[:, 0:1]

        swapped = core_ref[0] == 1
        mixed = []
        for mine, other in ((gbm_ref[...], gbo_ref[...]), (column(up[:, :width]), column(up[:, width:]))):
            lower, upper = jnp.where(swapped, other, mine), jnp.where(swapped, mine, other)
            for at in range(0, mine.shape[0], HALF):
                mixed += [lower[at : at + HALF], upper[at : at + HALF]]
        natural = jnp.concatenate(mixed, axis=0)
        natural = jnp.transpose(jnp.broadcast_to(natural, (natural.shape[0], LANES)))[0:1]
        for at in range(0, natural.shape[1], width):
            part = natural[:, at : at + width]
            sum_ref[6 + at // width : 7 + at // width, : part.shape[1]] = part
        hi, lo, kept = split_small(sum_ref[...])
        sum_ref[...] = kept
        more = count + out_refs[0].shape[1]
        for ref, total, half in ((mine_ref, m_sum, 0), (other_ref, o_sum, 1)):
            ref[:count, :] = total[...].astype(BF)
            ref[count:more, :] = sum((out[half] for out in out_refs[1:]), out_refs[0][half]).astype(BF)
        other_ref[more : more + 16, :] = hi
        other_ref[more + 16 :, :] = lo


def in_grads_call(grads, core, a1, x, w_m, w_o, gouts, mid_sums, gb_ups, deps=()):
    tok, width = a1.shape
    more = gouts[0].shape[1]
    count = w_m.shape[0] - more
    parts = [
        pl.BlockSpec(part.shape[:3] + (TILE,), lambda t: (0, 0, 0, t)) for part in grads
    ]
    return call(
        functools.partial(in_grads_kernel, len(grads), len(gouts)),
        (*grads, *gouts, *mid_sums, *gb_ups, core[None], a1, x, w_m, w_o),
        parts
        + [whole(part.shape) for part in (*gouts, *mid_sums, *gb_ups)]
        + [SMEM, rows(width), rows(width)]
        + [whole((count, width))] * 2,
        [whole((count + more, width)), whole((count + more + 32, width)), rows(width), whole((16, width))],
        [
            shaped((count + more, width), BF), shaped((count + more + 32, width), BF),
            shaped((tok, width), BF), shaped((16, width), F32),
        ],
        "in_grads",
        deps,
        scratch=[pltpu.VMEM((count, width), F32)] * 2 + [pltpu.VMEM((count, 1), F32)] * 2,
        grid=(tok // TILE,),
        cost_estimate=cost(8 * tok * width * count * 1.3, 1e7),
    )


def out_kernel(x1_ref, a_ref, b_ref, norm_ref, out_ref):
    out_ref[...] = x1_ref[...] + (a_ref[...].astype(F32) + b_ref[...].astype(F32)) + norm_ref[5:6]


def out_call(x1, ffn_a, ffn_b, norms, deps=()):
    tok, width = x1.shape
    return call(
        out_kernel,
        (x1, ffn_a, ffn_b, norms),
        [rows(width)] * 3 + [whole(norms.shape)],
        rows(width),
        shaped((tok, width), F32),
        "layer_out",
        deps,
        grid=(tok // TILE,),
        cost_estimate=cost(4e9, 1e7),
    )


def nothing_kernel(*refs):
    pass


def hand_call(arrays, deps):
    return call(
        nothing_kernel, arrays, [ANYWHERE] * len(arrays), [ANYWHERE] * len(arrays),
        [shaped(array.shape, array.dtype) for array in arrays], "hand", deps,
        input_output_aliases={at: at for at in range(len(arrays))},
    )


def keep_kernel(*refs):
    half = len(refs) // 2
    for source, target in zip(refs[:half], refs[half:]):
        target[...] = source[...]


def keep_call(arrays, deps=()):
    specs = [whole(array.shape) for array in arrays]
    return call(
        keep_kernel, arrays, specs, specs, [shaped(a.shape, a.dtype) for a in arrays], "keep", deps,
        cost_estimate=cost(4e9, 1e7),
    )


def last_kernel(x_ref, gx_ref, gh_a, gh_b, norm_ref, out_ref):
    n1, inv = normalized(x_ref[...].astype(F32))
    e = (gh_a[...].astype(F32) + gh_b[...].astype(F32)) * norm_ref[0:1]
    out_ref[...] = gx_ref[...] + inv * (
        e - jnp.mean(e, axis=-1, keepdims=True) - n1 * jnp.mean(e * n1, axis=-1, keepdims=True)
    )


def last_call(x, gx, gh_a, gh_b, norms):
    tok, width = x.shape
    return call(
        last_kernel,
        (x, gx, gh_a, gh_b, norms),
        [rows(width)] * 4 + [whole(norms.shape)],
        rows(width),
        shaped((tok, width), F32),
        "last_back",
        grid=(tok // TILE,),
        cost_estimate=cost(1e6, 1.2e7),
    )


def layout_kernel(core_ref, len_ref, freq_ref, bias_ref, cos_ref, sin_ref, row_ref, col_ref, bm_ref, bo_ref, bup_ref, start_ref):
    tok = cos_ref.shape[1]
    docs = len_ref.shape[1]
    begin, best, start = 0, len_ref[0, 0], 0
    begins, ends = [], []
    for doc in range(docs):
        size = len_ref[0, doc]
        if doc:
            start = jnp.where(size > best, begin, start)
            best = jnp.maximum(size, best)
        begins.append(begin)
        begin = begin + size
        ends.append(begin)
    start_ref[0] = start + jnp.zeros((), I32)

    def origin(places):
        at = places + start
        return jnp.where(at >= tok, at - tok, at)

    def document(at):
        return sum(((at >= end).astype(I32) for end in ends), jnp.zeros(at.shape, I32))

    row = origin(lax.broadcasted_iota(I32, (1, tok), 1))
    first = jnp.zeros((1, tok), I32)
    for begin in begins[1:]:
        first = jnp.where(row >= begin, begin, first)
    angles = freq_ref[...] * (row - first).astype(F32)
    cos_ref[...] = jnp.cos(angles)
    sine = jnp.sin(angles)
    sin_ref[...] = jnp.where(core_ref[0] == 0, sine, -sine)
    column = jnp.transpose(jnp.broadcast_to(bias_ref[...], (LANES, bias_ref.shape[1])))[:, 0:1]
    lower, upper = (
        jnp.concatenate(
            [column[at : at + HALF] for at in range(begin, column.shape[0], HEAD_DIM)], axis=0
        )
        for begin in (0, HALF)
    )
    swapped = core_ref[0] == 1
    mine, other = jnp.where(swapped, upper, lower), jnp.where(swapped, lower, upper)
    count = bm_ref.shape[0]
    bm_ref[...], bo_ref[...] = mine[:count], other[:count]
    for which, half in enumerate((mine[count:], other[count:])):
        length = half.shape[0]
        turned = jnp.transpose(jnp.broadcast_to(half, (length, LANES)))[0:1]
        bup_ref[:, which * length : (which + 1) * length] = turned
    rest = row_ref.shape[1]
    row_ref[...] = document(row[:, tok - rest :])
    col_ref[...] = document(origin(lax.broadcasted_iota(I32, (rest, 1), 0) + (tok - rest)))


def layout_call(core, lengths, biases, tok, n_qkv, deps=()):
    rest, n_up = tok - LONGEST, biases.shape[1] - 2 * n_qkv
    freq = np.float32(10000.0) ** -(np.arange(0, HEAD_DIM, 2).astype(np.float32) / HEAD_DIM)
    return call(
        layout_kernel,
        (core[None], lengths, jnp.asarray(freq[:, None], F32), biases),
        [SMEM, SMEM, whole((HALF, 1)), whole(biases.shape)],
        [whole((HALF, tok))] * 2
        + [whole((1, rest)), whole((rest, 1)), whole((n_qkv, 1)), whole((n_qkv, 1)), whole((1, n_up)), SMEM],
        [shaped((HALF, tok), F32)] * 2
        + [
            shaped((1, rest), I32), shaped((rest, 1), I32), shaped((n_qkv, 1), F32),
            shaped((n_qkv, 1), F32), shaped((1, n_up), F32), shaped((1,), I32),
        ],
        "layout",
        deps,
    )


def halves_kernel(core_ref, table_ref, mine_ref, other_ref):
    first = core_ref[0] == 0
    count = mine_ref.shape[1]
    upper, lower = table_ref[:, :count, :], table_ref[:, count:, :]
    mine_ref[...] = jnp.where(first, upper, lower).astype(BF)
    other_ref[...] = jnp.where(first, lower, upper).astype(BF)


def halves_call(core, table):
    cap, count, width = table.shape
    half = (cap, count // 2, width)
    return call(
        halves_kernel,
        (core[None], table),
        [SMEM, whole(table.shape)],
        [whole(half)] * 2,
        [shaped(half, BF)] * 2,
        "halves",
    )


def by_heads(kernel, which):
    def each(*refs):
        for head in range(HEADS_EACH):
            views = []
            for ref, dim in zip(refs, which):
                if dim is not None:
                    size = ref.shape[dim] // HEADS_EACH
                    ref = ref.at[(slice(None),) * dim + (pl.ds(head * size, size),)]
                views.append(ref)
            kernel(*views)

    return each


def attend_kernel(q_begin, q_end, last, safe_ref, seg_row, seg_col, m_ref, o_ref, ctx_ref, log_ref):
    tok = m_ref.shape[2]
    rest = tok - LONGEST
    span = slice(q_begin, tok if last else q_end)
    keys = tok if last else LONGEST
    q_t, k_t, v_t = (jnp.concatenate([m_ref[j], o_ref[j]], axis=0) for j in range(3))
    k_t, v_t = k_t[:, :keys], v_t[:, :keys]
    qs = q_t[:, span].astype(F32) * SCALE_LOG2
    hi, lo = split_two(qs)
    qx = jnp.transpose(jnp.concatenate([hi, lo], axis=0)).astype(BF)
    kx = jnp.concatenate([k_t, k_t], axis=0)
    v_f = v_t.astype(F32)
    vx = jnp.transpose(jnp.concatenate([v_f, jnp.ones((8, keys), F32)], axis=0)).astype(BF)
    safe = safe_ref[0] > 0

    def finish(sums, shift, at, count):
        turned = jnp.transpose(sums)
        total = turned[HEAD_DIM : HEAD_DIM + 1]
        ctx = (turned[0:HEAD_DIM] / total).astype(BF)
        ctx_ref[0, :, at : at + count] = ctx[:HALF]
        ctx_ref[1, :, at : at + count] = ctx[HALF:]
        log_total = jnp.log2(total)
        if shift is not None:
            log_total = log_total + jnp.transpose(jnp.broadcast_to(shift, (count, LANES)))[0:1]
        log_ref[0, :, at : at + count] = log_total

    def run(exact):
        for at in range(0, q_end - q_begin, TILE):
            scores = dot_nn(qx[at : at + TILE], kx[:, :LONGEST])
            shift = None
            if exact:
                shift = jnp.max(scores, axis=1, keepdims=True)
                scores = scores - shift
            finish(dot_nn(jnp.exp2(scores).astype(BF), vx[:LONGEST]), shift, at, TILE)
        if last and rest:
            at = LONGEST - q_begin
            same = seg_col[...] == seg_row[...]
            scores = jnp.where(same, dot_nn(qx[at:], kx[:, LONGEST:]), NEG_FILL)
            shift = None
            if exact:
                shift = jnp.max(scores, axis=1, keepdims=True)
                scores = scores - shift
            finish(dot_nn(jnp.exp2(scores).astype(BF), vx[LONGEST:]), shift, at, rest)

    @pl.when(safe)
    def _():
        run(False)

    @pl.when(jnp.logical_not(safe))
    def _():
        run(True)


def attend_call(q_begin, q_end, safe, segs, qkv_m, qkv_o, deps=()):
    tok = qkv_m.shape[2]
    rest = segs[0].shape[1]
    last = q_end == LONGEST
    count, length = qkv_m.shape[1] // HALF, (tok if last else q_end) - q_begin
    part = pl.BlockSpec((3, HEADS_EACH * HALF, tok), lambda h: (0, h, 0))
    return call(
        by_heads(
            functools.partial(attend_kernel, q_begin, q_end, last), (None, None, None, 1, 1, 1, 0)
        ),
        (safe, *segs, qkv_m, qkv_o),
        [SMEM, whole((1, rest)), whole((rest, 1)), part, part],
        [
            pl.BlockSpec((2, HEADS_EACH * HALF, length), lambda h: (0, h, 0)),
            pl.BlockSpec((HEADS_EACH, 1, length), lambda h: (h, 0, 0)),
        ],
        [shaped((2, count * HALF, length), BF), shaped((count, 1, length), F32)],
        "attend",
        deps,
        grid=(count // HEADS_EACH,),
        cost_estimate=cost(count * 1.2e9, 3e6),
    )


def attend_back_kernel(
    q_begin, q_end, last, seg_row, seg_col, cos_ref, sin_ref, m_ref, o_ref, g_ref, ctx_ref, log_ref,
    *refs,
):
    tok = m_ref.shape[2]
    rest = tok - LONGEST
    end = tok if last else q_end
    span = slice(q_begin, end)
    q_t, k_t, v_t = (jnp.concatenate([m_ref[j], o_ref[j]], axis=0) for j in range(3))
    q_f = q_t[:, span].astype(F32)
    ctx = jnp.concatenate([ctx_ref[0], ctx_ref[1]], axis=0).astype(F32)
    g_f = jnp.concatenate([g_ref[0], g_ref[1]], axis=0).astype(F32)
    hi, lo = split_two(q_f * SCALE_LOG2)
    weighted = jnp.sum(g_f * ctx, axis=0, keepdims=True)
    pad = jnp.zeros((13, end - q_begin), F32)
    qx = jnp.concatenate([hi, lo, *split_three(log_ref[0]), pad], axis=0).astype(BF)
    keys = tok if last else LONGEST
    k_f, v_f = k_t[:, :keys].astype(F32), v_t[:, :keys].astype(F32)
    minus = jnp.concatenate([jnp.full((3, keys), -1.0, F32), jnp.zeros((13, keys), F32)], axis=0)
    kx = jnp.transpose(jnp.concatenate([k_f, k_f, minus], axis=0)).astype(BF)
    gx = jnp.concatenate([g_f, *split_three(weighted), pad], axis=0).astype(BF)
    vx = jnp.transpose(jnp.concatenate([v_f, minus], axis=0)).astype(BF)
    qn = jnp.transpose(q_f).astype(BF)
    gn = jnp.transpose(g_f).astype(BF)

    if last:
        early_q, early_kv, out_ref = refs
    else:
        out_q, out_kv = refs

    def turned_back(grad, at, count):
        cos, sin = cos_ref[:, at : at + count], sin_ref[:, at : at + count]
        mine, other = grad[0:HALF] * SCALE, grad[HALF:] * SCALE
        return (mine * cos + other * sin).astype(BF), (other * cos - mine * sin).astype(BF)

    def block(k_at, k_count, q_at, q_count, mask, early):
        scores = dot_nn(kx[k_at : k_at + k_count], qx[:, q_at : q_at + q_count])
        if mask is not None:
            scores = jnp.where(mask, scores, NEG_FILL)
        prob = jnp.exp2(scores)
        grad_prob = dot_nn(vx[k_at : k_at + k_count], gx[:, q_at : q_at + q_count])
        grad_score = (prob * grad_prob).astype(BF)
        grad_v = jnp.transpose(dot_nn(prob.astype(BF), gn[q_at : q_at + q_count]))
        grad_k = jnp.transpose(dot_nn(grad_score, qn[q_at : q_at + q_count]))
        here = slice(k_at, k_at + k_count)
        if not last:
            out_kv[0, 0, :, here] = grad_k
            out_kv[1, 0, :, here] = grad_v
        else:
            if early:
                grad_k = grad_k + early_kv[0, 0, :, here]
                grad_v = grad_v + early_kv[1, 0, :, here]
            out_ref[0, 1, :, here], out_ref[1, 1, :, here] = turned_back(grad_k, k_at, k_count)
            out_ref[0, 2, :, here] = grad_v[:HALF].astype(BF)
            out_ref[1, 2, :, here] = grad_v[HALF:].astype(BF)
        return dot_nn(k_t[:, k_at : k_at + k_count], grad_score)

    grad_q = None
    for at in range(0, LONGEST, TILE):
        piece = block(at, TILE, 0, q_end - q_begin, None, True)
        grad_q = piece if grad_q is None else grad_q + piece
    mine, other = turned_back(grad_q, q_begin, q_end - q_begin)
    if not last:
        out_q[0], out_q[1] = mine, other
        return
    out_ref[0, 0, :, :q_begin] = early_q[0]
    out_ref[1, 0, :, :q_begin] = early_q[1]
    out_ref[0, 0, :, q_begin:q_end] = mine
    out_ref[1, 0, :, q_begin:q_end] = other
    if rest:
        same = seg_col[...] == seg_row[...]
        piece = block(LONGEST, rest, LONGEST - q_begin, rest, same, False)
        out_ref[0, 0, :, LONGEST:], out_ref[1, 0, :, LONGEST:] = turned_back(piece, LONGEST, rest)


def attend_back_call(
    q_begin, q_end, segs, cos, sin, qkv_m, qkv_o, g_ctx, ctx, logs, first, count, early=(), deps=()
):
    tok = qkv_m.shape[2]
    last = len(early) > 0
    rest = segs[0].shape[1]
    each = HEADS_EACH
    first = first // each
    part = pl.BlockSpec((3, each * HALF, tok), lambda h: (0, first + h, 0))
    table = whole((HALF, tok))

    def by_head(length, offset=0):
        return pl.BlockSpec((2, each * HALF, length), lambda h: (0, offset + h, 0))

    pair = pl.BlockSpec((2, each, HEAD_DIM, LONGEST), lambda h: (0, h, 0, 0))
    if last:
        out_specs = [pl.BlockSpec((2, 3, each * HALF, tok), lambda h: (0, 0, h, 0))]
        out_shape = [shaped((2, 3, count * HALF, tok), BF)]
    else:
        out_specs = [by_head(q_end), pair]
        out_shape = [
            shaped((2, count * HALF, q_end), BF), shaped((2, count, HEAD_DIM, LONGEST), F32)
        ]
    return call(
        by_heads(
            functools.partial(attend_back_kernel, q_begin, q_end, last),
            (None,) * 4 + (1, 1, 1, 1, 0, 1, 1) + ((2,) if last else ()),
        ),
        (*segs, cos, sin, qkv_m, qkv_o, g_ctx, ctx, logs, *early),
        [
            whole((1, rest)), whole((rest, 1)), table, table, part, part,
            by_head(g_ctx.shape[2], first), by_head(ctx.shape[2], first),
            pl.BlockSpec((each, 1, logs.shape[2]), lambda h: (first + h, 0, 0)),
        ]
        + ([by_head(q_begin), pair] if last else []),
        out_specs,
        out_shape,
        "attend_back",
        deps,
        grid=(count // each,),
        cost_estimate=cost(count * 2.1e9, 6e6),
    )


class Routes:
    def __init__(self, dp_size, slot_cap, pieces, ready, spans):
        self.dp = dp_size
        self.cap = slot_cap
        self.chips = dp_size // 2
        self.pieces = pieces
        self.ready = ready
        self.spans = spans
        if self.chips == 8:
            self.stages = ((2, 4), (1, 2))
        elif self.chips == 64:
            self.stages = ((1, 8), (8, 2), (16, 4))
        else:
            self.stages = ((1, self.chips),)
        self.depth = len(self.stages)
        straight = self.stages[::-1]
        paired = ((1, 2), (4, 2), (2, 2)) if self.chips == 8 else straight
        self.back = (straight, paired)
        self.out = (self.stages, ((4, 2), (2, 2), (1, 2)) if self.chips == 8 else self.stages)
        self.fill = [self.limit(last, self.chips) for last in ready]
        self.begins = [0] + self.fill[:-1]
        early, late = self.fill[0], self.fill[1] - self.fill[0]
        if self.chips == 8:
            self.bases = (
                [at * early for at in range(4)]
                + [4 * early]
                + [4 * early + self.fill[1] + at * early for at in range(3)],
                [7 * early + self.fill[1] + at * late for at in range(4)]
                + [5 * early]
                + [7 * early + self.fill[1] + at * late for at in range(4, 7)],
            )
        else:
            self.bases = tuple(
                [begin * self.chips + at * (end - begin) for at in range(self.chips)]
                for begin, end in zip(self.begins, self.fill)
            )

    def limit(self, count, groups):
        worst = min(count, self.dp // groups * self.cap)
        if self.chips != 8:
            return worst
        typical = {
            2: count * 11 // 20 + 8, 4: count * 3 // 10 + 10, 8: count // 5 + 5
        }[groups]
        return worst if count == self.pieces else min(worst, typical)

    def span_limit(self, number, level):
        groups = 1
        for _, size in self.back[number][:level]:
            groups *= size
        return self.limit(self.spans[number][1] - self.spans[number][0], groups)

    def move(self, array, stage, shift):
        stride, size = stage
        pairs = []
        for device in range(self.dp):
            chip, core = device // 2, device % 2
            at = (chip // stride) % size
            pairs.append((device, 2 * (chip + ((at + shift) % size - at) * stride) + core))
        return lax.ppermute(array, "dp", pairs)

    def swap_cores(self, array):
        return lax.ppermute(array, "dp", [(d, d ^ 1) for d in range(self.dp)])

    def around(self, array, stage):
        return [array] + [self.move(array, stage, shift) for shift in range(1, stage[1])]

    def onward(self, buffers, stage):
        return buffers + [
            self.move(buffer, stage, shift) for shift in range(1, stage[1]) for buffer in buffers
        ]

    def tables(self, owners, me):
        place = {}

        def kernel(me_ref, own_ref, out_ref, row_ref):
            here = me_ref[0]
            my_chip, my_core = here // 2, here % 2
            row_ref[...] = jnp.full((1, LANES), -2, I32)
            row_ref[:, : self.pieces] = own_ref[...]
            row = row_ref[...]
            col = jnp.transpose(jnp.broadcast_to(row, (LANES, LANES)))[:, 0:1]
            id_row = lax.broadcasted_iota(I32, (1, LANES), 1)
            id_col = lax.broadcasted_iota(I32, (LANES, 1), 0)
            lane = lax.broadcasted_iota(I32, (LANES, LANES), 1)
            sub = lax.broadcasted_iota(I32, (LANES, LANES), 0)

            def rank_col(key_row, key_col):
                hit = (key_row == key_col) & (lane < sub)
                return jnp.sum(hit.astype(F32), axis=1, keepdims=True).astype(I32)

            def rank_row(key_row, key_col):
                hit = (key_row == key_col) & (sub < lane)
                return jnp.sum(hit.astype(F32), axis=0, keepdims=True).astype(I32)

            def gather(valid_col, entry_col, value_col):
                hit = valid_col & (entry_col == lane)
                return jnp.sum(
                    jnp.where(hit, value_col.astype(F32), 0.0), axis=0, keepdims=True
                ).astype(I32)

            def put(name, value):
                at = place.setdefault(name, len(place))
                out_ref[at : at + 1, :] = value

            def coord(chip, stage):
                return (chip // stage[0]) % stage[1]

            def group(chip, stages):
                key = 0
                for stage in stages:
                    key = key * stage[1] + coord(chip, stage)
                return key

            def fullest(inside, rank):
                return jnp.max(jnp.where(inside, rank, -1), axis=0, keepdims=True) + 1

            slot_col = rank_col(row, col)
            put("piece", gather(col == here, slot_col, id_col + 1) - 1)
            sibling = my_chip * 2 + 1 - my_core
            put("sibling", gather(col == sibling, slot_col, id_col + 1) - 1)
            over = jnp.zeros((1, 1), I32)
            real = id_col < self.pieces
            chip_col, chip_row = col // 2, row // 2
            rank_c, rank_r = rank_col(chip_row, chip_col), rank_row(chip_row, chip_col)
            from_core = jnp.where(col % 2 == my_core, 0, self.cap)
            put("send", gather(real & (chip_col == my_chip), rank_c, from_core + slot_col))
            for last, fill in zip(self.ready, self.fill):
                over = jnp.maximum(over, fullest(id_col < last, rank_c) - fill)
            put("late", jnp.broadcast_to(over, (1, LANES)))
            over = jnp.zeros((1, 1), I32)
            take = jnp.zeros((1, LANES), I32)
            for begin, bases, stages in zip(self.begins, self.bases, self.out):
                way, scale = jnp.zeros((1, LANES), I32), 1
                for stage in stages:
                    away = (coord(my_chip, stage) - coord(chip_row, stage) + stage[1]) % stage[1]
                    way = way + away * scale
                    scale = scale * stage[1]
                spot = rank_r - begin
                for at, base in enumerate(bases):
                    spot = spot + jnp.where(way == at, base, 0)
                take = jnp.where(rank_r >= begin, spot, take)
            put("take", take)
            for number, span in enumerate(self.spans):
                in_col = (id_col >= span[0]) & (id_col < span[1])
                in_row = (id_row >= span[0]) & (id_row < span[1])
                stages = self.back[number]
                ranks = {}
                for level in range(1, len(stages) + 1):
                    key_col = jnp.where(in_col, group(chip_col, stages[:level]), -1)
                    key_row = jnp.where(in_row, group(chip_row, stages[:level]), -1)
                    ranks[level] = rank_col(key_row, key_col)
                    over = jnp.maximum(
                        over, fullest(in_col, ranks[level]) - self.span_limit(number, level)
                    )
                value = id_col - span[0]
                for level, stage in enumerate(stages, 1):
                    size = stage[1]
                    inside = in_col & (
                        group(chip_col, stages[: level - 1]) == group(my_chip, stages[: level - 1])
                    )
                    for shift in range(size):
                        goal = (coord(my_chip, stage) + shift) % size
                        put(
                            ("back", number, level, shift),
                            gather(inside & (coord(chip_col, stage) == goal), ranks[level], value),
                        )
                    value = ranks[level]
                for which in range(2):
                    goal = my_chip * 2 + (my_core + which) % 2
                    put(
                        ("slot", number, which),
                        gather(in_col & (col == goal), slot_col, ranks[len(stages)]),
                    )
            put("over", jnp.broadcast_to(over, (1, LANES)))

        count = 6 + sum(2 + sum(size for _, size in stages) for stages in self.back)
        height = -(-count // 8) * 8
        table = pl.pallas_call(
            kernel,
            in_specs=[SMEM, whole((1, self.pieces))],
            out_specs=whole((height, LANES)),
            out_shape=shaped((height, LANES), I32),
            scratch_shapes=[pltpu.VMEM((1, LANES), I32)],
            compiler_params=params(),
            name="routes",
        )(me[None], owners[None, :])
        return table, place


def fetch(sources, targets, sems):
    copies = [
        pltpu.make_async_copy(source, target, sems.at[at])
        for at, (source, target) in enumerate(zip(sources, targets))
    ]
    for copy in copies:
        copy.start()
    for copy in copies:
        copy.wait()


def places(kept, parts):
    return [ANYWHERE] * kept + [HBM] * (len(parts) - kept)


def pick_call(table, picks, parts, sizes, name, deps=(), kept=1):
    rows_each = [part.shape[0] for part in parts]
    shape = parts[0].shape[1:]

    def kernel(table_ref, *refs):
        ins, (*outs, source, sems) = refs[: len(parts)], refs[len(parts) :]
        at, targets = 0, []
        for count in rows_each:
            targets.append(source.at[pl.ds(at, count)])
            at += count
        fetch(ins, targets, sems)
        for (row, start), size, out in zip(picks, sizes, outs):
            for j in range(size):
                out[j] = source[table_ref[row, start + j]]

    return call(
        kernel,
        (table, *parts),
        [SMEM] + places(kept, parts),
        [whole((size,) + shape) for size in sizes],
        [shaped((size,) + shape, BF) for size in sizes],
        name,
        deps,
        scratch=[
            pltpu.VMEM((sum(rows_each),) + shape, BF), pltpu.SemaphoreType.DMA((len(parts),)),
        ],
    )


def join_call(parts, deps=()):
    counts = [part.shape[0] for part in parts]
    shape = (sum(counts),) + parts[0].shape[1:]

    def kernel(*refs):
        *ins, out, sems = refs
        at, targets = 0, []
        for count in counts:
            targets.append(out.at[pl.ds(at, count)])
            at += count
        fetch(ins, targets, sems)

    return call(
        kernel, parts, places(0, parts), whole(shape), shaped(shape, BF), "join", deps,
        scratch=[pltpu.SemaphoreType.DMA((len(parts),))],
    )


def add_pick_call(table, picks, parts, sizes, small=None, extra=(), deps=()):
    shape = parts[0].shape[1:]
    lengths = [size + 2 * (j in extra) for j, size in enumerate(sizes)]

    def kernel(table_ref, *refs):
        sources, refs = refs[: len(parts)], refs[len(parts) :]
        ins, sems, refs = refs[-len(parts) - 1 : -1], refs[-1], refs[: -len(parts) - 1]
        fetch(sources, ins, sems)
        if small is not None:
            small_ref, refs = refs[0], refs[1:]
            terms = [small_ref[...]] + [
                ref[ref.shape[0] - 2].astype(F32) + ref[ref.shape[0] - 1].astype(F32) for ref in ins[1:]
            ]
            while len(terms) > 1:
                middle = len(terms) // 2
                terms = [a + b for a, b in zip(terms[:middle], terms[middle:])]
            hi, lo, kept = split_small(terms[0])
            refs[len(sizes)][...] = kept
            for j in extra:
                refs[j][sizes[j]] = hi
                refs[j][sizes[j] + 1] = lo
        for (row, start), size, out in zip(picks, sizes, refs):
            for j in range(size):
                at = table_ref[row, start + j]
                total = ins[0][at].astype(F32)
                for ref in ins[1:]:
                    total = total + ref[at].astype(F32)
                out[j] = total.astype(BF)

    out_specs = [whole((length,) + shape) for length in lengths]
    out_shape = [shaped((length,) + shape, BF) for length in lengths]
    if small is not None:
        out_specs, out_shape = out_specs + [whole(shape)], out_shape + [shaped(shape, F32)]
    return call(
        kernel,
        (table, *parts) + (() if small is None else (small,)),
        [SMEM] + places(1, parts) + ([] if small is None else [whole(shape)]),
        out_specs,
        out_shape,
        "add_pick",
        late=deps,
        scratch=[pltpu.VMEM(part.shape, BF) for part in parts]
        + [pltpu.SemaphoreType.DMA((len(parts),))],
    )


def owned_call(table, place, routes, parts, small, deps=()):
    (parts_in, parts_mlp), cap = parts, routes.cap
    parts = (*parts_in, *parts_mlp)
    shape = parts_in[0].shape[1:]
    border = routes.spans[1][0]

    def kernel(table_ref, *refs):
        sources, refs = refs[: len(parts)], refs[len(parts) :]
        small_ref, kept_ref, sent_ref, total_ref, *held, sems = refs
        fetch(sources, held, sems)
        ins, mlps = held[: len(parts_in)], held[len(parts_in) :]
        terms = [small_ref[...]] + [
            ref[ref.shape[0] - 2].astype(F32) + ref[ref.shape[0] - 1].astype(F32) for ref in ins[1:]
        ]
        while len(terms) > 1:
            middle = len(terms) // 2
            terms = [a + b for a, b in zip(terms[:middle], terms[middle:])]
        total_ref[...] = terms[0]
        for which, (name, out) in enumerate((("piece", kept_ref), ("sibling", sent_ref))):
            for j in range(cap):
                sums = []
                for number, some in enumerate((ins, mlps)):
                    at = table_ref[place[("slot", number, which)], j]
                    total = some[0][at].astype(F32)
                    for ref in some[1:]:
                        total = total + ref[at].astype(F32)
                    sums.append(total)
                out[j] = jnp.where(table_ref[place[name], j] >= border, sums[1], sums[0])

    args = (table, *parts_in, *parts_mlp, small)
    return call(
        kernel,
        args,
        [SMEM]
        + places(1, parts_in)
        + places(1, parts_mlp)
        + [whole(shape)],
        [whole((cap,) + shape)] * 2 + [whole(shape)],
        [shaped((cap,) + shape, F32)] * 2 + [shaped(shape, F32)],
        "owned",
        deps,
        scratch=[pltpu.VMEM(part.shape, BF) for part in parts]
        + [pltpu.SemaphoreType.DMA((len(parts),))],
    )


def adam_step(weights, first_mom, second_mom, gradient, rate, decay_rate):
    first_new = BETA_ONE * first_mom + (1.0 - BETA_ONE) * gradient
    second_new = BETA_TWO * second_mom + (1.0 - BETA_TWO) * gradient * gradient
    first_fix = first_new / (1.0 - BETA_ONE**STEP)
    second_fix = second_new / (1.0 - BETA_TWO**STEP)
    weights_new = weights * (1.0 - rate * decay_rate) - rate * first_fix / (
        jnp.sqrt(second_fix) + ADAM_EPS
    )
    return (weights_new, first_new, second_new)


def adam_call(table, row, core, borders, kept, arrived, tables):
    cap, count, width = tables[0].shape
    half = count // 2
    group = max(g for g in range(1, 6) if cap % g == 0)

    def kernel(table_ref, core_ref, kept_ref, arrived_ref, w_ref, m_ref, v_ref, *outs):
        step = pl.program_id(0)
        swapped = core_ref[0] == 1
        for j in range(group):
            piece = table_ref[row, step * group + j]
            rate = jnp.where(piece < borders[2], 0.03, 0.015)
            rate = jnp.where(piece < borders[1], 0.2, rate)
            rate = jnp.where(piece < borders[0], 0.03, rate).astype(F32)
            halves = (kept_ref[j], arrived_ref[j])
            for at in range(2):
                here = pl.ds(at * half, half)
                grad = jnp.where(swapped, halves[1 - at], halves[at])
                new = adam_step(w_ref[j, here], m_ref[j, here], v_ref[j, here], grad, rate, DECAY_RATE)
                for out, value in zip(outs, new):
                    out[j, here] = jnp.where(piece >= 0, value, 0.0)

    def block(rows_each):
        return pl.BlockSpec((group, rows_each, width), lambda t: (t, 0, 0))

    return call(
        kernel,
        (table, core[None], kept, arrived, *tables),
        [SMEM, SMEM, block(half), block(half)] + [block(count)] * 3,
        [block(count)] * 3,
        [shaped((cap, count, width), F32)] * 3,
        "adam",
        grid=(cap // group,),
        cost_estimate=cost(1e7, 8e6),
    )


def small_kernel(total_ref, far_ref, norm_ref, nm_ref, nv_ref, bias_ref, bm_ref, bv_ref, *outs):
    gains = total_ref[0:2, :] + far_ref[0:2, :]
    for at, rate in enumerate(NORM_RATES):
        here = slice(at, at + 1)
        grad = gains[here] if at < 2 else total_ref[here, :]
        new = adam_step(norm_ref[here, :], nm_ref[here, :], nv_ref[here, :], grad, rate, 0.0)
        for out, value in zip(outs[:3], new):
            out[here, :] = value
    width = total_ref.shape[1]
    for at in range(0, bias_ref.shape[1], width):
        here = slice(at, min(at + width, bias_ref.shape[1]))
        row = 6 + at // width
        grad = total_ref[row : row + 1, : here.stop - at]
        new = adam_step(bias_ref[:, here], bm_ref[:, here], bv_ref[:, here], grad, BIAS_RATE, 0.0)
        for out, value in zip(outs[3:], new):
            out[:, here] = value


def small_call(total, far, norms, biases, deps=()):
    args = (total, far, *norms, *biases)
    kept = [shaped(part.shape, F32) for part in (*norms, *biases)]
    return call(
        small_kernel, args, [whole(arg.shape) for arg in args], [whole(k.shape) for k in kept], kept, "small_update",
        deps,
    )


def swap_mp(array):
    return lax.ppermute(array, "mp", [(0, 1), (1, 0)])


def roll_rows(array, start):
    return lax.dynamic_slice_in_dim(
        jnp.concatenate([array, array], axis=0), start, array.shape[0], axis=0
    )


def body(
    tokens, cotangent, lengths, owners, weight_table, moment_table, square_table,
    norm_params, norm_moment, norm_square, bias_params, bias_moment, bias_square,
):
    dp_size = lax.axis_size("dp")
    mp_size = lax.axis_size("mp")
    heads = HEADS // mp_size
    head_width = heads * HEAD_DIM
    hidden = FF // mp_size
    tok, width = tokens.shape
    slot_cap, piece_len = weight_table.shape[1:3]
    half_len = piece_len // 2
    piece_total = owners.shape[0]
    me = lax.axis_index("dp").astype(I32)
    core = me % 2
    first_core = core == 0

    n_qkv, n_out = 3 * head_width // piece_len, head_width // piece_len
    n_up = hidden // piece_len
    n_first = n_qkv + n_out
    ready = (n_first, piece_total)
    spans = ((0, n_first), (n_first, piece_total))
    routes = Routes(dp_size, slot_cap, piece_total, ready, spans)
    table, place = routes.tables(owners, me)

    own_half, sibling_half = halves_call(core, weight_table[0])
    chip_slots = [own_half, routes.swap_cores(sibling_half)]

    def half(array, which):
        return lax.dynamic_index_in_dim(array, which, axis=1, keepdims=False)

    def unless(bad, usual, other):
        return lax.while_loop(
            lambda state: state[0] > 0, lambda state: (jnp.zeros((), I32), other()), (bad, usual)
        )[1]

    def own_lists(ranges, deps=()):
        return pick_call(
            table, [(place["send"], begin) for begin, _ in ranges], chip_slots,
            [end - begin for begin, end in ranges], "pick_owned", deps,
        )

    def collect(buffers, ranges, deps=()):
        sizes = [high - low for low, high in ranges]
        return pick_call(
            table, [(place["take"], low) for low, _ in ranges], buffers, sizes, "pick_all", deps
        )

    def flat(array):
        return array.reshape(-1, width)

    def pairs_apart(bit):
        return [(device, device ^ bit) for device in range(dp_size)]

    def slow_first():
        everyone, bit = weight_table[0].astype(BF), 1
        while bit < dp_size:
            everyone = jnp.concatenate([everyone, lax.ppermute(everyone, "dp", pairs_apart(bit))], 0)
            bit *= 2
        earlier = (owners[None, :] == owners[:, None]) & (
            jnp.arange(piece_total)[None, :] < jnp.arange(piece_total)[:, None]
        )
        at = (owners ^ me) * slot_cap + jnp.sum(earlier.astype(I32), axis=1)
        mine = half(everyone[at[:n_first]].reshape(n_first, 2, half_len, width), core)
        return mine, mine[n_qkv:]

    stages = routes.out
    chunks = tuple(zip(routes.begins, routes.fill))
    relayed = routes.chips == 8
    if relayed:
        list_a, list_all = ticked(own_lists, (chunks[0], (0, routes.fill[1])))
    else:
        list_a, list_b = ticked(own_lists, [chunk for chunk in chunks if chunk[0] < chunk[1]] * 2)[:2]
    listed = Clock.tick
    list_a = routes.around(list_a, stages[0][0])
    cos, sin, *segs, b_mine, b_other, b_up, start = layout_call(
        core, lengths, bias_params, tok, 3 * head_width // 2, (listed,)
    )
    x, a1 = ticked(norm_call, start, tokens, norm_params)
    gy = ticked(roll_call, start, cotangent, (Clock.tick,))
    turned = Clock.tick

    if relayed:
        own_y = routes.move(list_all, stages[0][1], 1)
        arrived = ticked(join_call, list_a[1:], (turned,))
        buffers_a = list_a + [own_y, routes.move(arrived, stages[0][1], 1)]
        (list_b,) = own_lists(chunks[1:], (Clock.tick, own_y))
        from_two, from_one = (routes.move(list_b, stage, 1) for stage in stages[1][:2])
        joined = ticked(join_call, [from_two, from_one])
        turned = Clock.tick
        relay = routes.move(from_two, stages[1][1], 1)
        y_joined = routes.move(joined, stages[1][2], 1)
    else:
        buffers_a, buffers_b = list_a, [list_b]
        for stage in stages[0][1:]:
            buffers_a = routes.onward(buffers_a, stage)
    w_first_m, w_out_x = ticked(collect, buffers_a, ((0, n_first), (n_qkv, n_first)), (turned,))
    collected = Clock.tick
    w_first_m, w_out_x = unless(table[place["late"], 0], (w_first_m, w_out_x), slow_first)
    b_qkv = keep_call((b_mine, b_other), (collected,))
    w_first_o = routes.swap_cores(w_first_m)
    qkv_m, qkv_o, safe = ticked(
        qkv_call, a1, flat(w_first_m), flat(w_first_o), *b_qkv, cos, sin
    )
    w_out_x = swap_mp(w_out_x)
    if relayed:
        relay = ticked(join_call, [relay], (Clock.tick,))
        collected = Clock.tick
        y_relay = routes.move(relay, stages[1][2], 1)
        buffers_b = [list_b, from_two, from_one, relay, y_joined, y_relay]
    elif chunks[1][0] < chunks[1][1]:
        for stage in stages[1]:
            buffers_b = routes.onward(buffers_b, stage)
    else:
        buffers_b = []
    half_way = 2 * TILE
    ctx_a, logs_a = ticked(attend_call, 0, half_way, safe, segs, qkv_m, qkv_o, (collected,))
    attended = Clock.tick
    ctx_b, logs_b = attend_call(half_way, LONGEST, safe, segs, qkv_m, qkv_o, (attended,))
    (w_out_x,) = hand_call((w_out_x,), (attended,))
    w_out_x = [flat(w_out_x), flat(routes.swap_cores(w_out_x))]
    ctx_ax, ctx_bx = swap_mp(ctx_a), swap_mp(ctx_b)
    (w_mine,) = ticked(collect, buffers_a + buffers_b, ((n_first, piece_total),), (logs_b, ctx_ax))
    (b_up,) = keep_call((b_up,), (Clock.tick,))
    w_mine, w_other = flat(w_mine), flat(routes.swap_cores(w_mine))
    w_first = [flat(w_first_m), flat(w_first_o)]
    spans_tok = ((0, half_way // TILE), (half_way // TILE, tok // TILE))
    mlp_args = (w_first, w_out_x, w_mine, w_other, b_up, norm_params)
    *filled, g_h2_a, gb_up_a = mlp_call(spans_tok[0], x, gy, (ctx_a, ctx_ax), *mlp_args)
    *filled, g_h2_b, gb_up_b = mlp_call(spans_tok[1], x, gy, (ctx_b, ctx_bx), *mlp_args, filled)
    x1, a2, act, g_pre, ffn = filled
    g_h2_ax, g_h2_bx = swap_mp(g_h2_a), swap_mp(g_h2_b)
    g_mlp = mlp_grads_call(act, g_pre, a2, gy)

    def pieces(array):
        return array.reshape(-1, half_len, width)

    def sort_out(number, level, parts, small=None, deps=()):
        stage = routes.back[number][level - 1]
        size = stage[1]
        lists = ticked(
            add_pick_call,
            table,
            [(place[("back", number, level, shift)], 0) for shift in range(size)],
            parts,
            [routes.span_limit(number, level)] * size,
            small=small,
            extra=() if small is None else range(1, size),
            deps=deps,
        )
        moved = [routes.move(lists[shift], stage, shift) for shift in range(1, size)]
        return [lists[0]] + moved, lists[-1]

    gx1, g_ctx_a, g_out_a, mid_a, g_mlp_m, g_mlp_o = mid_call(
        spans_tok[0], x1, gy, g_h2_a, g_h2_ax, (ctx_a,), *w_first, norm_params, (), g_mlp
    )
    back = (segs, cos, sin, qkv_m, qkv_o)
    cut = heads * 6 // 10
    groups = ((0, cut), (cut, heads - cut))
    early_one = ticked(attend_back_call, 0, half_way, *back, g_ctx_a, ctx_a, logs_a, *groups[0])
    parts_mlp, listed = sort_out(
        1, 1, [pieces(g_mlp_m), routes.swap_cores(pieces(g_mlp_o))], deps=(Clock.tick,)
    )
    early_two = ticked(
        attend_back_call, 0, half_way, *back, g_ctx_a, ctx_a, logs_a, *groups[1], deps=(listed,)
    )
    attended = Clock.tick
    gx1, g_ctx_b, g_out_b, mid_b, ffn = mid_call(
        spans_tok[1], x1, gy, g_h2_b, g_h2_bx, (ctx_b,), *w_first, norm_params, (gx1,), (ffn,), (attended,)
    )
    ffn_other = swap_mp(ffn)

    (grads_one,) = ticked(
        attend_back_call, half_way, LONGEST, *back, g_ctx_b, ctx_b, logs_b, *groups[0], early_one
    )
    parts_mlp, listed = sort_out(1, 2, parts_mlp, deps=(Clock.tick,))
    sorted_mlp = Clock.tick
    (grads_two,) = attend_back_call(
        half_way, LONGEST, *back, g_ctx_b, ctx_b, logs_b, *groups[1], early_two, (listed,)
    )
    g_in_m, g_in_o, g_h1, small = ticked(
        in_grads_call, (grads_one, grads_two), core, a1, x, *w_first,
        (g_out_a, g_out_b), (mid_a, mid_b), (gb_up_a, gb_up_b),
    )
    g_h1_other = swap_mp(g_h1)
    ticked(keep_call, (norm_params,), (Clock.tick,))
    filled = Clock.tick
    out_roll = out_call(x1, ffn, ffn_other, norm_params, (sorted_mlp,))
    block_out = roll_rows(out_roll, tok - start[0])
    parts_in = [pieces(g_in_m), routes.swap_cores(pieces(g_in_o))]
    for level in range(1, len(routes.back[0])):
        parts_in, small = sort_out(0, level, parts_in, small, (filled,))
    for level in range(3, len(routes.back[1]) + 1):
        parts_mlp, _ = sort_out(1, level, parts_mlp, deps=(Clock.tick,))
    parts_in, small = sort_out(0, len(routes.back[0]), parts_in, small, (block_out,))
    grad_roll = ticked(last_call, x, gx1, g_h1, g_h1_other, norm_params)
    grad_tokens = roll_rows(grad_roll, tok - start[0])

    kept, sent, small = owned_call(table, place, routes, (parts_in, parts_mlp), small, (grad_tokens,))
    small_x = swap_mp(small)
    arrived = routes.swap_cores(sent)

    def slow_grads():
        def stack(in_part, mlp_part):
            return jnp.concatenate([pieces(in_part), pieces(mlp_part)], axis=0).astype(F32)

        mine, other = stack(g_in_m, g_mlp_m), stack(g_in_o[: g_in_m.shape[0]], g_mlp_o)
        both = jnp.where(first_core, jnp.stack([mine, other], 1), jnp.stack([other, mine], 1))
        total, bit = both, 1
        while bit < dp_size:
            total = total + lax.ppermute(total, "dp", pairs_apart(bit))
            bit *= 2
        total = total[jnp.maximum(table[place["piece"], :slot_cap], 0)]
        return half(total, core), half(total, 1 - core)

    def update(kept, arrived):
        return ticked(
            adam_call, table, place["piece"], core, (n_qkv, n_first, n_first + n_up), kept, arrived,
            (weight_table[0], moment_table[0], square_table[0]),
        )

    tables_next = update(kept, arrived)
    updated = Clock.tick
    tables_next = unless(table[place["over"], 0], tuple(tables_next), lambda: tuple(update(*slow_grads())))
    small_out = small_call(
        small, small_x,
        (norm_params, norm_moment, norm_square), (bias_params, bias_moment, bias_square),
        (updated,),
    )
    return (block_out, grad_tokens, *(part[None] for part in tables_next), *small_out)


def solution(mesh):
    flat = P("dp", None)
    pieces = P("mp", "dp", None, None)
    bias = P("mp", None)
    return jax.shard_map(
        body,
        mesh=mesh,
        in_specs=(flat, flat, flat, P(), pieces, pieces, pieces, P(), P(), P(), bias, bias, bias),
        out_specs=(flat, flat, pieces, pieces, pieces, P(), P(), P(), bias, bias, bias),
        check_vma=False,
    )
```

```python
import functools

import jax
import jax.numpy as jnp
import numpy as np
from jax import lax
from jax.experimental import pallas as pl
from jax.experimental.pallas import tpu as pltpu
from jax.sharding import PartitionSpec as P

HEADS = 20
HEAD_DIM = 32
HALF = HEAD_DIM // 2
FF = 2560
LONGEST = 1024
STEP = 10

EPS_NORM = 1e-05
BETA_ONE = 0.5
BETA_TWO = 0.5
ADAM_EPS = 1e-08
DECAY_RATE = 0.01
NEG_FILL = -1e30
NORM_RATES = (0.5, 0.1, 0.5, 0.1, 0.1, 0.1)
BIAS_RATE = 0.1
SCALE = HEAD_DIM**-0.5
LOG2_E = 1.4426950408889634
SCALE_LOG2 = SCALE * LOG2_E
SAFE_EXP = 100.0

BF = jnp.bfloat16
F32 = jnp.float32
I32 = jnp.int32
TILE = 256
LANES = 128
TICK = (8, 128)
HEADS_EACH = 5
VMEM_LIMIT = 16 << 20
SHRINK = 0.1


def params(*kinds):
    return pltpu.CompilerParams(dimension_semantics=kinds or None, vmem_limit_bytes=VMEM_LIMIT)


def cost(flops, moved):
    return pl.CostEstimate(flops=int(flops / SHRINK), bytes_accessed=int(moved / SHRINK), transcendentals=0)


def dot_nn(a, b):
    return lax.dot_general(a, b, (((1,), (0,)), ((), ())), preferred_element_type=F32)


def dot_nt(a, b):
    return lax.dot_general(a, b, (((1,), (1,)), ((), ())), preferred_element_type=F32)


def dot_tn(a, b):
    return lax.dot_general(a, b, (((0,), (0,)), ((), ())), preferred_element_type=F32)


def split_two(v):
    hi = v.astype(BF).astype(F32)
    return hi, v - hi


def split_three(v):
    hi = v.astype(BF).astype(F32)
    mid = (v - hi).astype(BF).astype(F32)
    return hi, mid, v - hi - mid


def normalized(v):
    centred = v - jnp.mean(v, axis=-1, keepdims=True)
    inv = lax.rsqrt(jnp.mean(centred * centred, axis=-1, keepdims=True) + EPS_NORM)
    return centred * inv, inv


ANYWHERE = pl.BlockSpec(memory_space=pl.ANY)
SMEM = pl.BlockSpec(memory_space=pltpu.SMEM)
HBM = pl.BlockSpec(memory_space=pltpu.HBM)


def whole(shape):
    return pl.BlockSpec(shape, lambda *_: (0,) * len(shape))


def rows(width, begin=0):
    return pl.BlockSpec((TILE, width), lambda t: (begin + t, 0))


def cols(height, begin=0):
    return pl.BlockSpec((height, TILE), lambda t: (0, begin + t))


def both(height, begin=0):
    return pl.BlockSpec((2, height, TILE), lambda t: (0, 0, begin + t))


def last_rows(array, count):
    return pl.BlockSpec((count, array.shape[1]), lambda *_: (array.shape[0] // count - 1, 0))


def shaped(shape, dtype):
    return jax.ShapeDtypeStruct(shape, dtype)


class Clock:
    wanted = False
    tick = None


def ticked(function, *args, **named):
    Clock.wanted = True
    results = function(*args, **named)
    Clock.wanted = False
    return results


def call(kernel, args, in_specs, out_specs, out_shape, name, deps=(), scratch=(), limit=VMEM_LIMIT, late=(), **more):
    count = len(args)
    single = not isinstance(out_shape, (list, tuple))
    out_specs, out_shape = ([out_specs], [out_shape]) if single else (list(out_specs), list(out_shape))
    if any(spec is not ANYWHERE for spec in in_specs):
        more.setdefault("grid", (1,))

    if "input_output_aliases" in more:
        aliases = more["input_output_aliases"]
        more["input_output_aliases"] = {len(deps) + at: to for at, to in aliases.items()}
    real, ticks = len(out_shape), Clock.wanted
    if ticks:
        out_specs, out_shape = out_specs + [whole(TICK)], out_shape + [shaped(TICK, F32)]

    def wrapped(*refs):
        ins, outs = refs[len(deps) : len(deps) + count], refs[len(deps) + count + len(late) :]
        if ticks:
            outs[real][...] = jnp.zeros(TICK, F32)
        kernel(*ins, *outs[:real], *outs[real + ticks :])

    results = pl.pallas_call(
        wrapped,
        in_specs=[ANYWHERE] * len(deps) + list(in_specs) + [ANYWHERE] * len(late),
        out_specs=out_specs,
        out_shape=out_shape,
        scratch_shapes=list(scratch),
        compiler_params=pltpu.CompilerParams(
            dimension_semantics=("arbitrary",) * len(more.get("grid", ())) or None,
            vmem_limit_bytes=limit,
        ),
        name=name,
        **more,
    )(*deps, *args, *late)
    if ticks:
        Clock.tick = results[-1]
        results = results[:-1]
    return results[0] if single else results


def rolled(array, start):
    tok = array.shape[0]
    shift = jnp.where(start == 0, 0, tok - start)
    return pltpu.roll(array.astype(F32), shift, 0)


def roll_kernel(start_ref, array_ref, out_ref):
    out_ref[...] = rolled(array_ref[...], start_ref[0]).astype(BF)


def roll_call(start, array, deps=()):
    return call(
        roll_kernel, (start, array), [SMEM, whole(array.shape)], whole(array.shape),
        shaped(array.shape, BF), "roll", deps,
    )


def norm_kernel(start_ref, x_ref, norm_ref, out_ref, a_ref, turned):
    turned[...] = rolled(x_ref[...], start_ref[0])
    for at in range(0, x_ref.shape[0], LANES):
        here = slice(at, at + LANES)
        value = turned[here, :]
        out_ref[here, :] = value.astype(BF)
        n1, _ = normalized(value)
        a_ref[here, :] = (n1 * norm_ref[0:1] + norm_ref[1:2]).astype(BF)


def norm_call(start, x, norms):
    return call(
        norm_kernel,
        (start, x, norms),
        [SMEM, whole(x.shape), whole(norms.shape)],
        [whole(x.shape)] * 2,
        [shaped(x.shape, BF)] * 2,
        "first_norm",
        scratch=[pltpu.VMEM(x.shape, F32)],
        limit=2 * VMEM_LIMIT,
    )


def qkv_kernel(a_ref, wm_ref, wo_ref, bm_ref, bo_ref, cos_ref, sin_ref, m_ref, o_ref, safe_ref, top, bias):
    step = pl.program_id(0)

    @pl.when(step == 0)
    def _():
        top[...] = jnp.zeros_like(top)
        for which, ref in enumerate((bm_ref, bo_ref)):
            bias[which] = jnp.transpose(jnp.broadcast_to(ref[...], (LANES, ref.shape[1])))

    a1 = a_ref[...]
    mine = dot_nt(wm_ref[...], a1) + bias[0, :, 0:1]
    other = dot_nt(wo_ref[...], a1) + bias[1, :, 0:1]
    width = m_ref.shape[1]
    cos, sin = cos_ref[...], sin_ref[...]
    for which in range(2):
        longest = top[which : which + 1, :]
        for at in range(0, width, HALF):
            here = which * width + at
            p, r = mine[here : here + HALF], other[here : here + HALF]
            longest = jnp.maximum(longest, jnp.sum(p * p + r * r, axis=0, keepdims=True))
            m_ref[which, at : at + HALF, :] = (p * cos - r * sin).astype(BF)
            o_ref[which, at : at + HALF, :] = (r * cos + p * sin).astype(BF)
        top[which : which + 1, :] = longest
    m_ref[2] = mine[2 * width :].astype(BF)
    o_ref[2] = other[2 * width :].astype(BF)

    @pl.when(step == pl.num_programs(0) - 1)
    def _():
        bound = jnp.max(top[0:1, :]) * jnp.max(top[1:2, :]) * SCALE_LOG2**2
        safe_ref[0] = (bound < SAFE_EXP**2).astype(I32)


def qkv_call(a1, w_mine, w_other, b_mine, b_other, cos, sin, deps=()):
    tok, width = a1.shape
    out = b_mine.shape[1]
    third = pl.BlockSpec((3, out // 3, TILE), lambda t: (0, 0, t))
    return call(
        qkv_kernel,
        (a1, w_mine, w_other, b_mine, b_other, cos, sin),
        [
            rows(width), whole((out, width)), whole((out, width)),
            whole(b_mine.shape), whole(b_mine.shape), cols(HALF), cols(HALF),
        ],
        [third, third, SMEM],
        [shaped((3, out // 3, tok), BF)] * 2 + [shaped((1,), I32)],
        "qkv",
        deps,
        scratch=[pltpu.VMEM((8, TILE), F32), pltpu.VMEM((2, out, LANES), F32)],
        grid=(tok // TILE,),
        cost_estimate=cost(4 * tok * width * out, 8e6),
    )


def normal_tables(u):
    return 0.5 * (1.0 + lax.erf(u * 0.7071067811865476)), jnp.exp(-0.5 * u * u)


def mlp_kernel(
    groups, chained, x_ref, gy_ref, *refs,
):
    ctx_refs, refs = refs[: 2 * groups], refs[2 * groups :]
    wp_mine, wp_other, wx_mine, wx_other, w_mine, w_other, bup_ref, norm_ref = refs[:8]
    refs = refs[8 + chained :]
    x1_ref, a2_ref, act_ref, gpre_ref, ffn_ref, gh_ref, gbup_ref, out_w, up_w, down_w = refs

    @pl.when(pl.program_id(0) == 0)
    def _():
        quarter, half = wx_mine.shape[0], up_w.shape[0] // 2
        for at, ref in enumerate((wp_mine, wp_other, wx_mine, wx_other)):
            out_w[at * quarter : (at + 1) * quarter, :] = ref[...]
        for at, ref in enumerate((w_mine, w_other)):
            up_w[at * half : (at + 1) * half, :] = ref[:half, :]
            down_w[at * half : (at + 1) * half, :] = ref[half:, :]

    gy = gy_ref[...]
    own, far = ctx_refs[:groups], ctx_refs[groups:]
    ctx = jnp.concatenate([ref[j] for some in (own, far) for j in range(2) for ref in some], axis=0)
    x1 = x_ref[...].astype(F32) + dot_tn(ctx, out_w[...]) + norm_ref[4:5]
    x1_ref[...] = x1
    n2, _ = normalized(x1)
    a2 = (n2 * norm_ref[2:3] + norm_ref[3:4]).astype(BF)
    a2_ref[...] = a2
    pre = dot_nt(a2, up_w[...]) + bup_ref[...]
    cdf, bell = normal_tables(pre)
    act = (pre * cdf).astype(BF)
    act_ref[...] = act
    slope = cdf + pre * (bell * 0.3989422804014327)
    gpre = (slope * dot_nt(gy, down_w[...])).astype(BF)
    gpre_ref[...] = gpre
    ffn_ref[...] = dot_nn(act, down_w[...]).astype(BF)
    gh_ref[...] = dot_nn(gpre, up_w[...]).astype(BF)
    part = jnp.sum(gpre.astype(F32), axis=0, keepdims=True)

    @pl.when(pl.program_id(0) == 0)
    def _():
        gbup_ref[...] = part

    @pl.when(pl.program_id(0) > 0)
    def _():
        gbup_ref[...] += part


def mlp_call(span, x, gy, ctx, wp, wx, w_mine, w_other, b_up, norms, before=(), deps=()):
    tok, width = x.shape
    hidden = b_up.shape[1]
    quarter = wx[0].shape[0]
    begin, count = span[0], span[1] - span[0]
    args = (x, gy, *ctx, *wp, *wx, w_mine, w_other, b_up, norms, *before)
    return call(
        functools.partial(mlp_kernel, len(ctx) // 2, len(before)),
        args,
        [rows(width, begin)] * 2
        + [both(part.shape[1]) for part in ctx]
        + [last_rows(wp[0], quarter)] * 2
        + [whole((quarter, width))] * 2
        + [whole(w_mine.shape)] * 2
        + [whole(b_up.shape), whole(norms.shape)]
        + [ANYWHERE] * len(before),
        [
            rows(width, begin), rows(width, begin), rows(hidden, begin), rows(hidden, begin),
            rows(width, begin), rows(width), whole((1, hidden)),
        ],
        [
            shaped((tok, width), F32), shaped((tok, width), BF), shaped((tok, hidden), BF),
            shaped((tok, hidden), BF), shaped((tok, width), BF), shaped((count * TILE, width), BF),
            shaped((1, hidden), F32),
        ],
        "mlp",
        deps,
        scratch=[
            pltpu.VMEM((4 * quarter, width), BF), pltpu.VMEM((hidden, width), BF),
            pltpu.VMEM((hidden, width), BF),
        ],
        grid=(count,),
        cost_estimate=cost(2 * count * TILE * width * (hidden * 4 + 4 * quarter) * 1.6, 2e7),
        input_output_aliases={len(args) - len(before) + j: j for j in range(len(before))},
    )


def mlp_grads_kernel(act_ref, gpre_ref, a2_ref, gy_ref, mine_ref, other_ref, down_sum, up_sum):
    step = pl.program_id(0)
    down = dot_tn(act_ref[...], gy_ref[...])
    up = dot_tn(gpre_ref[...], a2_ref[...])

    @pl.when(step == 0)
    def _():
        down_sum[...] = down
        up_sum[...] = up

    @pl.when(step > 0)
    def _():
        down_sum[...] += down
        up_sum[...] += up

    @pl.when(step == pl.num_programs(0) - 1)
    def _():
        half = down_sum.shape[0] // 2
        for which, out_ref in enumerate((mine_ref, other_ref)):
            here = pl.ds(which * half, half)
            out_ref[:half, :] = up_sum[here, :].astype(BF)
            out_ref[half:, :] = down_sum[here, :].astype(BF)


def mlp_grads_call(act, gpre, a2, gy, deps=()):
    tok, hidden = act.shape
    width = a2.shape[1]
    return call(
        mlp_grads_kernel,
        (act, gpre, a2, gy),
        [rows(hidden), rows(hidden), rows(width), rows(width)],
        [whole((hidden, width))] * 2,
        [shaped((hidden, width), BF)] * 2,
        "mlp_grads",
        deps,
        scratch=[pltpu.VMEM((hidden, width), F32)] * 2,
        grid=(tok // TILE,),
        cost_estimate=cost(4 * tok * width * hidden * 1.3, 1.4e7),
    )


def mid_kernel(
    groups, chained, handed, x1_ref, gy_ref, gh_a, gh_b, *refs,
):
    ctx_refs, refs = refs[:groups], refs[groups:]
    wm_ref, wo_ref, norm_ref = refs[:3]
    refs = refs[3 + chained + handed :]
    gx_ref, g_out, gout_ref, sum_ref = refs[:4]
    cm, co = (jnp.concatenate([ref[j] for ref in ctx_refs], axis=0) for j in range(2))
    step = pl.program_id(0)
    gy = gy_ref[...].astype(F32)
    gh = gh_a[...].astype(F32) + gh_b[...].astype(F32)
    n2, inv = normalized(x1_ref[...])
    e = gh * norm_ref[2:3]
    gx = gy + inv * (
        e - jnp.mean(e, axis=-1, keepdims=True) - n2 * jnp.mean(e * n2, axis=-1, keepdims=True)
    )
    gx_ref[...] = gx
    gm = gx.astype(BF)
    g_out[0] = dot_nt(wm_ref[...], gm).astype(BF)
    g_out[1] = dot_nt(wo_ref[...], gm).astype(BF)

    @pl.when(step == 0)
    def _():
        gout_ref[...] = jnp.zeros_like(gout_ref)
        sum_ref[...] = jnp.zeros_like(sum_ref)

    gout_ref[0] += dot_nn(cm, gm)
    gout_ref[1] += dot_nn(co, gm)
    for at, value in enumerate((gh * n2, gh, gx, gy)):
        sum_ref[at : at + 1, :] += jnp.sum(value, axis=0, keepdims=True)


def mid_call(span, x1, gy, gh, gh_other, ctx, w_m, w_o, norms, before=(), hand=(), deps=()):
    tok, width = x1.shape
    head = sum(part.shape[1] for part in ctx)
    begin, count = span[0], span[1] - span[0]
    args = (x1, gy, gh, gh_other, *ctx, w_m, w_o, norms, *before, *hand)
    fixed = len(args) - len(before) - len(hand)
    aliases = {fixed + j: j for j in range(len(before))}
    aliases.update({fixed + len(before) + j: 4 + j for j in range(len(hand))})
    return call(
        functools.partial(mid_kernel, len(ctx), len(before), len(hand)),
        args,
        [rows(width, begin)] * 2
        + [rows(width)] * 2
        + [both(part.shape[1]) for part in ctx]
        + [last_rows(w_m, head)] * 2
        + [whole(norms.shape)]
        + [ANYWHERE] * (len(before) + len(hand)),
        [rows(width, begin), both(head), whole((2, head, width)), whole((8, width))]
        + [ANYWHERE] * len(hand),
        [
            shaped((tok, width), F32), shaped((2, head, count * TILE), BF),
            shaped((2, head, width), F32), shaped((8, width), F32),
        ]
        + [shaped(part.shape, part.dtype) for part in hand],
        "mid_back",
        deps,
        grid=(count,),
        cost_estimate=cost(8 * count * TILE * width * head * 2, 1e7),
        input_output_aliases=aliases,
    )


def pack_small(value):
    hi = value.astype(BF).astype(F32)
    row = lax.broadcasted_iota(I32, value.shape, 0)
    rest = jnp.where(row < 6, value - hi, 0.0)
    return jnp.where(row < 10, hi, pltpu.roll(rest, 10, 0)).astype(BF)


def unpack_small(packed):
    packed = packed.astype(F32)
    row = lax.broadcasted_iota(I32, packed.shape, 0)
    return jnp.where(row < 10, packed, 0.0) + jnp.where(row < 6, pltpu.roll(packed, 6, 0), 0.0)


def in_grads_kernel(groups, gouts, *refs):
    g_refs, refs = refs[:groups], refs[groups:]
    out_refs, mid_refs, up_refs, refs = (
        refs[:gouts], refs[gouts : 2 * gouts], refs[2 * gouts : 3 * gouts], refs[3 * gouts :]
    )
    core_ref, a1_ref, x_ref, wm_ref, wo_ref, mine_ref, other_ref, gh_ref, sum_ref = refs[:9]
    m_sum, o_sum, gbm_ref, gbo_ref = refs[9:]
    step = pl.program_id(0)
    count = wm_ref.shape[0]
    a1 = a1_ref[...]
    gm, go = (
        jnp.concatenate([ref[half, j] for j in range(3) for ref in g_refs], axis=0)
        for half in range(2)
    )

    @pl.when(step == 0)
    def _():
        m_sum[...] = jnp.zeros_like(m_sum)
        o_sum[...] = jnp.zeros_like(o_sum)
        gbm_ref[...] = jnp.zeros_like(gbm_ref)
        gbo_ref[...] = jnp.zeros_like(gbo_ref)
        sum_ref[...] = jnp.zeros_like(sum_ref)

    m_sum[...] += dot_nn(gm, a1)
    o_sum[...] += dot_nn(go, a1)
    gbm_ref[...] += jnp.sum(gm.astype(F32), axis=1, keepdims=True)
    gbo_ref[...] += jnp.sum(go.astype(F32), axis=1, keepdims=True)
    gh = dot_tn(gm, wm_ref[...]) + dot_tn(go, wo_ref[...])
    gh_ref[...] = gh.astype(BF)
    n1, _ = normalized(x_ref[...].astype(F32))
    sum_ref[0:1, :] += jnp.sum(gh * n1, axis=0, keepdims=True)
    sum_ref[1:2, :] += jnp.sum(gh, axis=0, keepdims=True)

    @pl.when(step == pl.num_programs(0) - 1)
    def _():
        width = gh.shape[1]
        up = sum((ref[...] for ref in up_refs[1:]), up_refs[0][...])
        sum_ref[2:6, :] = sum((ref[0:4, :] for ref in mid_refs[1:]), mid_refs[0][0:4, :])

        def column(row):
            return jnp.transpose(jnp.broadcast_to(row, (LANES, row.shape[1])))[:, 0:1]

        swapped = core_ref[0] == 1
        mixed = []
        for mine, other in ((gbm_ref[...], gbo_ref[...]), (column(up[:, :width]), column(up[:, width:]))):
            lower, upper = jnp.where(swapped, other, mine), jnp.where(swapped, mine, other)
            for at in range(0, mine.shape[0], HALF):
                mixed += [lower[at : at + HALF], upper[at : at + HALF]]
        natural = jnp.concatenate(mixed, axis=0)
        natural = jnp.transpose(jnp.broadcast_to(natural, (natural.shape[0], LANES)))[0:1]
        for at in range(0, natural.shape[1], width):
            part = natural[:, at : at + width]
            sum_ref[6 + at // width : 7 + at // width, : part.shape[1]] = part
        packed = pack_small(sum_ref[...])
        sum_ref[...] = unpack_small(packed)
        more = count + out_refs[0].shape[1]
        for ref, total, half in ((mine_ref, m_sum, 0), (other_ref, o_sum, 1)):
            ref[:count, :] = total[...].astype(BF)
            ref[count:more, :] = sum((out[half] for out in out_refs[1:]), out_refs[0][half]).astype(BF)
        other_ref[more:, :] = packed


def in_grads_call(grads, core, a1, x, w_m, w_o, gouts, mid_sums, gb_ups, deps=()):
    tok, width = a1.shape
    more = gouts[0].shape[1]
    count = w_m.shape[0] - more
    parts = [
        pl.BlockSpec(part.shape[:3] + (TILE,), lambda t: (0, 0, 0, t)) for part in grads
    ]
    return call(
        functools.partial(in_grads_kernel, len(grads), len(gouts)),
        (*grads, *gouts, *mid_sums, *gb_ups, core[None], a1, x, w_m, w_o),
        parts
        + [whole(part.shape) for part in (*gouts, *mid_sums, *gb_ups)]
        + [SMEM, rows(width), rows(width)]
        + [whole((count, width))] * 2,
        [whole((count + more, width)), whole((count + more + 16, width)), rows(width), whole((16, width))],
        [
            shaped((count + more, width), BF), shaped((count + more + 16, width), BF),
            shaped((tok, width), BF), shaped((16, width), F32),
        ],
        "in_grads",
        deps,
        scratch=[pltpu.VMEM((count, width), F32)] * 2 + [pltpu.VMEM((count, 1), F32)] * 2,
        grid=(tok // TILE,),
        cost_estimate=cost(8 * tok * width * count * 1.3, 1e7),
    )


def out_kernel(x1_ref, a_ref, b_ref, norm_ref, out_ref):
    out_ref[...] = x1_ref[...] + (a_ref[...].astype(F32) + b_ref[...].astype(F32)) + norm_ref[5:6]


def out_call(x1, ffn_a, ffn_b, norms, deps=()):
    tok, width = x1.shape
    return call(
        out_kernel,
        (x1, ffn_a, ffn_b, norms),
        [rows(width)] * 3 + [whole(norms.shape)],
        rows(width),
        shaped((tok, width), F32),
        "layer_out",
        deps,
        grid=(tok // TILE,),
        cost_estimate=cost(4e9, 1e7),
    )


def nothing_kernel(*refs):
    pass


def hand_call(arrays, deps):
    return call(
        nothing_kernel, arrays, [ANYWHERE] * len(arrays), [ANYWHERE] * len(arrays),
        [shaped(array.shape, array.dtype) for array in arrays], "hand", deps,
        input_output_aliases={at: at for at in range(len(arrays))},
    )


def keep_kernel(*refs):
    half = len(refs) // 2
    for source, target in zip(refs[:half], refs[half:]):
        target[...] = source[...]


def keep_call(arrays, deps=()):
    specs = [whole(array.shape) for array in arrays]
    return call(
        keep_kernel, arrays, specs, specs, [shaped(a.shape, a.dtype) for a in arrays], "keep", deps,
        cost_estimate=cost(4e9, 1e7),
    )


def last_kernel(x_ref, gx_ref, gh_a, gh_b, norm_ref, out_ref):
    n1, inv = normalized(x_ref[...].astype(F32))
    e = (gh_a[...].astype(F32) + gh_b[...].astype(F32)) * norm_ref[0:1]
    out_ref[...] = gx_ref[...] + inv * (
        e - jnp.mean(e, axis=-1, keepdims=True) - n1 * jnp.mean(e * n1, axis=-1, keepdims=True)
    )


def last_call(x, gx, gh_a, gh_b, norms):
    tok, width = x.shape
    return call(
        last_kernel,
        (x, gx, gh_a, gh_b, norms),
        [rows(width)] * 4 + [whole(norms.shape)],
        rows(width),
        shaped((tok, width), F32),
        "last_back",
        grid=(tok // TILE,),
        cost_estimate=cost(1e6, 1.2e7),
    )


def layout_kernel(core_ref, len_ref, freq_ref, bias_ref, cos_ref, sin_ref, row_ref, col_ref, bm_ref, bo_ref, bup_ref, start_ref):
    tok = cos_ref.shape[1]
    docs = len_ref.shape[1]
    begin, best, start = 0, len_ref[0, 0], 0
    begins, ends = [], []
    for doc in range(docs):
        size = len_ref[0, doc]
        if doc:
            start = jnp.where(size > best, begin, start)
            best = jnp.maximum(size, best)
        begins.append(begin)
        begin = begin + size
        ends.append(begin)
    start_ref[0] = start + jnp.zeros((), I32)

    def origin(places):
        at = places + start
        return jnp.where(at >= tok, at - tok, at)

    def document(at):
        return sum(((at >= end).astype(I32) for end in ends), jnp.zeros(at.shape, I32))

    row = origin(lax.broadcasted_iota(I32, (1, tok), 1))
    first = jnp.zeros((1, tok), I32)
    for begin in begins[1:]:
        first = jnp.where(row >= begin, begin, first)
    angles = freq_ref[...] * (row - first).astype(F32)
    cos_ref[...] = jnp.cos(angles)
    sine = jnp.sin(angles)
    sin_ref[...] = jnp.where(core_ref[0] == 0, sine, -sine)
    column = jnp.transpose(jnp.broadcast_to(bias_ref[...], (LANES, bias_ref.shape[1])))[:, 0:1]
    lower, upper = (
        jnp.concatenate(
            [column[at : at + HALF] for at in range(begin, column.shape[0], HEAD_DIM)], axis=0
        )
        for begin in (0, HALF)
    )
    swapped = core_ref[0] == 1
    mine, other = jnp.where(swapped, upper, lower), jnp.where(swapped, lower, upper)
    count = bm_ref.shape[1]
    for which, (half, ref) in enumerate(((mine, bm_ref), (other, bo_ref))):
        turned = jnp.transpose(jnp.broadcast_to(half, (half.shape[0], LANES)))[0:1]
        length = half.shape[0] - count
        ref[...] = turned[:, :count]
        bup_ref[:, which * length : (which + 1) * length] = turned[:, count:]
    rest = row_ref.shape[1]
    row_ref[...] = document(row[:, tok - rest :])
    col_ref[...] = document(origin(lax.broadcasted_iota(I32, (rest, 1), 0) + (tok - rest)))


def layout_call(core, lengths, biases, tok, n_qkv, deps=()):
    rest, n_up = tok - LONGEST, biases.shape[1] - 2 * n_qkv
    freq = np.float32(10000.0) ** -(np.arange(0, HEAD_DIM, 2).astype(np.float32) / HEAD_DIM)
    return call(
        layout_kernel,
        (core[None], lengths, jnp.asarray(freq[:, None], F32), biases),
        [SMEM, SMEM, whole((HALF, 1)), whole(biases.shape)],
        [whole((HALF, tok))] * 2
        + [whole((1, rest)), whole((rest, 1)), whole((1, n_qkv)), whole((1, n_qkv)), whole((1, n_up)), SMEM],
        [shaped((HALF, tok), F32)] * 2
        + [
            shaped((1, rest), I32), shaped((rest, 1), I32), shaped((1, n_qkv), F32),
            shaped((1, n_qkv), F32), shaped((1, n_up), F32), shaped((1,), I32),
        ],
        "layout",
        deps,
    )


def halves_kernel(core_ref, table_ref, mine_ref, other_ref):
    first = core_ref[0] == 0
    count = mine_ref.shape[1]
    upper, lower = table_ref[:, :count, :], table_ref[:, count:, :]
    mine_ref[...] = jnp.where(first, upper, lower).astype(BF)
    other_ref[...] = jnp.where(first, lower, upper).astype(BF)


def halves_call(core, table):
    cap, count, width = table.shape
    half = (cap, count // 2, width)
    return call(
        halves_kernel,
        (core[None], table),
        [SMEM, whole(table.shape)],
        [whole(half)] * 2,
        [shaped(half, BF)] * 2,
        "halves",
    )


def by_heads(kernel, which):
    def each(*refs):
        for head in range(HEADS_EACH):
            views = []
            for ref, dim in zip(refs, which):
                if dim is not None:
                    size = ref.shape[dim] // HEADS_EACH
                    ref = ref.at[(slice(None),) * dim + (pl.ds(head * size, size),)]
                views.append(ref)
            kernel(*views)

    return each


def attend_kernel(q_begin, q_end, last, safe_ref, seg_row, seg_col, m_ref, o_ref, ctx_ref, log_ref):
    tok = m_ref.shape[2]
    rest = tok - LONGEST
    span = slice(q_begin, tok if last else q_end)
    keys = tok if last else LONGEST
    q_t, k_t, v_t = (jnp.concatenate([m_ref[j], o_ref[j]], axis=0) for j in range(3))
    k_t, v_t = k_t[:, :keys], v_t[:, :keys]
    qs = q_t[:, span].astype(F32) * SCALE_LOG2
    hi, lo = split_two(qs)
    qx = jnp.transpose(jnp.concatenate([hi, lo], axis=0)).astype(BF)
    kx = jnp.concatenate([k_t, k_t], axis=0)
    v_f = v_t.astype(F32)
    vx = jnp.transpose(jnp.concatenate([v_f, jnp.ones((8, keys), F32)], axis=0)).astype(BF)
    safe = safe_ref[0] > 0

    def finish(sums, shift, at, count):
        turned = jnp.transpose(sums)
        total = turned[HEAD_DIM : HEAD_DIM + 1]
        ctx = (turned[0:HEAD_DIM] / total).astype(BF)
        ctx_ref[0, :, at : at + count] = ctx[:HALF]
        ctx_ref[1, :, at : at + count] = ctx[HALF:]
        log_total = jnp.log2(total)
        if shift is not None:
            log_total = log_total + jnp.transpose(jnp.broadcast_to(shift, (count, LANES)))[0:1]
        log_ref[0, :, at : at + count] = log_total

    def run(exact):
        for at in range(0, q_end - q_begin, TILE):
            scores = dot_nn(qx[at : at + TILE], kx[:, :LONGEST])
            shift = None
            if exact:
                shift = jnp.max(scores, axis=1, keepdims=True)
                scores = scores - shift
            finish(dot_nn(jnp.exp2(scores).astype(BF), vx[:LONGEST]), shift, at, TILE)
        if last and rest:
            at = LONGEST - q_begin
            same = seg_col[...] == seg_row[...]
            scores = jnp.where(same, dot_nn(qx[at:], kx[:, LONGEST:]), NEG_FILL)
            shift = None
            if exact:
                shift = jnp.max(scores, axis=1, keepdims=True)
                scores = scores - shift
            finish(dot_nn(jnp.exp2(scores).astype(BF), vx[LONGEST:]), shift, at, rest)

    @pl.when(safe)
    def _():
        run(False)

    @pl.when(jnp.logical_not(safe))
    def _():
        run(True)


def attend_call(q_begin, q_end, safe, segs, qkv_m, qkv_o, deps=()):
    tok = qkv_m.shape[2]
    rest = segs[0].shape[1]
    last = q_end == LONGEST
    count, length = qkv_m.shape[1] // HALF, (tok if last else q_end) - q_begin
    part = pl.BlockSpec((3, HEADS_EACH * HALF, tok), lambda h: (0, h, 0))
    return call(
        by_heads(
            functools.partial(attend_kernel, q_begin, q_end, last), (None, None, None, 1, 1, 1, 0)
        ),
        (safe, *segs, qkv_m, qkv_o),
        [SMEM, whole((1, rest)), whole((rest, 1)), part, part],
        [
            pl.BlockSpec((2, HEADS_EACH * HALF, length), lambda h: (0, h, 0)),
            pl.BlockSpec((HEADS_EACH, 1, length), lambda h: (h, 0, 0)),
        ],
        [shaped((2, count * HALF, length), BF), shaped((count, 1, length), F32)],
        "attend",
        deps,
        grid=(count // HEADS_EACH,),
        cost_estimate=cost(count * 1.2e9, 3e6),
    )


def attend_back_kernel(
    q_begin, q_end, last, seg_row, seg_col, cos_ref, sin_ref, m_ref, o_ref, g_ref, ctx_ref, log_ref,
    *refs,
):
    tok = m_ref.shape[2]
    rest = tok - LONGEST
    end = tok if last else q_end
    span = slice(q_begin, end)
    q_t, k_t, v_t = (jnp.concatenate([m_ref[j], o_ref[j]], axis=0) for j in range(3))
    q_f = q_t[:, span].astype(F32)
    ctx = jnp.concatenate([ctx_ref[0], ctx_ref[1]], axis=0).astype(F32)
    g_f = jnp.concatenate([g_ref[0], g_ref[1]], axis=0).astype(F32)
    hi, lo = split_two(q_f * SCALE_LOG2)
    weighted = jnp.sum(g_f * ctx, axis=0, keepdims=True)
    pad = jnp.zeros((13, end - q_begin), F32)
    qx = jnp.concatenate([hi, lo, *split_three(log_ref[0]), pad], axis=0).astype(BF)
    keys = tok if last else LONGEST
    k_f, v_f = k_t[:, :keys].astype(F32), v_t[:, :keys].astype(F32)
    minus = jnp.concatenate([jnp.full((3, keys), -1.0, F32), jnp.zeros((13, keys), F32)], axis=0)
    kx = jnp.transpose(jnp.concatenate([k_f, k_f, minus], axis=0)).astype(BF)
    gx = jnp.concatenate([g_f, *split_three(weighted), pad], axis=0).astype(BF)
    vx = jnp.transpose(jnp.concatenate([v_f, minus], axis=0)).astype(BF)
    qn = jnp.transpose(q_f).astype(BF)
    gn = jnp.transpose(g_f).astype(BF)

    if last:
        early_q, early_kv, out_ref = refs
    else:
        out_q, out_kv = refs

    def turned_back(grad, at, count):
        cos, sin = cos_ref[:, at : at + count], sin_ref[:, at : at + count]
        mine, other = grad[0:HALF] * SCALE, grad[HALF:] * SCALE
        return (mine * cos + other * sin).astype(BF), (other * cos - mine * sin).astype(BF)

    def block(k_at, k_count, q_at, q_count, mask, early):
        scores = dot_nn(kx[k_at : k_at + k_count], qx[:, q_at : q_at + q_count])
        if mask is not None:
            scores = jnp.where(mask, scores, NEG_FILL)
        prob = jnp.exp2(scores)
        grad_prob = dot_nn(vx[k_at : k_at + k_count], gx[:, q_at : q_at + q_count])
        grad_score = (prob * grad_prob).astype(BF)
        grad_v = jnp.transpose(dot_nn(prob.astype(BF), gn[q_at : q_at + q_count]))
        grad_k = jnp.transpose(dot_nn(grad_score, qn[q_at : q_at + q_count]))
        here = slice(k_at, k_at + k_count)
        if not last:
            out_kv[0, 0, :, here] = grad_k
            out_kv[1, 0, :, here] = grad_v
        else:
            if early:
                grad_k = grad_k + early_kv[0, 0, :, here]
                grad_v = grad_v + early_kv[1, 0, :, here]
            out_ref[0, 1, :, here], out_ref[1, 1, :, here] = turned_back(grad_k, k_at, k_count)
            out_ref[0, 2, :, here] = grad_v[:HALF].astype(BF)
            out_ref[1, 2, :, here] = grad_v[HALF:].astype(BF)
        return dot_nn(k_t[:, k_at : k_at + k_count], grad_score)

    grad_q = None
    for at in range(0, LONGEST, TILE):
        piece = block(at, TILE, 0, q_end - q_begin, None, True)
        grad_q = piece if grad_q is None else grad_q + piece
    mine, other = turned_back(grad_q, q_begin, q_end - q_begin)
    if not last:
        out_q[0], out_q[1] = mine, other
        return
    out_ref[0, 0, :, :q_begin] = early_q[0]
    out_ref[1, 0, :, :q_begin] = early_q[1]
    out_ref[0, 0, :, q_begin:q_end] = mine
    out_ref[1, 0, :, q_begin:q_end] = other
    if rest:
        same = seg_col[...] == seg_row[...]
        piece = block(LONGEST, rest, LONGEST - q_begin, rest, same, False)
        out_ref[0, 0, :, LONGEST:], out_ref[1, 0, :, LONGEST:] = turned_back(piece, LONGEST, rest)


def attend_back_call(
    q_begin, q_end, segs, cos, sin, qkv_m, qkv_o, g_ctx, ctx, logs, first, count, early=(), deps=()
):
    tok = qkv_m.shape[2]
    last = len(early) > 0
    rest = segs[0].shape[1]
    each = HEADS_EACH
    first = first // each
    part = pl.BlockSpec((3, each * HALF, tok), lambda h: (0, first + h, 0))
    table = whole((HALF, tok))

    def by_head(length, offset=0):
        return pl.BlockSpec((2, each * HALF, length), lambda h: (0, offset + h, 0))

    pair = pl.BlockSpec((2, each, HEAD_DIM, LONGEST), lambda h: (0, h, 0, 0))
    if last:
        out_specs = [pl.BlockSpec((2, 3, each * HALF, tok), lambda h: (0, 0, h, 0))]
        out_shape = [shaped((2, 3, count * HALF, tok), BF)]
    else:
        out_specs = [by_head(q_end), pair]
        out_shape = [
            shaped((2, count * HALF, q_end), BF), shaped((2, count, HEAD_DIM, LONGEST), F32)
        ]
    return call(
        by_heads(
            functools.partial(attend_back_kernel, q_begin, q_end, last),
            (None,) * 4 + (1, 1, 1, 1, 0, 1, 1) + ((2,) if last else ()),
        ),
        (*segs, cos, sin, qkv_m, qkv_o, g_ctx, ctx, logs, *early),
        [
            whole((1, rest)), whole((rest, 1)), table, table, part, part,
            by_head(g_ctx.shape[2], first), by_head(ctx.shape[2], first),
            pl.BlockSpec((each, 1, logs.shape[2]), lambda h: (first + h, 0, 0)),
        ]
        + ([by_head(q_begin), pair] if last else []),
        out_specs,
        out_shape,
        "attend_back",
        deps,
        grid=(count // each,),
        cost_estimate=cost(count * 2.1e9, 6e6),
    )


class Routes:
    def __init__(self, dp_size, slot_cap, pieces, ready, spans):
        self.dp = dp_size
        self.cap = slot_cap
        self.chips = dp_size // 2
        self.pieces = pieces
        self.ready = ready
        self.spans = spans
        if self.chips == 8:
            self.stages = ((2, 4), (1, 2))
        elif self.chips == 64:
            self.stages = ((1, 8), (8, 2), (16, 4))
        else:
            self.stages = ((1, self.chips),)
        self.depth = len(self.stages)
        straight = self.stages[::-1]
        paired = ((1, 2), (4, 2), (2, 2)) if self.chips == 8 else straight
        self.back = (straight, paired)
        self.out = (self.stages, ((4, 2), (2, 2), (1, 2)) if self.chips == 8 else self.stages)
        self.fill = [self.limit(last, self.chips) for last in ready]
        self.begins = [0] + self.fill[:-1]
        early, late = self.fill[0], self.fill[1] - self.fill[0]
        if self.chips == 8:
            self.bases = (
                [at * early for at in range(4)]
                + [4 * early]
                + [4 * early + self.fill[1] + at * early for at in range(3)],
                [7 * early + self.fill[1] + at * late for at in range(4)]
                + [5 * early]
                + [7 * early + self.fill[1] + at * late for at in range(4, 7)],
            )
        else:
            self.bases = tuple(
                [begin * self.chips + at * (end - begin) for at in range(self.chips)]
                for begin, end in zip(self.begins, self.fill)
            )

    def limit(self, count, groups):
        worst = min(count, self.dp // groups * self.cap)
        if self.chips != 8:
            return worst
        typical = {
            2: count * 11 // 20 + 8, 4: count * 3 // 10 + 10, 8: count // 5 + 5
        }[groups]
        return worst if count == self.pieces else min(worst, typical)

    def span_limit(self, number, level):
        groups = 1
        for _, size in self.back[number][:level]:
            groups *= size
        return self.limit(self.spans[number][1] - self.spans[number][0], groups)

    def move(self, array, stage, shift):
        stride, size = stage
        pairs = []
        for device in range(self.dp):
            chip, core = device // 2, device % 2
            at = (chip // stride) % size
            pairs.append((device, 2 * (chip + ((at + shift) % size - at) * stride) + core))
        return lax.ppermute(array, "dp", pairs)

    def swap_cores(self, array):
        return lax.ppermute(array, "dp", [(d, d ^ 1) for d in range(self.dp)])

    def around(self, array, stage):
        return [array] + [self.move(array, stage, shift) for shift in range(1, stage[1])]

    def onward(self, buffers, stage):
        return buffers + [
            self.move(buffer, stage, shift) for shift in range(1, stage[1]) for buffer in buffers
        ]

    def tables(self, owners, me):
        place = {}

        def kernel(me_ref, own_ref, out_ref, row_ref):
            here = me_ref[0]
            my_chip, my_core = here // 2, here % 2
            row_ref[...] = jnp.full((1, LANES), -2, I32)
            row_ref[:, : self.pieces] = own_ref[...]
            row = row_ref[...]
            col = jnp.transpose(jnp.broadcast_to(row, (LANES, LANES)))[:, 0:1]
            id_row = lax.broadcasted_iota(I32, (1, LANES), 1)
            id_col = lax.broadcasted_iota(I32, (LANES, 1), 0)
            lane = lax.broadcasted_iota(I32, (LANES, LANES), 1)
            sub = lax.broadcasted_iota(I32, (LANES, LANES), 0)

            def rank_col(key_row, key_col):
                hit = (key_row == key_col) & (lane < sub)
                return jnp.sum(hit.astype(F32), axis=1, keepdims=True).astype(I32)

            def rank_row(key_row, key_col):
                hit = (key_row == key_col) & (sub < lane)
                return jnp.sum(hit.astype(F32), axis=0, keepdims=True).astype(I32)

            def gather(valid_col, entry_col, value_col):
                hit = valid_col & (entry_col == lane)
                return jnp.sum(
                    jnp.where(hit, value_col.astype(F32), 0.0), axis=0, keepdims=True
                ).astype(I32)

            def put(name, value):
                at = place.setdefault(name, len(place))
                out_ref[at : at + 1, :] = value

            def coord(chip, stage):
                return (chip // stage[0]) % stage[1]

            def group(chip, stages):
                key = 0
                for stage in stages:
                    key = key * stage[1] + coord(chip, stage)
                return key

            def fullest(inside, rank):
                return jnp.max(jnp.where(inside, rank, -1), axis=0, keepdims=True) + 1

            slot_col = rank_col(row, col)
            put("piece", gather(col == here, slot_col, id_col + 1) - 1)
            sibling = my_chip * 2 + 1 - my_core
            put("sibling", gather(col == sibling, slot_col, id_col + 1) - 1)
            over = jnp.zeros((1, 1), I32)
            real = id_col < self.pieces
            chip_col, chip_row = col // 2, row // 2
            rank_c, rank_r = rank_col(chip_row, chip_col), rank_row(chip_row, chip_col)
            from_core = jnp.where(col % 2 == my_core, 0, self.cap)
            put("send", gather(real & (chip_col == my_chip), rank_c, from_core + slot_col))
            for last, fill in zip(self.ready, self.fill):
                over = jnp.maximum(over, fullest(id_col < last, rank_c) - fill)
            put("late", jnp.broadcast_to(over, (1, LANES)))
            over = jnp.zeros((1, 1), I32)
            take = jnp.zeros((1, LANES), I32)
            for begin, bases, stages in zip(self.begins, self.bases, self.out):
                way, scale = jnp.zeros((1, LANES), I32), 1
                for stage in stages:
                    away = (coord(my_chip, stage) - coord(chip_row, stage) + stage[1]) % stage[1]
                    way = way + away * scale
                    scale = scale * stage[1]
                spot = rank_r - begin
                for at, base in enumerate(bases):
                    spot = spot + jnp.where(way == at, base, 0)
                take = jnp.where(rank_r >= begin, spot, take)
            put("take", take)
            for number, span in enumerate(self.spans):
                in_col = (id_col >= span[0]) & (id_col < span[1])
                in_row = (id_row >= span[0]) & (id_row < span[1])
                stages = self.back[number]
                ranks = {}
                for level in range(1, len(stages) + 1):
                    key_col = jnp.where(in_col, group(chip_col, stages[:level]), -1)
                    key_row = jnp.where(in_row, group(chip_row, stages[:level]), -1)
                    ranks[level] = rank_col(key_row, key_col)
                    over = jnp.maximum(
                        over, fullest(in_col, ranks[level]) - self.span_limit(number, level)
                    )
                value = id_col - span[0]
                for level, stage in enumerate(stages, 1):
                    size = stage[1]
                    inside = in_col & (
                        group(chip_col, stages[: level - 1]) == group(my_chip, stages[: level - 1])
                    )
                    for shift in range(size):
                        goal = (coord(my_chip, stage) + shift) % size
                        put(
                            ("back", number, level, shift),
                            gather(inside & (coord(chip_col, stage) == goal), ranks[level], value),
                        )
                    value = ranks[level]
                for which in range(2):
                    goal = my_chip * 2 + (my_core + which) % 2
                    put(
                        ("slot", number, which),
                        gather(in_col & (col == goal), slot_col, ranks[len(stages)]),
                    )
            put("over", jnp.broadcast_to(over, (1, LANES)))

        count = 6 + sum(2 + sum(size for _, size in stages) for stages in self.back)
        height = -(-count // 8) * 8
        table = pl.pallas_call(
            kernel,
            in_specs=[SMEM, whole((1, self.pieces))],
            out_specs=whole((height, LANES)),
            out_shape=shaped((height, LANES), I32),
            scratch_shapes=[pltpu.VMEM((1, LANES), I32)],
            compiler_params=params(),
            name="routes",
        )(me[None], owners[None, :])
        return table, place


def fetch(sources, targets, sems):
    copies = [
        pltpu.make_async_copy(source, target, sems.at[at])
        for at, (source, target) in enumerate(zip(sources, targets))
    ]
    for copy in copies:
        copy.start()
    for copy in copies:
        copy.wait()


def places(kept, parts):
    return [ANYWHERE] * kept + [HBM] * (len(parts) - kept)


def pick_call(table, picks, parts, sizes, name, deps=(), kept=1):
    rows_each = [part.shape[0] for part in parts]
    shape = parts[0].shape[1:]

    def kernel(table_ref, *refs):
        ins, (*outs, source, sems) = refs[: len(parts)], refs[len(parts) :]
        at, targets = 0, []
        for count in rows_each:
            targets.append(source.at[pl.ds(at, count)])
            at += count
        fetch(ins, targets, sems)
        for (row, start), size, out in zip(picks, sizes, outs):
            for j in range(size):
                out[j] = source[table_ref[row, start + j]]

    return call(
        kernel,
        (table, *parts),
        [SMEM] + places(kept, parts),
        [whole((size,) + shape) for size in sizes],
        [shaped((size,) + shape, BF) for size in sizes],
        name,
        deps,
        scratch=[
            pltpu.VMEM((sum(rows_each),) + shape, BF), pltpu.SemaphoreType.DMA((len(parts),)),
        ],
    )


def join_call(parts, deps=()):
    counts = [part.shape[0] for part in parts]
    shape = (sum(counts),) + parts[0].shape[1:]

    def kernel(*refs):
        *ins, out, sems = refs
        at, targets = 0, []
        for count in counts:
            targets.append(out.at[pl.ds(at, count)])
            at += count
        fetch(ins, targets, sems)

    return call(
        kernel, parts, places(0, parts), whole(shape), shaped(shape, BF), "join", deps,
        scratch=[pltpu.SemaphoreType.DMA((len(parts),))],
    )


def add_pick_call(table, picks, parts, sizes, small=None, extra=(), deps=()):
    shape = parts[0].shape[1:]
    lengths = [size + (j in extra) for j, size in enumerate(sizes)]

    def kernel(table_ref, *refs):
        sources, refs = refs[: len(parts)], refs[len(parts) :]
        ins, sems, refs = refs[-len(parts) - 1 : -1], refs[-1], refs[: -len(parts) - 1]
        fetch(sources, ins, sems)
        if small is not None:
            small_ref, refs = refs[0], refs[1:]
            terms = [small_ref[...]] + [
                unpack_small(ref[ref.shape[0] - 1]) for ref in ins[1:]
            ]
            while len(terms) > 1:
                middle = len(terms) // 2
                terms = [a + b for a, b in zip(terms[:middle], terms[middle:])]
            packed = pack_small(terms[0])
            refs[len(sizes)][...] = unpack_small(packed)
            for j in extra:
                refs[j][sizes[j]] = packed
        for (row, start), size, out in zip(picks, sizes, refs):
            for j in range(size):
                at = table_ref[row, start + j]
                total = ins[0][at].astype(F32)
                for ref in ins[1:]:
                    total = total + ref[at].astype(F32)
                out[j] = total.astype(BF)

    out_specs = [whole((length,) + shape) for length in lengths]
    out_shape = [shaped((length,) + shape, BF) for length in lengths]
    if small is not None:
        out_specs, out_shape = out_specs + [whole(shape)], out_shape + [shaped(shape, F32)]
    return call(
        kernel,
        (table, *parts) + (() if small is None else (small,)),
        [SMEM] + places(1, parts) + ([] if small is None else [whole(shape)]),
        out_specs,
        out_shape,
        "add_pick",
        late=deps,
        scratch=[pltpu.VMEM(part.shape, BF) for part in parts]
        + [pltpu.SemaphoreType.DMA((len(parts),))],
    )


def owned_call(table, place, routes, parts, small, deps=()):
    (parts_in, parts_mlp), cap = parts, routes.cap
    parts = (*parts_in, *parts_mlp)
    shape = parts_in[0].shape[1:]
    border = routes.spans[1][0]

    def kernel(table_ref, *refs):
        sources, refs = refs[: len(parts)], refs[len(parts) :]
        small_ref, kept_ref, sent_ref, total_ref, *held, sems = refs
        fetch(sources, held, sems)
        ins, mlps = held[: len(parts_in)], held[len(parts_in) :]
        terms = [small_ref[...]] + [
            unpack_small(ref[ref.shape[0] - 1]) for ref in ins[1:]
        ]
        while len(terms) > 1:
            middle = len(terms) // 2
            terms = [a + b for a, b in zip(terms[:middle], terms[middle:])]
        total_ref[...] = terms[0]
        for which, (name, out) in enumerate((("piece", kept_ref), ("sibling", sent_ref))):
            for j in range(cap):
                sums = []
                for number, some in enumerate((ins, mlps)):
                    at = table_ref[place[("slot", number, which)], j]
                    total = some[0][at].astype(F32)
                    for ref in some[1:]:
                        total = total + ref[at].astype(F32)
                    sums.append(total)
                out[j] = jnp.where(table_ref[place[name], j] >= border, sums[1], sums[0])

    args = (table, *parts_in, *parts_mlp, small)
    return call(
        kernel,
        args,
        [SMEM]
        + places(1, parts_in)
        + places(1, parts_mlp)
        + [whole(shape)],
        [whole((cap,) + shape)] * 2 + [whole(shape)],
        [shaped((cap,) + shape, F32)] * 2 + [shaped(shape, F32)],
        "owned",
        deps,
        scratch=[pltpu.VMEM(part.shape, BF) for part in parts]
        + [pltpu.SemaphoreType.DMA((len(parts),))],
    )


def adam_step(weights, first_mom, second_mom, gradient, rate, decay_rate):
    first_new = BETA_ONE * first_mom + (1.0 - BETA_ONE) * gradient
    second_new = BETA_TWO * second_mom + (1.0 - BETA_TWO) * gradient * gradient
    first_fix = first_new / (1.0 - BETA_ONE**STEP)
    second_fix = second_new / (1.0 - BETA_TWO**STEP)
    weights_new = weights * (1.0 - rate * decay_rate) - rate * first_fix / (
        jnp.sqrt(second_fix) + ADAM_EPS
    )
    return (weights_new, first_new, second_new)


def adam_call(table, row, core, borders, kept, arrived, tables):
    cap, count, width = tables[0].shape
    half = count // 2
    group = max(g for g in range(1, 6) if cap % g == 0)

    def kernel(table_ref, core_ref, kept_ref, arrived_ref, w_ref, m_ref, v_ref, *outs):
        step = pl.program_id(0)
        swapped = core_ref[0] == 1
        for j in range(group):
            piece = table_ref[row, step * group + j]
            rate = jnp.where(piece < borders[2], 0.03, 0.015)
            rate = jnp.where(piece < borders[1], 0.2, rate)
            rate = jnp.where(piece < borders[0], 0.03, rate).astype(F32)
            halves = (kept_ref[j], arrived_ref[j])
            for at in range(2):
                here = pl.ds(at * half, half)
                grad = jnp.where(swapped, halves[1 - at], halves[at])
                new = adam_step(w_ref[j, here], m_ref[j, here], v_ref[j, here], grad, rate, DECAY_RATE)
                for out, value in zip(outs, new):
                    out[j, here] = jnp.where(piece >= 0, value, 0.0)

    def block(rows_each):
        return pl.BlockSpec((group, rows_each, width), lambda t: (t, 0, 0))

    return call(
        kernel,
        (table, core[None], kept, arrived, *tables),
        [SMEM, SMEM, block(half), block(half)] + [block(count)] * 3,
        [block(count)] * 3,
        [shaped((cap, count, width), F32)] * 3,
        "adam",
        grid=(cap // group,),
        cost_estimate=cost(1e7, 8e6),
    )


def small_kernel(total_ref, far_ref, norm_ref, nm_ref, nv_ref, bias_ref, bm_ref, bv_ref, *outs):
    gains = total_ref[0:2, :] + far_ref[0:2, :]
    for at, rate in enumerate(NORM_RATES):
        here = slice(at, at + 1)
        grad = gains[here] if at < 2 else total_ref[here, :]
        new = adam_step(norm_ref[here, :], nm_ref[here, :], nv_ref[here, :], grad, rate, 0.0)
        for out, value in zip(outs[:3], new):
            out[here, :] = value
    width = total_ref.shape[1]
    for at in range(0, bias_ref.shape[1], width):
        here = slice(at, min(at + width, bias_ref.shape[1]))
        row = 6 + at // width
        grad = total_ref[row : row + 1, : here.stop - at]
        new = adam_step(bias_ref[:, here], bm_ref[:, here], bv_ref[:, here], grad, BIAS_RATE, 0.0)
        for out, value in zip(outs[3:], new):
            out[:, here] = value


def small_call(total, far, norms, biases, deps=()):
    args = (total, far, *norms, *biases)
    kept = [shaped(part.shape, F32) for part in (*norms, *biases)]
    return call(
        small_kernel, args, [whole(arg.shape) for arg in args], [whole(k.shape) for k in kept], kept, "small_update",
        deps,
    )


def swap_mp(array):
    return lax.ppermute(array, "mp", [(0, 1), (1, 0)])


def roll_rows(array, start):
    return lax.dynamic_slice_in_dim(
        jnp.concatenate([array, array], axis=0), start, array.shape[0], axis=0
    )


def body(
    tokens, cotangent, lengths, owners, weight_table, moment_table, square_table,
    norm_params, norm_moment, norm_square, bias_params, bias_moment, bias_square,
):
    dp_size = lax.axis_size("dp")
    mp_size = lax.axis_size("mp")
    heads = HEADS // mp_size
    head_width = heads * HEAD_DIM
    hidden = FF // mp_size
    tok, width = tokens.shape
    slot_cap, piece_len = weight_table.shape[1:3]
    half_len = piece_len // 2
    piece_total = owners.shape[0]
    me = lax.axis_index("dp").astype(I32)
    core = me % 2
    first_core = core == 0

    n_qkv, n_out = 3 * head_width // piece_len, head_width // piece_len
    n_up = hidden // piece_len
    n_first = n_qkv + n_out
    ready = (n_first, piece_total)
    spans = ((0, n_first), (n_first, piece_total))
    routes = Routes(dp_size, slot_cap, piece_total, ready, spans)
    table, place = routes.tables(owners, me)

    own_half, sibling_half = halves_call(core, weight_table[0])
    chip_slots = [own_half, routes.swap_cores(sibling_half)]

    def half(array, which):
        return lax.dynamic_index_in_dim(array, which, axis=1, keepdims=False)

    def unless(bad, usual, other):
        return lax.while_loop(
            lambda state: state[0] > 0, lambda state: (jnp.zeros((), I32), other()), (bad, usual)
        )[1]

    def own_lists(ranges, deps=()):
        return pick_call(
            table, [(place["send"], begin) for begin, _ in ranges], chip_slots,
            [end - begin for begin, end in ranges], "pick_owned", deps,
        )

    def collect(buffers, ranges, deps=()):
        sizes = [high - low for low, high in ranges]
        return pick_call(
            table, [(place["take"], low) for low, _ in ranges], buffers, sizes, "pick_all", deps
        )

    def flat(array):
        return array.reshape(-1, width)

    def pairs_apart(bit):
        return [(device, device ^ bit) for device in range(dp_size)]

    def slow_first():
        everyone, bit = weight_table[0].astype(BF), 1
        while bit < dp_size:
            everyone = jnp.concatenate([everyone, lax.ppermute(everyone, "dp", pairs_apart(bit))], 0)
            bit *= 2
        earlier = (owners[None, :] == owners[:, None]) & (
            jnp.arange(piece_total)[None, :] < jnp.arange(piece_total)[:, None]
        )
        at = (owners ^ me) * slot_cap + jnp.sum(earlier.astype(I32), axis=1)
        mine = half(everyone[at[:n_first]].reshape(n_first, 2, half_len, width), core)
        return mine, mine[n_qkv:]

    stages = routes.out
    chunks = tuple(zip(routes.begins, routes.fill))
    relayed = routes.chips == 8
    if relayed:
        list_a, list_all = ticked(own_lists, (chunks[0], (0, routes.fill[1])))
    else:
        list_a, list_b = ticked(own_lists, [chunk for chunk in chunks if chunk[0] < chunk[1]] * 2)[:2]
    listed = Clock.tick
    list_a = routes.around(list_a, stages[0][0])
    cos, sin, *segs, b_mine, b_other, b_up, start = layout_call(
        core, lengths, bias_params, tok, 3 * head_width // 2, (listed,)
    )
    x, a1 = ticked(norm_call, start, tokens, norm_params)
    gy = ticked(roll_call, start, cotangent, (Clock.tick,))
    turned = Clock.tick

    if relayed:
        own_y = routes.move(list_all, stages[0][1], 1)
        arrived = ticked(join_call, list_a[1:], (turned,))
        buffers_a = list_a + [own_y, routes.move(arrived, stages[0][1], 1)]
        (list_b,) = own_lists(chunks[1:], (Clock.tick, own_y))
        from_two, from_one = (routes.move(list_b, stage, 1) for stage in stages[1][:2])
        joined = ticked(join_call, [from_two, from_one])
        turned = Clock.tick
        relay = routes.move(from_two, stages[1][1], 1)
        y_joined = routes.move(joined, stages[1][2], 1)
    else:
        buffers_a, buffers_b = list_a, [list_b]
        for stage in stages[0][1:]:
            buffers_a = routes.onward(buffers_a, stage)
    w_first_m, w_out_x = ticked(collect, buffers_a, ((0, n_first), (n_qkv, n_first)), (turned,))
    collected = Clock.tick
    w_first_m, w_out_x = unless(table[place["late"], 0], (w_first_m, w_out_x), slow_first)
    b_qkv = keep_call((b_mine, b_other), (collected,))
    w_first_o = routes.swap_cores(w_first_m)
    qkv_m, qkv_o, safe = ticked(
        qkv_call, a1, flat(w_first_m), flat(w_first_o), *b_qkv, cos, sin
    )
    w_out_x = swap_mp(w_out_x)
    if relayed:
        relay = ticked(join_call, [relay], (Clock.tick,))
        collected = Clock.tick
        y_relay = routes.move(relay, stages[1][2], 1)
        buffers_b = [list_b, from_two, from_one, relay, y_joined, y_relay]
    elif chunks[1][0] < chunks[1][1]:
        for stage in stages[1]:
            buffers_b = routes.onward(buffers_b, stage)
    else:
        buffers_b = []
    half_way = 2 * TILE
    ctx_a, logs_a = ticked(attend_call, 0, half_way, safe, segs, qkv_m, qkv_o, (collected,))
    attended = Clock.tick
    ctx_b, logs_b = attend_call(half_way, LONGEST, safe, segs, qkv_m, qkv_o, (attended,))
    (w_out_x,) = hand_call((w_out_x,), (attended,))
    w_out_x = [flat(w_out_x), flat(routes.swap_cores(w_out_x))]
    ctx_ax, ctx_bx = swap_mp(ctx_a), swap_mp(ctx_b)
    (w_mine,) = ticked(collect, buffers_a + buffers_b, ((n_first, piece_total),), (logs_b, ctx_ax))
    (b_up,) = keep_call((b_up,), (Clock.tick,))
    w_mine, w_other = flat(w_mine), flat(routes.swap_cores(w_mine))
    w_first = [flat(w_first_m), flat(w_first_o)]
    spans_tok = ((0, half_way // TILE), (half_way // TILE, tok // TILE))
    mlp_args = (w_first, w_out_x, w_mine, w_other, b_up, norm_params)
    *filled, g_h2_a, gb_up_a = mlp_call(spans_tok[0], x, gy, (ctx_a, ctx_ax), *mlp_args)
    *filled, g_h2_b, gb_up_b = mlp_call(spans_tok[1], x, gy, (ctx_b, ctx_bx), *mlp_args, filled)
    x1, a2, act, g_pre, ffn = filled
    g_h2_ax, g_h2_bx = swap_mp(g_h2_a), swap_mp(g_h2_b)
    g_mlp = mlp_grads_call(act, g_pre, a2, gy)

    def pieces(array):
        return array.reshape(-1, half_len, width)

    def sort_out(number, level, parts, small=None, deps=()):
        stage = routes.back[number][level - 1]
        size = stage[1]
        lists = ticked(
            add_pick_call,
            table,
            [(place[("back", number, level, shift)], 0) for shift in range(size)],
            parts,
            [routes.span_limit(number, level)] * size,
            small=small,
            extra=() if small is None else range(1, size),
            deps=deps,
        )
        moved = [routes.move(lists[shift], stage, shift) for shift in range(1, size)]
        return [lists[0]] + moved, lists[-1]

    gx1, g_ctx_a, g_out_a, mid_a, g_mlp_m, g_mlp_o = mid_call(
        spans_tok[0], x1, gy, g_h2_a, g_h2_ax, (ctx_a,), *w_first, norm_params, (), g_mlp
    )
    back = (segs, cos, sin, qkv_m, qkv_o)
    cut = heads // 2
    groups = ((0, cut), (cut, heads - cut))
    early_one = ticked(attend_back_call, 0, half_way, *back, g_ctx_a, ctx_a, logs_a, *groups[0])
    parts_mlp, listed = sort_out(
        1, 1, [pieces(g_mlp_m), routes.swap_cores(pieces(g_mlp_o))], deps=(Clock.tick,)
    )
    early_two = ticked(
        attend_back_call, 0, half_way, *back, g_ctx_a, ctx_a, logs_a, *groups[1], deps=(listed,)
    )
    attended = Clock.tick
    gx1, g_ctx_b, g_out_b, mid_b, ffn = mid_call(
        spans_tok[1], x1, gy, g_h2_b, g_h2_bx, (ctx_b,), *w_first, norm_params, (gx1,), (ffn,), (attended,)
    )
    ffn_other = swap_mp(ffn)

    (grads_one,) = ticked(
        attend_back_call, half_way, LONGEST, *back, g_ctx_b, ctx_b, logs_b, *groups[0], early_one
    )
    (grads_two,) = ticked(
        attend_back_call, half_way, LONGEST, *back, g_ctx_b, ctx_b, logs_b, *groups[1], early_two, (Clock.tick,)
    )
    parts_mlp, listed = sort_out(1, 2, parts_mlp, deps=(Clock.tick,))
    sorted_mlp = Clock.tick
    g_in_m, g_in_o, g_h1, small = ticked(
        in_grads_call, (grads_one, grads_two), core, a1, x, *w_first,
        (g_out_a, g_out_b), (mid_a, mid_b), (gb_up_a, gb_up_b), (listed,),
    )
    g_h1_other = swap_mp(g_h1)
    ticked(keep_call, (norm_params,), (Clock.tick,))
    filled = Clock.tick
    out_roll = out_call(x1, ffn, ffn_other, norm_params, (sorted_mlp,))
    block_out = roll_rows(out_roll, tok - start[0])
    parts_in = [pieces(g_in_m), routes.swap_cores(pieces(g_in_o))]
    for level in range(1, len(routes.back[0])):
        parts_in, small = sort_out(0, level, parts_in, small, (filled,))
    for level in range(3, len(routes.back[1]) + 1):
        parts_mlp, _ = sort_out(1, level, parts_mlp, deps=(Clock.tick,))
    parts_in, small = sort_out(0, len(routes.back[0]), parts_in, small, (block_out,))
    staged = Clock.tick
    grad_roll = ticked(last_call, x, gx1, g_h1, g_h1_other, norm_params)
    grad_tokens = roll_rows(grad_roll, tok - start[0])

    kept, sent, small = owned_call(table, place, routes, (parts_in, parts_mlp), small, (grad_tokens,))
    small_x = swap_mp(small)
    arrived = routes.swap_cores(sent)

    def slow_grads():
        def stack(in_part, mlp_part):
            return jnp.concatenate([pieces(in_part), pieces(mlp_part)], axis=0).astype(F32)

        mine, other = stack(g_in_m, g_mlp_m), stack(g_in_o[: g_in_m.shape[0]], g_mlp_o)
        both = jnp.where(first_core, jnp.stack([mine, other], 1), jnp.stack([other, mine], 1))
        total, bit = both, 1
        while bit < dp_size:
            total = total + lax.ppermute(total, "dp", pairs_apart(bit))
            bit *= 2
        total = total[jnp.maximum(table[place["piece"], :slot_cap], 0)]
        return half(total, core), half(total, 1 - core)

    tables = (weight_table[0], moment_table[0], square_table[0])

    def update(kept, arrived, tables):
        return ticked(
            adam_call, table, place["piece"], core, (n_qkv, n_first, n_first + n_up), kept, arrived, tables
        )

    tables_next = update(kept, arrived, keep_call(tables, (staged,)))
    updated = Clock.tick
    tables_next = unless(table[place["over"], 0], tuple(tables_next), lambda: tuple(update(*slow_grads(), tables)))
    small_out = small_call(
        small, small_x,
        (norm_params, norm_moment, norm_square), (bias_params, bias_moment, bias_square),
        (updated,),
    )
    return (block_out, grad_tokens, *(part[None] for part in tables_next), *small_out)


def solution(mesh):
    flat = P("dp", None)
    pieces = P("mp", "dp", None, None)
    bias = P("mp", None)
    return jax.shard_map(
        body,
        mesh=mesh,
        in_specs=(flat, flat, flat, P(), pieces, pieces, pieces, P(), P(), P(), bias, bias, bias),
        out_specs=(flat, flat, pieces, pieces, pieces, P(), P(), P(), bias, bias, bias),
        check_vma=False,
    )
```

```python
import functools

import jax
import jax.numpy as jnp
import numpy as np
from jax import lax
from jax.experimental import pallas as pl
from jax.experimental.pallas import tpu as pltpu
from jax.sharding import PartitionSpec as P

HEADS = 20
HEAD_DIM = 32
HALF = HEAD_DIM // 2
FF = 2560
LONGEST = 1024
STEP = 10

EPS_NORM = 1e-05
BETA_ONE = 0.5
BETA_TWO = 0.5
ADAM_EPS = 1e-08
DECAY_RATE = 0.01
NEG_FILL = -1e30
NORM_RATES = (0.5, 0.1, 0.5, 0.1, 0.1, 0.1)
BIAS_RATE = 0.1
SCALE = HEAD_DIM**-0.5
LOG2_E = 1.4426950408889634
SCALE_LOG2 = SCALE * LOG2_E
SAFE_EXP = 100.0

BF = jnp.bfloat16
F32 = jnp.float32
I32 = jnp.int32
TILE = 256
LANES = 128
TICK = (8, 128)
HEADS_EACH = 5
FORWARD_HEADS_EACH = 1
VMEM_LIMIT = 16 << 20
SHRINK = 0.1


def params(*kinds):
    return pltpu.CompilerParams(dimension_semantics=kinds or None, vmem_limit_bytes=VMEM_LIMIT)


def cost(flops, moved):
    return pl.CostEstimate(flops=int(flops / SHRINK), bytes_accessed=int(moved / SHRINK), transcendentals=0)


def dot_nn(a, b):
    return lax.dot_general(a, b, (((1,), (0,)), ((), ())), preferred_element_type=F32)


def dot_nt(a, b):
    return lax.dot_general(a, b, (((1,), (1,)), ((), ())), preferred_element_type=F32)


def dot_tn(a, b):
    return lax.dot_general(a, b, (((0,), (0,)), ((), ())), preferred_element_type=F32)


def split_two(v):
    hi = v.astype(BF).astype(F32)
    return hi, v - hi


def split_three(v):
    hi = v.astype(BF).astype(F32)
    mid = (v - hi).astype(BF).astype(F32)
    return hi, mid, v - hi - mid


def normalized(v):
    centred = v - jnp.mean(v, axis=-1, keepdims=True)
    inv = lax.rsqrt(jnp.mean(centred * centred, axis=-1, keepdims=True) + EPS_NORM)
    return centred * inv, inv


ANYWHERE = pl.BlockSpec(memory_space=pl.ANY)
SMEM = pl.BlockSpec(memory_space=pltpu.SMEM)
HBM = pl.BlockSpec(memory_space=pltpu.HBM)


def whole(shape):
    return pl.BlockSpec(shape, lambda *_: (0,) * len(shape))


def rows(width, begin=0):
    return pl.BlockSpec((TILE, width), lambda t: (begin + t, 0))


def cols(height, begin=0):
    return pl.BlockSpec((height, TILE), lambda t: (0, begin + t))


def both(height, begin=0):
    return pl.BlockSpec((2, height, TILE), lambda t: (0, 0, begin + t))


def last_rows(array, count):
    return pl.BlockSpec((count, array.shape[1]), lambda *_: (array.shape[0] // count - 1, 0))


def shaped(shape, dtype):
    return jax.ShapeDtypeStruct(shape, dtype)


class Clock:
    wanted = False
    tick = None


def ticked(function, *args, **named):
    Clock.wanted = True
    results = function(*args, **named)
    Clock.wanted = False
    return results


def call(kernel, args, in_specs, out_specs, out_shape, name, deps=(), scratch=(), limit=VMEM_LIMIT, late=(), **more):
    count = len(args)
    single = not isinstance(out_shape, (list, tuple))
    out_specs, out_shape = ([out_specs], [out_shape]) if single else (list(out_specs), list(out_shape))
    if any(spec is not ANYWHERE for spec in in_specs):
        more.setdefault("grid", (1,))

    if "input_output_aliases" in more:
        aliases = more["input_output_aliases"]
        more["input_output_aliases"] = {len(deps) + at: to for at, to in aliases.items()}
    real, ticks = len(out_shape), Clock.wanted
    if ticks:
        out_specs, out_shape = out_specs + [whole(TICK)], out_shape + [shaped(TICK, F32)]

    def wrapped(*refs):
        ins, outs = refs[len(deps) : len(deps) + count], refs[len(deps) + count + len(late) :]
        if ticks:
            outs[real][...] = jnp.zeros(TICK, F32)
        kernel(*ins, *outs[:real], *outs[real + ticks :])

    results = pl.pallas_call(
        wrapped,
        in_specs=[ANYWHERE] * len(deps) + list(in_specs) + [ANYWHERE] * len(late),
        out_specs=out_specs,
        out_shape=out_shape,
        scratch_shapes=list(scratch),
        compiler_params=pltpu.CompilerParams(
            dimension_semantics=("arbitrary",) * len(more.get("grid", ())) or None,
            vmem_limit_bytes=limit,
        ),
        name=name,
        **more,
    )(*deps, *args, *late)
    if ticks:
        Clock.tick = results[-1]
        results = results[:-1]
    return results[0] if single else results


def rolled(array, start):
    tok = array.shape[0]
    shift = jnp.where(start == 0, 0, tok - start)
    return pltpu.roll(array.astype(F32), shift, 0)


def roll_kernel(start_ref, array_ref, out_ref):
    out_ref[...] = rolled(array_ref[...], start_ref[0]).astype(BF)


def roll_call(start, array, deps=()):
    return call(
        roll_kernel, (start, array), [SMEM, whole(array.shape)], whole(array.shape),
        shaped(array.shape, BF), "roll", deps,
    )


def norm_kernel(start_ref, x_ref, norm_ref, out_ref, a_ref, turned):
    turned[...] = rolled(x_ref[...], start_ref[0])
    for at in range(0, x_ref.shape[0], LANES):
        here = slice(at, at + LANES)
        value = turned[here, :]
        out_ref[here, :] = value.astype(BF)
        n1, _ = normalized(value)
        a_ref[here, :] = (n1 * norm_ref[0:1] + norm_ref[1:2]).astype(BF)


def norm_call(start, x, norms):
    return call(
        norm_kernel,
        (start, x, norms),
        [SMEM, whole(x.shape), whole(norms.shape)],
        [whole(x.shape)] * 2,
        [shaped(x.shape, BF)] * 2,
        "first_norm",
        scratch=[pltpu.VMEM(x.shape, F32)],
        limit=2 * VMEM_LIMIT,
    )


def qkv_kernel(a_ref, wm_ref, wo_ref, bm_ref, bo_ref, cos_ref, sin_ref, m_ref, o_ref, safe_ref, top, bias):
    step = pl.program_id(0)

    @pl.when(step == 0)
    def _():
        top[...] = jnp.zeros_like(top)
        for which, ref in enumerate((bm_ref, bo_ref)):
            bias[which] = jnp.transpose(jnp.broadcast_to(ref[...], (LANES, ref.shape[1])))

    a1 = a_ref[...]
    mine = dot_nt(wm_ref[...], a1) + bias[0, :, 0:1]
    other = dot_nt(wo_ref[...], a1) + bias[1, :, 0:1]
    width = m_ref.shape[1]
    cos, sin = cos_ref[...], sin_ref[...]
    for which in range(2):
        longest = top[which : which + 1, :]
        for at in range(0, width, HALF):
            here = which * width + at
            p, r = mine[here : here + HALF], other[here : here + HALF]
            longest = jnp.maximum(longest, jnp.sum(p * p + r * r, axis=0, keepdims=True))
            m_ref[which, at : at + HALF, :] = (p * cos - r * sin).astype(BF)
            o_ref[which, at : at + HALF, :] = (r * cos + p * sin).astype(BF)
        top[which : which + 1, :] = longest
    m_ref[2] = mine[2 * width :].astype(BF)
    o_ref[2] = other[2 * width :].astype(BF)

    @pl.when(step == pl.num_programs(0) - 1)
    def _():
        bound = jnp.max(top[0:1, :]) * jnp.max(top[1:2, :]) * SCALE_LOG2**2
        safe_ref[0] = (bound < SAFE_EXP**2).astype(I32)


def qkv_call(a1, w_mine, w_other, b_mine, b_other, cos, sin, deps=()):
    tok, width = a1.shape
    out = b_mine.shape[1]
    third = pl.BlockSpec((3, out // 3, TILE), lambda t: (0, 0, t))
    return call(
        qkv_kernel,
        (a1, w_mine, w_other, b_mine, b_other, cos, sin),
        [
            rows(width), whole((out, width)), whole((out, width)),
            whole(b_mine.shape), whole(b_mine.shape), cols(HALF), cols(HALF),
        ],
        [third, third, SMEM],
        [shaped((3, out // 3, tok), BF)] * 2 + [shaped((1,), I32)],
        "qkv",
        deps,
        scratch=[pltpu.VMEM((8, TILE), F32), pltpu.VMEM((2, out, LANES), F32)],
        grid=(tok // TILE,),
        cost_estimate=cost(4 * tok * width * out, 8e6),
    )


def normal_tables(u):
    return 0.5 * (1.0 + lax.erf(u * 0.7071067811865476)), jnp.exp(-0.5 * u * u)


def mlp_kernel(
    groups, chained, *refs,
):
    x_ref, gy_ref, *refs = refs[chained:]
    ctx_refs, refs = refs[: 2 * groups], refs[2 * groups :]
    wp_mine, wp_other, wx_mine, wx_other, w_mine, w_other, bup_ref, norm_ref = refs[:8]
    refs = refs[8:]
    x1_ref, a2_ref, act_ref, gpre_ref, ffn_ref, gh_ref, gbup_ref, out_w, up_w, down_w = refs

    @pl.when(pl.program_id(0) == 0)
    def _():
        quarter, half = wx_mine.shape[0], up_w.shape[0] // 2
        for at, ref in enumerate((wp_mine, wp_other, wx_mine, wx_other)):
            out_w[at * quarter : (at + 1) * quarter, :] = ref[...]
        for at, ref in enumerate((w_mine, w_other)):
            up_w[at * half : (at + 1) * half, :] = ref[:half, :]
            down_w[at * half : (at + 1) * half, :] = ref[half:, :]

    gy = gy_ref[...]
    own, far = ctx_refs[0::2], ctx_refs[1::2]
    ctx = jnp.concatenate([ref[j] for some in (own, far) for j in range(2) for ref in some], axis=0)
    x1 = x_ref[...].astype(F32) + dot_tn(ctx, out_w[...]) + norm_ref[4:5]
    x1_ref[...] = x1
    n2, _ = normalized(x1)
    a2 = (n2 * norm_ref[2:3] + norm_ref[3:4]).astype(BF)
    a2_ref[...] = a2
    pre = dot_nt(a2, up_w[...]) + bup_ref[...]
    cdf, bell = normal_tables(pre)
    act = (pre * cdf).astype(BF)
    act_ref[...] = act
    slope = cdf + pre * (bell * 0.3989422804014327)
    gpre = (slope * dot_nt(gy, down_w[...])).astype(BF)
    gpre_ref[...] = gpre
    ffn_ref[...] = dot_nn(act, down_w[...]).astype(BF)
    gh_ref[...] = dot_nn(gpre, up_w[...]).astype(BF)
    part = jnp.sum(gpre.astype(F32), axis=0, keepdims=True)

    @pl.when(pl.program_id(0) == 0)
    def _():
        gbup_ref[...] = part

    @pl.when(pl.program_id(0) > 0)
    def _():
        gbup_ref[...] += part


def mlp_call(span, x, gy, ctx, wp, wx, w_mine, w_other, b_up, norms, before=(), deps=()):
    tok, width = x.shape
    hidden = b_up.shape[1]
    quarter = wx[0].shape[0]
    begin, count = span[0], span[1] - span[0]
    args = (*before, x, gy, *ctx, *wp, *wx, w_mine, w_other, b_up, norms)
    return call(
        functools.partial(mlp_kernel, len(ctx) // 2, len(before)),
        args,
        [ANYWHERE] * len(before)
        + [rows(width, begin)] * 2
        + [both(part.shape[1]) for part in ctx]
        + [last_rows(wp[0], quarter)] * 2
        + [whole((quarter, width))] * 2
        + [whole(w_mine.shape)] * 2
        + [whole(b_up.shape), whole(norms.shape)],
        [
            rows(width, begin), rows(width, begin), rows(hidden, begin), rows(hidden, begin),
            rows(width, begin), rows(width), whole((1, hidden)),
        ],
        [
            shaped((tok, width), F32), shaped((tok, width), BF), shaped((tok, hidden), BF),
            shaped((tok, hidden), BF), shaped((tok, width), BF), shaped((count * TILE, width), BF),
            shaped((1, hidden), F32),
        ],
        "mlp",
        deps,
        scratch=[
            pltpu.VMEM((4 * quarter, width), BF), pltpu.VMEM((hidden, width), BF),
            pltpu.VMEM((hidden, width), BF),
        ],
        grid=(count,),
        cost_estimate=cost(2 * count * TILE * width * (hidden * 4 + 4 * quarter) * 1.6, 2e7),
        input_output_aliases={j: j for j in range(len(before))},
    )


def mlp_grads_kernel(act_ref, gpre_ref, a2_ref, gy_ref, mine_ref, other_ref, down_sum, up_sum):
    step = pl.program_id(0)
    down = dot_tn(act_ref[...], gy_ref[...])
    up = dot_tn(gpre_ref[...], a2_ref[...])

    @pl.when(step == 0)
    def _():
        down_sum[...] = down
        up_sum[...] = up

    @pl.when(step > 0)
    def _():
        down_sum[...] += down
        up_sum[...] += up

    @pl.when(step == pl.num_programs(0) - 1)
    def _():
        half = down_sum.shape[0] // 2
        for which, out_ref in enumerate((mine_ref, other_ref)):
            here = pl.ds(which * half, half)
            out_ref[:half, :] = up_sum[here, :].astype(BF)
            out_ref[half:, :] = down_sum[here, :].astype(BF)


def mlp_grads_call(act, gpre, a2, gy, deps=()):
    tok, hidden = act.shape
    width = a2.shape[1]
    return call(
        mlp_grads_kernel,
        (act, gpre, a2, gy),
        [rows(hidden), rows(hidden), rows(width), rows(width)],
        [whole((hidden, width))] * 2,
        [shaped((hidden, width), BF)] * 2,
        "mlp_grads",
        deps,
        scratch=[pltpu.VMEM((hidden, width), F32)] * 2,
        grid=(tok // TILE,),
        cost_estimate=cost(4 * tok * width * hidden * 1.3, 1.4e7),
    )


def mid_kernel(
    groups, chained, handed, x1_ref, gy_ref, gh_a, gh_b, *refs,
):
    ctx_refs, refs = refs[:groups], refs[groups:]
    wm_ref, wo_ref, norm_ref = refs[:3]
    refs = refs[3 + chained + handed :]
    gx_ref, g_out, gout_ref, sum_ref = refs[:4]
    cm, co = (jnp.concatenate([ref[j] for ref in ctx_refs], axis=0) for j in range(2))
    step = pl.program_id(0)
    gy = gy_ref[...].astype(F32)
    gh = gh_a[...].astype(F32) + gh_b[...].astype(F32)
    n2, inv = normalized(x1_ref[...])
    e = gh * norm_ref[2:3]
    gx = gy + inv * (
        e - jnp.mean(e, axis=-1, keepdims=True) - n2 * jnp.mean(e * n2, axis=-1, keepdims=True)
    )
    gx_ref[...] = gx
    gm = gx.astype(BF)
    g_out[0] = dot_nt(wm_ref[...], gm).astype(BF)
    g_out[1] = dot_nt(wo_ref[...], gm).astype(BF)

    @pl.when(step == 0)
    def _():
        gout_ref[...] = jnp.zeros_like(gout_ref)
        sum_ref[...] = jnp.zeros_like(sum_ref)

    gout_ref[0] += dot_nn(cm, gm)
    gout_ref[1] += dot_nn(co, gm)
    for at, value in enumerate((gh * n2, gh, gx, gy)):
        sum_ref[at : at + 1, :] += jnp.sum(value, axis=0, keepdims=True)


def mid_call(span, x1, gy, gh, gh_other, ctx, w_m, w_o, norms, before=(), hand=(), deps=()):
    tok, width = x1.shape
    head = sum(part.shape[1] for part in ctx)
    begin, count = span[0], span[1] - span[0]
    args = (x1, gy, gh, gh_other, *ctx, w_m, w_o, norms, *before, *hand)
    fixed = len(args) - len(before) - len(hand)
    aliases = {fixed + j: j for j in range(len(before))}
    aliases.update({fixed + len(before) + j: 4 + j for j in range(len(hand))})
    return call(
        functools.partial(mid_kernel, len(ctx), len(before), len(hand)),
        args,
        [rows(width, begin)] * 2
        + [rows(width)] * 2
        + [both(part.shape[1]) for part in ctx]
        + [last_rows(w_m, head)] * 2
        + [whole(norms.shape)]
        + [ANYWHERE] * (len(before) + len(hand)),
        [rows(width, begin), both(head), whole((2, head, width)), whole((8, width))]
        + [ANYWHERE] * len(hand),
        [
            shaped((tok, width), F32), shaped((2, head, count * TILE), BF),
            shaped((2, head, width), F32), shaped((8, width), F32),
        ]
        + [shaped(part.shape, part.dtype) for part in hand],
        "mid_back",
        deps,
        grid=(count,),
        cost_estimate=cost(8 * count * TILE * width * head * 2, 1e7),
        input_output_aliases=aliases,
    )


def pack_small(value):
    hi = value.astype(BF).astype(F32)
    row = lax.broadcasted_iota(I32, value.shape, 0)
    rest = jnp.where(row < 6, value - hi, 0.0)
    return jnp.where(row < 10, hi, pltpu.roll(rest, 10, 0)).astype(BF)


def unpack_small(packed):
    packed = packed.astype(F32)
    row = lax.broadcasted_iota(I32, packed.shape, 0)
    return jnp.where(row < 10, packed, 0.0) + jnp.where(row < 6, pltpu.roll(packed, 6, 0), 0.0)


def in_grads_kernel(groups, gouts, *refs):
    g_refs, refs = refs[:groups], refs[groups:]
    out_refs, mid_refs, up_refs, refs = (
        refs[:gouts], refs[gouts : 2 * gouts], refs[2 * gouts : 3 * gouts], refs[3 * gouts :]
    )
    core_ref, a1_ref, x_ref, wm_ref, wo_ref, mine_ref, other_ref, gh_ref, sum_ref = refs[:9]
    m_sum, o_sum, gbm_ref, gbo_ref = refs[9:]
    step = pl.program_id(0)
    count = wm_ref.shape[0]
    a1 = a1_ref[...]
    gm, go = (
        jnp.concatenate([ref[half, j] for j in range(3) for ref in g_refs], axis=0)
        for half in range(2)
    )

    @pl.when(step == 0)
    def _():
        m_sum[...] = jnp.zeros_like(m_sum)
        o_sum[...] = jnp.zeros_like(o_sum)
        gbm_ref[...] = jnp.zeros_like(gbm_ref)
        gbo_ref[...] = jnp.zeros_like(gbo_ref)
        sum_ref[...] = jnp.zeros_like(sum_ref)

    m_sum[...] += dot_nn(gm, a1)
    o_sum[...] += dot_nn(go, a1)
    gbm_ref[...] += jnp.sum(gm.astype(F32), axis=1, keepdims=True)
    gbo_ref[...] += jnp.sum(go.astype(F32), axis=1, keepdims=True)
    gh = dot_tn(gm, wm_ref[...]) + dot_tn(go, wo_ref[...])
    gh_ref[...] = gh.astype(BF)
    n1, _ = normalized(x_ref[...].astype(F32))
    sum_ref[0:1, :] += jnp.sum(gh * n1, axis=0, keepdims=True)
    sum_ref[1:2, :] += jnp.sum(gh, axis=0, keepdims=True)

    @pl.when(step == pl.num_programs(0) - 1)
    def _():
        width = gh.shape[1]
        up = sum((ref[...] for ref in up_refs[1:]), up_refs[0][...])
        sum_ref[2:6, :] = sum((ref[0:4, :] for ref in mid_refs[1:]), mid_refs[0][0:4, :])

        def column(row):
            return jnp.transpose(jnp.broadcast_to(row, (LANES, row.shape[1])))[:, 0:1]

        swapped = core_ref[0] == 1
        mixed = []
        for mine, other in ((gbm_ref[...], gbo_ref[...]), (column(up[:, :width]), column(up[:, width:]))):
            lower, upper = jnp.where(swapped, other, mine), jnp.where(swapped, mine, other)
            for at in range(0, mine.shape[0], HALF):
                mixed += [lower[at : at + HALF], upper[at : at + HALF]]
        natural = jnp.concatenate(mixed, axis=0)
        natural = jnp.transpose(jnp.broadcast_to(natural, (natural.shape[0], LANES)))[0:1]
        for at in range(0, natural.shape[1], width):
            part = natural[:, at : at + width]
            sum_ref[6 + at // width : 7 + at // width, : part.shape[1]] = part
        packed = pack_small(sum_ref[...])
        sum_ref[...] = unpack_small(packed)
        more = count + out_refs[0].shape[1]
        for ref, total, half in ((mine_ref, m_sum, 0), (other_ref, o_sum, 1)):
            ref[:count, :] = total[...].astype(BF)
            ref[count:more, :] = sum((out[half] for out in out_refs[1:]), out_refs[0][half]).astype(BF)
        other_ref[more:, :] = packed


def in_grads_call(grads, core, a1, x, w_m, w_o, gouts, mid_sums, gb_ups, deps=()):
    tok, width = a1.shape
    more = gouts[0].shape[1]
    count = w_m.shape[0] - more
    parts = [
        pl.BlockSpec(part.shape[:3] + (TILE,), lambda t: (0, 0, 0, t)) for part in grads
    ]
    return call(
        functools.partial(in_grads_kernel, len(grads), len(gouts)),
        (*grads, *gouts, *mid_sums, *gb_ups, core[None], a1, x, w_m, w_o),
        parts
        + [whole(part.shape) for part in (*gouts, *mid_sums, *gb_ups)]
        + [SMEM, rows(width), rows(width)]
        + [whole((count, width))] * 2,
        [whole((count + more, width)), whole((count + more + 16, width)), rows(width), whole((16, width))],
        [
            shaped((count + more, width), BF), shaped((count + more + 16, width), BF),
            shaped((tok, width), BF), shaped((16, width), F32),
        ],
        "in_grads",
        deps,
        scratch=[pltpu.VMEM((count, width), F32)] * 2 + [pltpu.VMEM((count, 1), F32)] * 2,
        grid=(tok // TILE,),
        cost_estimate=cost(8 * tok * width * count * 1.3, 1e7),
    )


def out_kernel(x1_ref, a_ref, b_ref, norm_ref, out_ref):
    out_ref[...] = x1_ref[...] + (a_ref[...].astype(F32) + b_ref[...].astype(F32)) + norm_ref[5:6]


def out_call(x1, ffn_a, ffn_b, norms, deps=()):
    tok, width = x1.shape
    return call(
        out_kernel,
        (x1, ffn_a, ffn_b, norms),
        [rows(width)] * 3 + [whole(norms.shape)],
        rows(width),
        shaped((tok, width), F32),
        "layer_out",
        deps,
        grid=(tok // TILE,),
        cost_estimate=cost(4e9, 1e7),
    )


def nothing_kernel(*refs):
    pass


def hand_call(arrays, deps):
    return call(
        nothing_kernel, arrays, [ANYWHERE] * len(arrays), [ANYWHERE] * len(arrays),
        [shaped(array.shape, array.dtype) for array in arrays], "hand", deps,
        input_output_aliases={at: at for at in range(len(arrays))},
    )


def keep_kernel(*refs):
    half = len(refs) // 2
    for source, target in zip(refs[:half], refs[half:]):
        target[...] = source[...]


def keep_call(arrays, deps=()):
    specs = [whole(array.shape) for array in arrays]
    return call(
        keep_kernel, arrays, specs, specs, [shaped(a.shape, a.dtype) for a in arrays], "keep", deps,
        cost_estimate=cost(4e9, 1e7),
    )


def last_kernel(x_ref, gx_ref, gh_a, gh_b, norm_ref, out_ref):
    n1, inv = normalized(x_ref[...].astype(F32))
    e = (gh_a[...].astype(F32) + gh_b[...].astype(F32)) * norm_ref[0:1]
    out_ref[...] = gx_ref[...] + inv * (
        e - jnp.mean(e, axis=-1, keepdims=True) - n1 * jnp.mean(e * n1, axis=-1, keepdims=True)
    )


def last_call(x, gx, gh_a, gh_b, norms):
    tok, width = x.shape
    return call(
        last_kernel,
        (x, gx, gh_a, gh_b, norms),
        [rows(width)] * 4 + [whole(norms.shape)],
        rows(width),
        shaped((tok, width), F32),
        "last_back",
        grid=(tok // TILE,),
        cost_estimate=cost(1e6, 1.2e7),
    )


def layout_kernel(core_ref, len_ref, freq_ref, bias_ref, cos_ref, sin_ref, row_ref, col_ref, bm_ref, bo_ref, bup_ref, start_ref):
    tok = cos_ref.shape[1]
    docs = len_ref.shape[1]
    begin, best, start = 0, len_ref[0, 0], 0
    begins, ends = [], []
    for doc in range(docs):
        size = len_ref[0, doc]
        if doc:
            start = jnp.where(size > best, begin, start)
            best = jnp.maximum(size, best)
        begins.append(begin)
        begin = begin + size
        ends.append(begin)
    start_ref[0] = start + jnp.zeros((), I32)

    def origin(places):
        at = places + start
        return jnp.where(at >= tok, at - tok, at)

    def document(at):
        return sum(((at >= end).astype(I32) for end in ends), jnp.zeros(at.shape, I32))

    row = origin(lax.broadcasted_iota(I32, (1, tok), 1))
    first = jnp.zeros((1, tok), I32)
    for begin in begins[1:]:
        first = jnp.where(row >= begin, begin, first)
    angles = freq_ref[...] * (row - first).astype(F32)
    cos_ref[...] = jnp.cos(angles)
    sine = jnp.sin(angles)
    sin_ref[...] = jnp.where(core_ref[0] == 0, sine, -sine)
    column = jnp.transpose(jnp.broadcast_to(bias_ref[...], (LANES, bias_ref.shape[1])))[:, 0:1]
    lower, upper = (
        jnp.concatenate(
            [column[at : at + HALF] for at in range(begin, column.shape[0], HEAD_DIM)], axis=0
        )
        for begin in (0, HALF)
    )
    swapped = core_ref[0] == 1
    mine, other = jnp.where(swapped, upper, lower), jnp.where(swapped, lower, upper)
    count = bm_ref.shape[1]
    for which, (half, ref) in enumerate(((mine, bm_ref), (other, bo_ref))):
        turned = jnp.transpose(jnp.broadcast_to(half, (half.shape[0], LANES)))[0:1]
        length = half.shape[0] - count
        ref[...] = turned[:, :count]
        bup_ref[:, which * length : (which + 1) * length] = turned[:, count:]
    rest = row_ref.shape[1]
    row_ref[...] = document(row[:, tok - rest :])
    col_ref[...] = document(origin(lax.broadcasted_iota(I32, (rest, 1), 0) + (tok - rest)))


def layout_call(core, lengths, biases, tok, n_qkv, deps=()):
    rest, n_up = tok - LONGEST, biases.shape[1] - 2 * n_qkv
    freq = np.float32(10000.0) ** -(np.arange(0, HEAD_DIM, 2).astype(np.float32) / HEAD_DIM)
    return call(
        layout_kernel,
        (core[None], lengths, jnp.asarray(freq[:, None], F32), biases),
        [SMEM, SMEM, whole((HALF, 1)), whole(biases.shape)],
        [whole((HALF, tok))] * 2
        + [whole((1, rest)), whole((rest, 1)), whole((1, n_qkv)), whole((1, n_qkv)), whole((1, n_up)), SMEM],
        [shaped((HALF, tok), F32)] * 2
        + [
            shaped((1, rest), I32), shaped((rest, 1), I32), shaped((1, n_qkv), F32),
            shaped((1, n_qkv), F32), shaped((1, n_up), F32), shaped((1,), I32),
        ],
        "layout",
        deps,
    )


def halves_kernel(core_ref, table_ref, mine_ref, other_ref):
    first = core_ref[0] == 0
    count = mine_ref.shape[1]
    upper, lower = table_ref[:, :count, :], table_ref[:, count:, :]
    mine_ref[...] = jnp.where(first, upper, lower).astype(BF)
    other_ref[...] = jnp.where(first, lower, upper).astype(BF)


def halves_call(core, table):
    cap, count, width = table.shape
    half = (cap, count // 2, width)
    return call(
        halves_kernel,
        (core[None], table),
        [SMEM, whole(table.shape)],
        [whole(half)] * 2,
        [shaped(half, BF)] * 2,
        "halves",
    )


def by_heads(kernel, which, each):
    def step(*refs):
        for head in range(each):
            views = []
            for ref, dim in zip(refs, which):
                if dim is not None:
                    size = ref.shape[dim] // each
                    ref = ref.at[(slice(None),) * dim + (pl.ds(head * size, size),)]
                views.append(ref)
            kernel(*views)

    return step


def attend_kernel(cut, safe_ref, seg_row, seg_col, m_ref, o_ref, *outs):
    tok = m_ref.shape[2]
    rest = tok - LONGEST
    q_t, k_t, v_t = (jnp.concatenate([m_ref[j], o_ref[j]], axis=0) for j in range(3))
    qs = q_t.astype(F32) * SCALE_LOG2
    hi, lo = split_two(qs)
    qx = jnp.transpose(jnp.concatenate([hi, lo], axis=0)).astype(BF)
    kx = jnp.concatenate([k_t, k_t], axis=0)
    v_f = v_t.astype(F32)
    vx = jnp.transpose(jnp.concatenate([v_f, jnp.ones((8, tok), F32)], axis=0)).astype(BF)
    safe = safe_ref[0] > 0

    def finish(sums, shift, at, count):
        turned = jnp.transpose(sums)
        total = turned[HEAD_DIM : HEAD_DIM + 1]
        ctx = (turned[0:HEAD_DIM] / total).astype(BF)
        ctx_ref, log_ref = outs[:2] if at < cut else outs[2:]
        here = slice(at, at + count) if at < cut else slice(at - cut, at - cut + count)
        ctx_ref[0, :, here] = ctx[:HALF]
        ctx_ref[1, :, here] = ctx[HALF:]
        log_total = jnp.log2(total)
        if shift is not None:
            log_total = log_total + jnp.transpose(jnp.broadcast_to(shift, (count, LANES)))[0:1]
        log_ref[0, :, here] = log_total

    def run(exact):
        for at in range(0, LONGEST, TILE):
            scores = dot_nn(qx[at : at + TILE], kx[:, :LONGEST])
            shift = None
            if exact:
                shift = jnp.max(scores, axis=1, keepdims=True)
                scores = scores - shift
            finish(dot_nn(jnp.exp2(scores).astype(BF), vx[:LONGEST]), shift, at, TILE)
        if rest:
            same = seg_col[...] == seg_row[...]
            scores = jnp.where(same, dot_nn(qx[LONGEST:], kx[:, LONGEST:]), NEG_FILL)
            shift = None
            if exact:
                shift = jnp.max(scores, axis=1, keepdims=True)
                scores = scores - shift
            finish(dot_nn(jnp.exp2(scores).astype(BF), vx[LONGEST:]), shift, LONGEST, rest)

    @pl.when(safe)
    def _():
        run(False)

    @pl.when(jnp.logical_not(safe))
    def _():
        run(True)


def attend_call(cut, safe, segs, qkv_m, qkv_o, first, count, deps=()):
    tok = qkv_m.shape[2]
    rest = segs[0].shape[1]
    each = FORWARD_HEADS_EACH
    first = first // each
    part = pl.BlockSpec((3, each * HALF, tok), lambda h: (0, first + h, 0))
    out_specs, out_shape = [], []
    for length in (cut, tok - cut):
        out_specs += [
            pl.BlockSpec((2, each * HALF, length), lambda h: (0, h, 0)),
            pl.BlockSpec((each, 1, length), lambda h: (h, 0, 0)),
        ]
        out_shape += [shaped((2, count * HALF, length), BF), shaped((count, 1, length), F32)]
    return call(
        by_heads(functools.partial(attend_kernel, cut), (None, None, None, 1, 1, 1, 0, 1, 0), each),
        (safe, *segs, qkv_m, qkv_o),
        [SMEM, whole((1, rest)), whole((rest, 1)), part, part],
        out_specs,
        out_shape,
        "attend",
        deps,
        grid=(count // each,),
        cost_estimate=cost(count * 2.2e9, 3e6),
    )


def attend_back_kernel(
    q_begin, q_end, last, seg_row, seg_col, cos_ref, sin_ref, m_ref, o_ref, g_ref, ctx_ref, log_ref,
    *refs,
):
    tok = m_ref.shape[2]
    rest = tok - LONGEST
    end = tok if last else q_end
    span = slice(q_begin, end)
    q_t, k_t, v_t = (jnp.concatenate([m_ref[j], o_ref[j]], axis=0) for j in range(3))
    q_f = q_t[:, span].astype(F32)
    ctx = jnp.concatenate([ctx_ref[0], ctx_ref[1]], axis=0).astype(F32)
    g_f = jnp.concatenate([g_ref[0], g_ref[1]], axis=0).astype(F32)
    hi, lo = split_two(q_f * SCALE_LOG2)
    weighted = jnp.sum(g_f * ctx, axis=0, keepdims=True)
    pad = jnp.zeros((13, end - q_begin), F32)
    qx = jnp.concatenate([hi, lo, *split_three(log_ref[0]), pad], axis=0).astype(BF)
    keys = tok if last else LONGEST
    k_f, v_f = k_t[:, :keys].astype(F32), v_t[:, :keys].astype(F32)
    minus = jnp.concatenate([jnp.full((3, keys), -1.0, F32), jnp.zeros((13, keys), F32)], axis=0)
    kx = jnp.transpose(jnp.concatenate([k_f, k_f, minus], axis=0)).astype(BF)
    gx = jnp.concatenate([g_f, *split_three(weighted), pad], axis=0).astype(BF)
    vx = jnp.transpose(jnp.concatenate([v_f, minus], axis=0)).astype(BF)
    qn = jnp.transpose(q_f).astype(BF)
    gn = jnp.transpose(g_f).astype(BF)

    if last:
        early_q, early_kv, out_ref = refs
    else:
        out_q, out_kv = refs

    def turned_back(grad, at, count):
        cos, sin = cos_ref[:, at : at + count], sin_ref[:, at : at + count]
        mine, other = grad[0:HALF] * SCALE, grad[HALF:] * SCALE
        return (mine * cos + other * sin).astype(BF), (other * cos - mine * sin).astype(BF)

    def block(k_at, k_count, q_at, q_count, mask, early):
        scores = dot_nn(kx[k_at : k_at + k_count], qx[:, q_at : q_at + q_count])
        if mask is not None:
            scores = jnp.where(mask, scores, NEG_FILL)
        prob = jnp.exp2(scores)
        grad_prob = dot_nn(vx[k_at : k_at + k_count], gx[:, q_at : q_at + q_count])
        grad_score = (prob * grad_prob).astype(BF)
        grad_v = jnp.transpose(dot_nn(prob.astype(BF), gn[q_at : q_at + q_count]))
        grad_k = jnp.transpose(dot_nn(grad_score, qn[q_at : q_at + q_count]))
        here = slice(k_at, k_at + k_count)
        if not last:
            out_kv[0, 0, :, here] = grad_k
            out_kv[1, 0, :, here] = grad_v
        else:
            if early:
                grad_k = grad_k + early_kv[0, 0, :, here]
                grad_v = grad_v + early_kv[1, 0, :, here]
            out_ref[0, 1, :, here], out_ref[1, 1, :, here] = turned_back(grad_k, k_at, k_count)
            out_ref[0, 2, :, here] = grad_v[:HALF].astype(BF)
            out_ref[1, 2, :, here] = grad_v[HALF:].astype(BF)
        return dot_nn(k_t[:, k_at : k_at + k_count], grad_score)

    grad_q = None
    for at in range(0, LONGEST, TILE):
        piece = block(at, TILE, 0, q_end - q_begin, None, True)
        grad_q = piece if grad_q is None else grad_q + piece
    mine, other = turned_back(grad_q, q_begin, q_end - q_begin)
    if not last:
        out_q[0], out_q[1] = mine, other
        return
    out_ref[0, 0, :, :q_begin] = early_q[0]
    out_ref[1, 0, :, :q_begin] = early_q[1]
    out_ref[0, 0, :, q_begin:q_end] = mine
    out_ref[1, 0, :, q_begin:q_end] = other
    if rest:
        same = seg_col[...] == seg_row[...]
        piece = block(LONGEST, rest, LONGEST - q_begin, rest, same, False)
        out_ref[0, 0, :, LONGEST:], out_ref[1, 0, :, LONGEST:] = turned_back(piece, LONGEST, rest)


def attend_back_call(
    q_begin, q_end, segs, cos, sin, qkv_m, qkv_o, g_ctx, ctx, logs, first, count, early=(), deps=()
):
    tok = qkv_m.shape[2]
    last = len(early) > 0
    rest = segs[0].shape[1]
    each = HEADS_EACH
    first = first // each
    part = pl.BlockSpec((3, each * HALF, tok), lambda h: (0, first + h, 0))
    table = whole((HALF, tok))

    def by_head(length, offset=0):
        return pl.BlockSpec((2, each * HALF, length), lambda h: (0, offset + h, 0))

    pair = pl.BlockSpec((2, each, HEAD_DIM, LONGEST), lambda h: (0, h, 0, 0))
    if last:
        out_specs = [pl.BlockSpec((2, 3, each * HALF, tok), lambda h: (0, 0, h, 0))]
        out_shape = [shaped((2, 3, count * HALF, tok), BF)]
    else:
        out_specs = [by_head(q_end), pair]
        out_shape = [
            shaped((2, count * HALF, q_end), BF), shaped((2, count, HEAD_DIM, LONGEST), F32)
        ]
    return call(
        by_heads(
            functools.partial(attend_back_kernel, q_begin, q_end, last),
            (None,) * 4 + (1, 1, 1, 1, 0, 1, 1) + ((2,) if last else ()),
            each,
        ),
        (*segs, cos, sin, qkv_m, qkv_o, g_ctx, ctx, logs, *early),
        [
            whole((1, rest)), whole((rest, 1)), table, table, part, part,
            by_head(g_ctx.shape[2], first), by_head(ctx.shape[2]),
            pl.BlockSpec((each, 1, logs.shape[2]), lambda h: (h, 0, 0)),
        ]
        + ([by_head(q_begin), pair] if last else []),
        out_specs,
        out_shape,
        "attend_back",
        deps,
        grid=(count // each,),
        cost_estimate=cost(count * 2.1e9, 6e6),
    )


class Routes:
    def __init__(self, dp_size, slot_cap, pieces, ready, spans):
        self.dp = dp_size
        self.cap = slot_cap
        self.chips = dp_size // 2
        self.pieces = pieces
        self.ready = ready
        self.spans = spans
        if self.chips == 8:
            self.stages = ((2, 4), (1, 2))
        elif self.chips == 64:
            self.stages = ((1, 8), (8, 2), (16, 4))
        else:
            self.stages = ((1, self.chips),)
        self.depth = len(self.stages)
        straight = self.stages[::-1]
        paired = ((1, 2), (4, 2), (2, 2)) if self.chips == 8 else straight
        self.back = (straight, paired)
        self.out = (self.stages, ((4, 2), (2, 2), (1, 2)) if self.chips == 8 else self.stages)
        self.fill = [self.limit(last, self.chips) for last in ready]
        self.begins = [0] + self.fill[:-1]
        early, late = self.fill[0], self.fill[1] - self.fill[0]
        if self.chips == 8:
            self.bases = (
                [at * early for at in range(4)]
                + [4 * early]
                + [4 * early + self.fill[1] + at * early for at in range(3)],
                [7 * early + self.fill[1] + at * late for at in range(4)]
                + [5 * early]
                + [7 * early + self.fill[1] + at * late for at in range(4, 7)],
            )
        else:
            self.bases = tuple(
                [begin * self.chips + at * (end - begin) for at in range(self.chips)]
                for begin, end in zip(self.begins, self.fill)
            )

    def limit(self, count, groups):
        worst = min(count, self.dp // groups * self.cap)
        if self.chips != 8:
            return worst
        typical = {
            2: count * 11 // 20 + 8, 4: count * 3 // 10 + 10, 8: count // 5 + 5
        }[groups]
        return worst if count == self.pieces else min(worst, typical)

    def span_limit(self, number, level):
        groups = 1
        for _, size in self.back[number][:level]:
            groups *= size
        return self.limit(self.spans[number][1] - self.spans[number][0], groups)

    def move(self, array, stage, shift):
        stride, size = stage
        pairs = []
        for device in range(self.dp):
            chip, core = device // 2, device % 2
            at = (chip // stride) % size
            pairs.append((device, 2 * (chip + ((at + shift) % size - at) * stride) + core))
        return lax.ppermute(array, "dp", pairs)

    def swap_cores(self, array):
        return lax.ppermute(array, "dp", [(d, d ^ 1) for d in range(self.dp)])

    def around(self, array, stage):
        return [array] + [self.move(array, stage, shift) for shift in range(1, stage[1])]

    def onward(self, buffers, stage):
        return buffers + [
            self.move(buffer, stage, shift) for shift in range(1, stage[1]) for buffer in buffers
        ]

    def tables(self, owners, me):
        place = {}

        def kernel(me_ref, own_ref, out_ref, row_ref):
            here = me_ref[0]
            my_chip, my_core = here // 2, here % 2
            row_ref[...] = jnp.full((1, LANES), -2, I32)
            row_ref[:, : self.pieces] = own_ref[...]
            row = row_ref[...]
            col = jnp.transpose(jnp.broadcast_to(row, (LANES, LANES)))[:, 0:1]
            id_row = lax.broadcasted_iota(I32, (1, LANES), 1)
            id_col = lax.broadcasted_iota(I32, (LANES, 1), 0)
            lane = lax.broadcasted_iota(I32, (LANES, LANES), 1)
            sub = lax.broadcasted_iota(I32, (LANES, LANES), 0)

            def rank_col(key_row, key_col):
                hit = (key_row == key_col) & (lane < sub)
                return jnp.sum(hit.astype(F32), axis=1, keepdims=True).astype(I32)

            def rank_row(key_row, key_col):
                hit = (key_row == key_col) & (sub < lane)
                return jnp.sum(hit.astype(F32), axis=0, keepdims=True).astype(I32)

            def gather(valid_col, entry_col, value_col):
                hit = valid_col & (entry_col == lane)
                return jnp.sum(
                    jnp.where(hit, value_col.astype(F32), 0.0), axis=0, keepdims=True
                ).astype(I32)

            def put(name, value):
                at = place.setdefault(name, len(place))
                out_ref[at : at + 1, :] = value

            def coord(chip, stage):
                return (chip // stage[0]) % stage[1]

            def group(chip, stages):
                key = 0
                for stage in stages:
                    key = key * stage[1] + coord(chip, stage)
                return key

            def fullest(inside, rank):
                return jnp.max(jnp.where(inside, rank, -1), axis=0, keepdims=True) + 1

            slot_col = rank_col(row, col)
            put("piece", gather(col == here, slot_col, id_col + 1) - 1)
            sibling = my_chip * 2 + 1 - my_core
            put("sibling", gather(col == sibling, slot_col, id_col + 1) - 1)
            over = jnp.zeros((1, 1), I32)
            real = id_col < self.pieces
            chip_col, chip_row = col // 2, row // 2
            rank_c, rank_r = rank_col(chip_row, chip_col), rank_row(chip_row, chip_col)
            from_core = jnp.where(col % 2 == my_core, 0, self.cap)
            put("send", gather(real & (chip_col == my_chip), rank_c, from_core + slot_col))
            for last, fill in zip(self.ready, self.fill):
                over = jnp.maximum(over, fullest(id_col < last, rank_c) - fill)
            put("late", jnp.broadcast_to(over, (1, LANES)))
            over = jnp.zeros((1, 1), I32)
            take = jnp.zeros((1, LANES), I32)
            for begin, bases, stages in zip(self.begins, self.bases, self.out):
                way, scale = jnp.zeros((1, LANES), I32), 1
                for stage in stages:
                    away = (coord(my_chip, stage) - coord(chip_row, stage) + stage[1]) % stage[1]
                    way = way + away * scale
                    scale = scale * stage[1]
                spot = rank_r - begin
                for at, base in enumerate(bases):
                    spot = spot + jnp.where(way == at, base, 0)
                take = jnp.where(rank_r >= begin, spot, take)
            put("take", take)
            for number, span in enumerate(self.spans):
                in_col = (id_col >= span[0]) & (id_col < span[1])
                in_row = (id_row >= span[0]) & (id_row < span[1])
                stages = self.back[number]
                ranks = {}
                for level in range(1, len(stages) + 1):
                    key_col = jnp.where(in_col, group(chip_col, stages[:level]), -1)
                    key_row = jnp.where(in_row, group(chip_row, stages[:level]), -1)
                    ranks[level] = rank_col(key_row, key_col)
                    over = jnp.maximum(
                        over, fullest(in_col, ranks[level]) - self.span_limit(number, level)
                    )
                value = id_col - span[0]
                for level, stage in enumerate(stages, 1):
                    size = stage[1]
                    inside = in_col & (
                        group(chip_col, stages[: level - 1]) == group(my_chip, stages[: level - 1])
                    )
                    for shift in range(size):
                        goal = (coord(my_chip, stage) + shift) % size
                        put(
                            ("back", number, level, shift),
                            gather(inside & (coord(chip_col, stage) == goal), ranks[level], value),
                        )
                    value = ranks[level]
                for which in range(2):
                    goal = my_chip * 2 + (my_core + which) % 2
                    put(
                        ("slot", number, which),
                        gather(in_col & (col == goal), slot_col, ranks[len(stages)]),
                    )
            put("over", jnp.broadcast_to(over, (1, LANES)))

        count = 6 + sum(2 + sum(size for _, size in stages) for stages in self.back)
        height = -(-count // 8) * 8
        table = pl.pallas_call(
            kernel,
            in_specs=[SMEM, whole((1, self.pieces))],
            out_specs=whole((height, LANES)),
            out_shape=shaped((height, LANES), I32),
            scratch_shapes=[pltpu.VMEM((1, LANES), I32)],
            compiler_params=params(),
            name="routes",
        )(me[None], owners[None, :])
        return table, place


def fetch(sources, targets, sems):
    copies = [
        pltpu.make_async_copy(source, target, sems.at[at])
        for at, (source, target) in enumerate(zip(sources, targets))
    ]
    for copy in copies:
        copy.start()
    for copy in copies:
        copy.wait()


def places(kept, parts):
    return [ANYWHERE] * kept + [HBM] * (len(parts) - kept)


def pick_call(table, picks, parts, sizes, name, deps=(), kept=1):
    rows_each = [part.shape[0] for part in parts]
    shape = parts[0].shape[1:]

    def kernel(table_ref, *refs):
        ins, (*outs, source, sems) = refs[: len(parts)], refs[len(parts) :]
        at, targets = 0, []
        for count in rows_each:
            targets.append(source.at[pl.ds(at, count)])
            at += count
        fetch(ins, targets, sems)
        for (row, start), size, out in zip(picks, sizes, outs):
            for j in range(size):
                out[j] = source[table_ref[row, start + j]]

    return call(
        kernel,
        (table, *parts),
        [SMEM] + places(kept, parts),
        [whole((size,) + shape) for size in sizes],
        [shaped((size,) + shape, BF) for size in sizes],
        name,
        deps,
        scratch=[
            pltpu.VMEM((sum(rows_each),) + shape, BF), pltpu.SemaphoreType.DMA((len(parts),)),
        ],
    )


def join_call(parts, deps=()):
    counts = [part.shape[0] for part in parts]
    shape = (sum(counts),) + parts[0].shape[1:]

    def kernel(*refs):
        *ins, out, sems = refs
        at, targets = 0, []
        for count in counts:
            targets.append(out.at[pl.ds(at, count)])
            at += count
        fetch(ins, targets, sems)

    return call(
        kernel, parts, places(0, parts), whole(shape), shaped(shape, BF), "join", deps,
        scratch=[pltpu.SemaphoreType.DMA((len(parts),))],
    )


def add_pick_call(table, picks, parts, sizes, small=None, extra=(), deps=()):
    shape = parts[0].shape[1:]
    lengths = [size + (j in extra) for j, size in enumerate(sizes)]

    def kernel(table_ref, *refs):
        sources, refs = refs[: len(parts)], refs[len(parts) :]
        ins, sems, refs = refs[-len(parts) - 1 : -1], refs[-1], refs[: -len(parts) - 1]
        fetch(sources, ins, sems)
        if small is not None:
            small_ref, refs = refs[0], refs[1:]
            terms = [small_ref[...]] + [
                unpack_small(ref[ref.shape[0] - 1]) for ref in ins[1:]
            ]
            while len(terms) > 1:
                middle = len(terms) // 2
                terms = [a + b for a, b in zip(terms[:middle], terms[middle:])]
            packed = pack_small(terms[0])
            refs[len(sizes)][...] = unpack_small(packed)
            for j in extra:
                refs[j][sizes[j]] = packed
        for (row, start), size, out in zip(picks, sizes, refs):
            for j in range(size):
                at = table_ref[row, start + j]
                total = ins[0][at].astype(F32)
                for ref in ins[1:]:
                    total = total + ref[at].astype(F32)
                out[j] = total.astype(BF)

    out_specs = [whole((length,) + shape) for length in lengths]
    out_shape = [shaped((length,) + shape, BF) for length in lengths]
    if small is not None:
        out_specs, out_shape = out_specs + [whole(shape)], out_shape + [shaped(shape, F32)]
    return call(
        kernel,
        (table, *parts) + (() if small is None else (small,)),
        [SMEM] + places(1, parts) + ([] if small is None else [whole(shape)]),
        out_specs,
        out_shape,
        "add_pick",
        late=deps,
        scratch=[pltpu.VMEM(part.shape, BF) for part in parts]
        + [pltpu.SemaphoreType.DMA((len(parts),))],
    )


def owned_call(table, place, routes, parts, small, deps=()):
    (parts_in, parts_mlp), cap = parts, routes.cap
    parts = (*parts_in, *parts_mlp)
    shape = parts_in[0].shape[1:]
    border = routes.spans[1][0]

    def kernel(table_ref, *refs):
        sources, refs = refs[: len(parts)], refs[len(parts) :]
        small_ref, kept_ref, sent_ref, total_ref, *held, sems = refs
        fetch(sources, held, sems)
        ins, mlps = held[: len(parts_in)], held[len(parts_in) :]
        terms = [small_ref[...]] + [
            unpack_small(ref[ref.shape[0] - 1]) for ref in ins[1:]
        ]
        while len(terms) > 1:
            middle = len(terms) // 2
            terms = [a + b for a, b in zip(terms[:middle], terms[middle:])]
        total_ref[...] = terms[0]
        for which, (name, out) in enumerate((("piece", kept_ref), ("sibling", sent_ref))):
            for j in range(cap):
                sums = []
                for number, some in enumerate((ins, mlps)):
                    at = table_ref[place[("slot", number, which)], j]
                    total = some[0][at].astype(F32)
                    for ref in some[1:]:
                        total = total + ref[at].astype(F32)
                    sums.append(total)
                out[j] = jnp.where(table_ref[place[name], j] >= border, sums[1], sums[0])

    args = (table, *parts_in, *parts_mlp, small)
    return call(
        kernel,
        args,
        [SMEM]
        + places(1, parts_in)
        + places(1, parts_mlp)
        + [whole(shape)],
        [whole((cap,) + shape)] * 2 + [whole(shape)],
        [shaped((cap,) + shape, F32)] * 2 + [shaped(shape, F32)],
        "owned",
        deps,
        scratch=[pltpu.VMEM(part.shape, BF) for part in parts]
        + [pltpu.SemaphoreType.DMA((len(parts),))],
    )


def adam_step(weights, first_mom, second_mom, gradient, rate, decay_rate):
    first_new = BETA_ONE * first_mom + (1.0 - BETA_ONE) * gradient
    second_new = BETA_TWO * second_mom + (1.0 - BETA_TWO) * gradient * gradient
    first_fix = first_new / (1.0 - BETA_ONE**STEP)
    second_fix = second_new / (1.0 - BETA_TWO**STEP)
    weights_new = weights * (1.0 - rate * decay_rate) - rate * first_fix / (
        jnp.sqrt(second_fix) + ADAM_EPS
    )
    return (weights_new, first_new, second_new)


def adam_call(table, row, core, borders, kept, arrived, tables):
    cap, count, width = tables[0].shape
    half = count // 2
    group = max(g for g in range(1, 6) if cap % g == 0)

    def kernel(table_ref, core_ref, kept_ref, arrived_ref, w_ref, m_ref, v_ref, *outs):
        step = pl.program_id(0)
        swapped = core_ref[0] == 1
        for j in range(group):
            piece = table_ref[row, step * group + j]
            rate = jnp.where(piece < borders[2], 0.03, 0.015)
            rate = jnp.where(piece < borders[1], 0.2, rate)
            rate = jnp.where(piece < borders[0], 0.03, rate).astype(F32)
            halves = (kept_ref[j], arrived_ref[j])
            for at in range(2):
                here = pl.ds(at * half, half)
                grad = jnp.where(swapped, halves[1 - at], halves[at])
                new = adam_step(w_ref[j, here], m_ref[j, here], v_ref[j, here], grad, rate, DECAY_RATE)
                for out, value in zip(outs, new):
                    out[j, here] = jnp.where(piece >= 0, value, 0.0)

    def block(rows_each):
        return pl.BlockSpec((group, rows_each, width), lambda t: (t, 0, 0))

    return call(
        kernel,
        (table, core[None], kept, arrived, *tables),
        [SMEM, SMEM, block(half), block(half)] + [block(count)] * 3,
        [block(count)] * 3,
        [shaped((cap, count, width), F32)] * 3,
        "adam",
        grid=(cap // group,),
        cost_estimate=cost(1e7, 8e6),
    )


def small_kernel(total_ref, far_ref, norm_ref, nm_ref, nv_ref, bias_ref, bm_ref, bv_ref, *outs):
    gains = total_ref[0:2, :] + far_ref[0:2, :]
    for at, rate in enumerate(NORM_RATES):
        here = slice(at, at + 1)
        grad = gains[here] if at < 2 else total_ref[here, :]
        new = adam_step(norm_ref[here, :], nm_ref[here, :], nv_ref[here, :], grad, rate, 0.0)
        for out, value in zip(outs[:3], new):
            out[here, :] = value
    width = total_ref.shape[1]
    for at in range(0, bias_ref.shape[1], width):
        here = slice(at, min(at + width, bias_ref.shape[1]))
        row = 6 + at // width
        grad = total_ref[row : row + 1, : here.stop - at]
        new = adam_step(bias_ref[:, here], bm_ref[:, here], bv_ref[:, here], grad, BIAS_RATE, 0.0)
        for out, value in zip(outs[3:], new):
            out[:, here] = value


def small_call(total, far, norms, biases, deps=()):
    args = (total, far, *norms, *biases)
    kept = [shaped(part.shape, F32) for part in (*norms, *biases)]
    return call(
        small_kernel, args, [whole(arg.shape) for arg in args], [whole(k.shape) for k in kept], kept, "small_update",
        deps,
    )


def swap_mp(array):
    return lax.ppermute(array, "mp", [(0, 1), (1, 0)])


def roll_rows(array, start):
    return lax.dynamic_slice_in_dim(
        jnp.concatenate([array, array], axis=0), start, array.shape[0], axis=0
    )


def body(
    tokens, cotangent, lengths, owners, weight_table, moment_table, square_table,
    norm_params, norm_moment, norm_square, bias_params, bias_moment, bias_square,
):
    dp_size = lax.axis_size("dp")
    mp_size = lax.axis_size("mp")
    heads = HEADS // mp_size
    head_width = heads * HEAD_DIM
    hidden = FF // mp_size
    tok, width = tokens.shape
    slot_cap, piece_len = weight_table.shape[1:3]
    half_len = piece_len // 2
    piece_total = owners.shape[0]
    me = lax.axis_index("dp").astype(I32)
    core = me % 2
    first_core = core == 0

    n_qkv, n_out = 3 * head_width // piece_len, head_width // piece_len
    n_up = hidden // piece_len
    n_first = n_qkv + n_out
    ready = (n_first, piece_total)
    spans = ((0, n_first), (n_first, piece_total))
    routes = Routes(dp_size, slot_cap, piece_total, ready, spans)
    table, place = routes.tables(owners, me)

    own_half, sibling_half = halves_call(core, weight_table[0])
    chip_slots = [own_half, routes.swap_cores(sibling_half)]

    def half(array, which):
        return lax.dynamic_index_in_dim(array, which, axis=1, keepdims=False)

    def unless(bad, usual, other):
        return lax.while_loop(
            lambda state: state[0] > 0, lambda state: (jnp.zeros((), I32), other()), (bad, usual)
        )[1]

    def own_lists(ranges, deps=()):
        return pick_call(
            table, [(place["send"], begin) for begin, _ in ranges], chip_slots,
            [end - begin for begin, end in ranges], "pick_owned", deps,
        )

    def collect(buffers, ranges, deps=()):
        sizes = [high - low for low, high in ranges]
        return pick_call(
            table, [(place["take"], low) for low, _ in ranges], buffers, sizes, "pick_all", deps
        )

    def flat(array):
        return array.reshape(-1, width)

    def pairs_apart(bit):
        return [(device, device ^ bit) for device in range(dp_size)]

    def slow_first():
        everyone, bit = weight_table[0].astype(BF), 1
        while bit < dp_size:
            everyone = jnp.concatenate([everyone, lax.ppermute(everyone, "dp", pairs_apart(bit))], 0)
            bit *= 2
        earlier = (owners[None, :] == owners[:, None]) & (
            jnp.arange(piece_total)[None, :] < jnp.arange(piece_total)[:, None]
        )
        at = (owners ^ me) * slot_cap + jnp.sum(earlier.astype(I32), axis=1)
        mine = half(everyone[at[:n_first]].reshape(n_first, 2, half_len, width), core)
        return mine, mine[n_qkv:]

    stages = routes.out
    chunks = tuple(zip(routes.begins, routes.fill))
    relayed = routes.chips == 8
    if relayed:
        list_a, list_all = ticked(own_lists, (chunks[0], (0, routes.fill[1])))
    else:
        list_a, list_b = ticked(own_lists, [chunk for chunk in chunks if chunk[0] < chunk[1]] * 2)[:2]
    listed = Clock.tick
    list_a = routes.around(list_a, stages[0][0])
    cos, sin, *segs, b_mine, b_other, b_up, start = layout_call(
        core, lengths, bias_params, tok, 3 * head_width // 2, (listed,)
    )
    x, a1 = ticked(norm_call, start, tokens, norm_params)
    gy = ticked(roll_call, start, cotangent, (Clock.tick,))
    turned = Clock.tick

    if relayed:
        own_y = routes.move(list_all, stages[0][1], 1)
        arrived = ticked(join_call, list_a[1:], (turned,))
        buffers_a = list_a + [own_y, routes.move(arrived, stages[0][1], 1)]
        (list_b,) = own_lists(chunks[1:], (Clock.tick, own_y))
        from_two, from_one = (routes.move(list_b, stage, 1) for stage in stages[1][:2])
        turned = Clock.tick
    else:
        buffers_a, buffers_b = list_a, [list_b]
        for stage in stages[0][1:]:
            buffers_a = routes.onward(buffers_a, stage)
    w_first_m, w_out_x = ticked(collect, buffers_a, ((0, n_first), (n_qkv, n_first)), (turned,))
    collected = Clock.tick
    if relayed:
        joined = join_call([from_two, from_one], (collected,))
        relay = routes.move(from_two, stages[1][1], 1)
        y_joined = routes.move(joined, stages[1][2], 1)
    w_first_m, w_out_x = unless(table[place["late"], 0], (w_first_m, w_out_x), slow_first)
    b_qkv = keep_call((b_mine, b_other), (collected,))
    w_first_o = routes.swap_cores(w_first_m)
    qkv_m, qkv_o, safe = ticked(
        qkv_call, a1, flat(w_first_m), flat(w_first_o), *b_qkv, cos, sin
    )
    w_out_x = swap_mp(hand_call((w_out_x,), (Clock.tick,))[0])
    if relayed:
        relay = ticked(join_call, [relay], (Clock.tick,))
        collected = Clock.tick
        y_relay = routes.move(relay, stages[1][2], 1)
        buffers_b = [list_b, from_two, from_one, relay, y_joined, y_relay]
    elif chunks[1][0] < chunks[1][1]:
        for stage in stages[1]:
            buffers_b = routes.onward(buffers_b, stage)
    else:
        buffers_b = []
    half_way = 2 * TILE
    cut = heads // 2
    groups = ((0, cut), (cut, heads - cut))
    ctx_a1, logs_a1, ctx_b1, logs_b1 = ticked(
        attend_call, half_way, safe, segs, qkv_m, qkv_o, *groups[0], (collected,)
    )
    attended = Clock.tick
    ctx_a2, logs_a2, ctx_b2, logs_b2 = attend_call(
        half_way, safe, segs, qkv_m, qkv_o, *groups[1], (attended,)
    )
    ctx_a, ctx_b = (ctx_a1, ctx_a2), (ctx_b1, ctx_b2)
    (w_out_x,) = hand_call((w_out_x,), (attended,))
    w_out_x = [flat(w_out_x), flat(routes.swap_cores(w_out_x))]
    ctx_ax, ctx_bx = ([swap_mp(part) for part in ctx] for ctx in (ctx_a, ctx_b))
    (w_mine,) = ticked(collect, buffers_a + buffers_b, ((n_first, piece_total),), (logs_b2,))
    (b_up,) = keep_call((b_up,), (Clock.tick,))
    w_mine, w_other = flat(w_mine), flat(routes.swap_cores(w_mine))
    w_first = [flat(w_first_m), flat(w_first_o)]
    spans_tok = ((0, half_way // TILE), (half_way // TILE, tok // TILE))
    def both_ways(own, far):
        return [part for pair in zip(own, far) for part in pair]

    mlp_args = (w_first, w_out_x, w_mine, w_other, b_up, norm_params)
    *filled, g_h2_a, gb_up_a = mlp_call(spans_tok[0], x, gy, both_ways(ctx_a, ctx_ax), *mlp_args)
    *filled, g_h2_b, gb_up_b = mlp_call(spans_tok[1], x, gy, both_ways(ctx_b, ctx_bx), *mlp_args, filled)
    x1, a2, act, g_pre, ffn = filled
    g_h2_ax, g_h2_bx = swap_mp(g_h2_a), swap_mp(g_h2_b)
    g_mlp = mlp_grads_call(act, g_pre, a2, gy)

    def pieces(array):
        return array.reshape(-1, half_len, width)

    def sort_out(number, level, parts, small=None, deps=()):
        stage = routes.back[number][level - 1]
        size = stage[1]
        lists = ticked(
            add_pick_call,
            table,
            [(place[("back", number, level, shift)], 0) for shift in range(size)],
            parts,
            [routes.span_limit(number, level)] * size,
            small=small,
            extra=() if small is None else range(1, size),
            deps=deps,
        )
        moved = [routes.move(lists[shift], stage, shift) for shift in range(1, size)]
        return [lists[0]] + moved, lists[-1]

    gx1, g_ctx_a, g_out_a, mid_a, g_mlp_m, g_mlp_o = mid_call(
        spans_tok[0], x1, gy, g_h2_a, g_h2_ax, ctx_a, *w_first, norm_params, (), g_mlp
    )
    back = (segs, cos, sin, qkv_m, qkv_o)
    early_one = ticked(attend_back_call, 0, half_way, *back, g_ctx_a, ctx_a1, logs_a1, *groups[0])
    parts_mlp, listed = sort_out(
        1, 1, [pieces(g_mlp_m), routes.swap_cores(pieces(g_mlp_o))], deps=(Clock.tick,)
    )
    early_two = ticked(
        attend_back_call, 0, half_way, *back, g_ctx_a, ctx_a2, logs_a2, *groups[1], deps=(listed,)
    )
    attended = Clock.tick
    gx1, g_ctx_b, g_out_b, mid_b, ffn = mid_call(
        spans_tok[1], x1, gy, g_h2_b, g_h2_bx, ctx_b, *w_first, norm_params, (gx1,), (ffn,), (attended,)
    )
    ffn_other = swap_mp(ffn)

    (grads_one,) = ticked(
        attend_back_call, half_way, LONGEST, *back, g_ctx_b, ctx_b1, logs_b1, *groups[0], early_one
    )
    (grads_two,) = ticked(
        attend_back_call, half_way, LONGEST, *back, g_ctx_b, ctx_b2, logs_b2, *groups[1], early_two, (Clock.tick,)
    )
    parts_mlp, listed = sort_out(1, 2, parts_mlp, deps=(Clock.tick,))
    sorted_mlp = Clock.tick
    g_in_m, g_in_o, g_h1, small = ticked(
        in_grads_call, (grads_one, grads_two), core, a1, x, *w_first,
        (g_out_a, g_out_b), (mid_a, mid_b), (gb_up_a, gb_up_b), (listed,),
    )
    g_h1_other = swap_mp(g_h1)
    ticked(keep_call, (norm_params,), (Clock.tick,))
    filled = Clock.tick
    out_roll = out_call(x1, ffn, ffn_other, norm_params, (sorted_mlp,))
    block_out = roll_rows(out_roll, tok - start[0])
    parts_in = [pieces(g_in_m), routes.swap_cores(pieces(g_in_o))]
    for level in range(1, len(routes.back[0])):
        parts_in, small = sort_out(0, level, parts_in, small, (filled,))
    for level in range(3, len(routes.back[1]) + 1):
        parts_mlp, _ = sort_out(1, level, parts_mlp, deps=(Clock.tick,))
    parts_in, small = sort_out(0, len(routes.back[0]), parts_in, small, (block_out,))
    staged = Clock.tick
    grad_roll = ticked(last_call, x, gx1, g_h1, g_h1_other, norm_params)
    grad_tokens = roll_rows(grad_roll, tok - start[0])

    kept, sent, small = owned_call(table, place, routes, (parts_in, parts_mlp), small, (grad_tokens,))
    small_x = swap_mp(small)
    arrived = routes.swap_cores(sent)

    def slow_grads():
        def stack(in_part, mlp_part):
            return jnp.concatenate([pieces(in_part), pieces(mlp_part)], axis=0).astype(F32)

        mine, other = stack(g_in_m, g_mlp_m), stack(g_in_o[: g_in_m.shape[0]], g_mlp_o)
        both = jnp.where(first_core, jnp.stack([mine, other], 1), jnp.stack([other, mine], 1))
        total, bit = both, 1
        while bit < dp_size:
            total = total + lax.ppermute(total, "dp", pairs_apart(bit))
            bit *= 2
        total = total[jnp.maximum(table[place["piece"], :slot_cap], 0)]
        return half(total, core), half(total, 1 - core)

    tables = (weight_table[0], moment_table[0], square_table[0])

    def update(kept, arrived, tables):
        return ticked(
            adam_call, table, place["piece"], core, (n_qkv, n_first, n_first + n_up), kept, arrived, tables
        )

    tables_next = update(kept, arrived, keep_call(tables, (staged,)))
    updated = Clock.tick
    tables_next = unless(table[place["over"], 0], tuple(tables_next), lambda: tuple(update(*slow_grads(), tables)))
    small_out = small_call(
        small, small_x,
        (norm_params, norm_moment, norm_square), (bias_params, bias_moment, bias_square),
        (updated,),
    )
    return (block_out, grad_tokens, *(part[None] for part in tables_next), *small_out)


def solution(mesh):
    flat = P("dp", None)
    pieces = P("mp", "dp", None, None)
    bias = P("mp", None)
    return jax.shard_map(
        body,
        mesh=mesh,
        in_specs=(flat, flat, flat, P(), pieces, pieces, pieces, P(), P(), P(), bias, bias, bias),
        out_specs=(flat, flat, pieces, pieces, pieces, P(), P(), P(), bias, bias, bias),
        check_vma=False,
    )
```

```python
import functools

import jax
import jax.numpy as jnp
import numpy as np
from jax import lax
from jax.experimental import pallas as pl
from jax.experimental.pallas import tpu as pltpu
from jax.sharding import PartitionSpec as P

HEADS = 20
HEAD_DIM = 32
HALF = HEAD_DIM // 2
FF = 2560
LONGEST = 1024
STEP = 10

EPS_NORM = 1e-05
BETA_ONE = 0.5
BETA_TWO = 0.5
ADAM_EPS = 1e-08
DECAY_RATE = 0.01
NEG_FILL = -1e30
NORM_RATES = (0.5, 0.1, 0.5, 0.1, 0.1, 0.1)
BIAS_RATE = 0.1
SCALE = HEAD_DIM**-0.5
LOG2_E = 1.4426950408889634
SCALE_LOG2 = SCALE * LOG2_E
SAFE_EXP = 100.0

BF = jnp.bfloat16
F32 = jnp.float32
I32 = jnp.int32
TILE = 256
LANES = 128
TICK = (8, 128)
HEADS_EACH = 5
FORWARD_HEADS_EACH = 1
VMEM_LIMIT = 16 << 20
SHRINK = 0.1


def params(*kinds):
    return pltpu.CompilerParams(dimension_semantics=kinds or None, vmem_limit_bytes=VMEM_LIMIT)


def cost(flops, moved):
    return pl.CostEstimate(flops=int(flops / SHRINK), bytes_accessed=int(moved / SHRINK), transcendentals=0)


def dot_nn(a, b):
    return lax.dot_general(a, b, (((1,), (0,)), ((), ())), preferred_element_type=F32)


def dot_nt(a, b):
    return lax.dot_general(a, b, (((1,), (1,)), ((), ())), preferred_element_type=F32)


def dot_tn(a, b):
    return lax.dot_general(a, b, (((0,), (0,)), ((), ())), preferred_element_type=F32)


def split_two(v):
    hi = v.astype(BF).astype(F32)
    return hi, v - hi


def split_three(v):
    hi = v.astype(BF).astype(F32)
    mid = (v - hi).astype(BF).astype(F32)
    return hi, mid, v - hi - mid


def normalized(v):
    centred = v - jnp.mean(v, axis=-1, keepdims=True)
    inv = lax.rsqrt(jnp.mean(centred * centred, axis=-1, keepdims=True) + EPS_NORM)
    return centred * inv, inv


ANYWHERE = pl.BlockSpec(memory_space=pl.ANY)
SMEM = pl.BlockSpec(memory_space=pltpu.SMEM)
HBM = pl.BlockSpec(memory_space=pltpu.HBM)


def whole(shape):
    return pl.BlockSpec(shape, lambda *_: (0,) * len(shape))


def rows(width, begin=0):
    return pl.BlockSpec((TILE, width), lambda t: (begin + t, 0))


def cols(height, begin=0):
    return pl.BlockSpec((height, TILE), lambda t: (0, begin + t))


def both(height, begin=0):
    return pl.BlockSpec((2, height, TILE), lambda t: (0, 0, begin + t))


def last_rows(array, count):
    return pl.BlockSpec((count, array.shape[1]), lambda *_: (array.shape[0] // count - 1, 0))


def shaped(shape, dtype):
    return jax.ShapeDtypeStruct(shape, dtype)


class Clock:
    wanted = False
    tick = None


def ticked(function, *args, **named):
    Clock.wanted = True
    results = function(*args, **named)
    Clock.wanted = False
    return results


def call(kernel, args, in_specs, out_specs, out_shape, name, deps=(), scratch=(), limit=VMEM_LIMIT, late=(), **more):
    count = len(args)
    single = not isinstance(out_shape, (list, tuple))
    out_specs, out_shape = ([out_specs], [out_shape]) if single else (list(out_specs), list(out_shape))
    if any(spec is not ANYWHERE for spec in in_specs):
        more.setdefault("grid", (1,))

    if "input_output_aliases" in more:
        aliases = more["input_output_aliases"]
        more["input_output_aliases"] = {len(deps) + at: to for at, to in aliases.items()}
    real, ticks = len(out_shape), Clock.wanted
    if ticks:
        out_specs, out_shape = out_specs + [whole(TICK)], out_shape + [shaped(TICK, F32)]

    def wrapped(*refs):
        ins, outs = refs[len(deps) : len(deps) + count], refs[len(deps) + count + len(late) :]
        if ticks:
            outs[real][...] = jnp.zeros(TICK, F32)
        kernel(*ins, *outs[:real], *outs[real + ticks :])

    results = pl.pallas_call(
        wrapped,
        in_specs=[ANYWHERE] * len(deps) + list(in_specs) + [ANYWHERE] * len(late),
        out_specs=out_specs,
        out_shape=out_shape,
        scratch_shapes=list(scratch),
        compiler_params=pltpu.CompilerParams(
            dimension_semantics=("arbitrary",) * len(more.get("grid", ())) or None,
            vmem_limit_bytes=limit,
        ),
        name=name,
        **more,
    )(*deps, *args, *late)
    if ticks:
        Clock.tick = results[-1]
        results = results[:-1]
    return results[0] if single else results


def rolled(array, start):
    tok = array.shape[0]
    shift = jnp.where(start == 0, 0, tok - start)
    return pltpu.roll(array.astype(F32), shift, 0)


def roll_kernel(start_ref, array_ref, out_ref):
    out_ref[...] = rolled(array_ref[...], start_ref[0]).astype(BF)


def roll_call(start, array, deps=()):
    return call(
        roll_kernel, (start, array), [SMEM, whole(array.shape)], whole(array.shape),
        shaped(array.shape, BF), "roll", deps,
    )


def norm_kernel(start_ref, x_ref, norm_ref, out_ref, a_ref, turned):
    turned[...] = rolled(x_ref[...], start_ref[0])
    for at in range(0, x_ref.shape[0], LANES):
        here = slice(at, at + LANES)
        value = turned[here, :]
        out_ref[here, :] = value.astype(BF)
        n1, _ = normalized(value)
        a_ref[here, :] = (n1 * norm_ref[0:1] + norm_ref[1:2]).astype(BF)


def norm_call(start, x, norms):
    return call(
        norm_kernel,
        (start, x, norms),
        [SMEM, whole(x.shape), whole(norms.shape)],
        [whole(x.shape)] * 2,
        [shaped(x.shape, BF)] * 2,
        "first_norm",
        scratch=[pltpu.VMEM(x.shape, F32)],
        limit=2 * VMEM_LIMIT,
    )


def qkv_kernel(a_ref, wm_ref, wo_ref, bm_ref, bo_ref, cos_ref, sin_ref, m_ref, o_ref, safe_ref, top, bias):
    step = pl.program_id(0)

    @pl.when(step == 0)
    def _():
        top[...] = jnp.zeros_like(top)
        for which, ref in enumerate((bm_ref, bo_ref)):
            bias[which] = jnp.transpose(jnp.broadcast_to(ref[...], (LANES, ref.shape[1])))

    a1 = a_ref[...]
    mine = dot_nt(wm_ref[...], a1) + bias[0, :, 0:1]
    other = dot_nt(wo_ref[...], a1) + bias[1, :, 0:1]
    width = m_ref.shape[1]
    cos, sin = cos_ref[...], sin_ref[...]
    for which in range(2):
        longest = top[which : which + 1, :]
        for at in range(0, width, HALF):
            here = which * width + at
            p, r = mine[here : here + HALF], other[here : here + HALF]
            longest = jnp.maximum(longest, jnp.sum(p * p + r * r, axis=0, keepdims=True))
            m_ref[which, at : at + HALF, :] = (p * cos - r * sin).astype(BF)
            o_ref[which, at : at + HALF, :] = (r * cos + p * sin).astype(BF)
        top[which : which + 1, :] = longest
    m_ref[2] = mine[2 * width :].astype(BF)
    o_ref[2] = other[2 * width :].astype(BF)

    @pl.when(step == pl.num_programs(0) - 1)
    def _():
        bound = jnp.max(top[0:1, :]) * jnp.max(top[1:2, :]) * SCALE_LOG2**2
        safe_ref[0] = (bound < SAFE_EXP**2).astype(I32)


def qkv_call(a1, w_mine, w_other, b_mine, b_other, cos, sin, deps=()):
    tok, width = a1.shape
    out = b_mine.shape[1]
    third = pl.BlockSpec((3, out // 3, TILE), lambda t: (0, 0, t))
    return call(
        qkv_kernel,
        (a1, w_mine, w_other, b_mine, b_other, cos, sin),
        [
            rows(width), whole((out, width)), whole((out, width)),
            whole(b_mine.shape), whole(b_mine.shape), cols(HALF), cols(HALF),
        ],
        [third, third, SMEM],
        [shaped((3, out // 3, tok), BF)] * 2 + [shaped((1,), I32)],
        "qkv",
        deps,
        scratch=[pltpu.VMEM((8, TILE), F32), pltpu.VMEM((2, out, LANES), F32)],
        grid=(tok // TILE,),
        cost_estimate=cost(4 * tok * width * out, 8e6),
    )


def normal_tables(u):
    return 0.5 * (1.0 + lax.erf(u * 0.7071067811865476)), jnp.exp(-0.5 * u * u)


def mlp_kernel(
    groups, chained, *refs,
):
    x_ref, gy_ref, *refs = refs[chained:]
    ctx_refs, refs = refs[: 2 * groups], refs[2 * groups :]
    wp_mine, wp_other, wx_mine, wx_other, w_mine, w_other, bup_ref, norm_ref = refs[:8]
    refs = refs[8:]
    x1_ref, a2_ref, act_ref, gpre_ref, ffn_ref, gh_ref, gbup_ref, out_w, up_w, down_w = refs

    @pl.when(pl.program_id(0) == 0)
    def _():
        quarter, half = wx_mine.shape[0], up_w.shape[0] // 2
        for at, ref in enumerate((wp_mine, wp_other, wx_mine, wx_other)):
            out_w[at * quarter : (at + 1) * quarter, :] = ref[...]
        for at, ref in enumerate((w_mine, w_other)):
            up_w[at * half : (at + 1) * half, :] = ref[:half, :]
            down_w[at * half : (at + 1) * half, :] = ref[half:, :]

    gy = gy_ref[...]
    own, far = ctx_refs[0::2], ctx_refs[1::2]
    ctx = jnp.concatenate([ref[j] for some in (own, far) for j in range(2) for ref in some], axis=0)
    x1 = x_ref[...].astype(F32) + dot_tn(ctx, out_w[...]) + norm_ref[4:5]
    x1_ref[...] = x1
    n2, _ = normalized(x1)
    a2 = (n2 * norm_ref[2:3] + norm_ref[3:4]).astype(BF)
    a2_ref[...] = a2
    pre = dot_nt(a2, up_w[...]) + bup_ref[...]
    cdf, bell = normal_tables(pre)
    act = (pre * cdf).astype(BF)
    act_ref[...] = act
    slope = cdf + pre * (bell * 0.3989422804014327)
    gpre = (slope * dot_nt(gy, down_w[...])).astype(BF)
    gpre_ref[...] = gpre
    ffn_ref[...] = dot_nn(act, down_w[...]).astype(BF)
    gh_ref[...] = dot_nn(gpre, up_w[...]).astype(BF)
    part = jnp.sum(gpre.astype(F32), axis=0, keepdims=True)

    @pl.when(pl.program_id(0) == 0)
    def _():
        gbup_ref[...] = part

    @pl.when(pl.program_id(0) > 0)
    def _():
        gbup_ref[...] += part


def mlp_call(span, x, gy, ctx, wp, wx, w_mine, w_other, b_up, norms, before=(), deps=()):
    tok, width = x.shape
    hidden = b_up.shape[1]
    quarter = wx[0].shape[0]
    begin, count = span[0], span[1] - span[0]
    args = (*before, x, gy, *ctx, *wp, *wx, w_mine, w_other, b_up, norms)
    return call(
        functools.partial(mlp_kernel, len(ctx) // 2, len(before)),
        args,
        [ANYWHERE] * len(before)
        + [rows(width, begin)] * 2
        + [both(part.shape[1]) for part in ctx]
        + [last_rows(wp[0], quarter)] * 2
        + [whole((quarter, width))] * 2
        + [whole(w_mine.shape)] * 2
        + [whole(b_up.shape), whole(norms.shape)],
        [
            rows(width, begin), rows(width, begin), rows(hidden, begin), rows(hidden, begin),
            rows(width, begin), rows(width), whole((1, hidden)),
        ],
        [
            shaped((tok, width), F32), shaped((tok, width), BF), shaped((tok, hidden), BF),
            shaped((tok, hidden), BF), shaped((tok, width), BF), shaped((count * TILE, width), BF),
            shaped((1, hidden), F32),
        ],
        "mlp",
        deps,
        scratch=[
            pltpu.VMEM((4 * quarter, width), BF), pltpu.VMEM((hidden, width), BF),
            pltpu.VMEM((hidden, width), BF),
        ],
        grid=(count,),
        cost_estimate=cost(2 * count * TILE * width * (hidden * 4 + 4 * quarter) * 1.6, 2e7),
        input_output_aliases={j: j for j in range(len(before))},
    )


def mlp_grads_kernel(act_ref, gpre_ref, a2_ref, gy_ref, mine_ref, other_ref, down_sum, up_sum):
    step = pl.program_id(0)
    down = dot_tn(act_ref[...], gy_ref[...])
    up = dot_tn(gpre_ref[...], a2_ref[...])

    @pl.when(step == 0)
    def _():
        down_sum[...] = down
        up_sum[...] = up

    @pl.when(step > 0)
    def _():
        down_sum[...] += down
        up_sum[...] += up

    @pl.when(step == pl.num_programs(0) - 1)
    def _():
        half = down_sum.shape[0] // 2
        for which, out_ref in enumerate((mine_ref, other_ref)):
            here = pl.ds(which * half, half)
            out_ref[:half, :] = up_sum[here, :].astype(BF)
            out_ref[half:, :] = down_sum[here, :].astype(BF)


def mlp_grads_call(act, gpre, a2, gy, deps=()):
    tok, hidden = act.shape
    width = a2.shape[1]
    return call(
        mlp_grads_kernel,
        (act, gpre, a2, gy),
        [rows(hidden), rows(hidden), rows(width), rows(width)],
        [whole((hidden, width))] * 2,
        [shaped((hidden, width), BF)] * 2,
        "mlp_grads",
        deps,
        scratch=[pltpu.VMEM((hidden, width), F32)] * 2,
        grid=(tok // TILE,),
        cost_estimate=cost(4 * tok * width * hidden * 1.3, 1.4e7),
    )


def mid_kernel(
    groups, chained, handed, x1_ref, gy_ref, gh_a, gh_b, *refs,
):
    ctx_refs, refs = refs[:groups], refs[groups:]
    wm_ref, wo_ref, norm_ref = refs[:3]
    refs = refs[3 + chained + handed :]
    gx_ref, g_out, gout_ref, sum_ref = refs[:4]
    cm, co = (jnp.concatenate([ref[j] for ref in ctx_refs], axis=0) for j in range(2))
    step = pl.program_id(0)
    gy = gy_ref[...].astype(F32)
    gh = gh_a[...].astype(F32) + gh_b[...].astype(F32)
    n2, inv = normalized(x1_ref[...])
    e = gh * norm_ref[2:3]
    gx = gy + inv * (
        e - jnp.mean(e, axis=-1, keepdims=True) - n2 * jnp.mean(e * n2, axis=-1, keepdims=True)
    )
    gx_ref[...] = gx
    gm = gx.astype(BF)
    g_out[0] = dot_nt(wm_ref[...], gm).astype(BF)
    g_out[1] = dot_nt(wo_ref[...], gm).astype(BF)

    @pl.when(step == 0)
    def _():
        gout_ref[...] = jnp.zeros_like(gout_ref)
        sum_ref[...] = jnp.zeros_like(sum_ref)

    gout_ref[0] += dot_nn(cm, gm)
    gout_ref[1] += dot_nn(co, gm)
    for at, value in enumerate((gh * n2, gh, gx, gy)):
        sum_ref[at : at + 1, :] += jnp.sum(value, axis=0, keepdims=True)


def mid_call(span, x1, gy, gh, gh_other, ctx, w_m, w_o, norms, before=(), hand=(), deps=()):
    tok, width = x1.shape
    head = sum(part.shape[1] for part in ctx)
    begin, count = span[0], span[1] - span[0]
    args = (x1, gy, gh, gh_other, *ctx, w_m, w_o, norms, *before, *hand)
    fixed = len(args) - len(before) - len(hand)
    aliases = {fixed + j: j for j in range(len(before))}
    aliases.update({fixed + len(before) + j: 4 + j for j in range(len(hand))})
    return call(
        functools.partial(mid_kernel, len(ctx), len(before), len(hand)),
        args,
        [rows(width, begin)] * 2
        + [rows(width)] * 2
        + [both(part.shape[1]) for part in ctx]
        + [last_rows(w_m, head)] * 2
        + [whole(norms.shape)]
        + [ANYWHERE] * (len(before) + len(hand)),
        [rows(width, begin), both(head), whole((2, head, width)), whole((8, width))]
        + [ANYWHERE] * len(hand),
        [
            shaped((tok, width), F32), shaped((2, head, count * TILE), BF),
            shaped((2, head, width), F32), shaped((8, width), F32),
        ]
        + [shaped(part.shape, part.dtype) for part in hand],
        "mid_back",
        deps,
        grid=(count,),
        cost_estimate=cost(8 * count * TILE * width * head * 2, 1e7),
        input_output_aliases=aliases,
    )


def pack_small(value):
    hi = value.astype(BF).astype(F32)
    row = lax.broadcasted_iota(I32, value.shape, 0)
    rest = jnp.where(row < 6, value - hi, 0.0)
    return jnp.where(row < 10, hi, pltpu.roll(rest, 10, 0)).astype(BF)


def unpack_small(packed):
    packed = packed.astype(F32)
    row = lax.broadcasted_iota(I32, packed.shape, 0)
    return jnp.where(row < 10, packed, 0.0) + jnp.where(row < 6, pltpu.roll(packed, 6, 0), 0.0)


def in_grads_kernel(groups, gouts, *refs):
    g_refs, out_refs, refs = refs[:groups], refs[groups : groups + gouts], refs[groups + gouts :]
    a1_ref, mine_ref, other_ref, m_sum, o_sum = refs
    step = pl.program_id(0)
    a1 = a1_ref[...]
    for half, total in enumerate((m_sum, o_sum)):
        part = dot_nn(jnp.concatenate([ref[half, j] for j in range(3) for ref in g_refs], axis=0), a1)

        @pl.when(step == 0)
        def _():
            total[...] = part

        @pl.when(step > 0)
        def _():
            total[...] += part

    @pl.when(step == pl.num_programs(0) - 1)
    def _():
        count = m_sum.shape[0]
        for ref, total, half in ((mine_ref, m_sum, 0), (other_ref, o_sum, 1)):
            ref[:count, :] = total[...].astype(BF)
            ref[count:, :] = sum((out[half] for out in out_refs[1:]), out_refs[0][half]).astype(BF)


def grad_tiles(grads):
    return [pl.BlockSpec(part.shape[:3] + (TILE,), lambda t: (0, 0, 0, t)) for part in grads]


def in_grads_call(grads, a1, gouts, deps=()):
    tok, width = a1.shape
    count = sum(part.shape[1] * part.shape[2] for part in grads)
    more = gouts[0].shape[1]
    return call(
        functools.partial(in_grads_kernel, len(grads), len(gouts)),
        (*grads, *gouts, a1),
        grad_tiles(grads) + [whole(part.shape) for part in gouts] + [rows(width)],
        [whole((count + more, width))] * 2,
        [shaped((count + more, width), BF)] * 2,
        "in_grads",
        deps,
        scratch=[pltpu.VMEM((count, width), F32)] * 2,
        grid=(tok // TILE,),
        cost_estimate=cost(4 * tok * width * count * 1.3, 1e7),
    )


def in_back_kernel(groups, gouts, *refs):
    g_refs, mid_refs, up_refs, refs = (
        refs[:groups], refs[groups : groups + gouts], refs[groups + gouts : groups + 2 * gouts],
        refs[groups + 2 * gouts :],
    )
    core_ref, x_ref, wm_ref, wo_ref, gh_ref, sum_ref, gbm_ref, gbo_ref = refs
    step = pl.program_id(0)
    count = wm_ref.shape[0]
    gm, go = (
        jnp.concatenate([ref[half, j] for j in range(3) for ref in g_refs], axis=0)
        for half in range(2)
    )

    @pl.when(step == 0)
    def _():
        gbm_ref[...] = jnp.zeros_like(gbm_ref)
        gbo_ref[...] = jnp.zeros_like(gbo_ref)
        sum_ref[...] = jnp.zeros_like(sum_ref)

    gbm_ref[...] += jnp.sum(gm.astype(F32), axis=1, keepdims=True)
    gbo_ref[...] += jnp.sum(go.astype(F32), axis=1, keepdims=True)
    gh = dot_tn(gm, wm_ref[...]) + dot_tn(go, wo_ref[...])
    gh_ref[...] = gh.astype(BF)
    n1, _ = normalized(x_ref[...].astype(F32))
    sum_ref[0:1, :] += jnp.sum(gh * n1, axis=0, keepdims=True)
    sum_ref[1:2, :] += jnp.sum(gh, axis=0, keepdims=True)

    @pl.when(step == pl.num_programs(0) - 1)
    def _():
        width = gh.shape[1]
        up = sum((ref[...] for ref in up_refs[1:]), up_refs[0][...])
        sum_ref[2:6, :] = sum((ref[0:4, :] for ref in mid_refs[1:]), mid_refs[0][0:4, :])

        def column(row):
            return jnp.transpose(jnp.broadcast_to(row, (LANES, row.shape[1])))[:, 0:1]

        swapped = core_ref[0] == 1
        mixed = []
        for mine, other in ((gbm_ref[...], gbo_ref[...]), (column(up[:, :width]), column(up[:, width:]))):
            lower, upper = jnp.where(swapped, other, mine), jnp.where(swapped, mine, other)
            for at in range(0, mine.shape[0], HALF):
                mixed += [lower[at : at + HALF], upper[at : at + HALF]]
        natural = jnp.concatenate(mixed, axis=0)
        natural = jnp.transpose(jnp.broadcast_to(natural, (natural.shape[0], LANES)))[0:1]
        for at in range(0, natural.shape[1], width):
            part = natural[:, at : at + width]
            sum_ref[6 + at // width : 7 + at // width, : part.shape[1]] = part


def in_back_call(grads, core, x, w_m, w_o, mid_sums, gb_ups, deps=()):
    tok, width = x.shape
    count = sum(part.shape[1] * part.shape[2] for part in grads)
    return call(
        functools.partial(in_back_kernel, len(grads), len(mid_sums)),
        (*grads, *mid_sums, *gb_ups, core[None], x, w_m, w_o),
        grad_tiles(grads)
        + [whole(part.shape) for part in (*mid_sums, *gb_ups)]
        + [SMEM, rows(width)]
        + [whole((count, width))] * 2,
        [rows(width), whole((16, width))],
        [shaped((tok, width), BF), shaped((16, width), F32)],
        "in_back",
        deps,
        scratch=[pltpu.VMEM((count, 1), F32)] * 2,
        grid=(tok // TILE,),
        cost_estimate=cost(4 * tok * width * count * 1.3, 1e7),
    )


def out_kernel(x1_ref, a_ref, b_ref, norm_ref, out_ref):
    out_ref[...] = x1_ref[...] + (a_ref[...].astype(F32) + b_ref[...].astype(F32)) + norm_ref[5:6]


def out_call(x1, ffn_a, ffn_b, norms, deps=()):
    tok, width = x1.shape
    return call(
        out_kernel,
        (x1, ffn_a, ffn_b, norms),
        [rows(width)] * 3 + [whole(norms.shape)],
        rows(width),
        shaped((tok, width), F32),
        "layer_out",
        late=deps,
        grid=(tok // TILE,),
        cost_estimate=cost(4e9, 1e7),
    )


def nothing_kernel(*refs):
    pass


def hand_call(arrays, deps):
    return call(
        nothing_kernel, arrays, [ANYWHERE] * len(arrays), [ANYWHERE] * len(arrays),
        [shaped(array.shape, array.dtype) for array in arrays], "hand", deps,
        input_output_aliases={at: at for at in range(len(arrays))},
    )


def keep_kernel(*refs):
    half = len(refs) // 2
    for source, target in zip(refs[:half], refs[half:]):
        target[...] = source[...]


def keep_call(arrays, deps=()):
    specs = [whole(array.shape) for array in arrays]
    return call(
        keep_kernel, arrays, specs, specs, [shaped(a.shape, a.dtype) for a in arrays], "keep", deps,
        cost_estimate=cost(4e9, 1e7),
    )


def sum_kernel(a_ref, b_ref, out_ref):
    out_ref[...] = a_ref[...] + b_ref[...]


def sum_call(a, b, deps):
    return call(
        sum_kernel, (a, b), [whole(a.shape)] * 2, whole(a.shape), shaped(a.shape, F32), "sum", deps
    )


def last_kernel(x_ref, gx_ref, gh_a, gh_b, norm_ref, out_ref):
    n1, inv = normalized(x_ref[...].astype(F32))
    e = (gh_a[...].astype(F32) + gh_b[...].astype(F32)) * norm_ref[0:1]
    out_ref[...] = gx_ref[...] + inv * (
        e - jnp.mean(e, axis=-1, keepdims=True) - n1 * jnp.mean(e * n1, axis=-1, keepdims=True)
    )


def last_call(x, gx, gh_a, gh_b, norms, deps=()):
    tok, width = x.shape
    return call(
        last_kernel,
        (x, gx, gh_a, gh_b, norms),
        [rows(width)] * 4 + [whole(norms.shape)],
        rows(width),
        shaped((tok, width), F32),
        "last_back",
        deps,
        grid=(tok // TILE,),
        cost_estimate=cost(1e6, 1.2e7),
    )


def layout_kernel(core_ref, len_ref, freq_ref, bias_ref, cos_ref, sin_ref, row_ref, col_ref, bm_ref, bo_ref, bup_ref, start_ref):
    tok = cos_ref.shape[1]
    docs = len_ref.shape[1]
    begin, best, start = 0, len_ref[0, 0], 0
    begins, ends = [], []
    for doc in range(docs):
        size = len_ref[0, doc]
        if doc:
            start = jnp.where(size > best, begin, start)
            best = jnp.maximum(size, best)
        begins.append(begin)
        begin = begin + size
        ends.append(begin)
    start_ref[0] = start + jnp.zeros((), I32)

    def origin(places):
        at = places + start
        return jnp.where(at >= tok, at - tok, at)

    def document(at):
        return sum(((at >= end).astype(I32) for end in ends), jnp.zeros(at.shape, I32))

    row = origin(lax.broadcasted_iota(I32, (1, tok), 1))
    first = jnp.zeros((1, tok), I32)
    for begin in begins[1:]:
        first = jnp.where(row >= begin, begin, first)
    angles = freq_ref[...] * (row - first).astype(F32)
    cos_ref[...] = jnp.cos(angles)
    sine = jnp.sin(angles)
    sin_ref[...] = jnp.where(core_ref[0] == 0, sine, -sine)
    column = jnp.transpose(jnp.broadcast_to(bias_ref[...], (LANES, bias_ref.shape[1])))[:, 0:1]
    lower, upper = (
        jnp.concatenate(
            [column[at : at + HALF] for at in range(begin, column.shape[0], HEAD_DIM)], axis=0
        )
        for begin in (0, HALF)
    )
    swapped = core_ref[0] == 1
    mine, other = jnp.where(swapped, upper, lower), jnp.where(swapped, lower, upper)
    count = bm_ref.shape[1]
    for which, (half, ref) in enumerate(((mine, bm_ref), (other, bo_ref))):
        turned = jnp.transpose(jnp.broadcast_to(half, (half.shape[0], LANES)))[0:1]
        length = half.shape[0] - count
        ref[...] = turned[:, :count]
        bup_ref[:, which * length : (which + 1) * length] = turned[:, count:]
    rest = row_ref.shape[1]
    row_ref[...] = document(row[:, tok - rest :])
    col_ref[...] = document(origin(lax.broadcasted_iota(I32, (rest, 1), 0) + (tok - rest)))


def layout_call(core, lengths, biases, tok, n_qkv, deps=()):
    rest, n_up = tok - LONGEST, biases.shape[1] - 2 * n_qkv
    freq = np.float32(10000.0) ** -(np.arange(0, HEAD_DIM, 2).astype(np.float32) / HEAD_DIM)
    return call(
        layout_kernel,
        (core[None], lengths, jnp.asarray(freq[:, None], F32), biases),
        [SMEM, SMEM, whole((HALF, 1)), whole(biases.shape)],
        [whole((HALF, tok))] * 2
        + [whole((1, rest)), whole((rest, 1)), whole((1, n_qkv)), whole((1, n_qkv)), whole((1, n_up)), SMEM],
        [shaped((HALF, tok), F32)] * 2
        + [
            shaped((1, rest), I32), shaped((rest, 1), I32), shaped((1, n_qkv), F32),
            shaped((1, n_qkv), F32), shaped((1, n_up), F32), shaped((1,), I32),
        ],
        "layout",
        deps,
    )


def halves_kernel(core_ref, table_ref, mine_ref, other_ref):
    first = core_ref[0] == 0
    count = mine_ref.shape[1]
    upper, lower = table_ref[:, :count, :], table_ref[:, count:, :]
    mine_ref[...] = jnp.where(first, upper, lower).astype(BF)
    other_ref[...] = jnp.where(first, lower, upper).astype(BF)


def halves_call(core, table):
    cap, count, width = table.shape
    half = (cap, count // 2, width)
    return call(
        halves_kernel,
        (core[None], table),
        [SMEM, whole(table.shape)],
        [whole(half)] * 2,
        [shaped(half, BF)] * 2,
        "halves",
    )


def by_heads(kernel, which, each):
    def step(*refs):
        for head in range(each):
            views = []
            for ref, dim in zip(refs, which):
                if dim is not None:
                    size = ref.shape[dim] // each
                    ref = ref.at[(slice(None),) * dim + (pl.ds(head * size, size),)]
                views.append(ref)
            kernel(*views)

    return step


def attend_kernel(cut, safe_ref, seg_row, seg_col, m_ref, o_ref, *outs):
    tok = m_ref.shape[2]
    rest = tok - LONGEST
    q_t, k_t, v_t = (jnp.concatenate([m_ref[j], o_ref[j]], axis=0) for j in range(3))
    qs = q_t.astype(F32) * SCALE_LOG2
    hi, lo = split_two(qs)
    qx = jnp.transpose(jnp.concatenate([hi, lo], axis=0)).astype(BF)
    kx = jnp.concatenate([k_t, k_t], axis=0)
    v_f = v_t.astype(F32)
    vx = jnp.transpose(jnp.concatenate([v_f, jnp.ones((8, tok), F32)], axis=0)).astype(BF)
    safe = safe_ref[0] > 0

    def finish(sums, shift, at, count):
        turned = jnp.transpose(sums)
        total = turned[HEAD_DIM : HEAD_DIM + 1]
        ctx = (turned[0:HEAD_DIM] / total).astype(BF)
        ctx_ref, log_ref = outs[:2] if at < cut else outs[2:]
        here = slice(at, at + count) if at < cut else slice(at - cut, at - cut + count)
        ctx_ref[0, :, here] = ctx[:HALF]
        ctx_ref[1, :, here] = ctx[HALF:]
        log_total = jnp.log2(total)
        if shift is not None:
            log_total = log_total + jnp.transpose(jnp.broadcast_to(shift, (count, LANES)))[0:1]
        log_ref[0, :, here] = log_total

    def run(exact):
        for at in range(0, LONGEST, TILE):
            scores = dot_nn(qx[at : at + TILE], kx[:, :LONGEST])
            shift = None
            if exact:
                shift = jnp.max(scores, axis=1, keepdims=True)
                scores = scores - shift
            finish(dot_nn(jnp.exp2(scores).astype(BF), vx[:LONGEST]), shift, at, TILE)
        if rest:
            same = seg_col[...] == seg_row[...]
            scores = jnp.where(same, dot_nn(qx[LONGEST:], kx[:, LONGEST:]), NEG_FILL)
            shift = None
            if exact:
                shift = jnp.max(scores, axis=1, keepdims=True)
                scores = scores - shift
            finish(dot_nn(jnp.exp2(scores).astype(BF), vx[LONGEST:]), shift, LONGEST, rest)

    @pl.when(safe)
    def _():
        run(False)

    @pl.when(jnp.logical_not(safe))
    def _():
        run(True)


def attend_call(cut, safe, segs, qkv_m, qkv_o, first, count, deps=()):
    tok = qkv_m.shape[2]
    rest = segs[0].shape[1]
    each = FORWARD_HEADS_EACH
    first = first // each
    part = pl.BlockSpec((3, each * HALF, tok), lambda h: (0, first + h, 0))
    out_specs, out_shape = [], []
    for length in (cut, tok - cut):
        out_specs += [
            pl.BlockSpec((2, each * HALF, length), lambda h: (0, h, 0)),
            pl.BlockSpec((each, 1, length), lambda h: (h, 0, 0)),
        ]
        out_shape += [shaped((2, count * HALF, length), BF), shaped((count, 1, length), F32)]
    return call(
        by_heads(functools.partial(attend_kernel, cut), (None, None, None, 1, 1, 1, 0, 1, 0), each),
        (safe, *segs, qkv_m, qkv_o),
        [SMEM, whole((1, rest)), whole((rest, 1)), part, part],
        out_specs,
        out_shape,
        "attend",
        deps,
        grid=(count // each,),
        cost_estimate=cost(count * 2.2e9, 3e6),
    )


def attend_back_kernel(
    q_begin, q_end, last, seg_row, seg_col, cos_ref, sin_ref, m_ref, o_ref, g_ref, ctx_ref, log_ref,
    *refs,
):
    tok = m_ref.shape[2]
    rest = tok - LONGEST
    end = tok if last else q_end
    span = slice(q_begin, end)
    q_t, k_t, v_t = (jnp.concatenate([m_ref[j], o_ref[j]], axis=0) for j in range(3))
    q_f = q_t[:, span].astype(F32)
    ctx = jnp.concatenate([ctx_ref[0], ctx_ref[1]], axis=0).astype(F32)
    g_f = jnp.concatenate([g_ref[0], g_ref[1]], axis=0).astype(F32)
    hi, lo = split_two(q_f * SCALE_LOG2)
    weighted = jnp.sum(g_f * ctx, axis=0, keepdims=True)
    pad = jnp.zeros((13, end - q_begin), F32)
    qx = jnp.concatenate([hi, lo, *split_three(log_ref[0]), pad], axis=0).astype(BF)
    keys = tok if last else LONGEST
    k_f, v_f = k_t[:, :keys].astype(F32), v_t[:, :keys].astype(F32)
    minus = jnp.concatenate([jnp.full((3, keys), -1.0, F32), jnp.zeros((13, keys), F32)], axis=0)
    kx = jnp.transpose(jnp.concatenate([k_f, k_f, minus], axis=0)).astype(BF)
    gx = jnp.concatenate([g_f, *split_three(weighted), pad], axis=0).astype(BF)
    vx = jnp.transpose(jnp.concatenate([v_f, minus], axis=0)).astype(BF)
    qn = jnp.transpose(q_f).astype(BF)
    gn = jnp.transpose(g_f).astype(BF)

    if last:
        early_q, early_kv, out_ref = refs
    else:
        out_q, out_kv = refs

    def turned_back(grad, at, count):
        cos, sin = cos_ref[:, at : at + count], sin_ref[:, at : at + count]
        mine, other = grad[0:HALF] * SCALE, grad[HALF:] * SCALE
        return (mine * cos + other * sin).astype(BF), (other * cos - mine * sin).astype(BF)

    def block(k_at, k_count, q_at, q_count, mask, early):
        scores = dot_nn(kx[k_at : k_at + k_count], qx[:, q_at : q_at + q_count])
        if mask is not None:
            scores = jnp.where(mask, scores, NEG_FILL)
        prob = jnp.exp2(scores)
        grad_prob = dot_nn(vx[k_at : k_at + k_count], gx[:, q_at : q_at + q_count])
        grad_score = (prob * grad_prob).astype(BF)
        grad_v = jnp.transpose(dot_nn(prob.astype(BF), gn[q_at : q_at + q_count]))
        grad_k = jnp.transpose(dot_nn(grad_score, qn[q_at : q_at + q_count]))
        here = slice(k_at, k_at + k_count)
        if not last:
            out_kv[0, 0, :, here] = grad_k
            out_kv[1, 0, :, here] = grad_v
        else:
            if early:
                grad_k = grad_k + early_kv[0, 0, :, here]
                grad_v = grad_v + early_kv[1, 0, :, here]
            out_ref[0, 1, :, here], out_ref[1, 1, :, here] = turned_back(grad_k, k_at, k_count)
            out_ref[0, 2, :, here] = grad_v[:HALF].astype(BF)
            out_ref[1, 2, :, here] = grad_v[HALF:].astype(BF)
        return dot_nn(k_t[:, k_at : k_at + k_count], grad_score)

    grad_q = None
    for at in range(0, LONGEST, TILE):
        piece = block(at, TILE, 0, q_end - q_begin, None, True)
        grad_q = piece if grad_q is None else grad_q + piece
    mine, other = turned_back(grad_q, q_begin, q_end - q_begin)
    if not last:
        out_q[0], out_q[1] = mine, other
        return
    out_ref[0, 0, :, :q_begin] = early_q[0]
    out_ref[1, 0, :, :q_begin] = early_q[1]
    out_ref[0, 0, :, q_begin:q_end] = mine
    out_ref[1, 0, :, q_begin:q_end] = other
    if rest:
        same = seg_col[...] == seg_row[...]
        piece = block(LONGEST, rest, LONGEST - q_begin, rest, same, False)
        out_ref[0, 0, :, LONGEST:], out_ref[1, 0, :, LONGEST:] = turned_back(piece, LONGEST, rest)


def attend_back_call(
    q_begin, q_end, segs, cos, sin, qkv_m, qkv_o, g_ctx, ctx, logs, first, count, early=(), deps=()
):
    tok = qkv_m.shape[2]
    last = len(early) > 0
    rest = segs[0].shape[1]
    each = HEADS_EACH
    first = first // each
    part = pl.BlockSpec((3, each * HALF, tok), lambda h: (0, first + h, 0))
    table = whole((HALF, tok))

    def by_head(length, offset=0):
        return pl.BlockSpec((2, each * HALF, length), lambda h: (0, offset + h, 0))

    pair = pl.BlockSpec((2, each, HEAD_DIM, LONGEST), lambda h: (0, h, 0, 0))
    if last:
        out_specs = [pl.BlockSpec((2, 3, each * HALF, tok), lambda h: (0, 0, h, 0))]
        out_shape = [shaped((2, 3, count * HALF, tok), BF)]
    else:
        out_specs = [by_head(q_end), pair]
        out_shape = [
            shaped((2, count * HALF, q_end), BF), shaped((2, count, HEAD_DIM, LONGEST), F32)
        ]
    return call(
        by_heads(
            functools.partial(attend_back_kernel, q_begin, q_end, last),
            (None,) * 4 + (1, 1, 1, 1, 0, 1, 1) + ((2,) if last else ()),
            each,
        ),
        (*segs, cos, sin, qkv_m, qkv_o, g_ctx, ctx, logs, *early),
        [
            whole((1, rest)), whole((rest, 1)), table, table, part, part,
            by_head(g_ctx.shape[2], first), by_head(ctx.shape[2]),
            pl.BlockSpec((each, 1, logs.shape[2]), lambda h: (h, 0, 0)),
        ]
        + ([by_head(q_begin), pair] if last else []),
        out_specs,
        out_shape,
        "attend_back",
        deps,
        grid=(count // each,),
        cost_estimate=cost(count * 2.1e9, 6e6),
    )


class Routes:
    def __init__(self, dp_size, slot_cap, pieces, ready, spans):
        self.dp = dp_size
        self.cap = slot_cap
        self.chips = dp_size // 2
        self.pieces = pieces
        self.ready = ready
        self.spans = spans
        if self.chips == 8:
            self.stages = ((2, 4), (1, 2))
        elif self.chips == 64:
            self.stages = ((1, 8), (8, 2), (16, 4))
        else:
            self.stages = ((1, self.chips),)
        self.depth = len(self.stages)
        straight = self.stages[::-1]
        paired = ((1, 2), (4, 2), (2, 2)) if self.chips == 8 else straight
        self.back = (straight, paired)
        self.out = (self.stages, ((4, 2), (2, 2), (1, 2)) if self.chips == 8 else self.stages)
        self.fill = [self.limit(last, self.chips) for last in ready]
        self.begins = [0] + self.fill[:-1]
        early, late = self.fill[0], self.fill[1] - self.fill[0]
        if self.chips == 8:
            self.bases = (
                [at * early for at in range(4)]
                + [4 * early]
                + [4 * early + self.fill[1] + at * early for at in range(3)],
                [7 * early + self.fill[1] + at * late for at in range(4)]
                + [5 * early]
                + [7 * early + self.fill[1] + at * late for at in range(4, 7)],
            )
        else:
            self.bases = tuple(
                [begin * self.chips + at * (end - begin) for at in range(self.chips)]
                for begin, end in zip(self.begins, self.fill)
            )

    def limit(self, count, groups):
        worst = min(count, self.dp // groups * self.cap)
        if self.chips != 8:
            return worst
        typical = {
            2: count * 11 // 20 + 8, 4: count * 3 // 10 + 10, 8: count // 5 + 5
        }[groups]
        return worst if count == self.pieces else min(worst, typical)

    def span_limit(self, number, level):
        groups = 1
        for _, size in self.back[number][:level]:
            groups *= size
        return self.limit(self.spans[number][1] - self.spans[number][0], groups)

    def move(self, array, stage, shift):
        stride, size = stage
        pairs = []
        for device in range(self.dp):
            chip, core = device // 2, device % 2
            at = (chip // stride) % size
            pairs.append((device, 2 * (chip + ((at + shift) % size - at) * stride) + core))
        return lax.ppermute(array, "dp", pairs)

    def swap_cores(self, array):
        return lax.ppermute(array, "dp", [(d, d ^ 1) for d in range(self.dp)])

    def around(self, array, stage):
        return [array] + [self.move(array, stage, shift) for shift in range(1, stage[1])]

    def onward(self, buffers, stage):
        return buffers + [
            self.move(buffer, stage, shift) for shift in range(1, stage[1]) for buffer in buffers
        ]

    def tables(self, owners, me):
        place = {}

        def kernel(me_ref, own_ref, out_ref, row_ref):
            here = me_ref[0]
            my_chip, my_core = here // 2, here % 2
            row_ref[...] = jnp.full((1, LANES), -2, I32)
            row_ref[:, : self.pieces] = own_ref[...]
            row = row_ref[...]
            col = jnp.transpose(jnp.broadcast_to(row, (LANES, LANES)))[:, 0:1]
            id_row = lax.broadcasted_iota(I32, (1, LANES), 1)
            id_col = lax.broadcasted_iota(I32, (LANES, 1), 0)
            lane = lax.broadcasted_iota(I32, (LANES, LANES), 1)
            sub = lax.broadcasted_iota(I32, (LANES, LANES), 0)

            def rank_col(key_row, key_col):
                hit = (key_row == key_col) & (lane < sub)
                return jnp.sum(hit.astype(F32), axis=1, keepdims=True).astype(I32)

            def rank_row(key_row, key_col):
                hit = (key_row == key_col) & (sub < lane)
                return jnp.sum(hit.astype(F32), axis=0, keepdims=True).astype(I32)

            def gather(valid_col, entry_col, value_col):
                hit = valid_col & (entry_col == lane)
                return jnp.sum(
                    jnp.where(hit, value_col.astype(F32), 0.0), axis=0, keepdims=True
                ).astype(I32)

            def put(name, value):
                at = place.setdefault(name, len(place))
                out_ref[at : at + 1, :] = value

            def coord(chip, stage):
                return (chip // stage[0]) % stage[1]

            def group(chip, stages):
                key = 0
                for stage in stages:
                    key = key * stage[1] + coord(chip, stage)
                return key

            def fullest(inside, rank):
                return jnp.max(jnp.where(inside, rank, -1), axis=0, keepdims=True) + 1

            slot_col = rank_col(row, col)
            put("piece", gather(col == here, slot_col, id_col + 1) - 1)
            sibling = my_chip * 2 + 1 - my_core
            put("sibling", gather(col == sibling, slot_col, id_col + 1) - 1)
            over = jnp.zeros((1, 1), I32)
            real = id_col < self.pieces
            chip_col, chip_row = col // 2, row // 2
            rank_c, rank_r = rank_col(chip_row, chip_col), rank_row(chip_row, chip_col)
            from_core = jnp.where(col % 2 == my_core, 0, self.cap)
            put("send", gather(real & (chip_col == my_chip), rank_c, from_core + slot_col))
            for last, fill in zip(self.ready, self.fill):
                over = jnp.maximum(over, fullest(id_col < last, rank_c) - fill)
            put("late", jnp.broadcast_to(over, (1, LANES)))
            over = jnp.zeros((1, 1), I32)
            take = jnp.zeros((1, LANES), I32)
            for begin, bases, stages in zip(self.begins, self.bases, self.out):
                way, scale = jnp.zeros((1, LANES), I32), 1
                for stage in stages:
                    away = (coord(my_chip, stage) - coord(chip_row, stage) + stage[1]) % stage[1]
                    way = way + away * scale
                    scale = scale * stage[1]
                spot = rank_r - begin
                for at, base in enumerate(bases):
                    spot = spot + jnp.where(way == at, base, 0)
                take = jnp.where(rank_r >= begin, spot, take)
            put("take", take)
            for number, span in enumerate(self.spans):
                in_col = (id_col >= span[0]) & (id_col < span[1])
                in_row = (id_row >= span[0]) & (id_row < span[1])
                stages = self.back[number]
                ranks = {}
                for level in range(1, len(stages) + 1):
                    key_col = jnp.where(in_col, group(chip_col, stages[:level]), -1)
                    key_row = jnp.where(in_row, group(chip_row, stages[:level]), -1)
                    ranks[level] = rank_col(key_row, key_col)
                    over = jnp.maximum(
                        over, fullest(in_col, ranks[level]) - self.span_limit(number, level)
                    )
                value = id_col - span[0]
                for level, stage in enumerate(stages, 1):
                    size = stage[1]
                    inside = in_col & (
                        group(chip_col, stages[: level - 1]) == group(my_chip, stages[: level - 1])
                    )
                    for shift in range(size):
                        goal = (coord(my_chip, stage) + shift) % size
                        put(
                            ("back", number, level, shift),
                            gather(inside & (coord(chip_col, stage) == goal), ranks[level], value),
                        )
                    value = ranks[level]
                for which in range(2):
                    goal = my_chip * 2 + (my_core + which) % 2
                    put(
                        ("slot", number, which),
                        gather(in_col & (col == goal), slot_col, ranks[len(stages)]),
                    )
            put("over", jnp.broadcast_to(over, (1, LANES)))

        count = 6 + sum(2 + sum(size for _, size in stages) for stages in self.back)
        height = -(-count // 8) * 8
        table = pl.pallas_call(
            kernel,
            in_specs=[SMEM, whole((1, self.pieces))],
            out_specs=whole((height, LANES)),
            out_shape=shaped((height, LANES), I32),
            scratch_shapes=[pltpu.VMEM((1, LANES), I32)],
            compiler_params=params(),
            name="routes",
        )(me[None], owners[None, :])
        return table, place


def fetch(sources, targets, sems):
    copies = [
        pltpu.make_async_copy(source, target, sems.at[at])
        for at, (source, target) in enumerate(zip(sources, targets))
    ]
    for copy in copies:
        copy.start()
    for copy in copies:
        copy.wait()


def places(kept, parts):
    return [ANYWHERE] * kept + [HBM] * (len(parts) - kept)


def pick_call(table, picks, parts, sizes, name, deps=(), kept=1):
    rows_each = [part.shape[0] for part in parts]
    shape = parts[0].shape[1:]

    def kernel(table_ref, *refs):
        ins, (*outs, source, sems) = refs[: len(parts)], refs[len(parts) :]
        at, targets = 0, []
        for count in rows_each:
            targets.append(source.at[pl.ds(at, count)])
            at += count
        fetch(ins, targets, sems)
        for (row, start), size, out in zip(picks, sizes, outs):
            for j in range(size):
                out[j] = source[table_ref[row, start + j]]

    return call(
        kernel,
        (table, *parts),
        [SMEM] + places(kept, parts),
        [whole((size,) + shape) for size in sizes],
        [shaped((size,) + shape, BF) for size in sizes],
        name,
        deps,
        scratch=[
            pltpu.VMEM((sum(rows_each),) + shape, BF), pltpu.SemaphoreType.DMA((len(parts),)),
        ],
    )


def join_call(parts, deps=()):
    counts = [part.shape[0] for part in parts]
    shape = (sum(counts),) + parts[0].shape[1:]

    def kernel(*refs):
        *ins, out, sems = refs
        at, targets = 0, []
        for count in counts:
            targets.append(out.at[pl.ds(at, count)])
            at += count
        fetch(ins, targets, sems)

    return call(
        kernel, parts, places(0, parts), whole(shape), shaped(shape, BF), "join", deps,
        scratch=[pltpu.SemaphoreType.DMA((len(parts),))],
    )


def add_pick_call(table, picks, parts, sizes, small=None, extra=(), deps=()):
    shape = parts[0].shape[1:]
    lengths = [size + (j in extra) for j, size in enumerate(sizes)]

    def kernel(table_ref, *refs):
        sources, refs = refs[: len(parts)], refs[len(parts) :]
        ins, sems, refs = refs[-len(parts) - 1 : -1], refs[-1], refs[: -len(parts) - 1]
        fetch(sources, ins, sems)
        if small is not None:
            small_ref, refs = refs[0], refs[1:]
            packed = pack_small(small_ref[...])
            refs[len(sizes)][...] = unpack_small(packed)
            for j in extra:
                refs[j][sizes[j]] = packed
        for (row, start), size, out in zip(picks, sizes, refs):
            for j in range(size):
                at = table_ref[row, start + j]
                total = ins[0][at].astype(F32)
                for ref in ins[1:]:
                    total = total + ref[at].astype(F32)
                out[j] = total.astype(BF)

    out_specs = [whole((length,) + shape) for length in lengths]
    out_shape = [shaped((length,) + shape, BF) for length in lengths]
    if small is not None:
        out_specs, out_shape = out_specs + [whole(shape)], out_shape + [shaped(shape, F32)]
    return call(
        kernel,
        (table, *parts) + (() if small is None else (small,)),
        [SMEM] + places(1, parts) + ([] if small is None else [whole(shape)]),
        out_specs,
        out_shape,
        "add_pick",
        late=deps,
        cost_estimate=cost(4e9, 1e7),
        scratch=[pltpu.VMEM(part.shape, BF) for part in parts]
        + [pltpu.SemaphoreType.DMA((len(parts),))],
    )


def owned_call(table, place, routes, parts, small, deps=()):
    (parts_in, parts_mlp), cap = parts, routes.cap
    parts = (*parts_in, *parts_mlp)
    shape = parts_in[0].shape[1:]
    border = routes.spans[1][0]

    def kernel(table_ref, *refs):
        sources, refs = refs[: len(parts)], refs[len(parts) :]
        small_ref, kept_ref, sent_ref, total_ref, *held, sems = refs
        fetch(sources, held, sems)
        ins, mlps = held[: len(parts_in)], held[len(parts_in) :]
        terms = [small_ref[...]] + [
            unpack_small(ref[ref.shape[0] - 1]) for ref in ins[1:]
        ]
        while len(terms) > 1:
            middle = len(terms) // 2
            terms = [a + b for a, b in zip(terms[:middle], terms[middle:])]
        total_ref[...] = terms[0]
        for which, (name, out) in enumerate((("piece", kept_ref), ("sibling", sent_ref))):
            for j in range(cap):
                sums = []
                for number, some in enumerate((ins, mlps)):
                    at = table_ref[place[("slot", number, which)], j]
                    total = some[0][at].astype(F32)
                    for ref in some[1:]:
                        total = total + ref[at].astype(F32)
                    sums.append(total)
                out[j] = jnp.where(table_ref[place[name], j] >= border, sums[1], sums[0])

    args = (table, *parts_in, *parts_mlp, small)
    return call(
        kernel,
        args,
        [SMEM]
        + places(1, parts_in)
        + places(1, parts_mlp)
        + [whole(shape)],
        [whole((cap,) + shape)] * 2 + [whole(shape)],
        [shaped((cap,) + shape, F32)] * 2 + [shaped(shape, F32)],
        "owned",
        deps,
        scratch=[pltpu.VMEM(part.shape, BF) for part in parts]
        + [pltpu.SemaphoreType.DMA((len(parts),))],
    )


def adam_step(weights, first_mom, second_mom, gradient, rate, decay_rate):
    first_new = BETA_ONE * first_mom + (1.0 - BETA_ONE) * gradient
    second_new = BETA_TWO * second_mom + (1.0 - BETA_TWO) * gradient * gradient
    first_fix = first_new / (1.0 - BETA_ONE**STEP)
    second_fix = second_new / (1.0 - BETA_TWO**STEP)
    weights_new = weights * (1.0 - rate * decay_rate) - rate * first_fix / (
        jnp.sqrt(second_fix) + ADAM_EPS
    )
    return (weights_new, first_new, second_new)


def adam_call(table, row, core, borders, kept, arrived, tables):
    cap, count, width = tables[0].shape
    half = count // 2
    group = max(g for g in range(1, 6) if cap % g == 0)

    def kernel(table_ref, core_ref, kept_ref, arrived_ref, w_ref, m_ref, v_ref, *outs):
        step = pl.program_id(0)
        swapped = core_ref[0] == 1
        for j in range(group):
            piece = table_ref[row, step * group + j]
            rate = jnp.where(piece < borders[2], 0.03, 0.015)
            rate = jnp.where(piece < borders[1], 0.2, rate)
            rate = jnp.where(piece < borders[0], 0.03, rate).astype(F32)
            halves = (kept_ref[j], arrived_ref[j])
            for at in range(2):
                here = pl.ds(at * half, half)
                grad = jnp.where(swapped, halves[1 - at], halves[at])
                new = adam_step(w_ref[j, here], m_ref[j, here], v_ref[j, here], grad, rate, DECAY_RATE)
                for out, value in zip(outs, new):
                    out[j, here] = jnp.where(piece >= 0, value, 0.0)

    def block(rows_each):
        return pl.BlockSpec((group, rows_each, width), lambda t: (t, 0, 0))

    return call(
        kernel,
        (table, core[None], kept, arrived, *tables),
        [SMEM, SMEM, block(half), block(half)] + [block(count)] * 3,
        [block(count)] * 3,
        [shaped((cap, count, width), F32)] * 3,
        "adam",
        grid=(cap // group,),
        cost_estimate=cost(1e7, 8e6),
    )


def small_kernel(total_ref, far_ref, norm_ref, nm_ref, nv_ref, bias_ref, bm_ref, bv_ref, *outs):
    gains = total_ref[0:2, :] + far_ref[0:2, :]
    for at, rate in enumerate(NORM_RATES):
        here = slice(at, at + 1)
        grad = gains[here] if at < 2 else total_ref[here, :]
        new = adam_step(norm_ref[here, :], nm_ref[here, :], nv_ref[here, :], grad, rate, 0.0)
        for out, value in zip(outs[:3], new):
            out[here, :] = value
    width = total_ref.shape[1]
    for at in range(0, bias_ref.shape[1], width):
        here = slice(at, min(at + width, bias_ref.shape[1]))
        row = 6 + at // width
        grad = total_ref[row : row + 1, : here.stop - at]
        new = adam_step(bias_ref[:, here], bm_ref[:, here], bv_ref[:, here], grad, BIAS_RATE, 0.0)
        for out, value in zip(outs[3:], new):
            out[:, here] = value


def small_call(total, far, norms, biases, deps=()):
    args = (total, far, *norms, *biases)
    kept = [shaped(part.shape, F32) for part in (*norms, *biases)]
    return call(
        small_kernel, args, [whole(arg.shape) for arg in args], [whole(k.shape) for k in kept], kept, "small_update",
        deps,
    )


def swap_mp(array):
    return lax.ppermute(array, "mp", [(0, 1), (1, 0)])


def roll_rows(array, start):
    return lax.dynamic_slice_in_dim(
        jnp.concatenate([array, array], axis=0), start, array.shape[0], axis=0
    )


def body(
    tokens, cotangent, lengths, owners, weight_table, moment_table, square_table,
    norm_params, norm_moment, norm_square, bias_params, bias_moment, bias_square,
):
    dp_size = lax.axis_size("dp")
    mp_size = lax.axis_size("mp")
    heads = HEADS // mp_size
    head_width = heads * HEAD_DIM
    hidden = FF // mp_size
    tok, width = tokens.shape
    slot_cap, piece_len = weight_table.shape[1:3]
    half_len = piece_len // 2
    piece_total = owners.shape[0]
    me = lax.axis_index("dp").astype(I32)
    core = me % 2
    first_core = core == 0

    n_qkv, n_out = 3 * head_width // piece_len, head_width // piece_len
    n_up = hidden // piece_len
    n_first = n_qkv + n_out
    ready = (n_first, piece_total)
    spans = ((0, n_first), (n_first, piece_total))
    routes = Routes(dp_size, slot_cap, piece_total, ready, spans)
    table, place = routes.tables(owners, me)

    own_half, sibling_half = halves_call(core, weight_table[0])
    chip_slots = [own_half, routes.swap_cores(sibling_half)]

    def half(array, which):
        return lax.dynamic_index_in_dim(array, which, axis=1, keepdims=False)

    def unless(bad, usual, other):
        return lax.while_loop(
            lambda state: state[0] > 0, lambda state: (jnp.zeros((), I32), other()), (bad, usual)
        )[1]

    def own_lists(ranges, deps=()):
        return pick_call(
            table, [(place["send"], begin) for begin, _ in ranges], chip_slots,
            [end - begin for begin, end in ranges], "pick_owned", deps,
        )

    def collect(buffers, ranges, deps=()):
        sizes = [high - low for low, high in ranges]
        return pick_call(
            table, [(place["take"], low) for low, _ in ranges], buffers, sizes, "pick_all", deps
        )

    def flat(array):
        return array.reshape(-1, width)

    def pairs_apart(bit):
        return [(device, device ^ bit) for device in range(dp_size)]

    def slow_first():
        everyone, bit = weight_table[0].astype(BF), 1
        while bit < dp_size:
            everyone = jnp.concatenate([everyone, lax.ppermute(everyone, "dp", pairs_apart(bit))], 0)
            bit *= 2
        earlier = (owners[None, :] == owners[:, None]) & (
            jnp.arange(piece_total)[None, :] < jnp.arange(piece_total)[:, None]
        )
        at = (owners ^ me) * slot_cap + jnp.sum(earlier.astype(I32), axis=1)
        mine = half(everyone[at[:n_first]].reshape(n_first, 2, half_len, width), core)
        return mine, mine[n_qkv:]

    stages = routes.out
    chunks = tuple(zip(routes.begins, routes.fill))
    relayed = routes.chips == 8
    if relayed:
        list_a, list_all = ticked(own_lists, (chunks[0], (0, routes.fill[1])))
    else:
        list_a, list_b = ticked(own_lists, [chunk for chunk in chunks if chunk[0] < chunk[1]] * 2)[:2]
    listed = Clock.tick
    list_a = routes.around(list_a, stages[0][0])
    cos, sin, *segs, b_mine, b_other, b_up, start = layout_call(
        core, lengths, bias_params, tok, 3 * head_width // 2, (listed,)
    )
    x, a1 = ticked(norm_call, start, tokens, norm_params)
    gy = ticked(roll_call, start, cotangent, (Clock.tick,))
    turned = Clock.tick

    if relayed:
        own_y = routes.move(list_all, stages[0][1], 1)
        arrived = ticked(join_call, list_a[1:], (turned,))
        buffers_a = list_a + [own_y, routes.move(arrived, stages[0][1], 1)]
        (list_b,) = own_lists(chunks[1:], (Clock.tick, own_y))
        from_two, from_one = (routes.move(list_b, stage, 1) for stage in stages[1][:2])
        turned = Clock.tick
    else:
        buffers_a, buffers_b = list_a, [list_b]
        for stage in stages[0][1:]:
            buffers_a = routes.onward(buffers_a, stage)
    w_first_m, w_out_x = ticked(collect, buffers_a, ((0, n_first), (n_qkv, n_first)), (turned,))
    collected = Clock.tick
    if relayed:
        joined = join_call([from_two, from_one], (collected,))
        relay = routes.move(from_two, stages[1][1], 1)
        y_joined = routes.move(joined, stages[1][2], 1)
    w_first_m, w_out_x = unless(table[place["late"], 0], (w_first_m, w_out_x), slow_first)
    b_qkv = keep_call((b_mine, b_other), (collected,))
    w_first_o = routes.swap_cores(w_first_m)
    qkv_m, qkv_o, safe = ticked(
        qkv_call, a1, flat(w_first_m), flat(w_first_o), *b_qkv, cos, sin
    )
    w_out_x = swap_mp(hand_call((w_out_x,), (Clock.tick,))[0])
    if relayed:
        relay = ticked(join_call, [relay], (Clock.tick,))
        collected = Clock.tick
        y_relay = routes.move(relay, stages[1][2], 1)
        buffers_b = [list_b, from_two, from_one, relay, y_joined, y_relay]
    elif chunks[1][0] < chunks[1][1]:
        for stage in stages[1]:
            buffers_b = routes.onward(buffers_b, stage)
    else:
        buffers_b = []
    half_way = 2 * TILE
    cut = heads // 2
    groups = ((0, cut), (cut, heads - cut))
    ctx_a1, logs_a1, ctx_b1, logs_b1 = ticked(
        attend_call, half_way, safe, segs, qkv_m, qkv_o, *groups[0], (collected,)
    )
    attended = Clock.tick
    ctx_a2, logs_a2, ctx_b2, logs_b2 = attend_call(
        half_way, safe, segs, qkv_m, qkv_o, *groups[1], (attended,)
    )
    ctx_a, ctx_b = (ctx_a1, ctx_a2), (ctx_b1, ctx_b2)
    (w_out_x,) = hand_call((w_out_x,), (attended,))
    w_out_x = [flat(w_out_x), flat(routes.swap_cores(w_out_x))]
    ctx_ax, ctx_bx = ([swap_mp(part) for part in ctx] for ctx in (ctx_a, ctx_b))
    (w_mine,) = ticked(collect, buffers_a + buffers_b, ((n_first, piece_total),), (logs_b2,))
    (b_up,) = keep_call((b_up,), (Clock.tick,))
    w_mine, w_other = flat(w_mine), flat(routes.swap_cores(w_mine))
    w_first = [flat(w_first_m), flat(w_first_o)]
    spans_tok = ((0, half_way // TILE), (half_way // TILE, tok // TILE))
    def both_ways(own, far):
        return [part for pair in zip(own, far) for part in pair]

    mlp_args = (w_first, w_out_x, w_mine, w_other, b_up, norm_params)
    *filled, g_h2_a, gb_up_a = mlp_call(spans_tok[0], x, gy, both_ways(ctx_a, ctx_ax), *mlp_args)
    *filled, g_h2_b, gb_up_b = mlp_call(spans_tok[1], x, gy, both_ways(ctx_b, ctx_bx), *mlp_args, filled)
    x1, a2, act, g_pre, ffn = filled
    g_h2_ax, g_h2_bx = swap_mp(g_h2_a), swap_mp(g_h2_b)
    g_mlp = mlp_grads_call(act, g_pre, a2, gy)

    def pieces(array):
        return array.reshape(-1, half_len, width)

    def sort_out(number, level, parts, small=None, deps=()):
        stage = routes.back[number][level - 1]
        size = stage[1]
        lists = ticked(
            add_pick_call,
            table,
            [(place[("back", number, level, shift)], 0) for shift in range(size)],
            parts,
            [routes.span_limit(number, level)] * size,
            small=small,
            extra=() if small is None else range(1, size),
            deps=deps,
        )
        moved = [routes.move(lists[shift], stage, shift) for shift in range(1, size)]
        return [lists[0]] + moved, lists[-1]

    gx1, g_ctx_a, g_out_a, mid_a, g_mlp_m, g_mlp_o = mid_call(
        spans_tok[0], x1, gy, g_h2_a, g_h2_ax, ctx_a, *w_first, norm_params, (), g_mlp
    )
    back = (segs, cos, sin, qkv_m, qkv_o)
    early_one = ticked(attend_back_call, 0, half_way, *back, g_ctx_a, ctx_a1, logs_a1, *groups[0])
    parts_mlp, listed = sort_out(
        1, 1, [pieces(g_mlp_m), routes.swap_cores(pieces(g_mlp_o))], deps=(Clock.tick,)
    )
    early_two = ticked(
        attend_back_call, 0, half_way, *back, g_ctx_a, ctx_a2, logs_a2, *groups[1], deps=(listed,)
    )
    attended = Clock.tick
    gx1, g_ctx_b, g_out_b, mid_b, ffn = mid_call(
        spans_tok[1], x1, gy, g_h2_b, g_h2_bx, ctx_b, *w_first, norm_params, (gx1,), (ffn,), (attended,)
    )
    ffn_other = swap_mp(ffn)

    (grads_one,) = ticked(
        attend_back_call, half_way, LONGEST, *back, g_ctx_b, ctx_b1, logs_b1, *groups[0], early_one
    )
    (grads_two,) = ticked(
        attend_back_call, half_way, LONGEST, *back, g_ctx_b, ctx_b2, logs_b2, *groups[1], early_two, (Clock.tick,)
    )
    back_grads = (grads_one, grads_two)
    g_in_m, g_in_o = ticked(in_grads_call, back_grads, a1, (g_out_a, g_out_b))
    in_ready = Clock.tick
    parts_mlp, listed = sort_out(1, 2, parts_mlp, deps=(in_ready,))
    sorted_mlp = Clock.tick
    parts_in = [pieces(g_in_m), routes.swap_cores(pieces(g_in_o))]
    parts_in, listed = sort_out(0, 1, parts_in, deps=(sorted_mlp,))
    g_h1, small = in_back_call(
        back_grads, core, x, *w_first, (mid_a, mid_b), (gb_up_a, gb_up_b), (listed,)
    )
    g_h1_other = swap_mp(g_h1)
    for level in range(2, len(routes.back[0])):
        parts_in, _ = sort_out(0, level, parts_in)
    out_roll = ticked(out_call, x1, ffn, ffn_other, norm_params, (sorted_mlp,))
    block_out = roll_rows(out_roll, tok - start[0])
    filled = Clock.tick
    (small,) = hand_call((small,), (filled,))
    apart = routes.swap_cores(small)
    ticked(keep_call, (norm_params,), (filled,))
    small = sum_call(small, apart, (Clock.tick,))
    for stage in routes.back[0][:-1]:
        terms = routes.around(small, stage)
        while len(terms) > 1:
            middle = len(terms) // 2
            terms = [a + b for a, b in zip(terms[:middle], terms[middle:])]
        small = terms[0]
    for level in range(3, len(routes.back[1]) + 1):
        parts_mlp, _ = sort_out(1, level, parts_mlp, deps=(filled,))
    late_mlp = Clock.tick
    lists = sort_out(0, len(routes.back[0]), parts_in, small, (block_out,))
    parts_in, small = lists
    staged = Clock.tick
    grad_roll = ticked(last_call, x, gx1, g_h1, g_h1_other, norm_params, (late_mlp, staged))
    grad_tokens = roll_rows(grad_roll, tok - start[0])

    kept, sent, small = owned_call(table, place, routes, (parts_in, parts_mlp), small, (grad_tokens,))
    small_x = swap_mp(small)
    arrived = routes.swap_cores(sent)

    def slow_grads():
        def stack(in_part, mlp_part):
            return jnp.concatenate([pieces(in_part), pieces(mlp_part)], axis=0).astype(F32)

        mine, other = stack(g_in_m, g_mlp_m), stack(g_in_o[: g_in_m.shape[0]], g_mlp_o)
        both = jnp.where(first_core, jnp.stack([mine, other], 1), jnp.stack([other, mine], 1))
        total, bit = both, 1
        while bit < dp_size:
            total = total + lax.ppermute(total, "dp", pairs_apart(bit))
            bit *= 2
        total = total[jnp.maximum(table[place["piece"], :slot_cap], 0)]
        return half(total, core), half(total, 1 - core)

    tables = (weight_table[0], moment_table[0], square_table[0])

    def update(kept, arrived, tables):
        return ticked(
            adam_call, table, place["piece"], core, (n_qkv, n_first, n_first + n_up), kept, arrived, tables
        )

    tables_next = update(kept, arrived, keep_call(tables, (staged,)))
    updated = Clock.tick
    tables_next = unless(table[place["over"], 0], tuple(tables_next), lambda: tuple(update(*slow_grads(), tables)))
    small_out = small_call(
        small, small_x,
        (norm_params, norm_moment, norm_square), (bias_params, bias_moment, bias_square),
        (updated,),
    )
    return (block_out, grad_tokens, *(part[None] for part in tables_next), *small_out)


def solution(mesh):
    flat = P("dp", None)
    pieces = P("mp", "dp", None, None)
    bias = P("mp", None)
    return jax.shard_map(
        body,
        mesh=mesh,
        in_specs=(flat, flat, flat, P(), pieces, pieces, pieces, P(), P(), P(), bias, bias, bias),
        out_specs=(flat, flat, pieces, pieces, pieces, P(), P(), P(), bias, bias, bias),
        check_vma=False,
    )
```
